32 devices in a mesh: band: 16 (over z, x, core), tile: 2 (over y).
Axes of the slice: x: 2, y: 2, z: 4, core: 2. Of those that a mesh axis runs over, the one named last changes fastest.
Arguments:
- alm: bfloat16 [1024, 9, 2, 1024], P('band', None, None, 'tile'), may hold values from -22 to 22
- legendre: bfloat16 [1024, 1024, 256], P('band', 'tile'), may hold values from -0.1875 to 0.1875
- order_of_slot: int32 [1024], replicated, may hold values from 0 to 1023, each once
Outputs:
- ilc_map: float32 [256, 4096], P('band', 'tile')
- ilc_alm: float32 [1024, 2, 1024], P('band', None, 'tile')
The draws below stay inside these ranges and needn't reach their ends.
Inputs may be any that keep to these rules, and one draw needn't show every extreme that they name: `order_of_slot`: every order 0 to 1023 stands in exactly one slot.
All inputs are finite; a program needn't handle non-finite values.
Results may differ from the reference program's by a relative error of at most 0.02.
Values may be sent and summed in bfloat16 or wider, within the bound.
No kernel may reach another device: no remote copies, remote signals or barrier semaphores. Data moves between devices by JAX's collectives and lax.ppermute only.
A program may use at most 128 MiB of HBM per device.

```python
import math
import jax
import jax.numpy as jnp
from jax import lax

C = 9
L = 1024
NLON = 4096
HALO = 32
CYCLES = 256
N_TILE = 2


def draw_alm(key, part):
    subkeys = jax.random.split(key, 4)
    response = jax.random.uniform(subkeys[0], (C,), jnp.float32, 0.6, 1.4)
    noise_level = jnp.exp(jax.random.uniform(subkeys[1], (C,), jnp.float32, math.log(0.3), math.log(3.0)))
    common = jnp.clip(jax.random.normal(subkeys[2], (L, 1, 2, L), jnp.float32), -5.0, 5.0)
    separate = jnp.clip(jax.random.normal(subkeys[3], (L, C, 2, L), jnp.float32), -5.0, 5.0)
    values = response[None, :, None, None] * common + noise_level[None, :, None, None] * separate
    return values.astype(jnp.bfloat16)


def shard_levels(stream_key, shape, cuts, least, high):
    level = 1.0
    for axis_at, blocks in cuts:
        heights = jax.random.uniform(jax.random.fold_in(jax.random.fold_in(stream_key, 6), axis_at), (blocks,), jnp.float32, least / len(cuts), high / len(cuts))
        level = level * jnp.repeat(jnp.exp(heights), shape[axis_at] // blocks).reshape((-1,) + (1,) * (len(shape) - 1 - axis_at))
    return level


def normal_values(stream_key, extent, spread, reach, shards=(), kind=jnp.bfloat16):
    array = spread * jax.random.normal(stream_key, extent, jnp.float32)
    if shards:
        array = array * shard_levels(stream_key, extent, shards, -0.22, 0.18)
    return jnp.clip(array, -reach, reach).astype(kind)


def setup_inputs(seed: int = 0) -> dict:
    keys = jax.random.split(jax.random.key(seed), 4)
    return {
        "alm": draw_alm(jax.random.fold_in(keys[3], 71), 0),
        "legendre": normal_values(keys[1], (L, L, CYCLES), L ** -0.5, 0.1875, ((0, 16), (1, 2))),
        "order_of_slot": jax.random.permutation(keys[2], L).astype(jnp.int32),
    }


RIDGE = 0.1
EPSILON = 1e-06

def make_basis(order_of_slot, begin_at, cell_count):
    columns = begin_at + jnp.arange(cell_count, dtype=jnp.int32)
    phases = order_of_slot[:, None] * columns[None, :] % NLON
    angles = phases.astype(jnp.float32) * (2.0 * math.pi / NLON)
    scaling = 1.0 / math.sqrt(L)
    return jnp.stack([jnp.cos(angles) * scaling, -jnp.sin(angles) * scaling]).astype(jnp.bfloat16)

def pair_table():
    return [(a_at, b_at) for a_at in range(C) for b_at in range(a_at, C)]

def window_sum(products):
    span_cells = products.shape[2]
    width_cells = span_cells - 2 * HALO
    total = products
    span = 1
    while span < 2 * HALO:
        total = total[:, :, :-span] + total[:, :, span:]
        span = span * 2
    return total[:, :, :width_cells] + products[:, :, 2 * HALO:2 * HALO + width_cells]

def smooth_pairs(padded):
    widened = padded.astype(jnp.float32)
    products = jnp.stack([widened[a_at] * widened[b_at] for a_at, b_at in pair_table()])
    return window_sum(products) / (2 * HALO + 1)

def solve_weights(smoothed):
    entries = {}
    for pair_at, (a_at, b_at) in enumerate(pair_table()):
        entries[a_at, b_at] = smoothed[pair_at]
    trace_mean = entries[0, 0]
    for chan_at in range(1, C):
        trace_mean = trace_mean + entries[chan_at, chan_at]
    ridge_term = RIDGE * (trace_mean / C + EPSILON)
    factor = {}
    for row_at in range(C):
        for col_at in range(row_at + 1):
            running = entries[col_at, row_at]
            if row_at == col_at:
                running = running + ridge_term
            for inner_at in range(col_at):
                running = running - factor[row_at, inner_at] * factor[col_at, inner_at]
            if row_at == col_at:
                factor[row_at, row_at] = jnp.sqrt(running)
            else:
                factor[row_at, col_at] = running / factor[col_at, col_at]
    forward = []
    for row_at in range(C):
        running = jnp.ones_like(ridge_term)
        for inner_at in range(row_at):
            running = running - factor[row_at, inner_at] * forward[inner_at]
        forward.append(running / factor[row_at, row_at])
    backward = [forward[0]] * C
    for row_at in reversed(range(C)):
        running = forward[row_at]
        for inner_at in range(row_at + 1, C):
            running = running - factor[inner_at, row_at] * backward[inner_at]
        backward[row_at] = running / factor[row_at, row_at]
    normal = backward[0]
    for chan_at in range(1, C):
        normal = normal + backward[chan_at]
    return jnp.stack([solved / normal for solved in backward])

def low_then_float(values):
    return lax.optimization_barrier(values.astype(jnp.bfloat16)).astype(jnp.float32)

def reference(alm, legendre, order_of_slot):
    cycle_total = legendre.shape[2]
    block_len = L // N_TILE
    cycle_sum = jnp.zeros((L, C, 2, cycle_total), jnp.float32)
    for block_at in range(N_TILE):
        alm_block = lax.slice_in_dim(alm, block_at * block_len, (block_at + 1) * block_len, axis=3).astype(jnp.float32)
        table_block = lax.slice_in_dim(legendre, block_at * block_len, (block_at + 1) * block_len, axis=1).astype(jnp.float32)
        block_term = jnp.einsum('scel,slr->scer', alm_block, table_block)
        cycle_sum = cycle_sum + low_then_float(block_term)
    cycle_modes = low_then_float(cycle_sum)
    basis = make_basis(order_of_slot, 0, NLON).astype(jnp.float32)
    channel_maps = jnp.einsum('scer,esx->crx', cycle_modes, basis).astype(jnp.bfloat16)
    padded = jnp.concatenate([channel_maps[:, :, NLON - HALO:], channel_maps, channel_maps[:, :, :HALO]], axis=2)
    block_cells = 512 if NLON % 512 == 0 else NLON
    pieces = []
    for block_at in range(NLON // block_cells):
        window = lax.slice_in_dim(padded, block_at * block_cells, block_at * block_cells + block_cells + 2 * HALO, axis=2)
        weights = solve_weights(smooth_pairs(window))
        source = lax.slice_in_dim(channel_maps, block_at * block_cells, (block_at + 1) * block_cells, axis=2).astype(jnp.float32)
        pieces.append(lax.optimization_barrier(jnp.sum(weights * source, axis=0)))
    ilc_map = jnp.concatenate(pieces, axis=1)
    map_float = low_then_float(ilc_map)
    cycle_spectra = low_then_float(jnp.einsum('rx,esx->res', map_float, basis))
    outputs = []
    for block_at in range(N_TILE):
        table_block = lax.slice_in_dim(legendre, block_at * block_len, (block_at + 1) * block_len, axis=1).astype(jnp.float32)
        outputs.append(jnp.einsum('slr,res->sel', table_block, cycle_spectra))
    ilc_alm = jnp.concatenate(outputs, axis=2)
    return (ilc_map, ilc_alm)
```

```python
import functools
import math

import jax
import jax.numpy as jnp
from jax import lax
from jax.experimental import pallas as pl
from jax.experimental.pallas import tpu as pltpu
from jax.sharding import PartitionSpec as P

C = 9
L = 1024
NLON = 4096
HALO = 32

RIDGE = 0.1
EPSILON = 1e-06

WINDOW = 2 * HALO + 1
LANES = NLON // HALO
HALF = LANES // 2
PAIRS = [(a_at, b_at) for a_at in range(C) for b_at in range(a_at, C)]
VMEM_LIMIT = 48 * 1024 * 1024


def round_up(value, multiple):
    return (value + multiple - 1) // multiple * multiple


def cos_turns(turns):
    away = jnp.abs(turns - jnp.floor(turns + 0.5))
    quarter = 1.0 - 4.0 * away
    square = quarter * quarter
    tail = square * (1.6044118478736e-04 - square * 3.598843235e-06)
    tail = square * (-4.68175413531868e-03 + tail)
    tail = square * (7.96926262461670e-02 + tail)
    tail = square * (-6.45964097506246e-01 + tail)
    return quarter * (1.57079632679490 + tail)


def basis_kernel(order_ref, basis_ref):
    rows = order_ref.shape[0]
    order = jnp.broadcast_to(order_ref[...], (rows, LANES))
    row = lax.broadcasted_iota(jnp.int32, (rows, LANES), 0)
    lane = lax.broadcasted_iota(jnp.int32, (rows, LANES), 1)
    cell = HALO * (lane % HALF) + lane // HALF
    turns = order * (cell.astype(jnp.float32) / NLON) + (row % 2).astype(jnp.float32) * 0.25
    step = order * (2.0 / NLON)
    scaling = 1.0 / math.sqrt(L)
    before = cos_turns(turns) * scaling
    now = cos_turns(turns + step) * scaling
    twice = 2.0 * cos_turns(step)
    for at in range(HALO // 2):
        basis_ref[at // 2, :, at % 2 * LANES : (at % 2 + 1) * LANES] = before.astype(jnp.bfloat16)
        if at < HALO // 2 - 1:
            before, now = now, twice * now - before


def make_basis(order_rows):
    rows = order_rows.shape[0]
    block = 128
    chunks = HALO // 4
    return pl.pallas_call(
        basis_kernel,
        grid=(rows // block,),
        in_specs=[pl.BlockSpec((block, 1), lambda at: (at, 0))],
        out_specs=pl.BlockSpec((chunks, block, 2 * LANES), lambda at: (0, at, 0)),
        out_shape=jax.ShapeDtypeStruct((chunks, rows, 2 * LANES), jnp.bfloat16),
        cost_estimate=pl.CostEstimate(
            flops=rows * chunks * 2 * LANES * 8, bytes_accessed=rows * chunks * 4 * LANES, transcendentals=0
        ),
        compiler_params=pltpu.CompilerParams(vmem_limit_bytes=VMEM_LIMIT),
    )(order_rows)


def combine(entries, maps):
    entries = dict(entries)
    trace = entries[0, 0]
    for at in range(1, C):
        trace = trace + entries[at, at]
    ridge = RIDGE * (trace * (1.0 / C) + WINDOW * EPSILON)
    for at in range(C):
        entries[at, at] = entries[at, at] + ridge
    ones = [None] * C
    maps = list(maps)
    top = bottom = None
    for at in range(C):
        inverse = 1.0 / entries[at, at]
        scaled = inverse if at == 0 else inverse * ones[at]
        term = scaled * maps[at]
        top = term if top is None else top + term
        term = scaled if at == 0 else scaled * ones[at]
        bottom = term if bottom is None else bottom + term
        for row in range(at + 1, C):
            ratio = entries[at, row] * inverse
            ones[row] = 1.0 - ratio if at == 0 else ones[row] - ratio * ones[at]
            maps[row] = maps[row] - ratio * maps[at]
            for col in range(row, C):
                entries[row, col] = entries[row, col] - ratio * entries[at, col]
    return top / bottom


def ilc_kernel(modes_ref, odd_ref, basis_hbm, ilc_ref, spectra_ref, basis_ref, lhs_ref, maps_ref, sums_ref, low_ref, sems):
    groups, rows, width = modes_ref.shape
    chunks = basis_ref.shape[0]
    cycles = rows // C
    second = round_up(rows, 16)
    for chunk in range(chunks):
        pltpu.make_async_copy(basis_hbm.at[chunk], basis_ref.at[chunk], sems.at[chunk]).start()
    for group in range(groups):
        span = slice(group * width, (group + 1) * width)
        odd = odd_ref[:, span]
        values = modes_ref[group].astype(jnp.float32)
        lhs_ref[0:rows, span] = (values * (1.0 - odd)).astype(jnp.bfloat16)
        lhs_ref[second : second + rows, span] = (values * odd).astype(jnp.bfloat16)
    low_half = lax.broadcasted_iota(jnp.int32, (cycles, LANES), 1) < HALF
    for chunk in range(chunks):
        pltpu.make_async_copy(basis_hbm.at[chunk], basis_ref.at[chunk], sems.at[chunk]).wait()
        result = jnp.dot(lhs_ref[...], basis_ref[chunk], preferred_element_type=jnp.float32)
        for part in range(2):
            at = 4 * chunk + 2 * part
            even_part = result[0:rows, part * LANES : (part + 1) * LANES]
            odd_part = result[second : second + rows, part * LANES : (part + 1) * LANES]
            near = even_part + odd_part
            far = even_part - odd_part
            wide = jnp.concatenate([low_half] * C, axis=0)
            maps_ref[at] = jnp.where(wide, near, pltpu.roll(far, HALF, 1))
            maps_ref[at + 1] = jnp.where(wide, pltpu.roll(near, HALF, 1), far)

    def maps_at(at):
        return [maps_ref[at, chan * cycles : (chan + 1) * cycles, :] for chan in range(C)]

    for first in range(0, len(PAIRS), 15):
        some = PAIRS[first : first + 15]

        def add(at, totals, some=some):
            values = maps_at(at)
            return tuple(total + values[a_at] * values[b_at] for total, (a_at, b_at) in zip(totals, some))

        zero = jnp.zeros((cycles, LANES), jnp.float32)
        totals = lax.fori_loop(0, HALO, add, (zero,) * len(some))
        for pair, total in enumerate(totals):
            sums_ref[first + pair] = total + pltpu.roll(total, 1, 1)

    def smooth(at, leaves):
        ahead = [pltpu.roll(value, LANES - 1, 1) for value in maps_at(at)]
        behind = [pltpu.roll(value, 1, 1) for value in maps_at(jnp.maximum(at - 1, 0))]
        behind = [value * leaves for value in behind]
        entries = {}
        for pair, (a_at, b_at) in enumerate(PAIRS):
            total = sums_ref[pair] + (ahead[a_at] * ahead[b_at] - behind[a_at] * behind[b_at])
            sums_ref[pair] = total
            entries[a_at, b_at] = total
        return entries

    def two_vectors(pair_at, carry):
        at = 2 * pair_at
        found = []
        for part in range(2):
            leaves = jnp.where(at == 0, 0.0, 1.0) if part == 0 else 1.0
            value = combine(smooth(at + part, leaves), maps_at(at + part))
            ilc_ref[at + part] = value
            found.append(value)
        near = jnp.where(low_half, found[0], pltpu.roll(found[1], HALF, 1))
        far = jnp.where(low_half, pltpu.roll(found[0], HALF, 1), found[1])
        low_ref[pair_at] = jnp.concatenate([near, far], axis=0).astype(jnp.bfloat16)
        return carry

    lax.fori_loop(0, HALO // 2, two_vectors, 0)

    result = jnp.zeros((2 * cycles, groups * width), jnp.float32)
    for chunk in range(chunks):
        lhs = jnp.concatenate([low_ref[2 * chunk], low_ref[2 * chunk + 1]], axis=1)
        result = result + lax.dot_general(
            lhs, basis_ref[chunk], (((1,), (1,)), ((), ())), preferred_element_type=jnp.float32
        )
    for group in range(groups):
        span = slice(group * width, (group + 1) * width)
        sign = 1.0 - 2.0 * odd_ref[:, span]
        spectra_ref[group] = (result[0:cycles, span] + sign * result[cycles:, span]).astype(jnp.bfloat16)


def run_ilc(modes, odd, basis):
    groups, rows, width = modes.shape
    chunks, depth, columns = basis.shape
    cycles = rows // C
    vmem = pl.BlockSpec(memory_space=pltpu.VMEM)
    return pl.pallas_call(
        ilc_kernel,
        in_specs=[vmem, vmem, pl.BlockSpec(memory_space=pl.ANY)],
        out_specs=[vmem, vmem],
        out_shape=[
            jax.ShapeDtypeStruct((HALO, cycles, LANES), jnp.float32),
            jax.ShapeDtypeStruct((groups, cycles, width), jnp.bfloat16),
        ],
        scratch_shapes=[
            pltpu.VMEM((chunks, depth, columns), jnp.bfloat16),
            pltpu.VMEM((2 * round_up(rows, 16), depth), jnp.bfloat16),
            pltpu.VMEM((HALO, rows, LANES), jnp.float32),
            pltpu.VMEM((len(PAIRS), cycles, LANES), jnp.float32),
            pltpu.VMEM((HALO // 2, 2 * cycles, LANES), jnp.bfloat16),
            pltpu.SemaphoreType.DMA((chunks,)),
        ],
        cost_estimate=pl.CostEstimate(
            flops=2 * chunks * depth * columns * (2 * rows + 2 * cycles),
            bytes_accessed=chunks * depth * columns * 2,
            transcendentals=0,
        ),
        compiler_params=pltpu.CompilerParams(vmem_limit_bytes=VMEM_LIMIT),
    )(modes, odd, basis)


def from_other_tiles(send):
    count = lax.axis_size("tile")
    got = [send(0)]
    for hop in range(1, count):
        got.append(lax.ppermute(send(hop), "tile", [(at, (at + hop) % count) for at in range(count)]))
    return got


def in_tile_order(got):
    count = len(got)
    tile_at = lax.axis_index("tile")
    stacked = jnp.stack(got)
    return jnp.stack(
        [lax.dynamic_index_in_dim(stacked, (tile_at - at) % count, 0, keepdims=False) for at in range(count)]
    )


def body(alm, legendre, order_of_slot):
    tile_count = lax.axis_size("tile")
    band_count = lax.axis_size("band")
    tile_at = lax.axis_index("tile")
    slot_count = alm.shape[0]
    cycles = legendre.shape[2] // (band_count * tile_count)
    padded = round_up(cycles, 8)
    depth = 2 * L
    width = 2 * slot_count
    group_width = math.lcm(width, LANES)
    groups = depth // group_width

    partial = jnp.einsum("scel,slr->scer", alm, legendre, preferred_element_type=jnp.float32)
    partial = partial.astype(jnp.bfloat16).reshape(slot_count, C, 2, band_count, tile_count, cycles)
    partial = partial.transpose(4, 3, 1, 5, 0, 2).reshape(tile_count, band_count, C * cycles, width)
    got = from_other_tiles(
        lambda hop: lax.dynamic_index_in_dim(partial, (tile_at + hop) % tile_count, 0, keepdims=False)
    )
    total = got[0].astype(jnp.float32)
    for other in got[1:]:
        total = total + other.astype(jnp.float32)
    modes = lax.all_to_all(total.astype(jnp.bfloat16), "band", split_axis=0, concat_axis=0, tiled=True)
    if group_width != width:
        modes = modes.reshape(groups, group_width // width, C * cycles, width)
        modes = modes.transpose(0, 2, 1, 3).reshape(groups, C * cycles, group_width)
    if padded != cycles:
        modes = modes.reshape(groups, C, cycles, group_width)
        modes = jnp.pad(modes, ((0, 0), (0, 0), (0, padded - cycles), (0, 0)))
        modes = modes.reshape(groups, C * padded, group_width)

    order_rows = jnp.repeat(order_of_slot, 2)
    basis = make_basis(order_rows.astype(jnp.float32)[:, None])
    odd = (order_rows % 2).astype(jnp.float32)[None, :]
    vectors, spectra = run_ilc(modes, odd, basis)

    spectra = spectra[:, :cycles]
    if group_width != width:
        spectra = spectra.reshape(groups, cycles, group_width // width, width)
        spectra = spectra.transpose(0, 2, 1, 3).reshape(band_count, cycles, width)
    routed = lax.all_to_all(spectra, "band", split_axis=0, concat_axis=0, tiled=True)
    cycle_spectra = in_tile_order(from_other_tiles(lambda hop: routed))
    cycle_spectra = cycle_spectra.transpose(1, 0, 2, 3).reshape(band_count * tile_count * cycles, slot_count, 2)
    ilc_alm = jnp.einsum("slr,rse->sel", legendre, cycle_spectra, preferred_element_type=jnp.float32)

    own = vectors[:, :cycles].transpose(1, 2, 0).reshape(cycles, tile_count, NLON // tile_count)
    own = own.transpose(1, 0, 2)
    ilc_map = in_tile_order(
        from_other_tiles(lambda hop: lax.dynamic_index_in_dim(own, (tile_at + hop) % tile_count, 0, keepdims=False))
    )
    return (ilc_map.reshape(tile_count * cycles, NLON // tile_count), ilc_alm)


def solution(mesh):
    placed = (P("band", None, None, "tile"), P("band", "tile", None), P())
    return jax.shard_map(
        body,
        mesh=mesh,
        in_specs=placed,
        out_specs=(P("band", "tile"), P("band", None, "tile")),
        check_vma=False,
    )
```

```python
import functools
import math

import jax
import jax.numpy as jnp
from jax import lax
from jax.experimental import pallas as pl
from jax.experimental.pallas import tpu as pltpu
from jax.sharding import PartitionSpec as P

C = 9
L = 1024
NLON = 4096
HALO = 32

RIDGE = 0.1
EPSILON = 1e-06

WINDOW = 2 * HALO + 1
LANES = NLON // HALO
HALF = LANES // 2
PAIRS = [(a_at, b_at) for a_at in range(C) for b_at in range(a_at, C)]
VMEM_LIMIT = 48 * 1024 * 1024


def round_up(value, multiple):
    return (value + multiple - 1) // multiple * multiple


def cos_turns(turns):
    away = jnp.abs(turns - jnp.floor(turns + 0.5))
    quarter = 1.0 - 4.0 * away
    square = quarter * quarter
    tail = square * (1.6044118478736e-04 - square * 3.598843235e-06)
    tail = square * (-4.68175413531868e-03 + tail)
    tail = square * (7.96926262461670e-02 + tail)
    tail = square * (-6.45964097506246e-01 + tail)
    return quarter * (1.57079632679490 + tail)


def basis_kernel(order_ref, basis_ref):
    rows = order_ref.shape[0]
    order = jnp.broadcast_to(order_ref[...], (rows, LANES))
    row = lax.broadcasted_iota(jnp.int32, (rows, LANES), 0)
    lane = lax.broadcasted_iota(jnp.int32, (rows, LANES), 1)
    cell = HALO * (lane % HALF) + lane // HALF
    turns = order * (cell.astype(jnp.float32) / NLON) + (row % 2).astype(jnp.float32) * 0.25
    step = order * (2.0 / NLON)
    scaling = 1.0 / math.sqrt(L)
    before = cos_turns(turns) * scaling
    now = cos_turns(turns + step) * scaling
    twice = 2.0 * cos_turns(step)
    for at in range(HALO // 2):
        basis_ref[at // 2, :, at % 2 * LANES : (at % 2 + 1) * LANES] = before.astype(jnp.bfloat16)
        if at < HALO // 2 - 1:
            before, now = now, twice * now - before


def make_basis(order_rows):
    rows = order_rows.shape[0]
    block = 128
    chunks = HALO // 4
    return pl.pallas_call(
        basis_kernel,
        grid=(rows // block,),
        in_specs=[pl.BlockSpec((block, 1), lambda at: (at, 0))],
        out_specs=pl.BlockSpec((chunks, block, 2 * LANES), lambda at: (0, at, 0)),
        out_shape=jax.ShapeDtypeStruct((chunks, rows, 2 * LANES), jnp.bfloat16),
        cost_estimate=pl.CostEstimate(
            flops=rows * chunks * 2 * LANES * 8, bytes_accessed=rows * chunks * 4 * LANES, transcendentals=0
        ),
        compiler_params=pltpu.CompilerParams(vmem_limit_bytes=VMEM_LIMIT),
    )(order_rows)


def combine(entries, maps):
    entries = dict(entries)
    trace = entries[0, 0]
    for at in range(1, C):
        trace = trace + entries[at, at]
    ridge = RIDGE * (trace * (1.0 / C) + WINDOW * EPSILON)
    for at in range(C):
        entries[at, at] = entries[at, at] + ridge
    ones = [None] * C
    maps = list(maps)
    top = bottom = None
    for at in range(C):
        inverse = 1.0 / entries[at, at]
        scaled = inverse if at == 0 else inverse * ones[at]
        term = scaled * maps[at]
        top = term if top is None else top + term
        term = scaled if at == 0 else scaled * ones[at]
        bottom = term if bottom is None else bottom + term
        for row in range(at + 1, C):
            ratio = entries[at, row] * inverse
            ones[row] = 1.0 - ratio if at == 0 else ones[row] - ratio * ones[at]
            maps[row] = maps[row] - ratio * maps[at]
            for col in range(row, C):
                entries[row, col] = entries[row, col] - ratio * entries[at, col]
    return top / bottom


def ilc_kernel(modes_ref, odd_ref, basis_hbm, ilc_ref, spectra_ref, basis_ref, lhs_ref, maps_ref, sums_ref, low_ref, sems):
    groups, rows, width = modes_ref.shape
    chunks = basis_ref.shape[0]
    cycles = rows // C
    second = round_up(rows, 16)
    for chunk in range(chunks):
        pltpu.make_async_copy(basis_hbm.at[chunk], basis_ref.at[chunk], sems.at[chunk]).start()
    for group in range(groups):
        span = slice(group * width, (group + 1) * width)
        odd = odd_ref[:, span]
        values = modes_ref[group].astype(jnp.float32)
        lhs_ref[0:rows, span] = (values * (1.0 - odd)).astype(jnp.bfloat16)
        lhs_ref[second : second + rows, span] = (values * odd).astype(jnp.bfloat16)
    low_half = lax.broadcasted_iota(jnp.int32, (cycles, LANES), 1) < HALF
    for chunk in range(chunks):
        pltpu.make_async_copy(basis_hbm.at[chunk], basis_ref.at[chunk], sems.at[chunk]).wait()
        result = jnp.dot(lhs_ref[...], basis_ref[chunk], preferred_element_type=jnp.float32)
        for part in range(2):
            at = 4 * chunk + 2 * part
            even_part = result[0:rows, part * LANES : (part + 1) * LANES]
            odd_part = result[second : second + rows, part * LANES : (part + 1) * LANES]
            near = even_part + odd_part
            far = even_part - odd_part
            wide = jnp.concatenate([low_half] * C, axis=0)
            maps_ref[at] = jnp.where(wide, near, pltpu.roll(far, HALF, 1))
            maps_ref[at + 1] = jnp.where(wide, pltpu.roll(near, HALF, 1), far)

    def maps_at(at):
        return [maps_ref[at, chan * cycles : (chan + 1) * cycles, :] for chan in range(C)]

    for first in range(0, len(PAIRS), 15):
        some = PAIRS[first : first + 15]

        def add(at, totals, some=some):
            values = maps_at(at)
            return tuple(total + values[a_at] * values[b_at] for total, (a_at, b_at) in zip(totals, some))

        zero = jnp.zeros((cycles, LANES), jnp.float32)
        totals = lax.fori_loop(0, HALO, add, (zero,) * len(some))
        for pair, total in enumerate(totals):
            sums_ref[first + pair] = total + pltpu.roll(total, 1, 1)

    def smooth(at, leaves):
        ahead = [pltpu.roll(value, LANES - 1, 1) for value in maps_at(at)]
        behind = [pltpu.roll(value, 1, 1) for value in maps_at(jnp.maximum(at - 1, 0))]
        behind = [value * leaves for value in behind]
        entries = {}
        for pair, (a_at, b_at) in enumerate(PAIRS):
            total = sums_ref[pair] + (ahead[a_at] * ahead[b_at] - behind[a_at] * behind[b_at])
            sums_ref[pair] = total
            entries[a_at, b_at] = total
        return entries

    def two_vectors(pair_at, carry):
        at = 2 * pair_at
        found = []
        for part in range(2):
            leaves = jnp.where(at == 0, 0.0, 1.0) if part == 0 else 1.0
            value = combine(smooth(at + part, leaves), maps_at(at + part))
            ilc_ref[at + part] = value
            found.append(value)
        near = jnp.where(low_half, found[0], pltpu.roll(found[1], HALF, 1))
        far = jnp.where(low_half, pltpu.roll(found[0], HALF, 1), found[1])
        low_ref[pair_at] = jnp.concatenate([near, far], axis=0).astype(jnp.bfloat16)
        return carry

    lax.fori_loop(0, HALO // 2, two_vectors, 0)

    result = jnp.zeros((2 * cycles, groups * width), jnp.float32)
    for chunk in range(chunks):
        lhs = jnp.concatenate([low_ref[2 * chunk], low_ref[2 * chunk + 1]], axis=1)
        result = result + lax.dot_general(
            lhs, basis_ref[chunk], (((1,), (1,)), ((), ())), preferred_element_type=jnp.float32
        )
    for group in range(groups):
        span = slice(group * width, (group + 1) * width)
        sign = 1.0 - 2.0 * odd_ref[:, span]
        spectra_ref[group] = (result[0:cycles, span] + sign * result[cycles:, span]).astype(jnp.bfloat16)


def run_ilc(modes, odd, basis):
    groups, rows, width = modes.shape
    chunks, depth, columns = basis.shape
    cycles = rows // C
    vmem = pl.BlockSpec(memory_space=pltpu.VMEM)
    return pl.pallas_call(
        ilc_kernel,
        in_specs=[vmem, vmem, pl.BlockSpec(memory_space=pl.ANY)],
        out_specs=[vmem, vmem],
        out_shape=[
            jax.ShapeDtypeStruct((HALO, cycles, LANES), jnp.float32),
            jax.ShapeDtypeStruct((groups, cycles, width), jnp.bfloat16),
        ],
        scratch_shapes=[
            pltpu.VMEM((chunks, depth, columns), jnp.bfloat16),
            pltpu.VMEM((2 * round_up(rows, 16), depth), jnp.bfloat16),
            pltpu.VMEM((HALO, rows, LANES), jnp.float32),
            pltpu.VMEM((len(PAIRS), cycles, LANES), jnp.float32),
            pltpu.VMEM((HALO // 2, 2 * cycles, LANES), jnp.bfloat16),
            pltpu.SemaphoreType.DMA((chunks,)),
        ],
        cost_estimate=pl.CostEstimate(
            flops=2 * chunks * depth * columns * (2 * rows + 2 * cycles),
            bytes_accessed=chunks * depth * columns * 2,
            transcendentals=0,
        ),
        compiler_params=pltpu.CompilerParams(vmem_limit_bytes=VMEM_LIMIT),
    )(modes, odd, basis)


def modes_kernel(alm_ref, table_ref, *refs):
    out_refs, (lhs_ref, held_ref, turned_ref) = refs[:-3], refs[-3:]
    tile_count = len(out_refs)
    slots = table_ref.shape[0]
    bands, rows = out_refs[0].shape[:2]
    cycles = rows // C
    step = pl.program_id(0)
    for slot in range(slots):
        for chan in range(C):
            lhs_ref[slot, 2 * chan : 2 * chan + 2, :] = alm_ref[slot, chan].astype(jnp.float32)
        result = jnp.dot(
            lhs_ref[slot].astype(jnp.bfloat16), table_ref[slot], preferred_element_type=jnp.float32
        )
        for chan in range(C):
            held_ref[chan, step, 2 * slot : 2 * slot + 2, :] = result[2 * chan : 2 * chan + 2]

    @pl.when(step == pl.num_programs(0) - 1)
    def _():
        for chan in range(C):
            turned_ref[chan] = held_ref[chan].reshape(turned_ref.shape[2], turned_ref.shape[1]).T
        tile_at = lax.axis_index("tile")
        for hop in range(tile_count):
            begin = (tile_at + hop) % tile_count * cycles
            for band in range(bands):
                at = band * tile_count * cycles + begin
                if cycles % 8 == 0:
                    at = pl.multiple_of(at, 8)
                block = jnp.concatenate([turned_ref[chan, pl.ds(at, cycles), :] for chan in range(C)], axis=0)
                out_refs[hop][band] = block.astype(jnp.bfloat16)


def make_modes(alm, legendre, band_count, tile_count):
    slot_count, degrees, total = legendre.shape
    slots = 8
    width = 2 * slot_count
    cycles = total // (band_count * tile_count)
    one = jax.ShapeDtypeStruct((band_count, C * cycles, width), jnp.bfloat16)
    whole = pl.BlockSpec(one.shape, lambda at: (0, 0, 0))
    return pl.pallas_call(
        modes_kernel,
        grid=(slot_count // slots,),
        in_specs=[
            pl.BlockSpec((slots, C, 2, degrees), lambda at: (at, 0, 0, 0)),
            pl.BlockSpec((slots, degrees, total), lambda at: (at, 0, 0)),
        ],
        out_specs=[whole] * tile_count,
        out_shape=[one] * tile_count,
        scratch_shapes=[
            pltpu.VMEM((slots, 2 * C, degrees), jnp.float32),
            pltpu.VMEM((C, slot_count // slots, 2 * slots, total), jnp.float32),
            pltpu.VMEM((C, total, width), jnp.float32),
        ],
        cost_estimate=pl.CostEstimate(
            flops=2 * slot_count * degrees * total * 2 * C,
            bytes_accessed=slot_count * degrees * (total + 2 * C) * 2,
            transcendentals=0,
        ),
        compiler_params=pltpu.CompilerParams(vmem_limit_bytes=VMEM_LIMIT),
    )(alm, legendre)


def analysis_kernel(table_ref, *refs):
    spectra_refs, (out_ref, gathered_ref, turned_ref) = refs[:-3], refs[-3:]
    tile_count = len(spectra_refs)
    slots = table_ref.shape[0]
    bands, cycles = spectra_refs[0].shape[:2]
    step = pl.program_id(0)

    @pl.when(step == 0)
    def _():
        tile_at = lax.axis_index("tile")
        for hop in range(tile_count):
            begin = (tile_at + tile_count - hop) % tile_count * cycles
            for band in range(bands):
                at = band * tile_count * cycles + begin
                if cycles % 8 == 0:
                    at = pl.multiple_of(at, 8)
                gathered_ref[pl.ds(at, cycles), :] = spectra_refs[hop][band].astype(jnp.float32)
        turned_ref[...] = gathered_ref[...].T.astype(jnp.bfloat16)

    lhs = turned_ref[pl.ds(pl.multiple_of(step * 2 * slots, 2 * slots), 2 * slots), :]
    for slot in range(slots):
        result = lax.dot_general(
            lhs, table_ref[slot], (((1,), (1,)), ((), ())), preferred_element_type=jnp.float32
        )
        out_ref[slot] = result[2 * slot : 2 * slot + 2]


def analyse(legendre, spectra):
    slot_count, degrees, total = legendre.shape
    slots = 8
    width = 2 * slot_count
    whole = pl.BlockSpec(spectra[0].shape, lambda at: (0, 0, 0))
    return pl.pallas_call(
        analysis_kernel,
        grid=(slot_count // slots,),
        in_specs=[pl.BlockSpec((slots, degrees, total), lambda at: (at, 0, 0))] + [whole] * len(spectra),
        out_specs=pl.BlockSpec((slots, 2, degrees), lambda at: (at, 0, 0)),
        out_shape=jax.ShapeDtypeStruct((slot_count, 2, degrees), jnp.float32),
        scratch_shapes=[pltpu.VMEM((total, width), jnp.float32), pltpu.VMEM((width, total), jnp.bfloat16)],
        cost_estimate=pl.CostEstimate(
            flops=2 * slot_count * degrees * total * 16,
            bytes_accessed=slot_count * degrees * total * 2,
            transcendentals=0,
        ),
        compiler_params=pltpu.CompilerParams(vmem_limit_bytes=VMEM_LIMIT),
    )(legendre, *spectra)


def from_other_tiles(sends):
    count = len(sends)
    got = [sends[0]]
    for hop in range(1, count):
        got.append(lax.ppermute(sends[hop], "tile", [(at, (at + hop) % count) for at in range(count)]))
    return got


def in_tile_order(got):
    count = len(got)
    tile_at = lax.axis_index("tile")
    stacked = jnp.stack(got)
    return jnp.stack(
        [lax.dynamic_index_in_dim(stacked, (tile_at - at) % count, 0, keepdims=False) for at in range(count)]
    )


def body(alm, legendre, order_of_slot):
    tile_count = lax.axis_size("tile")
    band_count = lax.axis_size("band")
    tile_at = lax.axis_index("tile")
    slot_count = alm.shape[0]
    cycles = legendre.shape[2] // (band_count * tile_count)
    padded = round_up(cycles, 8)
    depth = 2 * L
    width = 2 * slot_count
    group_width = math.lcm(width, LANES)
    groups = depth // group_width

    got = from_other_tiles(make_modes(alm, legendre, band_count, tile_count))
    total = got[0].astype(jnp.float32)
    for other in got[1:]:
        total = total + other.astype(jnp.float32)
    modes = lax.all_to_all(total.astype(jnp.bfloat16), "band", split_axis=0, concat_axis=0, tiled=True)
    if group_width != width:
        modes = modes.reshape(groups, group_width // width, C * cycles, width)
        modes = modes.transpose(0, 2, 1, 3).reshape(groups, C * cycles, group_width)
    if padded != cycles:
        modes = modes.reshape(groups, C, cycles, group_width)
        modes = jnp.pad(modes, ((0, 0), (0, 0), (0, padded - cycles), (0, 0)))
        modes = modes.reshape(groups, C * padded, group_width)

    order_rows = jnp.repeat(order_of_slot, 2)
    basis = make_basis(order_rows.astype(jnp.float32)[:, None])
    odd = (order_rows % 2).astype(jnp.float32)[None, :]
    vectors, spectra = run_ilc(modes, odd, basis)

    spectra = spectra[:, :cycles]
    if group_width != width:
        spectra = spectra.reshape(groups, cycles, group_width // width, width)
        spectra = spectra.transpose(0, 2, 1, 3).reshape(band_count, cycles, width)
    routed = lax.all_to_all(spectra, "band", split_axis=0, concat_axis=0, tiled=True)
    ilc_alm = analyse(legendre, from_other_tiles([routed] * tile_count))

    own = vectors[:, :cycles].transpose(1, 2, 0).reshape(cycles, tile_count, NLON // tile_count)
    own = own.transpose(1, 0, 2)
    sends = [
        lax.dynamic_index_in_dim(own, (tile_at + hop) % tile_count, 0, keepdims=False) for hop in range(tile_count)
    ]
    ilc_map = in_tile_order(from_other_tiles(sends))
    return (ilc_map.reshape(tile_count * cycles, NLON // tile_count), ilc_alm)


def solution(mesh):
    placed = (P("band", None, None, "tile"), P("band", "tile", None), P())
    return jax.shard_map(
        body,
        mesh=mesh,
        in_specs=placed,
        out_specs=(P("band", "tile"), P("band", None, "tile")),
        check_vma=False,
    )
```

```python
import functools
import math

import jax
import jax.numpy as jnp
from jax import lax
from jax.experimental import pallas as pl
from jax.experimental.pallas import tpu as pltpu
from jax.sharding import PartitionSpec as P

C = 9
L = 1024
NLON = 4096
HALO = 32

RIDGE = 0.1
EPSILON = 1e-06

WINDOW = 2 * HALO + 1
LANES = NLON // HALO
HALF = LANES // 2
PAIRS = [(a_at, b_at) for a_at in range(C) for b_at in range(a_at, C)]
VMEM_LIMIT = 24 * 1024 * 1024


def round_up(value, multiple):
    return (value + multiple - 1) // multiple * multiple


def cos_turns(turns):
    nearest = (turns + 12582912.0) - 12582912.0
    quarter = 1.0 - 4.0 * jnp.abs(turns - nearest)
    square = quarter * quarter
    tail = square * (1.6044118478736e-04 - square * 3.598843235e-06)
    tail = square * (-4.68175413531868e-03 + tail)
    tail = square * (7.96926262461670e-02 + tail)
    tail = square * (-6.45964097506246e-01 + tail)
    return quarter * (1.57079632679490 + tail)


def basis_kernel(order_ref, basis_ref):
    rows = 32
    row = lax.broadcasted_iota(jnp.int32, (rows, LANES), 0)
    lane = lax.broadcasted_iota(jnp.int32, (rows, LANES), 1)
    cell = (HALO * (lane % HALF) + lane // HALF).astype(jnp.float32) / NLON
    offset = (row % 2).astype(jnp.float32) * 0.25
    scaling = 1.0 / math.sqrt(L)

    def block(at, carry):
        span = pl.ds(pl.multiple_of(at * rows, rows), rows)
        order = jnp.broadcast_to(order_ref[span, :], (rows, LANES))
        turns = order * cell + offset
        step = order * (2.0 / NLON)
        before = cos_turns(turns) * scaling
        now = cos_turns(turns + step) * scaling
        twice = 2.0 * cos_turns(step)
        for column in range(HALO // 2):
            lanes = slice(column % 2 * LANES, (column % 2 + 1) * LANES)
            basis_ref[column // 2, span, lanes] = before.astype(jnp.bfloat16)
            if column < HALO // 2 - 1:
                before, now = now, twice * now - before
        return carry

    lax.fori_loop(0, order_ref.shape[0] // rows, block, 0)


def make_basis(order_rows):
    rows = order_rows.shape[0]
    block = 256
    chunks = HALO // 4
    return pl.pallas_call(
        basis_kernel,
        grid=(rows // block,),
        in_specs=[pl.BlockSpec((block, 1), lambda at: (at, 0))],
        out_specs=pl.BlockSpec((chunks, block, 2 * LANES), lambda at: (0, at, 0)),
        out_shape=jax.ShapeDtypeStruct((chunks, rows, 2 * LANES), jnp.bfloat16),
        cost_estimate=pl.CostEstimate(
            flops=rows * chunks * 2 * LANES * 8, bytes_accessed=rows * chunks * 4 * LANES, transcendentals=0
        ),
        compiler_params=pltpu.CompilerParams(vmem_limit_bytes=VMEM_LIMIT),
    )(order_rows)


def combine(entries, maps):
    entries = dict(entries)
    trace = entries[0, 0]
    for at in range(1, C):
        trace = trace + entries[at, at]
    ridge = RIDGE * (trace * (1.0 / C) + WINDOW * EPSILON)
    for at in range(C):
        entries[at, at] = entries[at, at] + ridge
    ones = [None] * C
    maps = list(maps)
    top = bottom = None
    for at in range(C):
        inverse = 1.0 / entries[at, at]
        scaled = inverse if at == 0 else inverse * ones[at]
        term = scaled * maps[at]
        top = term if top is None else top + term
        term = scaled if at == 0 else scaled * ones[at]
        bottom = term if bottom is None else bottom + term
        for row in range(at + 1, C):
            ratio = entries[at, row] * inverse
            ones[row] = 1.0 - ratio if at == 0 else ones[row] - ratio * ones[at]
            maps[row] = maps[row] - ratio * maps[at]
            for col in range(row, C):
                entries[row, col] = entries[row, col] - ratio * entries[at, col]
    return top / bottom


def ilc_kernel(modes_ref, odd_ref, basis_hbm, ilc_ref, spectra_ref, basis_ref, lhs_ref, maps_ref, sums_ref, low_ref, found_ref, sems):
    groups, rows, width = modes_ref.shape
    chunks = basis_ref.shape[0]
    cycles = rows // C
    second = round_up(rows, 16)
    for chunk in range(chunks):
        pltpu.make_async_copy(basis_hbm.at[chunk], basis_ref.at[chunk], sems.at[chunk]).start()
    for group in range(groups):
        span = slice(group * width, (group + 1) * width)
        odd = odd_ref[:, span]
        values = modes_ref[group].astype(jnp.float32)
        lhs_ref[0:rows, span] = (values * (1.0 - odd)).astype(jnp.bfloat16)
        lhs_ref[second : second + rows, span] = (values * odd).astype(jnp.bfloat16)
    low_half = lax.broadcasted_iota(jnp.int32, (cycles, LANES), 1) < HALF
    for chunk in range(chunks):
        pltpu.make_async_copy(basis_hbm.at[chunk], basis_ref.at[chunk], sems.at[chunk]).wait()
        result = jnp.dot(lhs_ref[...], basis_ref[chunk], preferred_element_type=jnp.float32)
        for part in range(2):
            at = 4 * chunk + 2 * part
            even_part = result[0:rows, part * LANES : (part + 1) * LANES]
            odd_part = result[second : second + rows, part * LANES : (part + 1) * LANES]
            near = even_part + odd_part
            far = even_part - odd_part
            wide = jnp.concatenate([low_half] * C, axis=0)
            maps_ref[at] = jnp.where(wide, near, pltpu.roll(far, HALF, 1))
            maps_ref[at + 1] = jnp.where(wide, pltpu.roll(near, HALF, 1), far)

    def maps_at(at):
        return [maps_ref[at, chan * cycles : (chan + 1) * cycles, :] for chan in range(C)]

    for first in range(0, len(PAIRS), 15):
        some = PAIRS[first : first + 15]

        def add(at, totals, some=some):
            values = maps_at(at)
            return tuple(total + values[a_at] * values[b_at] for total, (a_at, b_at) in zip(totals, some))

        zero = jnp.zeros((cycles, LANES), jnp.float32)
        totals = lax.fori_loop(0, HALO, add, (zero,) * len(some))
        for pair, total in enumerate(totals):
            sums_ref[first + pair] = total + pltpu.roll(total, 1, 1)

    def smooth(at, leaves):
        ahead = [pltpu.roll(value, LANES - 1, 1) for value in maps_at(at)]
        behind = [pltpu.roll(value, 1, 1) for value in maps_at(jnp.maximum(at - 1, 0))]
        behind = [value * leaves for value in behind]
        entries = {}
        for pair, (a_at, b_at) in enumerate(PAIRS):
            total = sums_ref[pair] + (ahead[a_at] * ahead[b_at] - behind[a_at] * behind[b_at])
            sums_ref[pair] = total
            entries[a_at, b_at] = total
        return entries

    def two_vectors(pair_at, carry):
        at = 2 * pair_at
        found = []
        for part in range(2):
            leaves = jnp.where(at == 0, 0.0, 1.0) if part == 0 else 1.0
            value = combine(smooth(at + part, leaves), maps_at(at + part))
            ilc_ref[at + part] = value
            found.append(value)
        near = jnp.where(low_half, found[0], pltpu.roll(found[1], HALF, 1))
        far = jnp.where(low_half, pltpu.roll(found[0], HALF, 1), found[1])
        low_ref[pair_at] = jnp.concatenate([near, far], axis=0).T.astype(jnp.bfloat16)
        return carry

    lax.fori_loop(0, HALO // 2, two_vectors, 0)

    for chunk in range(0, chunks, 2):
        lhs = jnp.concatenate([basis_ref[chunk], basis_ref[chunk + 1]], axis=1)
        rhs = jnp.concatenate([low_ref[2 * chunk + part] for part in range(4)], axis=0)
        term = jnp.dot(lhs, rhs, preferred_element_type=jnp.float32)
        found_ref[...] = term if chunk == 0 else found_ref[...] + term
    for group in range(groups):
        span = slice(group * width, (group + 1) * width)
        sign = 1.0 - 2.0 * odd_ref[:, span]
        result = found_ref[span, :].T
        spectra_ref[group] = (result[0:cycles] + sign * result[cycles:]).astype(jnp.bfloat16)


def run_ilc(modes, odd, basis):
    groups, rows, width = modes.shape
    chunks, depth, columns = basis.shape
    cycles = rows // C
    vmem = pl.BlockSpec(memory_space=pltpu.VMEM)
    return pl.pallas_call(
        ilc_kernel,
        in_specs=[vmem, vmem, pl.BlockSpec(memory_space=pl.ANY)],
        out_specs=[vmem, vmem],
        out_shape=[
            jax.ShapeDtypeStruct((HALO, cycles, LANES), jnp.float32),
            jax.ShapeDtypeStruct((groups, cycles, width), jnp.bfloat16),
        ],
        scratch_shapes=[
            pltpu.VMEM((chunks, depth, columns), jnp.bfloat16),
            pltpu.VMEM((2 * round_up(rows, 16), depth), jnp.bfloat16),
            pltpu.VMEM((HALO, rows, LANES), jnp.float32),
            pltpu.VMEM((len(PAIRS), cycles, LANES), jnp.float32),
            pltpu.VMEM((HALO // 2, LANES, 2 * cycles), jnp.bfloat16),
            pltpu.VMEM((depth, 2 * cycles), jnp.float32),
            pltpu.SemaphoreType.DMA((chunks,)),
        ],
        cost_estimate=pl.CostEstimate(
            flops=2 * chunks * depth * columns * (2 * rows + 2 * cycles),
            bytes_accessed=chunks * depth * columns * 2,
            transcendentals=0,
        ),
        compiler_params=pltpu.CompilerParams(vmem_limit_bytes=VMEM_LIMIT),
    )(modes, odd, basis)


def start_table(table_hbm, table_ref, sems):
    parts = sems.shape[0]
    slots = table_ref.shape[0] // parts
    for part in range(parts):
        span = slice(part * slots, (part + 1) * slots)
        pltpu.make_async_copy(table_hbm.at[span], table_ref.at[span], sems.at[part]).start()


def wait_table(table_hbm, table_ref, sems, part):
    slots = table_ref.shape[0] // sems.shape[0]
    span = pl.ds(part * slots, slots)
    pltpu.make_async_copy(table_hbm.at[span], table_ref.at[span], sems.at[part]).wait()


def tile_rows(band, tile, tile_count, cycles):
    at = (band * tile_count + tile) * cycles
    return pl.ds(pl.multiple_of(at, 8) if cycles % 8 == 0 else at, cycles)


def modes_kernel(alm_hbm, table_hbm, *refs):
    out_refs, (alm_ref, table_ref, lhs_ref, held_ref, turned_ref, alm_sem, sems) = refs[:-7], refs[-7:]
    tile_count = len(out_refs)
    parts = sems.shape[0]
    slots = table_ref.shape[0] // parts
    bands, rows = out_refs[0].shape[:2]
    cycles = rows // C
    alm_copy = pltpu.make_async_copy(alm_hbm, alm_ref, alm_sem)
    alm_copy.start()
    start_table(table_hbm, table_ref, sems)
    alm_copy.wait()

    def some_slots(part, carry):
        wait_table(table_hbm, table_ref, sems, part)
        for slot in range(slots):
            at = part * slots + slot
            for chan in range(C):
                lhs_ref[slot, 2 * chan : 2 * chan + 2, :] = alm_ref[at, chan].astype(jnp.float32)
            result = jnp.dot(
                lhs_ref[slot].astype(jnp.bfloat16), table_ref[at], preferred_element_type=jnp.float32
            )
            for chan in range(C):
                held_ref[chan, part, 2 * slot : 2 * slot + 2, :] = result[2 * chan : 2 * chan + 2]
        return carry

    lax.fori_loop(0, parts, some_slots, 0)
    for chan in range(C):
        turned_ref[chan] = held_ref[chan].reshape(turned_ref.shape[2], turned_ref.shape[1]).T
    tile_at = lax.axis_index("tile")
    for hop in range(tile_count):
        for band in range(bands):
            span = tile_rows(band, (tile_at + hop) % tile_count, tile_count, cycles)
            block = jnp.concatenate([turned_ref[chan, span, :] for chan in range(C)], axis=0)
            out_refs[hop][band] = block.astype(jnp.bfloat16)


def make_modes(alm, legendre, band_count, tile_count):
    slot_count, degrees, total = legendre.shape
    slots = 8
    parts = slot_count // slots
    width = 2 * slot_count
    cycles = total // (band_count * tile_count)
    one = jax.ShapeDtypeStruct((band_count, C * cycles, width), jnp.bfloat16)
    vmem = pl.BlockSpec(memory_space=pltpu.VMEM)
    return pl.pallas_call(
        modes_kernel,
        in_specs=[pl.BlockSpec(memory_space=pl.ANY)] * 2,
        out_specs=[vmem] * tile_count,
        out_shape=[one] * tile_count,
        scratch_shapes=[
            pltpu.VMEM(alm.shape, jnp.bfloat16),
            pltpu.VMEM(legendre.shape, jnp.bfloat16),
            pltpu.VMEM((slots, 2 * C, degrees), jnp.float32),
            pltpu.VMEM((C, parts, 2 * slots, total), jnp.float32),
            pltpu.VMEM((C, total, width), jnp.float32),
            pltpu.SemaphoreType.DMA,
            pltpu.SemaphoreType.DMA((parts,)),
        ],
        cost_estimate=pl.CostEstimate(
            flops=2 * slot_count * degrees * total * 2 * C,
            bytes_accessed=slot_count * degrees * (total + 2 * C) * 2,
            transcendentals=0,
        ),
        compiler_params=pltpu.CompilerParams(vmem_limit_bytes=61 * 1024 * 1024),
    )(alm, legendre)


def analysis_kernel(table_hbm, *refs):
    spectra_refs = refs[:-6]
    out_ref, table_ref, gathered_ref, rhs_ref, total_ref, sems = refs[-6:]
    tile_count = len(spectra_refs)
    parts = sems.shape[0]
    slots = table_ref.shape[0] // parts
    bands, cycles = spectra_refs[0].shape[:2]
    count = bands * tile_count * cycles
    start_table(table_hbm, table_ref, sems)
    tile_at = lax.axis_index("tile")
    for hop in range(tile_count):
        for band in range(bands):
            span = tile_rows(band, (tile_at + tile_count - hop) % tile_count, tile_count, cycles)
            gathered_ref[span, :] = spectra_refs[hop][band].astype(jnp.float32)
    lane = lax.broadcasted_iota(jnp.int32, gathered_ref.shape, 1) // 2
    total_ref[...] = jnp.zeros_like(total_ref)

    def some_slots(part, carry):
        for slot in range(slots):
            own = jnp.where(lane == part * slots + slot, gathered_ref[...], 0.0)
            rhs_ref[slot * count : (slot + 1) * count, :] = own.astype(jnp.bfloat16)
        wait_table(table_hbm, table_ref, sems, part)
        lhs = jnp.concatenate([table_ref[part * slots + slot] for slot in range(slots)], axis=1)
        total_ref[...] += jnp.dot(lhs, rhs_ref[...], preferred_element_type=jnp.float32)
        return carry

    lax.fori_loop(0, parts, some_slots, 0)
    turned = total_ref[...].T
    for slot in range(out_ref.shape[0]):
        out_ref[slot] = turned[2 * slot : 2 * slot + 2]


def analyse(legendre, spectra):
    slot_count, degrees, total = legendre.shape
    slots = 4
    width = 2 * slot_count
    vmem = pl.BlockSpec(memory_space=pltpu.VMEM)
    return pl.pallas_call(
        analysis_kernel,
        in_specs=[pl.BlockSpec(memory_space=pl.ANY)] + [vmem] * len(spectra),
        out_specs=vmem,
        out_shape=jax.ShapeDtypeStruct((slot_count, 2, degrees), jnp.float32),
        scratch_shapes=[
            pltpu.VMEM(legendre.shape, jnp.bfloat16),
            pltpu.VMEM((total, width), jnp.float32),
            pltpu.VMEM((slots * total, width), jnp.bfloat16),
            pltpu.VMEM((degrees, width), jnp.float32),
            pltpu.SemaphoreType.DMA((slot_count // slots,)),
        ],
        cost_estimate=pl.CostEstimate(
            flops=2 * slot_count * degrees * total * width,
            bytes_accessed=slot_count * degrees * total * 2,
            transcendentals=0,
        ),
        compiler_params=pltpu.CompilerParams(vmem_limit_bytes=24 * 1024 * 1024),
    )(legendre, *spectra)


def from_other_tiles(sends):
    count = len(sends)
    got = [sends[0]]
    for hop in range(1, count):
        got.append(lax.ppermute(sends[hop], "tile", [(at, (at + hop) % count) for at in range(count)]))
    return got


def in_tile_order(got):
    count = len(got)
    tile_at = lax.axis_index("tile")
    stacked = jnp.stack(got)
    return jnp.stack(
        [lax.dynamic_index_in_dim(stacked, (tile_at - at) % count, 0, keepdims=False) for at in range(count)]
    )


def body(alm, legendre, order_of_slot):
    tile_count = lax.axis_size("tile")
    band_count = lax.axis_size("band")
    tile_at = lax.axis_index("tile")
    slot_count = alm.shape[0]
    cycles = legendre.shape[2] // (band_count * tile_count)
    padded = round_up(cycles, 8)
    depth = 2 * L
    width = 2 * slot_count
    group_width = math.lcm(width, LANES)
    groups = depth // group_width

    got = from_other_tiles(make_modes(alm, legendre, band_count, tile_count))
    total = got[0].astype(jnp.float32)
    for other in got[1:]:
        total = total + other.astype(jnp.float32)
    modes = lax.all_to_all(total.astype(jnp.bfloat16), "band", split_axis=0, concat_axis=0, tiled=True)
    if group_width != width:
        modes = modes.reshape(groups, group_width // width, C * cycles, width)
        modes = modes.transpose(0, 2, 1, 3).reshape(groups, C * cycles, group_width)
    if padded != cycles:
        modes = modes.reshape(groups, C, cycles, group_width)
        modes = jnp.pad(modes, ((0, 0), (0, 0), (0, padded - cycles), (0, 0)))
        modes = modes.reshape(groups, C * padded, group_width)

    order_rows = jnp.repeat(order_of_slot, 2)
    basis = make_basis(order_rows.astype(jnp.float32)[:, None])
    odd = (order_rows % 2).astype(jnp.float32)[None, :]
    vectors, spectra = run_ilc(modes, odd, basis)

    spectra = spectra[:, :cycles]
    if group_width != width:
        spectra = spectra.reshape(groups, cycles, group_width // width, width)
        spectra = spectra.transpose(0, 2, 1, 3).reshape(band_count, cycles, width)
    routed = lax.all_to_all(spectra, "band", split_axis=0, concat_axis=0, tiled=True)
    ilc_alm = analyse(legendre, from_other_tiles([routed] * tile_count))

    own = vectors[:, :cycles].transpose(1, 2, 0).reshape(cycles, tile_count, NLON // tile_count)
    own = own.transpose(1, 0, 2)
    sends = [
        lax.dynamic_index_in_dim(own, (tile_at + hop) % tile_count, 0, keepdims=False) for hop in range(tile_count)
    ]
    ilc_map = in_tile_order(from_other_tiles(sends))
    return (ilc_map.reshape(tile_count * cycles, NLON // tile_count), ilc_alm)


def solution(mesh):
    placed = (P("band", None, None, "tile"), P("band", "tile", None), P())
    return jax.shard_map(
        body,
        mesh=mesh,
        in_specs=placed,
        out_specs=(P("band", "tile"), P("band", None, "tile")),
        check_vma=False,
    )
```

```python
import functools
import math

import jax
import jax.numpy as jnp
from jax import lax
from jax.experimental import pallas as pl
from jax.experimental.pallas import tpu as pltpu
from jax.sharding import PartitionSpec as P

C = 9
L = 1024
NLON = 4096
HALO = 32

RIDGE = 0.1
EPSILON = 1e-06

WINDOW = 2 * HALO + 1
LANES = NLON // HALO
HALF = LANES // 2
PAIRS = [(a_at, b_at) for a_at in range(C) for b_at in range(a_at, C)]
VMEM_LIMIT = 60 * 1024 * 1024


def round_up(value, multiple):
    return (value + multiple - 1) // multiple * multiple


def cos_turns(turns):
    nearest = (turns + 12582912.0) - 12582912.0
    quarter = 1.0 - 4.0 * jnp.abs(turns - nearest)
    square = quarter * quarter
    tail = square * (1.6044118478736e-04 - square * 3.598843235e-06)
    tail = square * (-4.68175413531868e-03 + tail)
    tail = square * (7.96926262461670e-02 + tail)
    tail = square * (-6.45964097506246e-01 + tail)
    return quarter * (1.57079632679490 + tail)


def basis_kernel(slots, order_ref, basis_ref):
    rows = 64
    begin = pl.program_id(0) * order_ref.shape[0]
    row = lax.broadcasted_iota(jnp.int32, (rows, LANES), 0)
    lane = lax.broadcasted_iota(jnp.int32, (rows, LANES), 1)
    cell = (HALO * (lane % HALF) + lane // HALF).astype(jnp.float32) / NLON
    scaling = 1.0 / math.sqrt(L)
    for first in range(0, order_ref.shape[0], rows):
        span = slice(first, first + rows)
        part = (row + (begin + first)) // slots % 2
        order = jnp.broadcast_to(order_ref[span, :], (rows, LANES))
        turns = order * cell + part.astype(jnp.float32) * 0.25
        step = order * (2.0 / NLON)
        before = cos_turns(turns) * scaling
        now = cos_turns(turns + step) * scaling
        twice = 2.0 * cos_turns(step)
        for column in range(HALO // 2):
            lanes = slice(column % 2 * LANES, (column % 2 + 1) * LANES)
            basis_ref[column // 2, span, lanes] = before.astype(jnp.bfloat16)
            if column < HALO // 2 - 1:
                before, now = now, twice * now - before


def make_basis(order_rows, slots):
    rows = order_rows.shape[0]
    block = 256
    chunks = HALO // 4
    return pl.pallas_call(
        functools.partial(basis_kernel, slots),
        grid=(rows // block,),
        in_specs=[pl.BlockSpec((block, 1), lambda at: (at, 0))],
        out_specs=pl.BlockSpec((chunks, block, 2 * LANES), lambda at: (0, at, 0)),
        out_shape=jax.ShapeDtypeStruct((chunks, rows, 2 * LANES), jnp.bfloat16),
        cost_estimate=pl.CostEstimate(
            flops=rows * chunks * 2 * LANES * 8, bytes_accessed=rows * chunks * 4 * LANES, transcendentals=0
        ),
        compiler_params=pltpu.CompilerParams(vmem_limit_bytes=VMEM_LIMIT),
    )(order_rows)


def reciprocal(value):
    guess = pl.reciprocal(value, approx=True)
    return guess * (2.0 - value * guess)


def combine(entries, maps):
    entries = dict(entries)
    trace = entries[0, 0]
    for at in range(1, C):
        trace = trace + entries[at, at]
    ridge = RIDGE * (trace * (1.0 / C) + WINDOW * EPSILON)
    for at in range(C):
        entries[at, at] = entries[at, at] + ridge
    ones = [None] * C
    maps = list(maps)
    top = bottom = None
    for at in range(C):
        inverse = reciprocal(entries[at, at])
        scaled = inverse if at == 0 else inverse * ones[at]
        term = scaled * maps[at]
        top = term if top is None else top + term
        term = scaled if at == 0 else scaled * ones[at]
        bottom = term if bottom is None else bottom + term
        for row in range(at + 1, C):
            ratio = entries[at, row] * inverse
            ones[row] = 1.0 - ratio if at == 0 else ones[row] - ratio * ones[at]
            maps[row] = maps[row] - ratio * maps[at]
            for col in range(row, C):
                entries[row, col] = entries[row, col] - ratio * entries[at, col]
    return top * reciprocal(bottom)


def ilc_kernel(modes_ref, odd_ref, basis_hbm, ilc_ref, spectra_ref, basis_ref, lhs_ref, maps_ref, sums_ref, low_ref, found_ref, sems):
    groups, shares, rows, width = modes_ref.shape
    chunks = basis_ref.shape[0]
    cycles = rows // C
    second = round_up(rows, 16)
    for chunk in range(chunks):
        pltpu.make_async_copy(basis_hbm.at[chunk], basis_ref.at[chunk], sems.at[chunk]).start()
    for group in range(groups):
        span = slice(group * width, (group + 1) * width)
        odd = odd_ref[:, span]
        values = modes_ref[group, 0].astype(jnp.float32)
        for share in range(1, shares):
            values = values + modes_ref[group, share].astype(jnp.float32)
        lhs_ref[0:rows, span] = (values * (1.0 - odd)).astype(jnp.bfloat16)
        lhs_ref[second : second + rows, span] = (values * odd).astype(jnp.bfloat16)
    low_half = lax.broadcasted_iota(jnp.int32, (cycles, LANES), 1) < HALF
    for chunk in range(chunks):
        pltpu.make_async_copy(basis_hbm.at[chunk], basis_ref.at[chunk], sems.at[chunk]).wait()
        result = jnp.dot(lhs_ref[...], basis_ref[chunk], preferred_element_type=jnp.float32)
        for part in range(2):
            at = 4 * chunk + 2 * part
            even_part = result[0:rows, part * LANES : (part + 1) * LANES]
            odd_part = result[second : second + rows, part * LANES : (part + 1) * LANES]
            near = even_part + odd_part
            far = even_part - odd_part
            wide = jnp.concatenate([low_half] * C, axis=0)
            maps_ref[at] = jnp.where(wide, near, pltpu.roll(far, HALF, 1))
            maps_ref[at + 1] = jnp.where(wide, pltpu.roll(near, HALF, 1), far)

    def maps_at(at):
        return [maps_ref[at, chan * cycles : (chan + 1) * cycles, :] for chan in range(C)]

    for first in range(0, len(PAIRS), 15):
        some = PAIRS[first : first + 15]

        def add(at, totals, some=some):
            values = maps_at(at)
            return tuple(total + values[a_at] * values[b_at] for total, (a_at, b_at) in zip(totals, some))

        zero = jnp.zeros((cycles, LANES), jnp.float32)
        totals = lax.fori_loop(0, HALO, add, (zero,) * len(some))
        for pair, total in enumerate(totals):
            sums_ref[first + pair] = total + pltpu.roll(total, 1, 1)

    def smooth(at, leaves):
        ahead = [pltpu.roll(value, LANES - 1, 1) for value in maps_at(at)]
        behind = [pltpu.roll(value, 1, 1) for value in maps_at(jnp.maximum(at - 1, 0))]
        behind = [value * leaves for value in behind]
        entries = {}
        for pair, (a_at, b_at) in enumerate(PAIRS):
            total = sums_ref[pair] + (ahead[a_at] * ahead[b_at] - behind[a_at] * behind[b_at])
            sums_ref[pair] = total
            entries[a_at, b_at] = total
        return entries

    def two_vectors(at, first):
        found = []
        for part in range(2):
            leaves = jnp.where(at == 0, 0.0, 1.0) if first and part == 0 else 1.0
            value = combine(smooth(at + part, leaves), maps_at(at + part))
            ilc_ref[at + part] = value
            found.append(value)
        near = jnp.where(low_half, found[0], pltpu.roll(found[1], HALF, 1))
        far = jnp.where(low_half, pltpu.roll(found[0], HALF, 1), found[1])
        return jnp.concatenate([near, far], axis=0).astype(jnp.bfloat16)

    def spectra_of(chunk):
        return lax.dot_general(
            low_ref[chunk], basis_ref[chunk], (((1,), (1,)), ((), ())), preferred_element_type=jnp.float32
        )

    found_ref[...] = jnp.zeros_like(found_ref)
    low_ref[...] = jnp.zeros_like(low_ref)

    def solve_chunk(chunk, carry):
        found_ref[...] += spectra_of(jnp.maximum(chunk - 1, 0))
        low_ref[chunk, :, 0:LANES] = two_vectors(4 * chunk, True)
        low_ref[chunk, :, LANES : 2 * LANES] = two_vectors(4 * chunk + 2, False)
        return carry

    lax.fori_loop(0, chunks, solve_chunk, 0)
    found_ref[...] += spectra_of(chunks - 1)
    for group in range(groups):
        span = slice(group * width, (group + 1) * width)
        sign = 1.0 - 2.0 * odd_ref[:, span]
        value = (found_ref[0:cycles, span] + sign * found_ref[cycles:, span]).astype(jnp.bfloat16)
        for share in range(shares):
            spectra_ref[group, share] = value


def run_ilc(modes, odd, basis):
    groups, shares, rows, width = modes.shape
    chunks, depth, columns = basis.shape
    cycles = rows // C
    vmem = pl.BlockSpec(memory_space=pltpu.VMEM)
    return pl.pallas_call(
        ilc_kernel,
        in_specs=[vmem, vmem, pl.BlockSpec(memory_space=pl.ANY)],
        out_specs=[vmem, vmem],
        out_shape=[
            jax.ShapeDtypeStruct((HALO, cycles, LANES), jnp.float32),
            jax.ShapeDtypeStruct((groups, shares, cycles, width), jnp.bfloat16),
        ],
        scratch_shapes=[
            pltpu.VMEM((chunks, depth, columns), jnp.bfloat16),
            pltpu.VMEM((2 * round_up(rows, 16), depth), jnp.bfloat16),
            pltpu.VMEM((HALO, rows, LANES), jnp.float32),
            pltpu.VMEM((len(PAIRS), cycles, LANES), jnp.float32),
            pltpu.VMEM((chunks, 2 * cycles, columns), jnp.bfloat16),
            pltpu.VMEM((2 * cycles, depth), jnp.float32),
            pltpu.SemaphoreType.DMA((chunks,)),
        ],
        cost_estimate=pl.CostEstimate(
            flops=2 * chunks * depth * columns * (2 * rows + 2 * cycles),
            bytes_accessed=chunks * depth * columns * 2,
            transcendentals=0,
        ),
        compiler_params=pltpu.CompilerParams(vmem_limit_bytes=VMEM_LIMIT),
    )(modes, odd, basis)


def start_table(table_hbm, table_ref, sems):
    parts = sems.shape[0]
    slots = table_ref.shape[0] // parts
    for part in range(parts):
        span = slice(part * slots, (part + 1) * slots)
        pltpu.make_async_copy(table_hbm.at[span], table_ref.at[span], sems.at[part]).start()


def wait_table(table_hbm, table_ref, sems, part):
    slots = table_ref.shape[0] // sems.shape[0]
    span = pl.ds(part * slots, slots)
    pltpu.make_async_copy(table_hbm.at[span], table_ref.at[span], sems.at[part]).wait()


def modes_kernel(alm_hbm, table_hbm, out_ref, alm_ref, table_ref, lhs_ref, held_ref, turned_ref, alm_sem, sems):
    parts = sems.shape[0]
    total_slots = table_ref.shape[0]
    slots = total_slots // parts
    targets, rows = out_ref.shape[:2]
    cycles = rows // C
    height = held_ref.shape[1] // total_slots
    alm_copy = pltpu.make_async_copy(alm_hbm, alm_ref, alm_sem)
    alm_copy.start()
    start_table(table_hbm, table_ref, sems)
    alm_copy.wait()

    def some_slots(part, carry):
        wait_table(table_hbm, table_ref, sems, part)
        for slot in range(slots):
            at = part * slots + slot
            for chan in range(C):
                lhs_ref[slot, 2 * chan : 2 * chan + 2, :] = alm_ref[at, chan].astype(jnp.float32)
            result = jnp.dot(
                lhs_ref[slot].astype(jnp.bfloat16), table_ref[at], preferred_element_type=jnp.float32
            )
            for lanes in range(held_ref.shape[0]):
                piece = result[:, lanes * LANES : (lanes + 1) * LANES]
                held_ref[lanes, pl.ds(pl.multiple_of(at * height, 8), height), :] = piece
        return carry

    lax.fori_loop(0, parts, some_slots, 0)
    for chan in range(C):
        for lanes in range(held_ref.shape[0]):
            both = [held_ref[lanes, pl.ds(2 * chan + part, total_slots, stride=height), :] for part in range(2)]
            turned_ref[chan, lanes * LANES : (lanes + 1) * LANES, :] = jnp.concatenate(both, axis=0).T
    for target in range(targets):
        span = slice(target * cycles, (target + 1) * cycles)
        block = jnp.concatenate([turned_ref[chan, span, :] for chan in range(C)], axis=0)
        out_ref[target] = block.astype(jnp.bfloat16)


def make_modes(alm, legendre, targets):
    slot_count, degrees, total = legendre.shape
    slots = 8
    parts = slot_count // slots
    width = 2 * slot_count
    height = round_up(2 * C, 8)
    return pl.pallas_call(
        modes_kernel,
        in_specs=[pl.BlockSpec(memory_space=pl.ANY)] * 2,
        out_specs=pl.BlockSpec(memory_space=pltpu.VMEM),
        out_shape=jax.ShapeDtypeStruct((targets, C * (total // targets), width), jnp.bfloat16),
        scratch_shapes=[
            pltpu.VMEM(alm.shape, jnp.bfloat16),
            pltpu.VMEM(legendre.shape, jnp.bfloat16),
            pltpu.VMEM((slots, height, degrees), jnp.float32),
            pltpu.VMEM((total // LANES, slot_count * height, LANES), jnp.float32),
            pltpu.VMEM((C, total, width), jnp.float32),
            pltpu.SemaphoreType.DMA,
            pltpu.SemaphoreType.DMA((parts,)),
        ],
        cost_estimate=pl.CostEstimate(
            flops=2 * slot_count * degrees * total * 2 * C,
            bytes_accessed=slot_count * degrees * (total + 2 * C) * 2,
            transcendentals=0,
        ),
        compiler_params=pltpu.CompilerParams(vmem_limit_bytes=62 * 1024 * 1024),
    )(alm, legendre)


def analysis_kernel(table_hbm, spectra_ref, out_ref, table_ref, total_ref, turned_ref, sems):
    parts = sems.shape[0]
    total_slots = table_ref.shape[0]
    slots = total_slots // parts
    start_table(table_hbm, table_ref, sems)
    spectra = spectra_ref[...]
    lane = lax.broadcasted_iota(jnp.int32, (1, spectra.shape[1]), 1) % total_slots
    total_ref[...] = jnp.zeros_like(total_ref)

    def some_slots(part, carry):
        masks = [(lane == part * slots + slot).astype(jnp.float32).astype(jnp.bfloat16) for slot in range(slots)]
        rhs = jnp.concatenate([spectra_ref[...] * mask for mask in masks], axis=0)
        wait_table(table_hbm, table_ref, sems, part)
        lhs = jnp.concatenate([table_ref[part * slots + slot] for slot in range(slots)], axis=1)
        total_ref[...] += jnp.dot(lhs, rhs, preferred_element_type=jnp.float32)
        return carry

    lax.fori_loop(0, parts, some_slots, 0)
    for lanes in range(turned_ref.shape[0]):
        span = slice(lanes * LANES, (lanes + 1) * LANES)
        turned_ref[lanes] = total_ref[span, :].T
        for slot in range(total_slots):
            out_ref[slot, :, span] = turned_ref[lanes, pl.ds(slot, 2, stride=total_slots), :]


def analyse(legendre, spectra):
    slot_count, degrees, total = legendre.shape
    slots = 8
    width = 2 * slot_count
    vmem = pl.BlockSpec(memory_space=pltpu.VMEM)
    return pl.pallas_call(
        analysis_kernel,
        in_specs=[pl.BlockSpec(memory_space=pl.ANY), vmem],
        out_specs=vmem,
        out_shape=jax.ShapeDtypeStruct((slot_count, 2, degrees), jnp.float32),
        scratch_shapes=[
            pltpu.VMEM(legendre.shape, jnp.bfloat16),
            pltpu.VMEM((degrees, width), jnp.float32),
            pltpu.VMEM((degrees // LANES, width, LANES), jnp.float32),
            pltpu.SemaphoreType.DMA((slot_count // slots,)),
        ],
        cost_estimate=pl.CostEstimate(
            flops=2 * slot_count * degrees * total * width,
            bytes_accessed=slot_count * degrees * total * 2,
            transcendentals=0,
        ),
        compiler_params=pltpu.CompilerParams(vmem_limit_bytes=62 * 1024 * 1024),
    )(legendre, spectra)


def from_other_tiles(sends):
    count = len(sends)
    got = [sends[0]]
    for hop in range(1, count):
        got.append(lax.ppermute(sends[hop], "tile", [(at, (at + hop) % count) for at in range(count)]))
    return got


def in_tile_order(got):
    count = len(got)
    tile_at = lax.axis_index("tile")
    stacked = jnp.stack(got)
    return jnp.stack(
        [lax.dynamic_index_in_dim(stacked, (tile_at - at) % count, 0, keepdims=False) for at in range(count)]
    )


def body(alm, legendre, order_of_slot):
    tile_count = lax.axis_size("tile")
    band_count = lax.axis_size("band")
    tile_at = lax.axis_index("tile")
    slot_count = alm.shape[0]
    targets = band_count * tile_count
    cycles = legendre.shape[2] // targets
    padded = round_up(cycles, 8)
    depth = 2 * L
    width = 2 * slot_count
    group_width = math.lcm(width, LANES)
    groups = depth // group_width
    plain = group_width == width and padded == cycles
    axes = ("band", "tile")

    partial = make_modes(alm, legendre, targets)
    partial = lax.all_to_all(partial, axes, split_axis=0, concat_axis=0, tiled=True)
    modes = partial.reshape(band_count, tile_count, C * cycles, width)
    if not plain:
        modes = jnp.sum(modes.astype(jnp.float32), axis=1).astype(jnp.bfloat16)
        modes = modes.reshape(groups, group_width // width, C, cycles, width)
        modes = modes.transpose(0, 2, 3, 1, 4).reshape(groups, C, cycles, group_width)
        modes = jnp.pad(modes, ((0, 0), (0, 0), (0, padded - cycles), (0, 0)))
        modes = modes.reshape(groups, 1, C * padded, group_width)

    order_rows = jnp.broadcast_to(order_of_slot.reshape(band_count, 1, slot_count), (band_count, 2, slot_count))
    order_rows = order_rows.reshape(depth)
    basis = make_basis(order_rows.astype(jnp.float32)[:, None], slot_count)
    odd = (order_rows % 2).astype(jnp.float32)[None, :]
    vectors, spectra = run_ilc(modes, odd, basis)

    if not plain:
        spectra = spectra[:, 0, :cycles].reshape(groups, cycles, group_width // width, width)
        spectra = spectra.transpose(0, 2, 1, 3).reshape(band_count, 1, cycles, width)
        spectra = jnp.broadcast_to(spectra, (band_count, tile_count, cycles, width))
    spectra = spectra.reshape(targets, cycles, width)
    routed = lax.all_to_all(spectra, axes, split_axis=0, concat_axis=0, tiled=True)
    vectors, routed = lax.optimization_barrier((vectors, routed))
    ilc_alm = analyse(legendre, routed.reshape(targets * cycles, width))

    own = vectors[:, :cycles].transpose(1, 2, 0).reshape(cycles, tile_count, NLON // tile_count)
    own = own.transpose(1, 0, 2)
    sends = [
        lax.dynamic_index_in_dim(own, (tile_at + hop) % tile_count, 0, keepdims=False) for hop in range(tile_count)
    ]
    ilc_map = in_tile_order(from_other_tiles(sends))
    return (ilc_map.reshape(tile_count * cycles, NLON // tile_count), ilc_alm)


def solution(mesh):
    placed = (P("band", None, None, "tile"), P("band", "tile", None), P())
    return jax.shard_map(
        body,
        mesh=mesh,
        in_specs=placed,
        out_specs=(P("band", "tile"), P("band", None, "tile")),
        check_vma=False,
    )
```

```python
import functools
import math

import jax
import jax.numpy as jnp
from jax import lax
from jax.experimental import pallas as pl
from jax.experimental.pallas import tpu as pltpu
from jax.sharding import PartitionSpec as P

C = 9
L = 1024
NLON = 4096
HALO = 32

RIDGE = 0.1
EPSILON = 1e-06

WINDOW = 2 * HALO + 1
LANES = NLON // HALO
HALF = LANES // 2
PAIRS = [(a_at, b_at) for a_at in range(C) for b_at in range(a_at, C)]
VMEM_LIMIT = 56 * 1024 * 1024
IN_FLIGHT = 4


def round_up(value, multiple):
    return (value + multiple - 1) // multiple * multiple


def cos_turns(turns):
    nearest = (turns + 12582912.0) - 12582912.0
    quarter = 1.0 - 4.0 * jnp.abs(turns - nearest)
    square = quarter * quarter
    tail = square * (1.6044118478736e-04 - square * 3.598843235e-06)
    tail = square * (-4.68175413531868e-03 + tail)
    tail = square * (7.96926262461670e-02 + tail)
    tail = square * (-6.45964097506246e-01 + tail)
    return quarter * (1.57079632679490 + tail)


def basis_kernel(slots, order_ref, basis_ref):
    rows = 64
    begin = pl.program_id(0) * order_ref.shape[0]
    row = lax.broadcasted_iota(jnp.int32, (rows, LANES), 0)
    lane = lax.broadcasted_iota(jnp.int32, (rows, LANES), 1)
    cell = (HALO * (lane % HALF) + lane // HALF).astype(jnp.float32) / NLON
    scaling = 1.0 / math.sqrt(L)
    for first in range(0, order_ref.shape[0], rows):
        span = slice(first, first + rows)
        part = (row + (begin + first)) // slots % 2
        order = jnp.broadcast_to(order_ref[span, :], (rows, LANES))
        turns = order * cell + part.astype(jnp.float32) * 0.25
        step = order * (2.0 / NLON)
        before = cos_turns(turns) * scaling
        now = cos_turns(turns + step) * scaling
        twice = 2.0 * cos_turns(step)
        for column in range(HALO // 2):
            lanes = slice(column % 2 * LANES, (column % 2 + 1) * LANES)
            basis_ref[column // 2, span, lanes] = before.astype(jnp.bfloat16)
            if column < HALO // 2 - 1:
                before, now = now, twice * now - before


def make_basis(order_rows, slots):
    rows = order_rows.shape[0]
    block = 256
    chunks = HALO // 4
    return pl.pallas_call(
        functools.partial(basis_kernel, slots),
        grid=(rows // block,),
        in_specs=[pl.BlockSpec((block, 1), lambda at: (at, 0))],
        out_specs=pl.BlockSpec((chunks, block, 2 * LANES), lambda at: (0, at, 0)),
        out_shape=jax.ShapeDtypeStruct((chunks, rows, 2 * LANES), jnp.bfloat16),
        cost_estimate=pl.CostEstimate(
            flops=rows * chunks * 2 * LANES * 8, bytes_accessed=rows * chunks * 4 * LANES, transcendentals=0
        ),
        compiler_params=pltpu.CompilerParams(vmem_limit_bytes=VMEM_LIMIT),
    )(order_rows)


def part_copy(source, target, sems, part):
    count = source.shape[0] // sems.shape[0]
    span = pl.ds(part * count, count)
    return pltpu.make_async_copy(source.at[span], target.at[span], sems.at[part])


def start_some(source, target, sems):
    for part in range(min(IN_FLIGHT, sems.shape[0])):
        part_copy(source, target, sems, part).start()


def next_part(source, target, sems, part):
    part_copy(source, target, sems, part).wait()

    @pl.when(part + IN_FLIGHT < sems.shape[0])
    def _():
        part_copy(source, target, sems, part + IN_FLIGHT).start()


def reciprocal(value):
    guess = pl.reciprocal(value, approx=True)
    return guess * (2.0 - value * guess)


def combine(entry, map_of):
    diagonal = [entry(at, at) for at in range(C)]
    trace = diagonal[0]
    for at in range(1, C):
        trace = trace + diagonal[at]
    ridge = RIDGE * (trace * (1.0 / C) + WINDOW * EPSILON)
    upper, inverses, ones, maps = {}, [], [], []
    top = bottom = None
    for row in range(C):
        ratios = [upper[at, row] * inverses[at] for at in range(row)]
        pivot = diagonal[row] + ridge
        for at in range(row):
            pivot = pivot - ratios[at] * upper[at, row]
        inverse = reciprocal(pivot)
        for col in range(row + 1, C):
            value = entry(row, col)
            for at in range(row):
                value = value - ratios[at] * upper[at, col]
            upper[row, col] = value
        one = 1.0
        own = map_of(row)
        for at in range(row):
            one = one - (ratios[at] if at == 0 else ratios[at] * ones[at])
            own = own - ratios[at] * maps[at]
        scaled = inverse if row == 0 else inverse * one
        term = scaled * own
        top = term if top is None else top + term
        term = scaled if row == 0 else scaled * one
        bottom = term if bottom is None else bottom + term
        inverses.append(inverse)
        ones.append(one)
        maps.append(own)
    return top * reciprocal(bottom)


def ilc_kernel(modes_ref, odd_ref, basis_hbm, ilc_ref, spectra_ref, basis_ref, lhs_ref, maps_ref, sums_ref, low_ref, found_ref, sems):
    groups, shares, rows, width = modes_ref.shape
    chunks = basis_ref.shape[0]
    cycles = rows // C
    second = round_up(rows, 16)
    start_some(basis_hbm, basis_ref, sems)
    for group in range(groups):
        span = slice(group * width, (group + 1) * width)
        odd = odd_ref[:, span]
        values = modes_ref[group, 0].astype(jnp.float32)
        for share in range(1, shares):
            values = values + modes_ref[group, share].astype(jnp.float32)
        lhs_ref[0:rows, span] = (values * (1.0 - odd)).astype(jnp.bfloat16)
        lhs_ref[second : second + rows, span] = (values * odd).astype(jnp.bfloat16)
    low_half = lax.broadcasted_iota(jnp.int32, (cycles, LANES), 1) < HALF
    sums_ref[...] = jnp.zeros_like(sums_ref)

    def map_of(at, chan):
        return maps_ref[at, chan * cycles : (chan + 1) * cycles, :]

    def maps_of_chunk(chunk):
        next_part(basis_hbm, basis_ref, sems, chunk)
        result = jnp.dot(lhs_ref[...], basis_ref[chunk], preferred_element_type=jnp.float32)
        for part in range(2):
            at = 4 * chunk + 2 * part
            for chan in range(C):
                span = slice(chan * cycles, (chan + 1) * cycles)
                even_part = result[span, part * LANES : (part + 1) * LANES]
                odd_part = result[second + chan * cycles : second + (chan + 1) * cycles, part * LANES : (part + 1) * LANES]
                near = even_part + odd_part
                far = even_part - odd_part
                maps_ref[at, span, :] = jnp.where(low_half, near, pltpu.roll(far, HALF, 1))
                maps_ref[at + 1, span, :] = jnp.where(low_half, pltpu.roll(near, HALF, 1), far)

    def add_totals(chunk):
        for pair, (a_at, b_at) in enumerate(PAIRS):
            total = sums_ref[pair]
            for part in range(4):
                total = total + map_of(4 * chunk + part, a_at) * map_of(4 * chunk + part, b_at)
            sums_ref[pair] = total

    maps_of_chunk(0)
    for chunk in range(1, chunks):
        maps_of_chunk(chunk)
        add_totals(chunk - 1)
    add_totals(chunks - 1)
    for pair in range(len(PAIRS)):
        total = sums_ref[pair]
        sums_ref[pair] = total + pltpu.roll(total, 1, 1)

    def solve(at, leaves):
        ahead = [pltpu.roll(map_of(at, chan), LANES - 1, 1) for chan in range(C)]
        before = jnp.maximum(at - 1, 0)
        behind = [pltpu.roll(map_of(before, chan), 1, 1) * leaves for chan in range(C)]

        def entry(a_at, b_at):
            pair = PAIRS.index((a_at, b_at))
            total = sums_ref[pair] + (ahead[a_at] * ahead[b_at] - behind[a_at] * behind[b_at])
            sums_ref[pair] = total
            return total

        value = combine(entry, lambda chan: map_of(at, chan))
        ilc_ref[at] = value
        return value

    def two_vectors(at, first):
        leaves = jnp.where(at == 0, 0.0, 1.0) if first else 1.0
        found = [solve(at, leaves), solve(at + 1, 1.0)]
        near = jnp.where(low_half, found[0], pltpu.roll(found[1], HALF, 1))
        far = jnp.where(low_half, pltpu.roll(found[0], HALF, 1), found[1])
        return jnp.concatenate([near, far], axis=0).astype(jnp.bfloat16)

    def spectra_of(chunk):
        return lax.dot_general(
            low_ref[chunk], basis_ref[chunk], (((1,), (1,)), ((), ())), preferred_element_type=jnp.float32
        )

    found_ref[...] = jnp.zeros_like(found_ref)
    low_ref[...] = jnp.zeros_like(low_ref)

    def solve_chunk(chunk, carry):
        found_ref[...] += spectra_of(jnp.maximum(chunk - 1, 0))
        low_ref[chunk, :, 0:LANES] = two_vectors(4 * chunk, True)
        low_ref[chunk, :, LANES : 2 * LANES] = two_vectors(4 * chunk + 2, False)
        return carry

    lax.fori_loop(0, chunks, solve_chunk, 0)
    found_ref[...] += spectra_of(chunks - 1)
    for group in range(groups):
        span = slice(group * width, (group + 1) * width)
        sign = 1.0 - 2.0 * odd_ref[:, span]
        value = (found_ref[0:cycles, span] + sign * found_ref[cycles:, span]).astype(jnp.bfloat16)
        for share in range(shares):
            spectra_ref[group, share] = value


def run_ilc(modes, odd, basis):
    groups, shares, rows, width = modes.shape
    chunks, depth, columns = basis.shape
    cycles = rows // C
    vmem = pl.BlockSpec(memory_space=pltpu.VMEM)
    return pl.pallas_call(
        ilc_kernel,
        in_specs=[vmem, vmem, pl.BlockSpec(memory_space=pl.ANY)],
        out_specs=[vmem, vmem],
        out_shape=[
            jax.ShapeDtypeStruct((HALO, cycles, LANES), jnp.float32),
            jax.ShapeDtypeStruct((groups, shares, cycles, width), jnp.bfloat16),
        ],
        scratch_shapes=[
            pltpu.VMEM((chunks, depth, columns), jnp.bfloat16),
            pltpu.VMEM((2 * round_up(rows, 16), depth), jnp.bfloat16),
            pltpu.VMEM((HALO, rows, LANES), jnp.float32),
            pltpu.VMEM((len(PAIRS), cycles, LANES), jnp.float32),
            pltpu.VMEM((chunks, 2 * cycles, columns), jnp.bfloat16),
            pltpu.VMEM((2 * cycles, depth), jnp.float32),
            pltpu.SemaphoreType.DMA((chunks,)),
        ],
        cost_estimate=pl.CostEstimate(
            flops=2 * chunks * depth * columns * (2 * rows + 2 * cycles),
            bytes_accessed=chunks * depth * columns * 2,
            transcendentals=0,
        ),
        compiler_params=pltpu.CompilerParams(vmem_limit_bytes=VMEM_LIMIT),
    )(modes, odd, basis)


def modes_kernel(alm_hbm, table_hbm, out_ref, alm_ref, table_ref, lhs_ref, low_ref, held_ref, turned_ref, alm_sem, sems):
    parts = sems.shape[0]
    total_slots = table_ref.shape[0]
    slots = total_slots // parts
    targets, rows = out_ref.shape[:2]
    cycles = rows // C
    height = held_ref.shape[1] // total_slots
    alm_copy = pltpu.make_async_copy(alm_hbm, alm_ref, alm_sem)
    alm_copy.start()
    start_some(table_hbm, table_ref, sems)
    lhs_ref[...] = jnp.zeros_like(lhs_ref)
    alm_copy.wait()

    def stack_rows(part, carry):
        for slot in range(slots):
            at = part * slots + slot
            for chan in range(C):
                lhs_ref[slot, 2 * chan : 2 * chan + 2, :] = alm_ref[at, chan].astype(jnp.float32)
            low_ref[at] = lhs_ref[slot].astype(jnp.bfloat16)
        return carry

    lax.fori_loop(0, parts, stack_rows, 0)

    def some_slots(part, carry):
        next_part(table_hbm, table_ref, sems, part)
        for slot in range(slots):
            at = part * slots + slot
            result = jnp.dot(low_ref[at], table_ref[at], preferred_element_type=jnp.float32)
            for lanes in range(held_ref.shape[0]):
                piece = result[0:height, lanes * LANES : (lanes + 1) * LANES]
                held_ref[lanes, pl.ds(pl.multiple_of(at * height, 8), height), :] = piece
        return carry

    lax.fori_loop(0, parts, some_slots, 0)
    for chan in range(C):
        for lanes in range(held_ref.shape[0]):
            both = [held_ref[lanes, pl.ds(2 * chan + part, total_slots, stride=height), :] for part in range(2)]
            turned_ref[chan, lanes * LANES : (lanes + 1) * LANES, :] = jnp.concatenate(both, axis=0).T
    for target in range(targets):
        span = slice(target * cycles, (target + 1) * cycles)
        block = jnp.concatenate([turned_ref[chan, span, :] for chan in range(C)], axis=0)
        out_ref[target] = block.astype(jnp.bfloat16)


def make_modes(alm, legendre, targets):
    slot_count, degrees, total = legendre.shape
    slots = 4
    parts = slot_count // slots
    width = 2 * slot_count
    height = round_up(2 * C, 8)
    return pl.pallas_call(
        modes_kernel,
        in_specs=[pl.BlockSpec(memory_space=pl.ANY)] * 2,
        out_specs=pl.BlockSpec(memory_space=pltpu.VMEM),
        out_shape=jax.ShapeDtypeStruct((targets, C * (total // targets), width), jnp.bfloat16),
        scratch_shapes=[
            pltpu.VMEM(alm.shape, jnp.bfloat16),
            pltpu.VMEM(legendre.shape, jnp.bfloat16),
            pltpu.VMEM((slots, round_up(2 * C, 16), degrees), jnp.float32),
            pltpu.VMEM((slot_count, round_up(2 * C, 16), degrees), jnp.bfloat16),
            pltpu.VMEM((total // LANES, slot_count * height, LANES), jnp.float32),
            pltpu.VMEM((C, total, width), jnp.float32),
            pltpu.SemaphoreType.DMA,
            pltpu.SemaphoreType.DMA((parts,)),
        ],
        cost_estimate=pl.CostEstimate(
            flops=2 * slot_count * degrees * total * 2 * C,
            bytes_accessed=slot_count * degrees * (total + 2 * C) * 2,
            transcendentals=0,
        ),
        compiler_params=pltpu.CompilerParams(vmem_limit_bytes=62 * 1024 * 1024),
    )(alm, legendre)


def analysis_kernel(table_hbm, spectra_ref, out_ref, table_ref, total_ref, turned_ref, sems):
    parts = sems.shape[0]
    total_slots = table_ref.shape[0]
    slots = total_slots // parts
    start_some(table_hbm, table_ref, sems)
    spectra = spectra_ref[...]
    lane = lax.broadcasted_iota(jnp.int32, (1, spectra.shape[1]), 1) % total_slots
    total_ref[...] = jnp.zeros_like(total_ref)

    def some_slots(part, carry):
        masks = [(lane == part * slots + slot).astype(jnp.float32).astype(jnp.bfloat16) for slot in range(slots)]
        rhs = jnp.concatenate([spectra_ref[...] * mask for mask in masks], axis=0)
        next_part(table_hbm, table_ref, sems, part)
        lhs = jnp.concatenate([table_ref[part * slots + slot] for slot in range(slots)], axis=1)
        total_ref[...] += jnp.dot(lhs, rhs, preferred_element_type=jnp.float32)
        return carry

    lax.fori_loop(0, parts, some_slots, 0)
    for lanes in range(turned_ref.shape[0]):
        span = slice(lanes * LANES, (lanes + 1) * LANES)
        turned_ref[lanes] = total_ref[span, :].T
        for slot in range(total_slots):
            out_ref[slot, :, span] = turned_ref[lanes, pl.ds(slot, 2, stride=total_slots), :]


def analyse(legendre, spectra):
    slot_count, degrees, total = legendre.shape
    slots = 4
    width = 2 * slot_count
    vmem = pl.BlockSpec(memory_space=pltpu.VMEM)
    return pl.pallas_call(
        analysis_kernel,
        in_specs=[pl.BlockSpec(memory_space=pl.ANY), vmem],
        out_specs=vmem,
        out_shape=jax.ShapeDtypeStruct((slot_count, 2, degrees), jnp.float32),
        scratch_shapes=[
            pltpu.VMEM(legendre.shape, jnp.bfloat16),
            pltpu.VMEM((degrees, width), jnp.float32),
            pltpu.VMEM((degrees // LANES, width, LANES), jnp.float32),
            pltpu.SemaphoreType.DMA((slot_count // slots,)),
        ],
        cost_estimate=pl.CostEstimate(
            flops=2 * slot_count * degrees * total * width,
            bytes_accessed=slot_count * degrees * total * 2,
            transcendentals=0,
        ),
        compiler_params=pltpu.CompilerParams(vmem_limit_bytes=62 * 1024 * 1024),
    )(legendre, spectra)


def from_other_tiles(sends):
    count = len(sends)
    got = [sends[0]]
    for hop in range(1, count):
        got.append(lax.ppermute(sends[hop], "tile", [(at, (at + hop) % count) for at in range(count)]))
    return got


def in_tile_order(got):
    count = len(got)
    tile_at = lax.axis_index("tile")
    stacked = jnp.stack(got)
    return jnp.stack(
        [lax.dynamic_index_in_dim(stacked, (tile_at - at) % count, 0, keepdims=False) for at in range(count)]
    )


def body(alm, legendre, order_of_slot):
    tile_count = lax.axis_size("tile")
    band_count = lax.axis_size("band")
    tile_at = lax.axis_index("tile")
    slot_count = alm.shape[0]
    targets = band_count * tile_count
    cycles = legendre.shape[2] // targets
    padded = round_up(cycles, 8)
    depth = 2 * L
    width = 2 * slot_count
    group_width = math.lcm(width, LANES)
    groups = depth // group_width
    plain = group_width == width and padded == cycles
    axes = ("band", "tile")

    partial = make_modes(alm, legendre, targets)
    partial = lax.all_to_all(partial, axes, split_axis=0, concat_axis=0, tiled=True)
    modes = partial.reshape(band_count, tile_count, C * cycles, width)
    if not plain:
        modes = jnp.sum(modes.astype(jnp.float32), axis=1).astype(jnp.bfloat16)
        modes = modes.reshape(groups, group_width // width, C, cycles, width)
        modes = modes.transpose(0, 2, 3, 1, 4).reshape(groups, C, cycles, group_width)
        modes = jnp.pad(modes, ((0, 0), (0, 0), (0, padded - cycles), (0, 0)))
        modes = modes.reshape(groups, 1, C * padded, group_width)

    order_rows = jnp.broadcast_to(order_of_slot.reshape(band_count, 1, slot_count), (band_count, 2, slot_count))
    order_rows = order_rows.reshape(depth)
    basis = make_basis(order_rows.astype(jnp.float32)[:, None], slot_count)
    odd = (order_rows % 2).astype(jnp.float32)[None, :]
    vectors, spectra = run_ilc(modes, odd, basis)

    if not plain:
        spectra = spectra[:, 0, :cycles].reshape(groups, cycles, group_width // width, width)
        spectra = spectra.transpose(0, 2, 1, 3).reshape(band_count, 1, cycles, width)
        spectra = jnp.broadcast_to(spectra, (band_count, tile_count, cycles, width))
    spectra = spectra.reshape(targets, cycles, width)
    routed = lax.all_to_all(spectra, axes, split_axis=0, concat_axis=0, tiled=True)
    vectors, routed = lax.optimization_barrier((vectors, routed))
    ilc_alm = analyse(legendre, routed.reshape(targets * cycles, width))

    own = vectors[:, :cycles].transpose(1, 2, 0).reshape(cycles, tile_count, NLON // tile_count)
    own = own.transpose(1, 0, 2)
    sends = [
        lax.dynamic_index_in_dim(own, (tile_at + hop) % tile_count, 0, keepdims=False) for hop in range(tile_count)
    ]
    ilc_map = in_tile_order(from_other_tiles(sends))
    return (ilc_map.reshape(tile_count * cycles, NLON // tile_count), ilc_alm)


def solution(mesh):
    placed = (P("band", None, None, "tile"), P("band", "tile", None), P())
    return jax.shard_map(
        body,
        mesh=mesh,
        in_specs=placed,
        out_specs=(P("band", "tile"), P("band", None, "tile")),
        check_vma=False,
    )
```

```python
import functools
import math

import jax
import jax.numpy as jnp
from jax import lax
from jax.experimental import pallas as pl
from jax.experimental.pallas import tpu as pltpu
from jax.sharding import PartitionSpec as P

C = 9
L = 1024
NLON = 4096
HALO = 32

RIDGE = 0.1
EPSILON = 1e-06

WINDOW = 2 * HALO + 1
LANES = NLON // HALO
HALF = LANES // 2
PAIRS = [(a_at, b_at) for a_at in range(C) for b_at in range(a_at, C)]
VMEM_LIMIT = 48 * 1024 * 1024
CHUNK = 8
IN_FLIGHT = 4


def round_up(value, multiple):
    return (value + multiple - 1) // multiple * multiple


def cos_turns(turns):
    nearest = (turns + 12582912.0) - 12582912.0
    quarter = 1.0 - 4.0 * jnp.abs(turns - nearest)
    square = quarter * quarter
    tail = square * (1.6044118478736e-04 - square * 3.598843235e-06)
    tail = square * (-4.68175413531868e-03 + tail)
    tail = square * (7.96926262461670e-02 + tail)
    tail = square * (-6.45964097506246e-01 + tail)
    return quarter * (1.57079632679490 + tail)


def basis_kernel(slots, order_ref, basis_ref):
    rows = 64
    begin = pl.program_id(0) * order_ref.shape[0]
    row = lax.broadcasted_iota(jnp.int32, (rows, LANES), 0)
    lane = lax.broadcasted_iota(jnp.int32, (rows, LANES), 1)
    cell = (HALO * (lane % HALF) + lane // HALF).astype(jnp.float32) / NLON
    scaling = 1.0 / math.sqrt(L)
    for first in range(0, order_ref.shape[0], rows):
        span = slice(first, first + rows)
        part = (row + (begin + first)) // slots % 2
        order = jnp.broadcast_to(order_ref[span, :], (rows, LANES))
        turns = order * cell + part.astype(jnp.float32) * 0.25
        step = order * (2.0 / NLON)
        before = cos_turns(turns) * scaling
        now = cos_turns(turns + step) * scaling
        twice = 2.0 * cos_turns(step)
        for column in range(HALO // 2):
            at = column % (CHUNK // 2) * LANES
            basis_ref[column // (CHUNK // 2), span, at : at + LANES] = before.astype(jnp.bfloat16)
            if column < HALO // 2 - 1:
                before, now = now, twice * now - before


def make_basis(order_rows, slots):
    rows = order_rows.shape[0]
    block = 256
    chunks = HALO // CHUNK
    columns = CHUNK // 2 * LANES
    return pl.pallas_call(
        functools.partial(basis_kernel, slots),
        grid=(rows // block,),
        in_specs=[pl.BlockSpec((block, 1), lambda at: (at, 0))],
        out_specs=pl.BlockSpec((chunks, block, columns), lambda at: (0, at, 0)),
        out_shape=jax.ShapeDtypeStruct((chunks, rows, columns), jnp.bfloat16),
        cost_estimate=pl.CostEstimate(
            flops=rows * chunks * columns * 8, bytes_accessed=rows * chunks * columns * 2, transcendentals=0
        ),
        compiler_params=pltpu.CompilerParams(vmem_limit_bytes=VMEM_LIMIT),
    )(order_rows)


def part_copy(source, target, sems, part):
    count = source.shape[0] // sems.shape[0]
    span = pl.ds(part * count, count)
    return pltpu.make_async_copy(source.at[span], target.at[span], sems.at[part])


def start_some(source, target, sems):
    for part in range(min(IN_FLIGHT, sems.shape[0])):
        part_copy(source, target, sems, part).start()


def next_part(source, target, sems, part):
    part_copy(source, target, sems, part).wait()

    @pl.when(part + IN_FLIGHT < sems.shape[0])
    def _():
        part_copy(source, target, sems, part + IN_FLIGHT).start()


def reciprocal(value):
    guess = pl.reciprocal(value, approx=True)
    return guess * (2.0 - value * guess)


def combine(entry, map_of):
    diagonal = [entry(at, at) for at in range(C)]
    trace = diagonal[0]
    for at in range(1, C):
        trace = trace + diagonal[at]
    ridge = RIDGE * (trace * (1.0 / C) + WINDOW * EPSILON)
    upper, inverses, ones, maps = {}, [], [], []
    top = bottom = None
    for row in range(C):
        ratios = [upper[at, row] * inverses[at] for at in range(row)]
        pivot = diagonal[row] + ridge
        for at in range(row):
            pivot = pivot - ratios[at] * upper[at, row]
        inverse = reciprocal(pivot)
        for col in range(row + 1, C):
            value = entry(row, col)
            for at in range(row):
                value = value - ratios[at] * upper[at, col]
            upper[row, col] = value
        one = 1.0
        own = map_of(row)
        for at in range(row):
            one = one - (ratios[at] if at == 0 else ratios[at] * ones[at])
            own = own - ratios[at] * maps[at]
        scaled = inverse if row == 0 else inverse * one
        term = scaled * own
        top = term if top is None else top + term
        term = scaled if row == 0 else scaled * one
        bottom = term if bottom is None else bottom + term
        inverses.append(inverse)
        ones.append(one)
        maps.append(own)
    return top * reciprocal(bottom)


def ilc_kernel(modes_ref, odd_ref, basis_hbm, ilc_ref, spectra_ref, basis_ref, lhs_ref, maps_ref, sums_ref, low_ref, found_ref, sems):
    groups, shares, rows, width = modes_ref.shape
    chunks = basis_ref.shape[0]
    cycles = rows // C
    second = round_up(rows, 16)
    start_some(basis_hbm, basis_ref, sems)
    for group in range(groups):
        span = slice(group * width, (group + 1) * width)
        odd = odd_ref[:, span]
        values = modes_ref[group, 0].astype(jnp.float32)
        for share in range(1, shares):
            values = values + modes_ref[group, share].astype(jnp.float32)
        lhs_ref[0:rows, span] = (values * (1.0 - odd)).astype(jnp.bfloat16)
        lhs_ref[second : second + rows, span] = (values * odd).astype(jnp.bfloat16)
    low_half = lax.broadcasted_iota(jnp.int32, (cycles, LANES), 1) < HALF
    sums_ref[...] = jnp.zeros_like(sums_ref)

    def map_of(at, chan):
        return maps_ref[at, chan * cycles : (chan + 1) * cycles, :]

    def maps_of_chunk(chunk):
        next_part(basis_hbm, basis_ref, sems, chunk)
        result = jnp.dot(lhs_ref[...], basis_ref[chunk], preferred_element_type=jnp.float32)
        for part in range(CHUNK // 2):
            at = CHUNK * chunk + 2 * part
            for chan in range(C):
                span = slice(chan * cycles, (chan + 1) * cycles)
                even_part = result[span, part * LANES : (part + 1) * LANES]
                odd_part = result[second + chan * cycles : second + (chan + 1) * cycles, part * LANES : (part + 1) * LANES]
                near = even_part + odd_part
                far = even_part - odd_part
                maps_ref[at, span, :] = jnp.where(low_half, near, pltpu.roll(far, HALF, 1))
                maps_ref[at + 1, span, :] = jnp.where(low_half, pltpu.roll(near, HALF, 1), far)

    def add_totals(chunk):
        for pair, (a_at, b_at) in enumerate(PAIRS):
            total = sums_ref[pair]
            for at in range(CHUNK * chunk, CHUNK * (chunk + 1)):
                total = total + map_of(at, a_at) * map_of(at, b_at)
            sums_ref[pair] = total

    maps_of_chunk(0)
    for chunk in range(1, chunks):
        maps_of_chunk(chunk)
        add_totals(chunk - 1)
    add_totals(chunks - 1)
    for pair in range(len(PAIRS)):
        total = sums_ref[pair]
        sums_ref[pair] = total + pltpu.roll(total, 1, 1)

    def solve(at, leaves):
        ahead = [pltpu.roll(map_of(at, chan), LANES - 1, 1) for chan in range(C)]
        before = jnp.maximum(at - 1, 0)
        behind = [pltpu.roll(map_of(before, chan), 1, 1) * leaves for chan in range(C)]

        def entry(a_at, b_at):
            pair = PAIRS.index((a_at, b_at))
            total = sums_ref[pair] + (ahead[a_at] * ahead[b_at] - behind[a_at] * behind[b_at])
            sums_ref[pair] = total
            return total

        value = combine(entry, lambda chan: map_of(at, chan))
        ilc_ref[at] = value
        return value

    def two_vectors(at, first):
        leaves = jnp.where(at == 0, 0.0, 1.0) if first else 1.0
        found = [solve(at, leaves), solve(at + 1, 1.0)]
        near = jnp.where(low_half, found[0], pltpu.roll(found[1], HALF, 1))
        far = jnp.where(low_half, pltpu.roll(found[0], HALF, 1), found[1])
        return jnp.concatenate([near, far], axis=0).astype(jnp.bfloat16)

    def spectra_of(chunk):
        return lax.dot_general(
            low_ref[chunk], basis_ref[chunk], (((1,), (1,)), ((), ())), preferred_element_type=jnp.float32
        )

    found_ref[...] = jnp.zeros_like(found_ref)
    low_ref[...] = jnp.zeros_like(low_ref)

    def solve_chunk(chunk, carry):
        found_ref[...] += spectra_of(jnp.maximum(chunk - 1, 0))
        for part in range(CHUNK // 2):
            low_ref[chunk, :, part * LANES : (part + 1) * LANES] = two_vectors(CHUNK * chunk + 2 * part, part == 0)
        return carry

    lax.fori_loop(0, chunks, solve_chunk, 0)
    found_ref[...] += spectra_of(chunks - 1)
    for group in range(groups):
        span = slice(group * width, (group + 1) * width)
        sign = 1.0 - 2.0 * odd_ref[:, span]
        value = (found_ref[0:cycles, span] + sign * found_ref[cycles:, span]).astype(jnp.bfloat16)
        for share in range(shares):
            spectra_ref[group, share] = value


def run_ilc(modes, odd, basis):
    groups, shares, rows, width = modes.shape
    chunks, depth, columns = basis.shape
    cycles = rows // C
    vmem = pl.BlockSpec(memory_space=pltpu.VMEM)
    return pl.pallas_call(
        ilc_kernel,
        in_specs=[vmem, vmem, pl.BlockSpec(memory_space=pl.ANY)],
        out_specs=[vmem, vmem],
        out_shape=[
            jax.ShapeDtypeStruct((HALO, cycles, LANES), jnp.float32),
            jax.ShapeDtypeStruct((groups, shares, cycles, width), jnp.bfloat16),
        ],
        scratch_shapes=[
            pltpu.VMEM((chunks, depth, columns), jnp.bfloat16),
            pltpu.VMEM((2 * round_up(rows, 16), depth), jnp.bfloat16),
            pltpu.VMEM((HALO, rows, LANES), jnp.float32),
            pltpu.VMEM((len(PAIRS), cycles, LANES), jnp.float32),
            pltpu.VMEM((chunks, 2 * cycles, columns), jnp.bfloat16),
            pltpu.VMEM((2 * cycles, depth), jnp.float32),
            pltpu.SemaphoreType.DMA((chunks,)),
        ],
        cost_estimate=pl.CostEstimate(
            flops=2 * chunks * depth * columns * (2 * rows + 2 * cycles),
            bytes_accessed=chunks * depth * columns * 2,
            transcendentals=0,
        ),
        compiler_params=pltpu.CompilerParams(vmem_limit_bytes=VMEM_LIMIT),
    )(modes, odd, basis)


def modes_kernel(alm_hbm, table_hbm, out_ref, alm_ref, table_ref, lhs_ref, low_ref, held_ref, turned_ref, alm_sem, sems):
    parts = sems.shape[0]
    total_slots = table_ref.shape[0]
    slots = total_slots // parts
    targets, rows = out_ref.shape[:2]
    cycles = rows // C
    height = held_ref.shape[1] // total_slots
    total = table_ref.shape[2]
    alm_copy = pltpu.make_async_copy(alm_hbm, alm_ref, alm_sem)
    alm_copy.start()
    start_some(table_hbm, table_ref, sems)
    lhs_ref[...] = jnp.zeros_like(lhs_ref)
    alm_copy.wait()

    def stack_rows(part, carry):
        for slot in range(slots):
            first = slot % 2 * height
            for chan in range(C):
                span = slice(first + 2 * chan, first + 2 * chan + 2)
                lhs_ref[slot // 2, span, :] = alm_ref[part * slots + slot, chan].astype(jnp.float32)
        for pair in range(slots // 2):
            low_ref[part * (slots // 2) + pair] = lhs_ref[pair].astype(jnp.bfloat16)
        return carry

    lax.fori_loop(0, parts, stack_rows, 0)

    def some_slots(part, carry):
        next_part(table_hbm, table_ref, sems, part)
        for pair in range(slots // 2):
            at = part * slots + 2 * pair
            both = jnp.concatenate([table_ref[at], table_ref[at + 1]], axis=1)
            result = jnp.dot(low_ref[part * (slots // 2) + pair], both, preferred_element_type=jnp.float32)
            for slot in range(2):
                rows = pl.ds(pl.multiple_of((at + slot) * height, 8), height)
                own = result[slot * height : (slot + 1) * height, slot * total : (slot + 1) * total]
                for lanes in range(held_ref.shape[0]):
                    held_ref[lanes, rows, :] = own[:, lanes * LANES : (lanes + 1) * LANES]
        return carry

    lax.fori_loop(0, parts, some_slots, 0)
    for chan in range(C):
        for lanes in range(held_ref.shape[0]):
            both = [held_ref[lanes, pl.ds(2 * chan + part, total_slots, stride=height), :] for part in range(2)]
            turned_ref[chan, lanes * LANES : (lanes + 1) * LANES, :] = jnp.concatenate(both, axis=0).T
    for target in range(targets):
        span = slice(target * cycles, (target + 1) * cycles)
        block = jnp.concatenate([turned_ref[chan, span, :] for chan in range(C)], axis=0)
        out_ref[target] = block.astype(jnp.bfloat16)


def make_modes(alm, legendre, targets):
    slot_count, degrees, total = legendre.shape
    slots = 4
    parts = slot_count // slots
    width = 2 * slot_count
    height = round_up(2 * C, 8)
    return pl.pallas_call(
        modes_kernel,
        in_specs=[pl.BlockSpec(memory_space=pl.ANY)] * 2,
        out_specs=pl.BlockSpec(memory_space=pltpu.VMEM),
        out_shape=jax.ShapeDtypeStruct((targets, C * (total // targets), width), jnp.bfloat16),
        scratch_shapes=[
            pltpu.VMEM(alm.shape, jnp.bfloat16),
            pltpu.VMEM(legendre.shape, jnp.bfloat16),
            pltpu.VMEM((slots // 2, 2 * height, degrees), jnp.float32),
            pltpu.VMEM((slot_count // 2, 2 * height, degrees), jnp.bfloat16),
            pltpu.VMEM((total // LANES, slot_count * height, LANES), jnp.float32),
            pltpu.VMEM((C, total, width), jnp.float32),
            pltpu.SemaphoreType.DMA,
            pltpu.SemaphoreType.DMA((parts,)),
        ],
        cost_estimate=pl.CostEstimate(
            flops=2 * slot_count * degrees * total * 2 * C,
            bytes_accessed=slot_count * degrees * (total + 2 * C) * 2,
            transcendentals=0,
        ),
        compiler_params=pltpu.CompilerParams(vmem_limit_bytes=62 * 1024 * 1024),
    )(alm, legendre)


def analysis_kernel(table_hbm, spectra_ref, out_ref, table_ref, turned_ref, sems):
    parts = sems.shape[0]
    total_slots, degrees, total = table_ref.shape
    slots = total_slots // parts
    start_some(table_hbm, table_ref, sems)
    turned_ref[...] = spectra_ref[...].astype(jnp.float32).T

    def some_slots(part, carry):
        first = pl.multiple_of(part * slots, slots)
        rows = [turned_ref[pl.ds(first + share * total_slots, slots), :] for share in range(2)]
        lhs = jnp.concatenate(rows, axis=0).astype(jnp.bfloat16)
        next_part(table_hbm, table_ref, sems, part)
        table = table_ref[pl.ds(first, slots)].reshape(slots * degrees, total)
        result = lax.dot_general(lhs, table, (((1,), (1,)), ((), ())), preferred_element_type=jnp.float32)
        for slot in range(slots):
            span = slice(slot * degrees, (slot + 1) * degrees)
            out_ref[part * slots + slot, 0:1, :] = result[slot : slot + 1, span]
            out_ref[part * slots + slot, 1:2, :] = result[slots + slot : slots + slot + 1, span]
        return carry

    lax.fori_loop(0, parts, some_slots, 0)


def analyse(legendre, spectra):
    slot_count, degrees, total = legendre.shape
    slots = 8
    width = 2 * slot_count
    vmem = pl.BlockSpec(memory_space=pltpu.VMEM)
    return pl.pallas_call(
        analysis_kernel,
        in_specs=[pl.BlockSpec(memory_space=pl.ANY), vmem],
        out_specs=vmem,
        out_shape=jax.ShapeDtypeStruct((slot_count, 2, degrees), jnp.float32),
        scratch_shapes=[
            pltpu.VMEM(legendre.shape, jnp.bfloat16),
            pltpu.VMEM((width, total), jnp.float32),
            pltpu.SemaphoreType.DMA((slot_count // slots,)),
        ],
        cost_estimate=pl.CostEstimate(
            flops=2 * slot_count * degrees * total * 2 * slots,
            bytes_accessed=slot_count * degrees * total * 2,
            transcendentals=0,
        ),
        compiler_params=pltpu.CompilerParams(vmem_limit_bytes=50 * 1024 * 1024),
    )(legendre, spectra)


def from_other_tiles(sends):
    count = len(sends)
    got = [sends[0]]
    for hop in range(1, count):
        got.append(lax.ppermute(sends[hop], "tile", [(at, (at + hop) % count) for at in range(count)]))
    return got


def in_tile_order(got):
    count = len(got)
    tile_at = lax.axis_index("tile")
    stacked = jnp.stack(got)
    return jnp.stack(
        [lax.dynamic_index_in_dim(stacked, (tile_at - at) % count, 0, keepdims=False) for at in range(count)]
    )


def body(alm, legendre, order_of_slot):
    tile_count = lax.axis_size("tile")
    band_count = lax.axis_size("band")
    tile_at = lax.axis_index("tile")
    slot_count = alm.shape[0]
    targets = band_count * tile_count
    cycles = legendre.shape[2] // targets
    padded = round_up(cycles, 8)
    depth = 2 * L
    width = 2 * slot_count
    group_width = math.lcm(width, LANES)
    groups = depth // group_width
    plain = group_width == width and padded == cycles
    axes = ("band", "tile")

    partial = make_modes(alm, legendre, targets)
    partial = lax.all_to_all(partial, axes, split_axis=0, concat_axis=0, tiled=True)
    modes = partial.reshape(band_count, tile_count, C * cycles, width)
    if not plain:
        modes = jnp.sum(modes.astype(jnp.float32), axis=1).astype(jnp.bfloat16)
        modes = modes.reshape(groups, group_width // width, C, cycles, width)
        modes = modes.transpose(0, 2, 3, 1, 4).reshape(groups, C, cycles, group_width)
        modes = jnp.pad(modes, ((0, 0), (0, 0), (0, padded - cycles), (0, 0)))
        modes = modes.reshape(groups, 1, C * padded, group_width)

    order_rows = jnp.broadcast_to(order_of_slot.reshape(band_count, 1, slot_count), (band_count, 2, slot_count))
    order_rows = order_rows.reshape(depth)
    basis = make_basis(order_rows.astype(jnp.float32)[:, None], slot_count)
    odd = (order_rows % 2).astype(jnp.float32)[None, :]
    vectors, spectra = run_ilc(modes, odd, basis)

    if not plain:
        spectra = spectra[:, 0, :cycles].reshape(groups, cycles, group_width // width, width)
        spectra = spectra.transpose(0, 2, 1, 3).reshape(band_count, 1, cycles, width)
        spectra = jnp.broadcast_to(spectra, (band_count, tile_count, cycles, width))
    spectra = spectra.reshape(targets, cycles, width)
    routed = lax.all_to_all(spectra, axes, split_axis=0, concat_axis=0, tiled=True)
    vectors, routed = lax.optimization_barrier((vectors, routed))
    ilc_alm = analyse(legendre, routed.reshape(targets * cycles, width))

    own = vectors[:, :cycles].transpose(1, 2, 0).reshape(cycles, tile_count, NLON // tile_count)
    own = own.transpose(1, 0, 2)
    sends = [
        lax.dynamic_index_in_dim(own, (tile_at + hop) % tile_count, 0, keepdims=False) for hop in range(tile_count)
    ]
    ilc_map = in_tile_order(from_other_tiles(sends))
    return (ilc_map.reshape(tile_count * cycles, NLON // tile_count), ilc_alm)


def solution(mesh):
    placed = (P("band", None, None, "tile"), P("band", "tile", None), P())
    return jax.shard_map(
        body,
        mesh=mesh,
        in_specs=placed,
        out_specs=(P("band", "tile"), P("band", None, "tile")),
        check_vma=False,
    )
```

```python
import functools
import math

import jax
import jax.numpy as jnp
from jax import lax
from jax.experimental import pallas as pl
from jax.experimental.pallas import tpu as pltpu
from jax.sharding import PartitionSpec as P

C = 9
L = 1024
NLON = 4096
HALO = 32

RIDGE = 0.1
EPSILON = 1e-06

WINDOW = 2 * HALO + 1
LANES = NLON // HALO
HALF = LANES // 2
REST = C - 1
PAIRS = [(a_at, b_at) for a_at in range(REST) for b_at in range(a_at, REST)] + [(a_at, REST) for a_at in range(REST)]
SUMS = len(PAIRS) + 1
VMEM_LIMIT = 48 * 1024 * 1024
CHUNK = 8
IN_FLIGHT = 3


def round_up(value, multiple):
    return (value + multiple - 1) // multiple * multiple


def cos_turns(turns):
    nearest = (turns + 12582912.0) - 12582912.0
    quarter = 1.0 - 4.0 * jnp.abs(turns - nearest)
    square = quarter * quarter
    tail = square * (1.6044118478736e-04 - square * 3.598843235e-06)
    tail = square * (-4.68175413531868e-03 + tail)
    tail = square * (7.96926262461670e-02 + tail)
    tail = square * (-6.45964097506246e-01 + tail)
    return quarter * (1.57079632679490 + tail)


def basis_kernel(slots, order_ref, basis_ref):
    rows = 64
    begin = pl.program_id(0) * order_ref.shape[0]
    row = lax.broadcasted_iota(jnp.int32, (rows, LANES), 0)
    lane = lax.broadcasted_iota(jnp.int32, (rows, LANES), 1)
    cell = (HALO * (lane % HALF) + lane // HALF).astype(jnp.float32) / NLON
    scaling = 1.0 / math.sqrt(L)
    for first in range(0, order_ref.shape[0], rows):
        span = slice(first, first + rows)
        part = (row + (begin + first)) // slots % 2
        order = jnp.broadcast_to(order_ref[span, :], (rows, LANES))
        turns = order * cell + part.astype(jnp.float32) * 0.25
        step = order * (2.0 / NLON)
        before = cos_turns(turns) * scaling
        now = cos_turns(turns + step) * scaling
        twice = 2.0 * cos_turns(step)
        for column in range(HALO // 2):
            at = column % (CHUNK // 2) * LANES
            basis_ref[column // (CHUNK // 2), span, at : at + LANES] = before.astype(jnp.bfloat16)
            if column < HALO // 2 - 1:
                before, now = now, twice * now - before


def make_basis(order_rows, slots):
    rows = order_rows.shape[0]
    block = 256
    chunks = HALO // CHUNK
    columns = CHUNK // 2 * LANES
    return pl.pallas_call(
        functools.partial(basis_kernel, slots),
        grid=(rows // block,),
        in_specs=[pl.BlockSpec((block, 1), lambda at: (at, 0))],
        out_specs=pl.BlockSpec((chunks, block, columns), lambda at: (0, at, 0)),
        out_shape=jax.ShapeDtypeStruct((chunks, rows, columns), jnp.bfloat16),
        cost_estimate=pl.CostEstimate(
            flops=rows * chunks * columns * 8, bytes_accessed=rows * chunks * columns * 2, transcendentals=0
        ),
        compiler_params=pltpu.CompilerParams(vmem_limit_bytes=VMEM_LIMIT),
    )(order_rows)


def part_copy(source, target, sems, part):
    count = source.shape[0] // sems.shape[0]
    span = pl.ds(part * count, count)
    return pltpu.make_async_copy(source.at[span], target.at[span], sems.at[part])


def start_some(source, target, sems):
    for part in range(min(IN_FLIGHT, sems.shape[0])):
        part_copy(source, target, sems, part).start()


def next_part(source, target, sems, part):
    part_copy(source, target, sems, part).wait()

    @pl.when(part + IN_FLIGHT < sems.shape[0])
    def _():
        part_copy(source, target, sems, part + IN_FLIGHT).start()


def reciprocal(value):
    guess = pl.reciprocal(value, approx=True)
    return guess * (2.0 - value * guess)


def combine(sum_of, map_of):
    ridge = RIDGE * (sum_of(SUMS - 1) * (1.0 / C) + WINDOW * EPSILON)
    upper, inverses, rights, maps = {}, [], [], []
    value = map_of(REST)
    for row in range(REST):
        ratios = [upper[at, row] * inverses[at] for at in range(row)]
        pivot = sum_of(PAIRS.index((row, row))) + (ridge + ridge)
        for at in range(row):
            pivot = pivot - ratios[at] * upper[at, row]
        inverse = reciprocal(pivot)
        right = ridge - sum_of(PAIRS.index((row, REST)))
        own = map_of(row)
        for at in range(row):
            right = right - ratios[at] * rights[at]
            own = own - ratios[at] * maps[at]
        for col in range(row + 1, REST):
            entry = sum_of(PAIRS.index((row, col))) + ridge
            for at in range(row):
                entry = entry - ratios[at] * upper[at, col]
            upper[row, col] = entry
        value = value + (right * inverse) * own
        inverses.append(inverse)
        rights.append(right)
        maps.append(own)
    return value


def ilc_kernel(modes_ref, odd_ref, basis_hbm, ilc_ref, spectra_ref, basis_ref, lhs_ref, maps_ref, sums_ref, low_ref, found_ref, sems):
    groups, shares, rows, width = modes_ref.shape
    columns = basis_ref.shape[2]
    depth = lhs_ref.shape[1]
    pieces = depth // basis_ref.shape[1]
    chunks = basis_ref.shape[0] // pieces
    cycles = rows // C
    second = round_up(rows, 16)
    start_some(basis_hbm, basis_ref, sems)
    for group in range(groups):
        span = slice(group * width, (group + 1) * width)
        odd = odd_ref[:, span]
        values = modes_ref[group, 0].astype(jnp.float32)
        for share in range(1, shares):
            values = values + modes_ref[group, share].astype(jnp.float32)
        lhs_ref[0:rows, span] = (values * (1.0 - odd)).astype(jnp.bfloat16)
        lhs_ref[second : second + rows, span] = (values * odd).astype(jnp.bfloat16)
    low_half = lax.broadcasted_iota(jnp.int32, (cycles, LANES), 1) < HALF
    sums_ref[...] = jnp.zeros_like(sums_ref)

    def store_maps(at, maps):
        squares = maps[0] * maps[0]
        for chan in range(1, C):
            squares = squares + maps[chan] * maps[chan]
            maps_ref[at, chan - 1] = maps[chan] - maps[0]
        maps_ref[at, REST] = maps[0]
        maps_ref[at, C] = squares

    def maps_of_chunk(chunk):
        for piece in range(pieces):
            next_part(basis_hbm, basis_ref, sems, chunk * pieces + piece)
        basis = basis_ref[chunk * pieces : (chunk + 1) * pieces].reshape(depth, columns)
        result = jnp.dot(lhs_ref[...], basis, preferred_element_type=jnp.float32)
        for part in range(CHUNK // 2):
            at = CHUNK * chunk + 2 * part
            lanes = slice(part * LANES, (part + 1) * LANES)
            left, right = [], []
            for chan in range(C):
                even_part = result[chan * cycles : (chan + 1) * cycles, lanes]
                odd_part = result[second + chan * cycles : second + (chan + 1) * cycles, lanes]
                near = even_part + odd_part
                far = even_part - odd_part
                left.append(jnp.where(low_half, near, pltpu.roll(far, HALF, 1)))
                right.append(jnp.where(low_half, pltpu.roll(near, HALF, 1), far))
            store_maps(at, left)
            store_maps(at + 1, right)

    def product(at, pair):
        if pair == SUMS - 1:
            return maps_ref[at, C]
        a_at, b_at = PAIRS[pair]
        return maps_ref[at, a_at] * maps_ref[at, b_at]

    def add_totals(chunk):
        for pair in range(SUMS):
            total = sums_ref[pair]
            for at in range(CHUNK * chunk, CHUNK * (chunk + 1)):
                total = total + product(at, pair)
            sums_ref[pair] = total

    maps_of_chunk(0)
    for chunk in range(1, chunks):
        maps_of_chunk(chunk)
        add_totals(chunk - 1)
    add_totals(chunks - 1)
    for pair in range(SUMS):
        total = sums_ref[pair]
        sums_ref[pair] = pltpu.roll(total, 1, 1) + pltpu.roll(total, 2, 1)

    def solve(at):
        def sum_of(pair):
            own = product(at, pair)
            total = sums_ref[pair] + own
            sums_ref[pair] = total - pltpu.roll(own, 2, 1)
            return total

        value = combine(sum_of, lambda chan: pltpu.roll(maps_ref[at, chan], 1, 1))
        value = pltpu.roll(value, LANES - 1, 1)
        ilc_ref[at] = value
        return value

    def two_vectors(at):
        found = [solve(at), solve(at + 1)]
        near = jnp.where(low_half, found[0], pltpu.roll(found[1], HALF, 1))
        far = jnp.where(low_half, pltpu.roll(found[0], HALF, 1), found[1])
        return jnp.concatenate([near, far], axis=0).astype(jnp.bfloat16)

    def spectra_of(chunk):
        basis = basis_ref[pl.ds(chunk * pieces, pieces)].reshape(depth, columns)
        return lax.dot_general(
            low_ref[chunk], basis, (((1,), (1,)), ((), ())), preferred_element_type=jnp.float32
        )

    found_ref[...] = jnp.zeros_like(found_ref)
    low_ref[...] = jnp.zeros_like(low_ref)

    def solve_chunk(chunk, carry):
        found_ref[...] += spectra_of(jnp.maximum(chunk - 1, 0))
        for part in range(CHUNK // 2):
            low_ref[chunk, :, part * LANES : (part + 1) * LANES] = two_vectors(CHUNK * chunk + 2 * part)
        return carry

    lax.fori_loop(0, chunks, solve_chunk, 0)
    found_ref[...] += spectra_of(chunks - 1)
    for group in range(groups):
        span = slice(group * width, (group + 1) * width)
        sign = 1.0 - 2.0 * odd_ref[:, span]
        value = (found_ref[0:cycles, span] + sign * found_ref[cycles:, span]).astype(jnp.bfloat16)
        for share in range(shares):
            spectra_ref[group, share] = value


def run_ilc(modes, odd, basis):
    groups, shares, rows, width = modes.shape
    chunks, depth, columns = basis.shape
    pieces = 2
    basis = basis.reshape(chunks * pieces, depth // pieces, columns)
    cycles = rows // C
    vmem = pl.BlockSpec(memory_space=pltpu.VMEM)
    return pl.pallas_call(
        ilc_kernel,
        in_specs=[vmem, vmem, pl.BlockSpec(memory_space=pl.ANY)],
        out_specs=[vmem, vmem],
        out_shape=[
            jax.ShapeDtypeStruct((HALO, cycles, LANES), jnp.float32),
            jax.ShapeDtypeStruct((groups, shares, cycles, width), jnp.bfloat16),
        ],
        scratch_shapes=[
            pltpu.VMEM(basis.shape, jnp.bfloat16),
            pltpu.VMEM((2 * round_up(rows, 16), depth), jnp.bfloat16),
            pltpu.VMEM((HALO, C + 1, cycles, LANES), jnp.float32),
            pltpu.VMEM((SUMS, cycles, LANES), jnp.float32),
            pltpu.VMEM((chunks, 2 * cycles, columns), jnp.bfloat16),
            pltpu.VMEM((2 * cycles, depth), jnp.float32),
            pltpu.SemaphoreType.DMA((chunks * pieces,)),
        ],
        cost_estimate=pl.CostEstimate(
            flops=2 * chunks * depth * columns * (2 * rows + 2 * cycles),
            bytes_accessed=chunks * depth * columns * 2,
            transcendentals=0,
        ),
        compiler_params=pltpu.CompilerParams(vmem_limit_bytes=VMEM_LIMIT),
    )(modes, odd, basis)


def modes_kernel(alm_hbm, table_hbm, out_ref, alm_ref, table_ref, lhs_ref, held_ref, turned_ref, alm_sem, sems):
    parts = sems.shape[0]
    total_slots = table_ref.shape[0]
    slots = total_slots // parts
    targets, rows = out_ref.shape[:2]
    cycles = rows // C
    height = held_ref.shape[1] // total_slots
    total = table_ref.shape[2]
    alm_copy = pltpu.make_async_copy(alm_hbm, alm_ref, alm_sem)
    alm_copy.start()
    start_some(table_hbm, table_ref, sems)
    lhs_ref[...] = jnp.zeros_like(lhs_ref)
    alm_copy.wait()

    def stack_rows(part):
        for slot in range(slots):
            first = slot % 2 * height
            for chan in range(C):
                span = slice(first + 2 * chan, first + 2 * chan + 2)
                lhs_ref[part % 2, slot // 2, span, :] = alm_ref[part * slots + slot, chan].astype(jnp.float32)

    stack_rows(0)

    def some_slots(part, carry):
        next_part(table_hbm, table_ref, sems, part)
        for pair in range(slots // 2):
            at = part * slots + 2 * pair
            both = jnp.concatenate([table_ref[at], table_ref[at + 1]], axis=1)
            lhs = lhs_ref[part % 2, pair].astype(jnp.bfloat16)
            result = jnp.dot(lhs, both, preferred_element_type=jnp.float32)
            for slot in range(2):
                rows = pl.ds(pl.multiple_of((at + slot) * height, 8), height)
                own = result[slot * height : (slot + 1) * height, slot * total : (slot + 1) * total]
                for lanes in range(held_ref.shape[0]):
                    held_ref[lanes, rows, :] = own[:, lanes * LANES : (lanes + 1) * LANES]

        stack_rows(jnp.minimum(part + 1, parts - 1))
        return carry

    lax.fori_loop(0, parts, some_slots, 0)
    for chan in range(C):
        for lanes in range(held_ref.shape[0]):
            both = [held_ref[lanes, pl.ds(2 * chan + part, total_slots, stride=height), :] for part in range(2)]
            turned_ref[chan, lanes * LANES : (lanes + 1) * LANES, :] = jnp.concatenate(both, axis=0).T
    for target in range(targets):
        span = slice(target * cycles, (target + 1) * cycles)
        block = jnp.concatenate([turned_ref[chan, span, :] for chan in range(C)], axis=0)
        out_ref[target] = block.astype(jnp.bfloat16)


def make_modes(alm, legendre, targets):
    slot_count, degrees, total = legendre.shape
    slots = 4
    parts = slot_count // slots
    width = 2 * slot_count
    height = round_up(2 * C, 8)
    return pl.pallas_call(
        modes_kernel,
        in_specs=[pl.BlockSpec(memory_space=pl.ANY)] * 2,
        out_specs=pl.BlockSpec(memory_space=pltpu.VMEM),
        out_shape=jax.ShapeDtypeStruct((targets, C * (total // targets), width), jnp.bfloat16),
        scratch_shapes=[
            pltpu.VMEM(alm.shape, jnp.bfloat16),
            pltpu.VMEM(legendre.shape, jnp.bfloat16),
            pltpu.VMEM((2, slots // 2, 2 * height, degrees), jnp.float32),
            pltpu.VMEM((total // LANES, slot_count * height, LANES), jnp.float32),
            pltpu.VMEM((C, total, width), jnp.float32),
            pltpu.SemaphoreType.DMA,
            pltpu.SemaphoreType.DMA((parts,)),
        ],
        cost_estimate=pl.CostEstimate(
            flops=2 * slot_count * degrees * total * 2 * C,
            bytes_accessed=slot_count * degrees * (total + 2 * C) * 2,
            transcendentals=0,
        ),
        compiler_params=pltpu.CompilerParams(vmem_limit_bytes=62 * 1024 * 1024),
    )(alm, legendre)


def analysis_kernel(table_hbm, spectra_ref, out_ref, table_ref, turned_ref, sems):
    total_slots, degrees, total = table_ref.shape
    slots = 8
    pieces = sems.shape[0] * slots // total_slots
    few = slots // pieces
    start_some(table_hbm, table_ref, sems)
    turned_ref[...] = spectra_ref[...].astype(jnp.float32).T

    def some_slots(part, carry):
        first = pl.multiple_of(part * slots, slots)
        rows = [turned_ref[pl.ds(first + share * total_slots, slots), :] for share in range(2)]
        lhs = jnp.concatenate(rows, axis=0).astype(jnp.bfloat16)
        for piece in range(pieces):
            next_part(table_hbm, table_ref, sems, part * pieces + piece)
            table = table_ref[pl.ds(first + piece * few, few)].reshape(few * degrees, total)
            result = lax.dot_general(lhs, table, (((1,), (1,)), ((), ())), preferred_element_type=jnp.float32)
            for at in range(few):
                slot = piece * few + at
                span = slice(at * degrees, (at + 1) * degrees)
                out_ref[first + slot, 0:1, :] = result[slot : slot + 1, span]
                out_ref[first + slot, 1:2, :] = result[slots + slot : slots + slot + 1, span]
        return carry

    lax.fori_loop(0, total_slots // slots, some_slots, 0)


def analyse(legendre, spectra):
    slot_count, degrees, total = legendre.shape
    slots = 8
    width = 2 * slot_count
    vmem = pl.BlockSpec(memory_space=pltpu.VMEM)
    return pl.pallas_call(
        analysis_kernel,
        in_specs=[pl.BlockSpec(memory_space=pl.ANY), vmem],
        out_specs=vmem,
        out_shape=jax.ShapeDtypeStruct((slot_count, 2, degrees), jnp.float32),
        scratch_shapes=[
            pltpu.VMEM(legendre.shape, jnp.bfloat16),
            pltpu.VMEM((width, total), jnp.float32),
            pltpu.SemaphoreType.DMA((slot_count // 4,)),
        ],
        cost_estimate=pl.CostEstimate(
            flops=2 * slot_count * degrees * total * 2 * slots,
            bytes_accessed=slot_count * degrees * total * 2,
            transcendentals=0,
        ),
        compiler_params=pltpu.CompilerParams(vmem_limit_bytes=50 * 1024 * 1024),
    )(legendre, spectra)


def from_other_tiles(sends):
    count = len(sends)
    got = [sends[0]]
    for hop in range(1, count):
        got.append(lax.ppermute(sends[hop], "tile", [(at, (at + hop) % count) for at in range(count)]))
    return got


def in_tile_order(got):
    count = len(got)
    tile_at = lax.axis_index("tile")
    stacked = jnp.stack(got)
    return jnp.stack(
        [lax.dynamic_index_in_dim(stacked, (tile_at - at) % count, 0, keepdims=False) for at in range(count)]
    )


def body(alm, legendre, order_of_slot):
    tile_count = lax.axis_size("tile")
    band_count = lax.axis_size("band")
    tile_at = lax.axis_index("tile")
    slot_count = alm.shape[0]
    targets = band_count * tile_count
    cycles = legendre.shape[2] // targets
    padded = round_up(cycles, 8)
    depth = 2 * L
    width = 2 * slot_count
    group_width = math.lcm(width, LANES)
    groups = depth // group_width
    plain = group_width == width and padded == cycles
    axes = ("band", "tile")

    partial = make_modes(alm, legendre, targets)
    partial = lax.all_to_all(partial, axes, split_axis=0, concat_axis=0, tiled=True)
    modes = partial.reshape(band_count, tile_count, C * cycles, width)
    if not plain:
        modes = jnp.sum(modes.astype(jnp.float32), axis=1).astype(jnp.bfloat16)
        modes = modes.reshape(groups, group_width // width, C, cycles, width)
        modes = modes.transpose(0, 2, 3, 1, 4).reshape(groups, C, cycles, group_width)
        modes = jnp.pad(modes, ((0, 0), (0, 0), (0, padded - cycles), (0, 0)))
        modes = modes.reshape(groups, 1, C * padded, group_width)

    order_rows = jnp.broadcast_to(order_of_slot.reshape(band_count, 1, slot_count), (band_count, 2, slot_count))
    order_rows = order_rows.reshape(depth)
    basis = make_basis(order_rows.astype(jnp.float32)[:, None], slot_count)
    odd = (order_rows % 2).astype(jnp.float32)[None, :]
    vectors, spectra = run_ilc(modes, odd, basis)

    if not plain:
        spectra = spectra[:, 0, :cycles].reshape(groups, cycles, group_width // width, width)
        spectra = spectra.transpose(0, 2, 1, 3).reshape(band_count, 1, cycles, width)
        spectra = jnp.broadcast_to(spectra, (band_count, tile_count, cycles, width))
    spectra = spectra.reshape(targets, cycles, width)
    routed = lax.all_to_all(spectra, axes, split_axis=0, concat_axis=0, tiled=True)
    found = in_tile_order(from_other_tiles([vectors[:, :cycles]] * tile_count))
    lanes = LANES // tile_count
    found = lax.dynamic_slice_in_dim(found, tile_at * lanes, lanes, axis=3)
    ilc_map = found.transpose(0, 2, 3, 1).reshape(tile_count * cycles, NLON // tile_count)
    routed, ilc_map = lax.optimization_barrier((routed, ilc_map))
    ilc_alm = analyse(legendre, routed.reshape(targets * cycles, width))
    return (ilc_map, ilc_alm)


def solution(mesh):
    placed = (P("band", None, None, "tile"), P("band", "tile", None), P())
    return jax.shard_map(
        body,
        mesh=mesh,
        in_specs=placed,
        out_specs=(P("band", "tile"), P("band", None, "tile")),
        check_vma=False,
    )
```

```python
import functools
import math

import jax
import jax.numpy as jnp
from jax import lax
from jax.experimental import pallas as pl
from jax.experimental.pallas import tpu as pltpu
from jax.sharding import PartitionSpec as P

C = 9
L = 1024
NLON = 4096
HALO = 32

RIDGE = 0.1
EPSILON = 1e-06

WINDOW = 2 * HALO + 1
LANES = NLON // HALO
HALF = LANES // 2
REST = C - 1
PAIRS = [(a_at, b_at) for a_at in range(REST) for b_at in range(a_at, REST)] + [(a_at, REST) for a_at in range(REST)]
SUMS = len(PAIRS) + 1
VMEM_LIMIT = 48 * 1024 * 1024
CHUNK = 8


def round_up(value, multiple):
    return (value + multiple - 1) // multiple * multiple


def cos_turns(turns):
    nearest = (turns + 12582912.0) - 12582912.0
    quarter = 1.0 - 4.0 * jnp.abs(turns - nearest)
    square = quarter * quarter
    tail = square * (1.6044118478736e-04 - square * 3.598843235e-06)
    tail = square * (-4.68175413531868e-03 + tail)
    tail = square * (7.96926262461670e-02 + tail)
    tail = square * (-6.45964097506246e-01 + tail)
    return quarter * (1.57079632679490 + tail)


def basis_kernel(slots, order_ref, basis_ref):
    rows = 64
    begin = pl.program_id(0) * order_ref.shape[0]
    row = lax.broadcasted_iota(jnp.int32, (rows, LANES), 0)
    lane = lax.broadcasted_iota(jnp.int32, (rows, LANES), 1)
    cell = (HALO * (lane % HALF) + lane // HALF).astype(jnp.float32) / NLON
    scaling = 1.0 / math.sqrt(L)
    for first in range(0, order_ref.shape[0], rows):
        span = slice(first, first + rows)
        part = (row + (begin + first)) // slots % 2
        order = jnp.broadcast_to(order_ref[span, :], (rows, LANES))
        turns = order * cell + part.astype(jnp.float32) * 0.25
        step = order * (2.0 / NLON)
        before = cos_turns(turns) * scaling
        now = cos_turns(turns + step) * scaling
        twice = 2.0 * cos_turns(step)
        for column in range(HALO // 2):
            at = column % (CHUNK // 2) * LANES
            basis_ref[column // (CHUNK // 2), span, at : at + LANES] = before.astype(jnp.bfloat16)
            if column < HALO // 2 - 1:
                before, now = now, twice * now - before


def make_basis(order_rows, slots):
    rows = order_rows.shape[0]
    block = 256
    chunks = HALO // CHUNK
    columns = CHUNK // 2 * LANES
    return pl.pallas_call(
        functools.partial(basis_kernel, slots),
        grid=(rows // block,),
        in_specs=[pl.BlockSpec((block, 1), lambda at: (at, 0))],
        out_specs=pl.BlockSpec((chunks, block, columns), lambda at: (0, at, 0)),
        out_shape=jax.ShapeDtypeStruct((chunks, rows, columns), jnp.bfloat16),
        cost_estimate=pl.CostEstimate(
            flops=rows * chunks * columns * 8, bytes_accessed=rows * chunks * columns * 2, transcendentals=0
        ),
        compiler_params=pltpu.CompilerParams(vmem_limit_bytes=VMEM_LIMIT),
    )(order_rows)


def part_copy(source, target, sems, part):
    count = source.shape[0] // sems.shape[0]
    span = pl.ds(part * count, count)
    return pltpu.make_async_copy(source.at[span], target.at[span], sems.at[part])


def start_parts(source, target, sems):
    for part in range(sems.shape[0]):
        part_copy(source, target, sems, part).start()


def reciprocal(value):
    guess = pl.reciprocal(value, approx=True)
    return guess * (2.0 - value * guess)


def combine(sum_of, map_of):
    ridge = RIDGE * (sum_of(SUMS - 1) * (1.0 / C) + WINDOW * EPSILON)
    upper, inverses, rights, maps = {}, [], [], []
    value = map_of(REST)
    for row in range(REST):
        ratios = [upper[at, row] * inverses[at] for at in range(row)]
        pivot = sum_of(PAIRS.index((row, row))) + (ridge + ridge)
        for at in range(row):
            pivot = pivot - ratios[at] * upper[at, row]
        inverse = reciprocal(pivot)
        right = ridge - sum_of(PAIRS.index((row, REST)))
        own = map_of(row)
        for at in range(row):
            right = right - ratios[at] * rights[at]
            own = own - ratios[at] * maps[at]
        for col in range(row + 1, REST):
            entry = sum_of(PAIRS.index((row, col))) + ridge
            for at in range(row):
                entry = entry - ratios[at] * upper[at, col]
            upper[row, col] = entry
        value = value + (right * inverse) * own
        inverses.append(inverse)
        rights.append(right)
        maps.append(own)
    return value


def ilc_kernel(modes_ref, odd_ref, basis_hbm, ilc_ref, spectra_ref, basis_ref, lhs_ref, maps_ref, sums_ref, low_ref, found_ref, sems):
    groups, shares, rows, width = modes_ref.shape
    columns = basis_ref.shape[2]
    depth = lhs_ref.shape[1]
    pieces = depth // basis_ref.shape[1]
    chunks = basis_ref.shape[0] // pieces
    cycles = rows // C
    second = round_up(rows, 16)
    start_parts(basis_hbm, basis_ref, sems)
    for group in range(groups):
        span = slice(group * width, (group + 1) * width)
        odd = odd_ref[:, span]
        values = modes_ref[group, 0].astype(jnp.float32)
        for share in range(1, shares):
            values = values + modes_ref[group, share].astype(jnp.float32)
        lhs_ref[0:rows, span] = (values * (1.0 - odd)).astype(jnp.bfloat16)
        lhs_ref[second : second + rows, span] = (values * odd).astype(jnp.bfloat16)
    low_half = lax.broadcasted_iota(jnp.int32, (cycles, LANES), 1) < HALF
    sums_ref[...] = jnp.zeros_like(sums_ref)

    def store_maps(at, maps):
        squares = maps[0] * maps[0]
        for chan in range(1, C):
            squares = squares + maps[chan] * maps[chan]
            maps_ref[at, chan - 1] = maps[chan] - maps[0]
        maps_ref[at, REST] = maps[0]
        maps_ref[at, C] = squares

    def maps_of_chunk(chunk):
        for piece in range(pieces):
            part_copy(basis_hbm, basis_ref, sems, chunk * pieces + piece).wait()
        basis = basis_ref[chunk * pieces : (chunk + 1) * pieces].reshape(depth, columns)
        result = jnp.dot(lhs_ref[...], basis, preferred_element_type=jnp.float32)
        for part in range(CHUNK // 2):
            at = CHUNK * chunk + 2 * part
            lanes = slice(part * LANES, (part + 1) * LANES)
            left, right = [], []
            for chan in range(C):
                even_part = result[chan * cycles : (chan + 1) * cycles, lanes]
                odd_part = result[second + chan * cycles : second + (chan + 1) * cycles, lanes]
                near = even_part + odd_part
                far = even_part - odd_part
                left.append(jnp.where(low_half, near, pltpu.roll(far, HALF, 1)))
                right.append(jnp.where(low_half, pltpu.roll(near, HALF, 1), far))
            store_maps(at, left)
            store_maps(at + 1, right)

    def product(at, pair):
        if pair == SUMS - 1:
            return maps_ref[at, C]
        a_at, b_at = PAIRS[pair]
        return maps_ref[at, a_at] * maps_ref[at, b_at]

    def add_totals(chunk):
        for pair in range(SUMS):
            total = sums_ref[pair]
            for at in range(CHUNK * chunk, CHUNK * (chunk + 1)):
                total = total + product(at, pair)
            sums_ref[pair] = total

    maps_of_chunk(0)
    for chunk in range(1, chunks):
        maps_of_chunk(chunk)
        add_totals(chunk - 1)
    add_totals(chunks - 1)
    for pair in range(SUMS):
        total = sums_ref[pair]
        sums_ref[pair] = pltpu.roll(total, 1, 1) + pltpu.roll(total, 2, 1)

    def solve(at):
        def sum_of(pair):
            own = product(at, pair)
            total = sums_ref[pair] + own
            sums_ref[pair] = total - pltpu.roll(own, 2, 1)
            return total

        value = combine(sum_of, lambda chan: pltpu.roll(maps_ref[at, chan], 1, 1))
        value = pltpu.roll(value, LANES - 1, 1)
        ilc_ref[at] = value
        return value

    def two_vectors(at):
        found = [solve(at), solve(at + 1)]
        near = jnp.where(low_half, found[0], pltpu.roll(found[1], HALF, 1))
        far = jnp.where(low_half, pltpu.roll(found[0], HALF, 1), found[1])
        return jnp.concatenate([near, far], axis=0).astype(jnp.bfloat16)

    def spectra_of(chunk):
        basis = basis_ref[pl.ds(chunk * pieces, pieces)].reshape(depth, columns)
        return lax.dot_general(
            low_ref[chunk], basis, (((1,), (1,)), ((), ())), preferred_element_type=jnp.float32
        )

    found_ref[...] = jnp.zeros_like(found_ref)
    low_ref[...] = jnp.zeros_like(low_ref)

    def solve_chunk(chunk, carry):
        found_ref[...] += spectra_of(jnp.maximum(chunk - 1, 0))
        for part in range(CHUNK // 2):
            low_ref[chunk, :, part * LANES : (part + 1) * LANES] = two_vectors(CHUNK * chunk + 2 * part)
        return carry

    lax.fori_loop(0, chunks, solve_chunk, 0)
    found_ref[...] += spectra_of(chunks - 1)
    for group in range(groups):
        span = slice(group * width, (group + 1) * width)
        sign = 1.0 - 2.0 * odd_ref[:, span]
        value = (found_ref[0:cycles, span] + sign * found_ref[cycles:, span]).astype(jnp.bfloat16)
        for share in range(shares):
            spectra_ref[group, share] = value


def run_ilc(modes, odd, basis):
    groups, shares, rows, width = modes.shape
    chunks, depth, columns = basis.shape
    pieces = 2
    basis = basis.reshape(chunks * pieces, depth // pieces, columns)
    cycles = rows // C
    vmem = pl.BlockSpec(memory_space=pltpu.VMEM)
    return pl.pallas_call(
        ilc_kernel,
        in_specs=[vmem, vmem, pl.BlockSpec(memory_space=pl.ANY)],
        out_specs=[vmem, vmem],
        out_shape=[
            jax.ShapeDtypeStruct((HALO, cycles, LANES), jnp.float32),
            jax.ShapeDtypeStruct((groups, shares, cycles, width), jnp.bfloat16),
        ],
        scratch_shapes=[
            pltpu.VMEM(basis.shape, jnp.bfloat16),
            pltpu.VMEM((2 * round_up(rows, 16), depth), jnp.bfloat16),
            pltpu.VMEM((HALO, C + 1, cycles, LANES), jnp.float32),
            pltpu.VMEM((SUMS, cycles, LANES), jnp.float32),
            pltpu.VMEM((chunks, 2 * cycles, columns), jnp.bfloat16),
            pltpu.VMEM((2 * cycles, depth), jnp.float32),
            pltpu.SemaphoreType.DMA((chunks * pieces,)),
        ],
        cost_estimate=pl.CostEstimate(
            flops=2 * chunks * depth * columns * (2 * rows + 2 * cycles),
            bytes_accessed=chunks * depth * columns * 2,
            transcendentals=0,
        ),
        compiler_params=pltpu.CompilerParams(vmem_limit_bytes=VMEM_LIMIT),
    )(modes, odd, basis)


def modes_kernel(alm_hbm, table_hbm, out_ref, alm_ref, table_ref, lhs_ref, held_ref, turned_ref, alm_sem, sems):
    parts = sems.shape[0]
    total_slots = table_ref.shape[0]
    slots = total_slots // parts
    targets, rows = out_ref.shape[:2]
    cycles = rows // C
    height = held_ref.shape[1] // total_slots
    total = table_ref.shape[2]
    alm_copy = pltpu.make_async_copy(alm_hbm, alm_ref, alm_sem)
    alm_copy.start()
    start_parts(table_hbm, table_ref, sems)
    lhs_ref[...] = jnp.zeros_like(lhs_ref)
    alm_copy.wait()

    def stack_rows(part):
        for slot in range(slots):
            first = slot % 2 * height
            for chan in range(C):
                span = slice(first + 2 * chan, first + 2 * chan + 2)
                lhs_ref[part % 2, slot // 2, span, :] = alm_ref[part * slots + slot, chan].astype(jnp.float32)

    stack_rows(0)

    def some_slots(part, carry):
        part_copy(table_hbm, table_ref, sems, part).wait()
        for pair in range(slots // 2):
            at = part * slots + 2 * pair
            both = jnp.concatenate([table_ref[at], table_ref[at + 1]], axis=1)
            lhs = lhs_ref[part % 2, pair].astype(jnp.bfloat16)
            result = jnp.dot(lhs, both, preferred_element_type=jnp.float32)
            for slot in range(2):
                rows = pl.ds(pl.multiple_of((at + slot) * height, 8), height)
                own = result[slot * height : (slot + 1) * height, slot * total : (slot + 1) * total]
                for lanes in range(held_ref.shape[0]):
                    held_ref[lanes, rows, :] = own[:, lanes * LANES : (lanes + 1) * LANES]

        stack_rows(jnp.minimum(part + 1, parts - 1))
        return carry

    lax.fori_loop(0, parts, some_slots, 0)
    for chan in range(C):
        for lanes in range(held_ref.shape[0]):
            both = [held_ref[lanes, pl.ds(2 * chan + part, total_slots, stride=height), :] for part in range(2)]
            turned_ref[chan, lanes * LANES : (lanes + 1) * LANES, :] = jnp.concatenate(both, axis=0).T
    for target in range(targets):
        span = slice(target * cycles, (target + 1) * cycles)
        block = jnp.concatenate([turned_ref[chan, span, :] for chan in range(C)], axis=0)
        out_ref[target] = block.astype(jnp.bfloat16)


def make_modes(alm, legendre, targets):
    slot_count, degrees, total = legendre.shape
    slots = 4
    parts = slot_count // slots
    width = 2 * slot_count
    height = round_up(2 * C, 8)
    return pl.pallas_call(
        modes_kernel,
        in_specs=[pl.BlockSpec(memory_space=pl.ANY)] * 2,
        out_specs=pl.BlockSpec(memory_space=pltpu.VMEM),
        out_shape=jax.ShapeDtypeStruct((targets, C * (total // targets), width), jnp.bfloat16),
        scratch_shapes=[
            pltpu.VMEM(alm.shape, jnp.bfloat16),
            pltpu.VMEM(legendre.shape, jnp.bfloat16),
            pltpu.VMEM((2, slots // 2, 2 * height, degrees), jnp.float32),
            pltpu.VMEM((total // LANES, slot_count * height, LANES), jnp.float32),
            pltpu.VMEM((C, total, width), jnp.float32),
            pltpu.SemaphoreType.DMA,
            pltpu.SemaphoreType.DMA((parts,)),
        ],
        cost_estimate=pl.CostEstimate(
            flops=2 * slot_count * degrees * total * 2 * C,
            bytes_accessed=slot_count * degrees * (total + 2 * C) * 2,
            transcendentals=0,
        ),
        compiler_params=pltpu.CompilerParams(vmem_limit_bytes=62 * 1024 * 1024),
    )(alm, legendre)


def analysis_kernel(table_hbm, spectra_ref, out_ref, table_ref, turned_ref, sems):
    total_slots, degrees, total = table_ref.shape
    slots = 8
    pieces = sems.shape[0] * slots // total_slots
    few = slots // pieces
    start_parts(table_hbm, table_ref, sems)
    turned_ref[...] = spectra_ref[...].astype(jnp.float32).T

    def some_slots(part, carry):
        first = pl.multiple_of(part * slots, slots)
        rows = [turned_ref[pl.ds(first + share * total_slots, slots), :] for share in range(2)]
        lhs = jnp.concatenate(rows, axis=0).astype(jnp.bfloat16)
        for piece in range(pieces):
            part_copy(table_hbm, table_ref, sems, part * pieces + piece).wait()
            table = table_ref[pl.ds(first + piece * few, few)].reshape(few * degrees, total)
            result = lax.dot_general(lhs, table, (((1,), (1,)), ((), ())), preferred_element_type=jnp.float32)
            for at in range(few):
                slot = piece * few + at
                span = slice(at * degrees, (at + 1) * degrees)
                out_ref[first + slot, 0:1, :] = result[slot : slot + 1, span]
                out_ref[first + slot, 1:2, :] = result[slots + slot : slots + slot + 1, span]
        return carry

    lax.fori_loop(0, total_slots // slots, some_slots, 0)


def analyse(legendre, spectra):
    slot_count, degrees, total = legendre.shape
    slots = 8
    width = 2 * slot_count
    vmem = pl.BlockSpec(memory_space=pltpu.VMEM)
    return pl.pallas_call(
        analysis_kernel,
        in_specs=[pl.BlockSpec(memory_space=pl.ANY), vmem],
        out_specs=vmem,
        out_shape=jax.ShapeDtypeStruct((slot_count, 2, degrees), jnp.float32),
        scratch_shapes=[
            pltpu.VMEM(legendre.shape, jnp.bfloat16),
            pltpu.VMEM((width, total), jnp.float32),
            pltpu.SemaphoreType.DMA((slot_count // 4,)),
        ],
        cost_estimate=pl.CostEstimate(
            flops=2 * slot_count * degrees * total * 2 * slots,
            bytes_accessed=slot_count * degrees * total * 2,
            transcendentals=0,
        ),
        compiler_params=pltpu.CompilerParams(vmem_limit_bytes=50 * 1024 * 1024),
    )(legendre, spectra)


def from_other_tiles(sends):
    count = len(sends)
    got = [sends[0]]
    for hop in range(1, count):
        got.append(lax.ppermute(sends[hop], "tile", [(at, (at + hop) % count) for at in range(count)]))
    return got


def in_tile_order(got):
    count = len(got)
    tile_at = lax.axis_index("tile")
    stacked = jnp.stack(got)
    return jnp.stack(
        [lax.dynamic_index_in_dim(stacked, (tile_at - at) % count, 0, keepdims=False) for at in range(count)]
    )


def body(alm, legendre, order_of_slot):
    tile_count = lax.axis_size("tile")
    band_count = lax.axis_size("band")
    tile_at = lax.axis_index("tile")
    slot_count = alm.shape[0]
    targets = band_count * tile_count
    cycles = legendre.shape[2] // targets
    padded = round_up(cycles, 8)
    depth = 2 * L
    width = 2 * slot_count
    group_width = math.lcm(width, LANES)
    groups = depth // group_width
    plain = group_width == width and padded == cycles
    axes = ("band", "tile")

    partial = make_modes(alm, legendre, targets)
    partial = lax.all_to_all(partial, axes, split_axis=0, concat_axis=0, tiled=True)
    modes = partial.reshape(band_count, tile_count, C * cycles, width)
    if not plain:
        modes = jnp.sum(modes.astype(jnp.float32), axis=1).astype(jnp.bfloat16)
        modes = modes.reshape(groups, group_width // width, C, cycles, width)
        modes = modes.transpose(0, 2, 3, 1, 4).reshape(groups, C, cycles, group_width)
        modes = jnp.pad(modes, ((0, 0), (0, 0), (0, padded - cycles), (0, 0)))
        modes = modes.reshape(groups, 1, C * padded, group_width)

    order_rows = jnp.broadcast_to(order_of_slot.reshape(band_count, 1, slot_count), (band_count, 2, slot_count))
    order_rows = order_rows.reshape(depth)
    basis = make_basis(order_rows.astype(jnp.float32)[:, None], slot_count)
    odd = (order_rows % 2).astype(jnp.float32)[None, :]
    vectors, spectra = run_ilc(modes, odd, basis)

    if not plain:
        spectra = spectra[:, 0, :cycles].reshape(groups, cycles, group_width // width, width)
        spectra = spectra.transpose(0, 2, 1, 3).reshape(band_count, 1, cycles, width)
        spectra = jnp.broadcast_to(spectra, (band_count, tile_count, cycles, width))
    spectra = spectra.reshape(targets, cycles, width)
    routed = lax.all_to_all(spectra, axes, split_axis=0, concat_axis=0, tiled=True)
    found = in_tile_order(from_other_tiles([vectors[:, :cycles]] * tile_count))
    lanes = LANES // tile_count
    found = lax.dynamic_slice_in_dim(found, tile_at * lanes, lanes, axis=3)
    ilc_map = found.transpose(0, 2, 3, 1).reshape(tile_count * cycles, NLON // tile_count)
    routed, ilc_map = lax.optimization_barrier((routed, ilc_map))
    ilc_alm = analyse(legendre, routed.reshape(targets * cycles, width))
    return (ilc_map, ilc_alm)


def solution(mesh):
    placed = (P("band", None, None, "tile"), P("band", "tile", None), P())
    return jax.shard_map(
        body,
        mesh=mesh,
        in_specs=placed,
        out_specs=(P("band", "tile"), P("band", None, "tile")),
        check_vma=False,
    )
```

```python
import functools
import math

import jax
import jax.numpy as jnp
from jax import lax
from jax.experimental import pallas as pl
from jax.experimental.pallas import tpu as pltpu
from jax.sharding import PartitionSpec as P

C = 9
L = 1024
NLON = 4096
HALO = 32

RIDGE = 0.1
EPSILON = 1e-06

WINDOW = 2 * HALO + 1
LANES = NLON // HALO
HALF = LANES // 2
REST = C - 1
PAIRS = [(a_at, b_at) for a_at in range(REST) for b_at in range(a_at, REST)] + [(a_at, REST) for a_at in range(REST)]
SUMS = len(PAIRS) + 1
VMEM_LIMIT = 48 * 1024 * 1024
IN_FLIGHT = 6
HALVES = 2
CHUNK = 8


def round_up(value, multiple):
    return (value + multiple - 1) // multiple * multiple


def cos_turns(turns):
    nearest = (turns + 12582912.0) - 12582912.0
    quarter = 1.0 - 4.0 * jnp.abs(turns - nearest)
    square = quarter * quarter
    tail = square * (1.6044118478736e-04 - square * 3.598843235e-06)
    tail = square * (-4.68175413531868e-03 + tail)
    tail = square * (7.96926262461670e-02 + tail)
    tail = square * (-6.45964097506246e-01 + tail)
    return quarter * (1.57079632679490 + tail)


def basis_kernel(slots, order_ref, basis_ref):
    rows = 64
    begin = pl.program_id(0) * order_ref.shape[0]
    row = lax.broadcasted_iota(jnp.int32, (rows, LANES), 0)
    lane = lax.broadcasted_iota(jnp.int32, (rows, LANES), 1)
    cell = (HALO * (lane % HALF) + lane // HALF).astype(jnp.float32) / NLON
    scaling = 1.0 / math.sqrt(L)
    for first in range(0, order_ref.shape[0], rows):
        span = slice(first, first + rows)
        part = (row + (begin + first)) // (slots // HALVES) % 2
        order = jnp.broadcast_to(order_ref[span, :], (rows, LANES))
        turns = order * cell + part.astype(jnp.float32) * 0.25
        step = order * (2.0 / NLON)
        before = cos_turns(turns) * scaling
        now = cos_turns(turns + step) * scaling
        twice = 2.0 * cos_turns(step)
        for column in range(HALO // 2):
            at = column % (CHUNK // 2) * LANES
            basis_ref[column // (CHUNK // 2), span, at : at + LANES] = before.astype(jnp.bfloat16)
            if column < HALO // 2 - 1:
                before, now = now, twice * now - before


def make_basis(order_rows, slots):
    rows = order_rows.shape[0]
    block = 256
    chunks = HALO // CHUNK
    columns = CHUNK // 2 * LANES
    return pl.pallas_call(
        functools.partial(basis_kernel, slots),
        grid=(rows // block,),
        in_specs=[pl.BlockSpec((block, 1), lambda at: (at, 0))],
        out_specs=pl.BlockSpec((chunks, block, columns), lambda at: (0, at, 0)),
        out_shape=jax.ShapeDtypeStruct((chunks, rows, columns), jnp.bfloat16),
        cost_estimate=pl.CostEstimate(
            flops=rows * chunks * columns * 8, bytes_accessed=rows * chunks * columns * 2, transcendentals=0
        ),
        compiler_params=pltpu.CompilerParams(vmem_limit_bytes=VMEM_LIMIT),
    )(order_rows)


def part_copy(source, target, sems, part):
    count = source.shape[0] // sems.shape[0]
    span = pl.ds(part * count, count)
    return pltpu.make_async_copy(source.at[span], target.at[span], sems.at[part])


def start_parts(source, target, sems, count):
    for part in range(min(count, sems.shape[0])):
        part_copy(source, target, sems, part).start()


def next_part(source, target, sems, part):
    part_copy(source, target, sems, part).wait()
    if part + IN_FLIGHT < sems.shape[0]:
        part_copy(source, target, sems, part + IN_FLIGHT).start()


def reciprocal(value):
    guess = pl.reciprocal(value, approx=True)
    return guess * (2.0 - value * guess)


def combine(sum_of, map_of):
    ridge = RIDGE * (sum_of(SUMS - 1) * (1.0 / C) + WINDOW * EPSILON)
    upper, inverses, rights, maps = {}, [], [], []
    value = map_of(REST)
    for row in range(REST):
        ratios = [upper[at, row] * inverses[at] for at in range(row)]
        pivot = sum_of(PAIRS.index((row, row))) + (ridge + ridge)
        for at in range(row):
            pivot = pivot - ratios[at] * upper[at, row]
        inverse = reciprocal(pivot)
        right = ridge - sum_of(PAIRS.index((row, REST)))
        own = map_of(row)
        for at in range(row):
            right = right - ratios[at] * rights[at]
            own = own - ratios[at] * maps[at]
        for col in range(row + 1, REST):
            entry = sum_of(PAIRS.index((row, col))) + ridge
            for at in range(row):
                entry = entry - ratios[at] * upper[at, col]
            upper[row, col] = entry
        value = value + (right * inverse) * own
        inverses.append(inverse)
        rights.append(right)
        maps.append(own)
    return value


def ilc_kernel(modes_ref, odd_ref, basis_hbm, ilc_ref, spectra_ref, basis_ref, lhs_ref, maps_ref, sums_ref, low_ref, found_ref, sems):
    groups, shares, rows, width = modes_ref.shape
    columns = basis_ref.shape[2]
    depth = lhs_ref.shape[1]
    pieces = depth // basis_ref.shape[1]
    chunks = basis_ref.shape[0] // pieces
    cycles = rows // C
    second = round_up(rows, 16)
    start_parts(basis_hbm, basis_ref, sems, IN_FLIGHT)
    for group in range(groups):
        span = slice(group * width, (group + 1) * width)
        odd = odd_ref[:, span]
        values = modes_ref[group, 0].astype(jnp.float32)
        for share in range(1, shares):
            values = values + modes_ref[group, share].astype(jnp.float32)
        lhs_ref[0:rows, span] = (values * (1.0 - odd)).astype(jnp.bfloat16)
        lhs_ref[second : second + rows, span] = (values * odd).astype(jnp.bfloat16)
    low_half = lax.broadcasted_iota(jnp.int32, (cycles, LANES), 1) < HALF
    sums_ref[...] = jnp.zeros_like(sums_ref)

    def store_maps(at, maps):
        squares = maps[0] * maps[0]
        for chan in range(1, C):
            squares = squares + maps[chan] * maps[chan]
            maps_ref[at, chan - 1] = maps[chan] - maps[0]
        maps_ref[at, REST] = maps[0]
        maps_ref[at, C] = squares

    def maps_of_chunk(chunk):
        for piece in range(pieces):
            next_part(basis_hbm, basis_ref, sems, chunk * pieces + piece)
        basis = basis_ref[chunk * pieces : (chunk + 1) * pieces].reshape(depth, columns)
        result = jnp.dot(lhs_ref[...], basis, preferred_element_type=jnp.float32)
        for part in range(CHUNK // 2):
            at = CHUNK * chunk + 2 * part
            lanes = slice(part * LANES, (part + 1) * LANES)
            left, right = [], []
            for chan in range(C):
                even_part = result[chan * cycles : (chan + 1) * cycles, lanes]
                odd_part = result[second + chan * cycles : second + (chan + 1) * cycles, lanes]
                near = even_part + odd_part
                far = even_part - odd_part
                left.append(jnp.where(low_half, near, pltpu.roll(far, HALF, 1)))
                right.append(jnp.where(low_half, pltpu.roll(near, HALF, 1), far))
            store_maps(at, left)
            store_maps(at + 1, right)

    def product(at, pair):
        if pair == SUMS - 1:
            return maps_ref[at, C]
        a_at, b_at = PAIRS[pair]
        return maps_ref[at, a_at] * maps_ref[at, b_at]

    def add_totals(chunk):
        for pair in range(SUMS):
            total = sums_ref[pair]
            for at in range(CHUNK * chunk, CHUNK * (chunk + 1)):
                total = total + product(at, pair)
            sums_ref[pair] = total

    maps_of_chunk(0)
    for chunk in range(1, chunks):
        maps_of_chunk(chunk)
        add_totals(chunk - 1)
    add_totals(chunks - 1)
    for pair in range(SUMS):
        total = sums_ref[pair]
        sums_ref[pair] = pltpu.roll(total, 1, 1) + pltpu.roll(total, 2, 1)

    def solve(at):
        def sum_of(pair):
            own = product(at, pair)
            total = sums_ref[pair] + own
            sums_ref[pair] = total - pltpu.roll(own, 2, 1)
            return total

        value = combine(sum_of, lambda chan: pltpu.roll(maps_ref[at, chan], 1, 1))
        value = pltpu.roll(value, LANES - 1, 1)
        ilc_ref[at] = value
        return value

    def two_vectors(at):
        found = [solve(at), solve(at + 1)]
        near = jnp.where(low_half, found[0], pltpu.roll(found[1], HALF, 1))
        far = jnp.where(low_half, pltpu.roll(found[0], HALF, 1), found[1])
        return jnp.concatenate([near, far], axis=0).astype(jnp.bfloat16)

    def spectra_of(chunk):
        basis = basis_ref[pl.ds(chunk * pieces, pieces)].reshape(depth, columns)
        return lax.dot_general(
            low_ref[chunk], basis, (((1,), (1,)), ((), ())), preferred_element_type=jnp.float32
        )

    found_ref[...] = jnp.zeros_like(found_ref)
    low_ref[...] = jnp.zeros_like(low_ref)

    def solve_chunk(chunk, carry):
        found_ref[...] += spectra_of(jnp.maximum(chunk - 1, 0))
        for part in range(CHUNK // 2):
            low_ref[chunk, :, part * LANES : (part + 1) * LANES] = two_vectors(CHUNK * chunk + 2 * part)
        return carry

    lax.fori_loop(0, chunks, solve_chunk, 0)
    found_ref[...] += spectra_of(chunks - 1)
    for group in range(groups):
        span = slice(group * width, (group + 1) * width)
        sign = 1.0 - 2.0 * odd_ref[:, span]
        value = (found_ref[0:cycles, span] + sign * found_ref[cycles:, span]).astype(jnp.bfloat16)
        for share in range(shares):
            spectra_ref[group, share] = value


def run_ilc(modes, odd, basis):
    groups, shares, rows, width = modes.shape
    chunks, depth, columns = basis.shape
    pieces = 2
    basis = basis.reshape(chunks * pieces, depth // pieces, columns)
    cycles = rows // C
    vmem = pl.BlockSpec(memory_space=pltpu.VMEM)
    return pl.pallas_call(
        ilc_kernel,
        in_specs=[vmem, vmem, pl.BlockSpec(memory_space=pl.ANY)],
        out_specs=[vmem, vmem],
        out_shape=[
            jax.ShapeDtypeStruct((HALO, cycles, LANES), jnp.float32),
            jax.ShapeDtypeStruct((groups, shares, cycles, width), jnp.bfloat16),
        ],
        scratch_shapes=[
            pltpu.VMEM(basis.shape, jnp.bfloat16),
            pltpu.VMEM((2 * round_up(rows, 16), depth), jnp.bfloat16),
            pltpu.VMEM((HALO, C + 1, cycles, LANES), jnp.float32),
            pltpu.VMEM((SUMS, cycles, LANES), jnp.float32),
            pltpu.VMEM((chunks, 2 * cycles, columns), jnp.bfloat16),
            pltpu.VMEM((2 * cycles, depth), jnp.float32),
            pltpu.SemaphoreType.DMA((chunks * pieces,)),
        ],
        cost_estimate=pl.CostEstimate(
            flops=2 * chunks * depth * columns * (2 * rows + 2 * cycles),
            bytes_accessed=chunks * depth * columns * 2,
            transcendentals=0,
        ),
        compiler_params=pltpu.CompilerParams(vmem_limit_bytes=VMEM_LIMIT),
    )(modes, odd, basis)


def modes_kernel(alm_hbm, table_hbm, out_ref, alm_ref, table_ref, lhs_ref, held_ref, turned_ref, alm_sems, sems):
    parts = sems.shape[0]
    total_slots, _, total = table_ref.shape
    slots = total_slots // parts
    targets, rows = out_ref.shape[:2]
    cycles = rows // C
    height = held_ref.shape[1] // total_slots
    start_parts(alm_hbm, alm_ref, alm_sems, parts)
    start_parts(table_hbm, table_ref, sems, IN_FLIGHT)
    lhs_ref[...] = jnp.zeros_like(lhs_ref)

    def stack_rows(part):
        part_copy(alm_hbm, alm_ref, alm_sems, part).wait()
        for slot in range(slots):
            first = slot % 2 * height
            for chan in range(C):
                span = slice(first + 2 * chan, first + 2 * chan + 2)
                lhs_ref[part % 2, slot // 2, span, :] = alm_ref[part * slots + slot, chan].astype(jnp.float32)

    def some_slots(part):
        next_part(table_hbm, table_ref, sems, part)
        for pair in range(slots // 2):
            at = part * slots + 2 * pair
            both = jnp.concatenate([table_ref[at], table_ref[at + 1]], axis=1)
            lhs = lhs_ref[part % 2, pair].astype(jnp.bfloat16)
            result = jnp.dot(lhs, both, preferred_element_type=jnp.float32)
            for slot in range(2):
                rows = slice((at + slot) * height, (at + slot + 1) * height)
                own = result[slot * height : (slot + 1) * height, slot * total : (slot + 1) * total]
                for lanes in range(held_ref.shape[0]):
                    held_ref[lanes, rows, :] = own[:, lanes * LANES : (lanes + 1) * LANES]

    def turn(half):
        count = total_slots // HALVES
        first = half * count * height
        for chan in range(C):
            for lanes in range(held_ref.shape[0]):
                both = [held_ref[lanes, pl.ds(first + 2 * chan + part, count, stride=height), :] for part in range(2)]
                span = slice(half * 2 * count, (half + 1) * 2 * count)
                turned_ref[chan, lanes * LANES : (lanes + 1) * LANES, span] = jnp.concatenate(both, axis=0).T

    stack_rows(0)
    for part in range(parts):
        if part + 1 < parts:
            stack_rows(part + 1)
        some_slots(part)
        if (part + 1) * HALVES % parts == 0:
            turn((part + 1) * HALVES // parts - 1)
    for target in range(targets):
        span = slice(target * cycles, (target + 1) * cycles)
        block = jnp.concatenate([turned_ref[chan, span, :] for chan in range(C)], axis=0)
        out_ref[target] = block.astype(jnp.bfloat16)


def make_modes(alm, legendre, targets):
    slot_count, degrees, total = legendre.shape
    slots = 4
    parts = slot_count // slots
    width = 2 * slot_count
    height = round_up(2 * C, 8)
    return pl.pallas_call(
        modes_kernel,
        in_specs=[pl.BlockSpec(memory_space=pl.ANY)] * 2,
        out_specs=pl.BlockSpec(memory_space=pltpu.VMEM),
        out_shape=jax.ShapeDtypeStruct((targets, C * (total // targets), width), jnp.bfloat16),
        scratch_shapes=[
            pltpu.VMEM(alm.shape, jnp.bfloat16),
            pltpu.VMEM(legendre.shape, jnp.bfloat16),
            pltpu.VMEM((2, slots // 2, 2 * height, degrees), jnp.float32),
            pltpu.VMEM((total // LANES, slot_count * height, LANES), jnp.float32),
            pltpu.VMEM((C, total, width), jnp.float32),
            pltpu.SemaphoreType.DMA((parts,)),
            pltpu.SemaphoreType.DMA((parts,)),
        ],
        cost_estimate=pl.CostEstimate(
            flops=2 * slot_count * degrees * total * 2 * C,
            bytes_accessed=slot_count * degrees * (total + 2 * C) * 2,
            transcendentals=0,
        ),
        compiler_params=pltpu.CompilerParams(vmem_limit_bytes=62 * 1024 * 1024),
    )(alm, legendre)


def analysis_kernel(table_hbm, spectra_ref, out_ref, table_ref, turned_ref, sems):
    total_slots, degrees, total = table_ref.shape
    slots = 8
    pieces = sems.shape[0] * slots // total_slots
    start_parts(table_hbm, table_ref, sems, IN_FLIGHT)
    turned_ref[...] = spectra_ref[...].astype(jnp.float32).T
    count = total_slots // HALVES
    for first in range(0, total_slots, slots):
        row = first // count * 2 * count + first % count
        rows = [turned_ref[row + share * count : row + share * count + slots, :] for share in range(2)]
        lhs = jnp.concatenate(rows, axis=0).astype(jnp.bfloat16)
        for piece in range(pieces):
            next_part(table_hbm, table_ref, sems, first // slots * pieces + piece)
        table = table_ref[first : first + slots].reshape(slots * degrees, total)
        result = lax.dot_general(lhs, table, (((1,), (1,)), ((), ())), preferred_element_type=jnp.float32)
        for slot in range(slots):
            span = slice(slot * degrees, (slot + 1) * degrees)
            out_ref[first + slot, 0:1, :] = result[slot : slot + 1, span]
            out_ref[first + slot, 1:2, :] = result[slots + slot : slots + slot + 1, span]


def analyse(legendre, spectra):
    slot_count, degrees, total = legendre.shape
    slots = 8
    width = 2 * slot_count
    vmem = pl.BlockSpec(memory_space=pltpu.VMEM)
    return pl.pallas_call(
        analysis_kernel,
        in_specs=[pl.BlockSpec(memory_space=pl.ANY), vmem],
        out_specs=vmem,
        out_shape=jax.ShapeDtypeStruct((slot_count, 2, degrees), jnp.float32),
        scratch_shapes=[
            pltpu.VMEM(legendre.shape, jnp.bfloat16),
            pltpu.VMEM((width, total), jnp.float32),
            pltpu.SemaphoreType.DMA((slot_count // 4,)),
        ],
        cost_estimate=pl.CostEstimate(
            flops=2 * slot_count * degrees * total * 2 * slots,
            bytes_accessed=slot_count * degrees * total * 2,
            transcendentals=0,
        ),
        compiler_params=pltpu.CompilerParams(vmem_limit_bytes=50 * 1024 * 1024),
    )(legendre, spectra)


def from_other_tiles(sends):
    count = len(sends)
    got = [sends[0]]
    for hop in range(1, count):
        got.append(lax.ppermute(sends[hop], "tile", [(at, (at + hop) % count) for at in range(count)]))
    return got


def in_tile_order(got):
    count = len(got)
    tile_at = lax.axis_index("tile")
    stacked = jnp.stack(got)
    return jnp.stack(
        [lax.dynamic_index_in_dim(stacked, (tile_at - at) % count, 0, keepdims=False) for at in range(count)]
    )


def body(alm, legendre, order_of_slot):
    tile_count = lax.axis_size("tile")
    band_count = lax.axis_size("band")
    tile_at = lax.axis_index("tile")
    slot_count = alm.shape[0]
    targets = band_count * tile_count
    cycles = legendre.shape[2] // targets
    padded = round_up(cycles, 8)
    depth = 2 * L
    width = 2 * slot_count
    group_width = math.lcm(width, LANES)
    groups = depth // group_width
    plain = group_width == width and padded == cycles
    axes = ("band", "tile")

    partial = make_modes(alm, legendre, targets)
    partial = lax.all_to_all(partial, axes, split_axis=0, concat_axis=0, tiled=True)
    modes = partial.reshape(band_count, tile_count, C * cycles, width)
    if not plain:
        modes = jnp.sum(modes.astype(jnp.float32), axis=1).astype(jnp.bfloat16)
        modes = modes.reshape(groups, group_width // width, C, cycles, width)
        modes = modes.transpose(0, 2, 3, 1, 4).reshape(groups, C, cycles, group_width)
        modes = jnp.pad(modes, ((0, 0), (0, 0), (0, padded - cycles), (0, 0)))
        modes = modes.reshape(groups, 1, C * padded, group_width)

    order_rows = order_of_slot.reshape(band_count * HALVES, 1, slot_count // HALVES)
    order_rows = jnp.broadcast_to(order_rows, (band_count * HALVES, 2, slot_count // HALVES)).reshape(depth)
    basis = make_basis(order_rows.astype(jnp.float32)[:, None], slot_count)
    odd = (order_rows % 2).astype(jnp.float32)[None, :]
    vectors, spectra = run_ilc(modes, odd, basis)

    if not plain:
        spectra = spectra[:, 0, :cycles].reshape(groups, cycles, group_width // width, width)
        spectra = spectra.transpose(0, 2, 1, 3).reshape(band_count, 1, cycles, width)
        spectra = jnp.broadcast_to(spectra, (band_count, tile_count, cycles, width))
    spectra = spectra.reshape(targets, cycles, width)
    routed = lax.all_to_all(spectra, axes, split_axis=0, concat_axis=0, tiled=True)
    found = in_tile_order(from_other_tiles([vectors[:, :cycles]] * tile_count))
    lanes = LANES // tile_count
    found = lax.dynamic_slice_in_dim(found, tile_at * lanes, lanes, axis=3)
    ilc_map = found.transpose(0, 2, 3, 1).reshape(tile_count * cycles, NLON // tile_count)
    routed, ilc_map = lax.optimization_barrier((routed, ilc_map))
    ilc_alm = analyse(legendre, routed.reshape(targets * cycles, width))
    return (ilc_map, ilc_alm)


def solution(mesh):
    placed = (P("band", None, None, "tile"), P("band", "tile", None), P())
    return jax.shard_map(
        body,
        mesh=mesh,
        in_specs=placed,
        out_specs=(P("band", "tile"), P("band", None, "tile")),
        check_vma=False,
    )
```

```python
import functools
import math

import jax
import jax.numpy as jnp
from jax import lax
from jax.experimental import pallas as pl
from jax.experimental.pallas import tpu as pltpu
from jax.sharding import PartitionSpec as P

C = 9
L = 1024
NLON = 4096
HALO = 32

RIDGE = 0.1
EPSILON = 1e-06

WINDOW = 2 * HALO + 1
LANES = NLON // HALO
HALF = LANES // 2
REST = C - 1
PAIRS = [(a_at, b_at) for a_at in range(REST) for b_at in range(a_at, REST)] + [(a_at, REST) for a_at in range(REST)]
SUMS = len(PAIRS) + 1
VMEM_LIMIT = 48 * 1024 * 1024
IN_FLIGHT = 6
HALVES = 2
CHUNK = 8


def round_up(value, multiple):
    return (value + multiple - 1) // multiple * multiple


def cos_turns(turns):
    nearest = (turns + 12582912.0) - 12582912.0
    quarter = 1.0 - 4.0 * jnp.abs(turns - nearest)
    square = quarter * quarter
    tail = square * (1.6044118478736e-04 - square * 3.598843235e-06)
    tail = square * (-4.68175413531868e-03 + tail)
    tail = square * (7.96926262461670e-02 + tail)
    tail = square * (-6.45964097506246e-01 + tail)
    return quarter * (1.57079632679490 + tail)


def basis_kernel(slots, order_ref, basis_ref):
    rows = 64
    begin = pl.program_id(0) * order_ref.shape[0]
    row = lax.broadcasted_iota(jnp.int32, (rows, LANES), 0)
    lane = lax.broadcasted_iota(jnp.int32, (rows, LANES), 1)
    cell = (HALO * (lane % HALF) + lane // HALF).astype(jnp.float32) / NLON
    scaling = 1.0 / math.sqrt(L)
    for first in range(0, order_ref.shape[0], rows):
        span = slice(first, first + rows)
        part = (row + (begin + first)) // (slots // HALVES) % 2
        order = jnp.broadcast_to(order_ref[span, :], (rows, LANES))
        turns = order * cell + part.astype(jnp.float32) * 0.25
        step = order * (2.0 / NLON)
        before = cos_turns(turns) * scaling
        now = cos_turns(turns + step) * scaling
        twice = 2.0 * cos_turns(step)
        for column in range(HALO // 2):
            at = column % (CHUNK // 2) * LANES
            basis_ref[column // (CHUNK // 2), span, at : at + LANES] = before.astype(jnp.bfloat16)
            if column < HALO // 2 - 1:
                before, now = now, twice * now - before


def make_basis(order_rows, slots):
    rows = order_rows.shape[0]
    block = 256
    chunks = HALO // CHUNK
    columns = CHUNK // 2 * LANES
    return pl.pallas_call(
        functools.partial(basis_kernel, slots),
        grid=(rows // block,),
        in_specs=[pl.BlockSpec((block, 1), lambda at: (at, 0))],
        out_specs=pl.BlockSpec((chunks, block, columns), lambda at: (0, at, 0)),
        out_shape=jax.ShapeDtypeStruct((chunks, rows, columns), jnp.bfloat16),
        cost_estimate=pl.CostEstimate(
            flops=rows * chunks * columns * 8, bytes_accessed=rows * chunks * columns * 2, transcendentals=0
        ),
        compiler_params=pltpu.CompilerParams(vmem_limit_bytes=VMEM_LIMIT),
    )(order_rows)


def part_copy(source, target, sems, part):
    count = source.shape[0] // sems.shape[0]
    span = pl.ds(part * count, count)
    return pltpu.make_async_copy(source.at[span], target.at[span], sems.at[part])


def start_parts(source, target, sems, count):
    for part in range(min(count, sems.shape[0])):
        part_copy(source, target, sems, part).start()


def next_part(source, target, sems, part):
    part_copy(source, target, sems, part).wait()
    if part + IN_FLIGHT < sems.shape[0]:
        part_copy(source, target, sems, part + IN_FLIGHT).start()


def reciprocal(value):
    guess = pl.reciprocal(value, approx=True)
    return guess * (2.0 - value * guess)


def combine_steps(sum_of, map_of):
    ridge = RIDGE * (sum_of(SUMS - 1) * (1.0 / C) + WINDOW * EPSILON)
    upper, inverses, rights, maps = {}, [], [], []
    value = map_of(REST)
    for row in range(REST):
        ratios = [upper[at, row] * inverses[at] for at in range(row)]
        pivot = sum_of(PAIRS.index((row, row))) + (ridge + ridge)
        for at in range(row):
            pivot = pivot - ratios[at] * upper[at, row]
        inverse = reciprocal(pivot)
        yield None
        right = ridge - sum_of(PAIRS.index((row, REST)))
        own = map_of(row)
        for at in range(row):
            right = right - ratios[at] * rights[at]
            own = own - ratios[at] * maps[at]
        yield None
        for col in range(row + 1, REST):
            entry = sum_of(PAIRS.index((row, col))) + ridge
            for at in range(row):
                entry = entry - ratios[at] * upper[at, col]
            upper[row, col] = entry
            yield None
        value = value + (right * inverse) * own
        inverses.append(inverse)
        rights.append(right)
        maps.append(own)
    yield value


def in_step(generators):
    for found in zip(*generators):
        pass
    return found


def ilc_kernel(modes_ref, odd_ref, basis_hbm, ilc_ref, spectra_ref, basis_ref, lhs_ref, maps_ref, sums_ref, low_ref, found_ref, sems):
    groups, shares, rows, width = modes_ref.shape
    columns = basis_ref.shape[2]
    depth = lhs_ref.shape[1]
    pieces = depth // basis_ref.shape[1]
    chunks = basis_ref.shape[0] // pieces
    cycles = rows // C
    second = round_up(rows, 16)
    start_parts(basis_hbm, basis_ref, sems, IN_FLIGHT)
    for group in range(groups):
        span = slice(group * width, (group + 1) * width)
        odd = odd_ref[:, span]
        values = modes_ref[group, 0].astype(jnp.float32)
        for share in range(1, shares):
            values = values + modes_ref[group, share].astype(jnp.float32)
        lhs_ref[0:rows, span] = (values * (1.0 - odd)).astype(jnp.bfloat16)
        lhs_ref[second : second + rows, span] = (values * odd).astype(jnp.bfloat16)
    low_half = lax.broadcasted_iota(jnp.int32, (cycles, LANES), 1) < HALF
    sums_ref[...] = jnp.zeros_like(sums_ref)

    def store_maps(at, maps):
        squares = maps[0] * maps[0]
        for chan in range(1, C):
            squares = squares + maps[chan] * maps[chan]
            maps_ref[at, chan - 1] = maps[chan] - maps[0]
        maps_ref[at, REST] = maps[0]
        maps_ref[at, C] = squares

    def maps_of_chunk(chunk):
        for piece in range(pieces):
            next_part(basis_hbm, basis_ref, sems, chunk * pieces + piece)
        basis = basis_ref[chunk * pieces : (chunk + 1) * pieces].reshape(depth, columns)
        result = jnp.dot(lhs_ref[...], basis, preferred_element_type=jnp.float32)
        for part in range(CHUNK // 2):
            at = CHUNK * chunk + 2 * part
            lanes = slice(part * LANES, (part + 1) * LANES)
            left, right = [], []
            for chan in range(C):
                even_part = result[chan * cycles : (chan + 1) * cycles, lanes]
                odd_part = result[second + chan * cycles : second + (chan + 1) * cycles, lanes]
                near = even_part + odd_part
                far = even_part - odd_part
                left.append(jnp.where(low_half, near, pltpu.roll(far, HALF, 1)))
                right.append(jnp.where(low_half, pltpu.roll(near, HALF, 1), far))
            store_maps(at, left)
            store_maps(at + 1, right)

    def product(at, pair):
        if pair == SUMS - 1:
            return maps_ref[at, C]
        a_at, b_at = PAIRS[pair]
        return maps_ref[at, a_at] * maps_ref[at, b_at]

    def add_totals(chunk):
        for pair in range(SUMS):
            total = sums_ref[pair]
            for at in range(CHUNK * chunk, CHUNK * (chunk + 1)):
                total = total + product(at, pair)
            sums_ref[pair] = total

    maps_of_chunk(0)
    for chunk in range(1, chunks):
        maps_of_chunk(chunk)
        add_totals(chunk - 1)
    add_totals(chunks - 1)
    for pair in range(SUMS):
        total = sums_ref[pair]
        sums_ref[pair] = pltpu.roll(total, 1, 1) + pltpu.roll(total, 2, 1)

    def solve_steps(at):
        def sum_of(pair):
            own = product(at, pair)
            total = sums_ref[pair] + own
            sums_ref[pair] = total - pltpu.roll(own, 2, 1)
            return total

        return combine_steps(sum_of, lambda chan: pltpu.roll(maps_ref[at, chan], 1, 1))

    def two_vectors(at):
        found = [pltpu.roll(value, LANES - 1, 1) for value in in_step([solve_steps(at), solve_steps(at + 1)])]
        ilc_ref[at] = found[0]
        ilc_ref[at + 1] = found[1]
        near = jnp.where(low_half, found[0], pltpu.roll(found[1], HALF, 1))
        far = jnp.where(low_half, pltpu.roll(found[0], HALF, 1), found[1])
        return jnp.concatenate([near, far], axis=0).astype(jnp.bfloat16)

    def spectra_of(chunk):
        basis = basis_ref[pl.ds(chunk * pieces, pieces)].reshape(depth, columns)
        return lax.dot_general(
            low_ref[chunk], basis, (((1,), (1,)), ((), ())), preferred_element_type=jnp.float32
        )

    found_ref[...] = jnp.zeros_like(found_ref)
    low_ref[...] = jnp.zeros_like(low_ref)

    def solve_chunk(chunk, carry):
        found_ref[...] += spectra_of(jnp.maximum(chunk - 1, 0))
        for part in range(CHUNK // 2):
            low_ref[chunk, :, part * LANES : (part + 1) * LANES] = two_vectors(CHUNK * chunk + 2 * part)
        return carry

    lax.fori_loop(0, chunks, solve_chunk, 0)
    found_ref[...] += spectra_of(chunks - 1)
    for group in range(groups):
        span = slice(group * width, (group + 1) * width)
        sign = 1.0 - 2.0 * odd_ref[:, span]
        value = (found_ref[0:cycles, span] + sign * found_ref[cycles:, span]).astype(jnp.bfloat16)
        for share in range(shares):
            spectra_ref[group, share] = value


def run_ilc(modes, odd, basis):
    groups, shares, rows, width = modes.shape
    chunks, depth, columns = basis.shape
    pieces = 2
    basis = basis.reshape(chunks * pieces, depth // pieces, columns)
    cycles = rows // C
    vmem = pl.BlockSpec(memory_space=pltpu.VMEM)
    return pl.pallas_call(
        ilc_kernel,
        in_specs=[vmem, vmem, pl.BlockSpec(memory_space=pl.ANY)],
        out_specs=[vmem, vmem],
        out_shape=[
            jax.ShapeDtypeStruct((HALO, cycles, LANES), jnp.float32),
            jax.ShapeDtypeStruct((groups, shares, cycles, width), jnp.bfloat16),
        ],
        scratch_shapes=[
            pltpu.VMEM(basis.shape, jnp.bfloat16),
            pltpu.VMEM((2 * round_up(rows, 16), depth), jnp.bfloat16),
            pltpu.VMEM((HALO, C + 1, cycles, LANES), jnp.float32),
            pltpu.VMEM((SUMS, cycles, LANES), jnp.float32),
            pltpu.VMEM((chunks, 2 * cycles, columns), jnp.bfloat16),
            pltpu.VMEM((2 * cycles, depth), jnp.float32),
            pltpu.SemaphoreType.DMA((chunks * pieces,)),
        ],
        cost_estimate=pl.CostEstimate(
            flops=2 * chunks * depth * columns * (2 * rows + 2 * cycles),
            bytes_accessed=chunks * depth * columns * 2,
            transcendentals=0,
        ),
        compiler_params=pltpu.CompilerParams(vmem_limit_bytes=VMEM_LIMIT),
    )(modes, odd, basis)


def modes_kernel(
    alm_hbm, table_hbm, out_hbm, alm_ref, table_ref, lhs_ref, held_ref, turned_ref, out_ref, alm_sems, sems, out_sems
):
    parts = sems.shape[0]
    total_slots, _, total = table_ref.shape
    slots = total_slots // parts
    targets, rows = out_ref.shape[:2]
    cycles = rows // C
    height = held_ref.shape[1] // total_slots
    start_parts(alm_hbm, alm_ref, alm_sems, parts)
    start_parts(table_hbm, table_ref, sems, IN_FLIGHT)
    lhs_ref[...] = jnp.zeros_like(lhs_ref)

    def stack_rows(part):
        part_copy(alm_hbm, alm_ref, alm_sems, part).wait()
        for slot in range(slots):
            first = slot % 2 * height
            for chan in range(C):
                span = slice(first + 2 * chan, first + 2 * chan + 2)
                lhs_ref[part % 2, slot // 2, span, :] = alm_ref[part * slots + slot, chan].astype(jnp.float32)

    def some_slots(part):
        next_part(table_hbm, table_ref, sems, part)
        for pair in range(slots // 2):
            at = part * slots + 2 * pair
            both = jnp.concatenate([table_ref[at], table_ref[at + 1]], axis=1)
            lhs = lhs_ref[part % 2, pair].astype(jnp.bfloat16)
            result = jnp.dot(lhs, both, preferred_element_type=jnp.float32)
            for slot in range(2):
                rows = slice((at + slot) * height, (at + slot + 1) * height)
                own = result[slot * height : (slot + 1) * height, slot * total : (slot + 1) * total]
                for lanes in range(held_ref.shape[0]):
                    held_ref[lanes, rows, :] = own[:, lanes * LANES : (lanes + 1) * LANES]

    def turn(half):
        count = total_slots // HALVES
        first = half * count * height
        for chan in range(C):
            for lanes in range(held_ref.shape[0]):
                both = [held_ref[lanes, pl.ds(first + 2 * chan + part, count, stride=height), :] for part in range(2)]
                span = slice(half * 2 * count, (half + 1) * 2 * count)
                turned_ref[chan, lanes * LANES : (lanes + 1) * LANES, span] = jnp.concatenate(both, axis=0).T

    stack_rows(0)
    for part in range(parts):
        if part + 1 < parts:
            stack_rows(part + 1)
        some_slots(part)
        if (part + 1) * HALVES % parts == 0:
            turn((part + 1) * HALVES // parts - 1)
    each = targets // out_sems.shape[0]
    for target in range(targets):
        span = slice(target * cycles, (target + 1) * cycles)
        block = jnp.concatenate([turned_ref[chan, span, :] for chan in range(C)], axis=0)
        out_ref[target] = block.astype(jnp.bfloat16)
        if (target + 1) % each == 0:
            part_copy(out_ref, out_hbm, out_sems, target // each).start()
    for part in range(out_sems.shape[0]):
        part_copy(out_ref, out_hbm, out_sems, part).wait()


def make_modes(alm, legendre, targets):
    slot_count, degrees, total = legendre.shape
    slots = 4
    parts = slot_count // slots
    width = 2 * slot_count
    height = round_up(2 * C, 8)
    out = jax.ShapeDtypeStruct((targets, C * (total // targets), width), jnp.bfloat16)
    return pl.pallas_call(
        modes_kernel,
        in_specs=[pl.BlockSpec(memory_space=pl.ANY)] * 2,
        out_specs=pl.BlockSpec(memory_space=pl.ANY),
        out_shape=out,
        scratch_shapes=[
            pltpu.VMEM(alm.shape, jnp.bfloat16),
            pltpu.VMEM(legendre.shape, jnp.bfloat16),
            pltpu.VMEM((2, slots // 2, 2 * height, degrees), jnp.float32),
            pltpu.VMEM((total // LANES, slot_count * height, LANES), jnp.float32),
            pltpu.VMEM((C, total, width), jnp.float32),
            pltpu.VMEM(out.shape, out.dtype),
            pltpu.SemaphoreType.DMA((parts,)),
            pltpu.SemaphoreType.DMA((parts,)),
            pltpu.SemaphoreType.DMA((4,)),
        ],
        cost_estimate=pl.CostEstimate(
            flops=2 * slot_count * degrees * total * 2 * C,
            bytes_accessed=slot_count * degrees * (total + 2 * C) * 2,
            transcendentals=0,
        ),
        compiler_params=pltpu.CompilerParams(vmem_limit_bytes=62 * 1024 * 1024),
    )(alm, legendre)


def analysis_kernel(table_hbm, spectra_ref, out_hbm, table_ref, turned_ref, out_ref, sems, out_sems):
    total_slots, degrees, total = table_ref.shape
    slots = 8
    few = total_slots // sems.shape[0]
    start_parts(table_hbm, table_ref, sems, IN_FLIGHT)
    turned_ref[...] = spectra_ref[...].astype(jnp.float32).T
    count = total_slots // HALVES
    each = total_slots // out_sems.shape[0]
    for first in range(0, total_slots, few):
        group = first // slots * slots
        row = group // count * 2 * count + group % count
        rows = [turned_ref[row + share * count : row + share * count + slots, :] for share in range(2)]
        lhs = jnp.concatenate(rows, axis=0).astype(jnp.bfloat16)
        next_part(table_hbm, table_ref, sems, first // few)
        table = table_ref[first : first + few].reshape(few * degrees, total)
        result = lax.dot_general(lhs, table, (((1,), (1,)), ((), ())), preferred_element_type=jnp.float32)
        for at in range(few):
            slot = first - group + at
            span = slice(at * degrees, (at + 1) * degrees)
            out_ref[first + at, 0:1, :] = result[slot : slot + 1, span]
            out_ref[first + at, 1:2, :] = result[slots + slot : slots + slot + 1, span]
        if (first + few) % each == 0:
            part_copy(out_ref, out_hbm, out_sems, first // each).start()
    for part in range(out_sems.shape[0]):
        part_copy(out_ref, out_hbm, out_sems, part).wait()


def analyse(legendre, spectra):
    slot_count, degrees, total = legendre.shape
    slots = 8
    width = 2 * slot_count
    vmem = pl.BlockSpec(memory_space=pltpu.VMEM)
    return pl.pallas_call(
        analysis_kernel,
        in_specs=[pl.BlockSpec(memory_space=pl.ANY), vmem],
        out_specs=pl.BlockSpec(memory_space=pl.ANY),
        out_shape=jax.ShapeDtypeStruct((slot_count, 2, degrees), jnp.float32),
        scratch_shapes=[
            pltpu.VMEM(legendre.shape, jnp.bfloat16),
            pltpu.VMEM((width, total), jnp.float32),
            pltpu.VMEM((slot_count, 2, degrees), jnp.float32),
            pltpu.SemaphoreType.DMA((slot_count // 4,)),
            pltpu.SemaphoreType.DMA((4,)),
        ],
        cost_estimate=pl.CostEstimate(
            flops=2 * slot_count * degrees * total * 2 * slots,
            bytes_accessed=slot_count * degrees * total * 2,
            transcendentals=0,
        ),
        compiler_params=pltpu.CompilerParams(vmem_limit_bytes=50 * 1024 * 1024),
    )(legendre, spectra)


def from_other_tiles(sends):
    count = len(sends)
    got = [sends[0]]
    for hop in range(1, count):
        got.append(lax.ppermute(sends[hop], "tile", [(at, (at + hop) % count) for at in range(count)]))
    return got


def in_tile_order(got):
    count = len(got)
    tile_at = lax.axis_index("tile")
    stacked = jnp.stack(got)
    return jnp.stack(
        [lax.dynamic_index_in_dim(stacked, (tile_at - at) % count, 0, keepdims=False) for at in range(count)]
    )


def body(alm, legendre, order_of_slot):
    tile_count = lax.axis_size("tile")
    band_count = lax.axis_size("band")
    tile_at = lax.axis_index("tile")
    slot_count = alm.shape[0]
    targets = band_count * tile_count
    cycles = legendre.shape[2] // targets
    padded = round_up(cycles, 8)
    depth = 2 * L
    width = 2 * slot_count
    group_width = math.lcm(width, LANES)
    groups = depth // group_width
    plain = group_width == width and padded == cycles
    axes = ("band", "tile")

    partial = make_modes(alm, legendre, targets)
    partial = lax.all_to_all(partial, axes, split_axis=0, concat_axis=0, tiled=True)
    modes = partial.reshape(band_count, tile_count, C * cycles, width)
    if not plain:
        modes = jnp.sum(modes.astype(jnp.float32), axis=1).astype(jnp.bfloat16)
        modes = modes.reshape(groups, group_width // width, C, cycles, width)
        modes = modes.transpose(0, 2, 3, 1, 4).reshape(groups, C, cycles, group_width)
        modes = jnp.pad(modes, ((0, 0), (0, 0), (0, padded - cycles), (0, 0)))
        modes = modes.reshape(groups, 1, C * padded, group_width)

    order_rows = order_of_slot.reshape(band_count * HALVES, 1, slot_count // HALVES)
    order_rows = jnp.broadcast_to(order_rows, (band_count * HALVES, 2, slot_count // HALVES)).reshape(depth)
    basis = make_basis(order_rows.astype(jnp.float32)[:, None], slot_count)
    odd = (order_rows % 2).astype(jnp.float32)[None, :]
    vectors, spectra = run_ilc(modes, odd, basis)

    if not plain:
        spectra = spectra[:, 0, :cycles].reshape(groups, cycles, group_width // width, width)
        spectra = spectra.transpose(0, 2, 1, 3).reshape(band_count, 1, cycles, width)
        spectra = jnp.broadcast_to(spectra, (band_count, tile_count, cycles, width))
    spectra = spectra.reshape(targets, cycles, width)
    routed = lax.all_to_all(spectra, axes, split_axis=0, concat_axis=0, tiled=True)
    found = in_tile_order(from_other_tiles([vectors[:, :cycles]] * tile_count))
    lanes = LANES // tile_count
    found = lax.dynamic_slice_in_dim(found, tile_at * lanes, lanes, axis=3)
    ilc_map = found.transpose(0, 2, 3, 1).reshape(tile_count * cycles, NLON // tile_count)
    routed, ilc_map = lax.optimization_barrier((routed, ilc_map))
    ilc_alm = analyse(legendre, routed.reshape(targets * cycles, width))
    return (ilc_map, ilc_alm)


def solution(mesh):
    placed = (P("band", None, None, "tile"), P("band", "tile", None), P())
    return jax.shard_map(
        body,
        mesh=mesh,
        in_specs=placed,
        out_specs=(P("band", "tile"), P("band", None, "tile")),
        check_vma=False,
    )
```

```python
import functools
import math

import jax
import jax.numpy as jnp
from jax import lax
from jax.experimental import pallas as pl
from jax.experimental.pallas import tpu as pltpu
from jax.sharding import PartitionSpec as P

C = 9
L = 1024
NLON = 4096
HALO = 32

RIDGE = 0.1
EPSILON = 1e-06

WINDOW = 2 * HALO + 1
LANES = NLON // HALO
HALF = LANES // 2
REST = C - 1
PAIRS = [(a_at, b_at) for a_at in range(REST) for b_at in range(a_at, REST)] + [(a_at, REST) for a_at in range(REST)]
SUMS = len(PAIRS) + 1
VMEM_LIMIT = 48 * 1024 * 1024
IN_FLIGHT = 6
HALVES = 2
CHUNK = 8


def round_up(value, multiple):
    return (value + multiple - 1) // multiple * multiple


def cos_turns(turns):
    nearest = (turns + 12582912.0) - 12582912.0
    quarter = 1.0 - 4.0 * jnp.abs(turns - nearest)
    square = quarter * quarter
    tail = square * (1.6044118478736e-04 - square * 3.598843235e-06)
    tail = square * (-4.68175413531868e-03 + tail)
    tail = square * (7.96926262461670e-02 + tail)
    tail = square * (-6.45964097506246e-01 + tail)
    return quarter * (1.57079632679490 + tail)


def basis_kernel(slots, order_ref, basis_ref):
    rows = 64
    begin = pl.program_id(0) * order_ref.shape[0]
    row = lax.broadcasted_iota(jnp.int32, (rows, LANES), 0)
    lane = lax.broadcasted_iota(jnp.int32, (rows, LANES), 1)
    cell = (HALO * (lane % HALF) + lane // HALF).astype(jnp.float32) / NLON
    scaling = 1.0 / math.sqrt(L)
    for first in range(0, order_ref.shape[0], rows):
        span = slice(first, first + rows)
        part = (row + (begin + first)) // (slots // HALVES) % 2
        order = jnp.broadcast_to(order_ref[span, :], (rows, LANES))
        turns = order * cell + part.astype(jnp.float32) * 0.25
        step = order * (2.0 / NLON)
        before = cos_turns(turns) * scaling
        now = cos_turns(turns + step) * scaling
        twice = 2.0 * cos_turns(step)
        for column in range(HALO // 2):
            at = column % (CHUNK // 2) * LANES
            basis_ref[column // (CHUNK // 2), span, at : at + LANES] = before.astype(jnp.bfloat16)
            if column < HALO // 2 - 1:
                before, now = now, twice * now - before


def make_basis(order_rows, slots):
    rows = order_rows.shape[0]
    block = 256
    chunks = HALO // CHUNK
    columns = CHUNK // 2 * LANES
    return pl.pallas_call(
        functools.partial(basis_kernel, slots),
        grid=(rows // block,),
        in_specs=[pl.BlockSpec((block, 1), lambda at: (at, 0))],
        out_specs=pl.BlockSpec((chunks, block, columns), lambda at: (0, at, 0)),
        out_shape=jax.ShapeDtypeStruct((chunks, rows, columns), jnp.bfloat16),
        cost_estimate=pl.CostEstimate(
            flops=rows * chunks * columns * 8, bytes_accessed=rows * chunks * columns * 2, transcendentals=0
        ),
        compiler_params=pltpu.CompilerParams(vmem_limit_bytes=VMEM_LIMIT),
    )(order_rows)


def part_copy(source, target, sems, part):
    count = source.shape[0] // sems.shape[0]
    span = pl.ds(part * count, count)
    return pltpu.make_async_copy(source.at[span], target.at[span], sems.at[part])


def start_parts(source, target, sems, count):
    for part in range(min(count, sems.shape[0])):
        part_copy(source, target, sems, part).start()


def next_part(source, target, sems, part):
    part_copy(source, target, sems, part).wait()
    if part + IN_FLIGHT < sems.shape[0]:
        part_copy(source, target, sems, part + IN_FLIGHT).start()


def reciprocal(value):
    guess = pl.reciprocal(value, approx=True)
    return guess * (2.0 - value * guess)


def combine_steps(sum_of, map_of):
    ridge = RIDGE * (sum_of(SUMS - 1) * (1.0 / C) + WINDOW * EPSILON)
    upper, inverses, rights, maps = {}, [], [], []
    value = map_of(REST)
    for row in range(REST):
        ratios = [upper[at, row] * inverses[at] for at in range(row)]
        pivot = sum_of(PAIRS.index((row, row))) + (ridge + ridge)
        for at in range(row):
            pivot = pivot - ratios[at] * upper[at, row]
        inverse = reciprocal(pivot)
        yield None
        right = ridge - sum_of(PAIRS.index((row, REST)))
        own = map_of(row)
        for at in range(row):
            right = right - ratios[at] * rights[at]
            own = own - ratios[at] * maps[at]
        yield None
        for col in range(row + 1, REST):
            entry = sum_of(PAIRS.index((row, col))) + ridge
            for at in range(row):
                entry = entry - ratios[at] * upper[at, col]
            upper[row, col] = entry
            yield None
        value = value + (right * inverse) * own
        inverses.append(inverse)
        rights.append(right)
        maps.append(own)
    yield value


def in_step(generators):
    for found in zip(*generators):
        pass
    return found


def ilc_kernel(modes_ref, odd_ref, basis_hbm, ilc_ref, spectra_ref, basis_ref, lhs_ref, maps_ref, sums_ref, low_ref, found_ref, sems):
    groups, shares, rows, width = modes_ref.shape
    columns = basis_ref.shape[2]
    depth = lhs_ref.shape[1]
    pieces = depth // basis_ref.shape[1]
    chunks = basis_ref.shape[0] // pieces
    cycles = rows // C
    second = round_up(rows, 16)
    start_parts(basis_hbm, basis_ref, sems, IN_FLIGHT)
    for group in range(groups):
        span = slice(group * width, (group + 1) * width)
        odd = odd_ref[:, span]
        values = modes_ref[group, 0].astype(jnp.float32)
        for share in range(1, shares):
            values = values + modes_ref[group, share].astype(jnp.float32)
        lhs_ref[0:rows, span] = (values * (1.0 - odd)).astype(jnp.bfloat16)
        lhs_ref[second : second + rows, span] = (values * odd).astype(jnp.bfloat16)
    low_half = lax.broadcasted_iota(jnp.int32, (cycles, LANES), 1) < HALF
    sums_ref[...] = jnp.zeros_like(sums_ref)

    def store_maps(at, maps):
        squares = maps[0] * maps[0]
        for chan in range(1, C):
            squares = squares + maps[chan] * maps[chan]
            maps_ref[at, chan - 1] = maps[chan] - maps[0]
        maps_ref[at, REST] = maps[0]
        maps_ref[at, C] = squares

    def maps_of_chunk(chunk):
        for piece in range(pieces):
            next_part(basis_hbm, basis_ref, sems, chunk * pieces + piece)
        basis = basis_ref[chunk * pieces : (chunk + 1) * pieces].reshape(depth, columns)
        result = jnp.dot(lhs_ref[...], basis, preferred_element_type=jnp.float32)
        for part in range(CHUNK // 2):
            at = CHUNK * chunk + 2 * part
            lanes = slice(part * LANES, (part + 1) * LANES)
            left, right = [], []
            for chan in range(C):
                even_part = result[chan * cycles : (chan + 1) * cycles, lanes]
                odd_part = result[second + chan * cycles : second + (chan + 1) * cycles, lanes]
                near = even_part + odd_part
                far = even_part - odd_part
                left.append(jnp.where(low_half, near, pltpu.roll(far, HALF, 1)))
                right.append(jnp.where(low_half, pltpu.roll(near, HALF, 1), far))
            store_maps(at, left)
            store_maps(at + 1, right)

    def product(at, pair):
        if pair == SUMS - 1:
            return maps_ref[at, C]
        a_at, b_at = PAIRS[pair]
        return maps_ref[at, a_at] * maps_ref[at, b_at]

    def add_totals(chunk):
        for pair in range(SUMS):
            total = sums_ref[pair]
            for at in range(CHUNK * chunk, CHUNK * (chunk + 1)):
                total = total + product(at, pair)
            sums_ref[pair] = total

    maps_of_chunk(0)
    for chunk in range(1, chunks):
        maps_of_chunk(chunk)
        add_totals(chunk - 1)
    add_totals(chunks - 1)
    for pair in range(SUMS):
        total = sums_ref[pair]
        sums_ref[pair] = pltpu.roll(total, 1, 1) + pltpu.roll(total, 2, 1)

    def solve_steps(at):
        def sum_of(pair):
            own = product(at, pair)
            total = sums_ref[pair] + own
            sums_ref[pair] = total - pltpu.roll(own, 2, 1)
            return total

        return combine_steps(sum_of, lambda chan: pltpu.roll(maps_ref[at, chan], 1, 1))

    def two_vectors(at, beside):
        found = in_step([solve_steps(at), solve_steps(at + 1), beside])[:2]
        found = [pltpu.roll(value, LANES - 1, 1) for value in found]
        ilc_ref[at] = found[0]
        ilc_ref[at + 1] = found[1]
        near = jnp.where(low_half, found[0], pltpu.roll(found[1], HALF, 1))
        far = jnp.where(low_half, pltpu.roll(found[0], HALF, 1), found[1])
        return jnp.concatenate([near, far], axis=0).astype(jnp.bfloat16)

    share_rows = depth // (CHUNK // 2)
    per_piece = depth // pieces // share_rows

    def add_spectra(chunk, part):
        first = part % per_piece * share_rows
        basis = basis_ref[chunk * pieces + part // per_piece, first : first + share_rows, :]
        found_ref[:, part * share_rows : (part + 1) * share_rows] += lax.dot_general(
            low_ref[chunk], basis, (((1,), (1,)), ((), ())), preferred_element_type=jnp.float32
        )

    def spectra_steps(chunk, part):
        for _ in range(8):
            yield None
        add_spectra(chunk, part)
        while True:
            yield None

    found_ref[...] = jnp.zeros_like(found_ref)
    low_ref[...] = jnp.zeros_like(low_ref)

    def solve_chunk(chunk, carry):
        before = jnp.maximum(chunk - 1, 0)
        found = [two_vectors(CHUNK * chunk + 2 * part, spectra_steps(before, part)) for part in range(CHUNK // 2)]
        low_ref[chunk] = jnp.concatenate(found, axis=1)
        return carry

    lax.fori_loop(0, chunks, solve_chunk, 0)
    for part in range(CHUNK // 2):
        add_spectra(chunks - 1, part)
    for group in range(groups):
        span = slice(group * width, (group + 1) * width)
        sign = 1.0 - 2.0 * odd_ref[:, span]
        value = (found_ref[0:cycles, span] + sign * found_ref[cycles:, span]).astype(jnp.bfloat16)
        for share in range(shares):
            spectra_ref[group, share] = value


def run_ilc(modes, odd, basis):
    groups, shares, rows, width = modes.shape
    chunks, depth, columns = basis.shape
    pieces = 2
    basis = basis.reshape(chunks * pieces, depth // pieces, columns)
    cycles = rows // C
    vmem = pl.BlockSpec(memory_space=pltpu.VMEM)
    return pl.pallas_call(
        ilc_kernel,
        in_specs=[vmem, vmem, pl.BlockSpec(memory_space=pl.ANY)],
        out_specs=[vmem, vmem],
        out_shape=[
            jax.ShapeDtypeStruct((HALO, cycles, LANES), jnp.float32),
            jax.ShapeDtypeStruct((groups, shares, cycles, width), jnp.bfloat16),
        ],
        scratch_shapes=[
            pltpu.VMEM(basis.shape, jnp.bfloat16),
            pltpu.VMEM((2 * round_up(rows, 16), depth), jnp.bfloat16),
            pltpu.VMEM((HALO, C + 1, cycles, LANES), jnp.float32),
            pltpu.VMEM((SUMS, cycles, LANES), jnp.float32),
            pltpu.VMEM((chunks, 2 * cycles, columns), jnp.bfloat16),
            pltpu.VMEM((2 * cycles, depth), jnp.float32),
            pltpu.SemaphoreType.DMA((chunks * pieces,)),
        ],
        cost_estimate=pl.CostEstimate(
            flops=2 * chunks * depth * columns * (2 * rows + 2 * cycles),
            bytes_accessed=chunks * depth * columns * 2,
            transcendentals=0,
        ),
        compiler_params=pltpu.CompilerParams(vmem_limit_bytes=VMEM_LIMIT),
    )(modes, odd, basis)


def modes_kernel(
    alm_hbm, table_hbm, out_hbm, alm_ref, table_ref, lhs_ref, held_ref, turned_ref, out_ref, alm_sems, sems, out_sems
):
    parts = sems.shape[0]
    total_slots, _, total = table_ref.shape
    slots = total_slots // parts
    targets, rows = out_ref.shape[:2]
    cycles = rows // C
    height = held_ref.shape[1] // total_slots
    start_parts(alm_hbm, alm_ref, alm_sems, parts)
    start_parts(table_hbm, table_ref, sems, IN_FLIGHT)
    lhs_ref[...] = jnp.zeros_like(lhs_ref)

    def stack_rows(part, pair):
        for slot in range(2):
            for chan in range(C):
                span = slice(slot * height + 2 * chan, slot * height + 2 * chan + 2)
                own = alm_ref[part * slots + 2 * pair + slot, chan]
                lhs_ref[part % 2, pair, span, :] = own.astype(jnp.float32)

    def two_slots(part, pair):
        at = part * slots + 2 * pair
        both = jnp.concatenate([table_ref[at], table_ref[at + 1]], axis=1)
        lhs = lhs_ref[part % 2, pair].astype(jnp.bfloat16)
        result = jnp.dot(lhs, both, preferred_element_type=jnp.float32)
        for slot in range(2):
            rows = slice((at + slot) * height, (at + slot + 1) * height)
            own = result[slot * height : (slot + 1) * height, slot * total : (slot + 1) * total]
            for lanes in range(held_ref.shape[0]):
                held_ref[lanes, rows, :] = own[:, lanes * LANES : (lanes + 1) * LANES]

    def turn(half):
        count = total_slots // HALVES
        first = half * count * height
        for chan in range(C):
            for lanes in range(held_ref.shape[0]):
                both = [held_ref[lanes, pl.ds(first + 2 * chan + part, count, stride=height), :] for part in range(2)]
                span = slice(half * 2 * count, (half + 1) * 2 * count)
                turned_ref[chan, lanes * LANES : (lanes + 1) * LANES, span] = jnp.concatenate(both, axis=0).T

    for part in range(-1, parts):
        if part + 1 < parts:
            part_copy(alm_hbm, alm_ref, alm_sems, part + 1).wait()
        if part >= 0:
            next_part(table_hbm, table_ref, sems, part)
        for pair in range(slots // 2):
            if part >= 0:
                two_slots(part, pair)
            if part + 1 < parts:
                stack_rows(part + 1, pair)
        if (part + 1) * HALVES % parts == 0 and part >= 0:
            turn((part + 1) * HALVES // parts - 1)
    each = targets // out_sems.shape[0]
    for target in range(targets):
        span = slice(target * cycles, (target + 1) * cycles)
        block = jnp.concatenate([turned_ref[chan, span, :] for chan in range(C)], axis=0)
        out_ref[target] = block.astype(jnp.bfloat16)
        if (target + 1) % each == 0:
            part_copy(out_ref, out_hbm, out_sems, target // each).start()
    for part in range(out_sems.shape[0]):
        part_copy(out_ref, out_hbm, out_sems, part).wait()


def make_modes(alm, legendre, targets):
    slot_count, degrees, total = legendre.shape
    slots = 4
    parts = slot_count // slots
    width = 2 * slot_count
    height = round_up(2 * C, 8)
    out = jax.ShapeDtypeStruct((targets, C * (total // targets), width), jnp.bfloat16)
    return pl.pallas_call(
        modes_kernel,
        in_specs=[pl.BlockSpec(memory_space=pl.ANY)] * 2,
        out_specs=pl.BlockSpec(memory_space=pl.ANY),
        out_shape=out,
        scratch_shapes=[
            pltpu.VMEM(alm.shape, jnp.bfloat16),
            pltpu.VMEM(legendre.shape, jnp.bfloat16),
            pltpu.VMEM((2, slots // 2, 2 * height, degrees), jnp.float32),
            pltpu.VMEM((total // LANES, slot_count * height, LANES), jnp.float32),
            pltpu.VMEM((C, total, width), jnp.float32),
            pltpu.VMEM(out.shape, out.dtype),
            pltpu.SemaphoreType.DMA((parts,)),
            pltpu.SemaphoreType.DMA((parts,)),
            pltpu.SemaphoreType.DMA((4,)),
        ],
        cost_estimate=pl.CostEstimate(
            flops=2 * slot_count * degrees * total * 2 * C,
            bytes_accessed=slot_count * degrees * (total + 2 * C) * 2,
            transcendentals=0,
        ),
        compiler_params=pltpu.CompilerParams(vmem_limit_bytes=62 * 1024 * 1024),
    )(alm, legendre)


def analysis_kernel(table_hbm, spectra_ref, out_ref, table_ref, turned_ref, sems):
    total_slots, degrees, total = table_ref.shape
    slots = 8
    pieces = sems.shape[0] * slots // total_slots
    start_parts(table_hbm, table_ref, sems, IN_FLIGHT)
    turned_ref[...] = spectra_ref[...].astype(jnp.float32).T
    count = total_slots // HALVES
    for first in range(0, total_slots, slots):
        row = first // count * 2 * count + first % count
        rows = [turned_ref[row + share * count : row + share * count + slots, :] for share in range(2)]
        lhs = jnp.concatenate(rows, axis=0).astype(jnp.bfloat16)
        for piece in range(pieces):
            next_part(table_hbm, table_ref, sems, first // slots * pieces + piece)
        table = table_ref[first : first + slots].reshape(slots * degrees, total)
        result = lax.dot_general(lhs, table, (((1,), (1,)), ((), ())), preferred_element_type=jnp.float32)
        for slot in range(slots):
            span = slice(slot * degrees, (slot + 1) * degrees)
            out_ref[first + slot, 0:1, :] = result[slot : slot + 1, span]
            out_ref[first + slot, 1:2, :] = result[slots + slot : slots + slot + 1, span]


def analyse(legendre, spectra):
    slot_count, degrees, total = legendre.shape
    slots = 8
    width = 2 * slot_count
    vmem = pl.BlockSpec(memory_space=pltpu.VMEM)
    return pl.pallas_call(
        analysis_kernel,
        in_specs=[pl.BlockSpec(memory_space=pl.ANY), vmem],
        out_specs=vmem,
        out_shape=jax.ShapeDtypeStruct((slot_count, 2, degrees), jnp.float32),
        scratch_shapes=[
            pltpu.VMEM(legendre.shape, jnp.bfloat16),
            pltpu.VMEM((width, total), jnp.float32),
            pltpu.SemaphoreType.DMA((slot_count // 4,)),
        ],
        cost_estimate=pl.CostEstimate(
            flops=2 * slot_count * degrees * total * 2 * slots,
            bytes_accessed=slot_count * degrees * total * 2,
            transcendentals=0,
        ),
        compiler_params=pltpu.CompilerParams(vmem_limit_bytes=50 * 1024 * 1024),
    )(legendre, spectra)


def from_other_tiles(sends):
    count = len(sends)
    got = [sends[0]]
    for hop in range(1, count):
        got.append(lax.ppermute(sends[hop], "tile", [(at, (at + hop) % count) for at in range(count)]))
    return got


def in_tile_order(got):
    count = len(got)
    tile_at = lax.axis_index("tile")
    stacked = jnp.stack(got)
    return jnp.stack(
        [lax.dynamic_index_in_dim(stacked, (tile_at - at) % count, 0, keepdims=False) for at in range(count)]
    )


def body(alm, legendre, order_of_slot):
    tile_count = lax.axis_size("tile")
    band_count = lax.axis_size("band")
    tile_at = lax.axis_index("tile")
    slot_count = alm.shape[0]
    targets = band_count * tile_count
    cycles = legendre.shape[2] // targets
    padded = round_up(cycles, 8)
    depth = 2 * L
    width = 2 * slot_count
    group_width = math.lcm(width, LANES)
    groups = depth // group_width
    plain = group_width == width and padded == cycles
    axes = ("band", "tile")

    partial = make_modes(alm, legendre, targets)
    partial = lax.all_to_all(partial, axes, split_axis=0, concat_axis=0, tiled=True)
    modes = partial.reshape(band_count, tile_count, C * cycles, width)
    if not plain:
        modes = jnp.sum(modes.astype(jnp.float32), axis=1).astype(jnp.bfloat16)
        modes = modes.reshape(groups, group_width // width, C, cycles, width)
        modes = modes.transpose(0, 2, 3, 1, 4).reshape(groups, C, cycles, group_width)
        modes = jnp.pad(modes, ((0, 0), (0, 0), (0, padded - cycles), (0, 0)))
        modes = modes.reshape(groups, 1, C * padded, group_width)

    order_rows = order_of_slot.reshape(band_count * HALVES, 1, slot_count // HALVES)
    order_rows = jnp.broadcast_to(order_rows, (band_count * HALVES, 2, slot_count // HALVES)).reshape(depth)
    basis = make_basis(order_rows.astype(jnp.float32)[:, None], slot_count)
    odd = (order_rows % 2).astype(jnp.float32)[None, :]
    vectors, spectra = run_ilc(modes, odd, basis)

    if not plain:
        spectra = spectra[:, 0, :cycles].reshape(groups, cycles, group_width // width, width)
        spectra = spectra.transpose(0, 2, 1, 3).reshape(band_count, 1, cycles, width)
        spectra = jnp.broadcast_to(spectra, (band_count, tile_count, cycles, width))
    spectra = spectra.reshape(targets, cycles, width)
    routed = lax.all_to_all(spectra, axes, split_axis=0, concat_axis=0, tiled=True)
    found = in_tile_order(from_other_tiles([vectors[:, :cycles]] * tile_count))
    lanes = LANES // tile_count
    found = lax.dynamic_slice_in_dim(found, tile_at * lanes, lanes, axis=3)
    ilc_map = found.transpose(0, 2, 3, 1).reshape(tile_count * cycles, NLON // tile_count)
    routed, ilc_map = lax.optimization_barrier((routed, ilc_map))
    ilc_alm = analyse(legendre, routed.reshape(targets * cycles, width))
    return (ilc_map, ilc_alm)


def solution(mesh):
    placed = (P("band", None, None, "tile"), P("band", "tile", None), P())
    return jax.shard_map(
        body,
        mesh=mesh,
        in_specs=placed,
        out_specs=(P("band", "tile"), P("band", None, "tile")),
        check_vma=False,
    )
```

```python
import functools
import math

import jax
import jax.numpy as jnp
from jax import lax
from jax.experimental import pallas as pl
from jax.experimental.pallas import tpu as pltpu
from jax.sharding import PartitionSpec as P

C = 9
L = 1024
NLON = 4096
HALO = 32

RIDGE = 0.1
EPSILON = 1e-06

WINDOW = 2 * HALO + 1
LANES = NLON // HALO
HALF = LANES // 2
REST = C - 1
PAIRS = [(a_at, b_at) for a_at in range(REST) for b_at in range(a_at, REST)] + [(a_at, REST) for a_at in range(REST)]
SUMS = len(PAIRS) + 1
VMEM_LIMIT = 48 * 1024 * 1024
IN_FLIGHT = 6
HALVES = 2
CHUNK = 8


def round_up(value, multiple):
    return (value + multiple - 1) // multiple * multiple


def cos_turns(turns):
    nearest = (turns + 12582912.0) - 12582912.0
    quarter = 1.0 - 4.0 * jnp.abs(turns - nearest)
    square = quarter * quarter
    tail = square * (1.6044118478736e-04 - square * 3.598843235e-06)
    tail = square * (-4.68175413531868e-03 + tail)
    tail = square * (7.96926262461670e-02 + tail)
    tail = square * (-6.45964097506246e-01 + tail)
    return quarter * (1.57079632679490 + tail)


def basis_kernel(slots, order_ref, basis_ref):
    rows = 64
    begin = pl.program_id(0) * order_ref.shape[0]
    row = lax.broadcasted_iota(jnp.int32, (rows, LANES), 0)
    lane = lax.broadcasted_iota(jnp.int32, (rows, LANES), 1)
    cell = (HALO * (lane % HALF) + lane // HALF).astype(jnp.float32) / NLON
    scaling = 1.0 / math.sqrt(L)
    for first in range(0, order_ref.shape[0], rows):
        span = slice(first, first + rows)
        part = (row + (begin + first)) // (slots // HALVES) % 2
        order = jnp.broadcast_to(order_ref[span, :], (rows, LANES))
        turns = order * cell + part.astype(jnp.float32) * 0.25
        step = order * (2.0 / NLON)
        before = cos_turns(turns) * scaling
        now = cos_turns(turns + step) * scaling
        twice = 2.0 * cos_turns(step)
        for column in range(HALO // 2):
            at = column % (CHUNK // 2) * LANES
            basis_ref[column // (CHUNK // 2), span, at : at + LANES] = before.astype(jnp.bfloat16)
            if column < HALO // 2 - 1:
                before, now = now, twice * now - before


def make_basis(order_rows, slots):
    rows = order_rows.shape[0]
    block = 256
    chunks = HALO // CHUNK
    columns = CHUNK // 2 * LANES
    return pl.pallas_call(
        functools.partial(basis_kernel, slots),
        grid=(rows // block,),
        in_specs=[pl.BlockSpec((block, 1), lambda at: (at, 0))],
        out_specs=pl.BlockSpec((chunks, block, columns), lambda at: (0, at, 0)),
        out_shape=jax.ShapeDtypeStruct((chunks, rows, columns), jnp.bfloat16),
        cost_estimate=pl.CostEstimate(
            flops=rows * chunks * columns * 8, bytes_accessed=rows * chunks * columns * 2, transcendentals=0
        ),
        compiler_params=pltpu.CompilerParams(vmem_limit_bytes=VMEM_LIMIT),
    )(order_rows)


def part_copy(source, target, sems, part):
    count = source.shape[0] // sems.shape[0]
    span = pl.ds(part * count, count)
    return pltpu.make_async_copy(source.at[span], target.at[span], sems.at[part])


def start_parts(source, target, sems, count):
    for part in range(min(count, sems.shape[0])):
        part_copy(source, target, sems, part).start()


def next_part(source, target, sems, part, ahead):
    part_copy(source, target, sems, part).wait()
    more = part + ahead < sems.shape[0]
    if isinstance(part, int):
        if more:
            part_copy(source, target, sems, part + ahead).start()
    else:

        @pl.when(more)
        def _():
            part_copy(source, target, sems, part + ahead).start()


def reciprocal(value):
    guess = pl.reciprocal(value, approx=True)
    return guess * (2.0 - value * guess)


def combine_steps(sum_of, map_of):
    ridge = RIDGE * (sum_of(SUMS - 1) * (1.0 / C) + WINDOW * EPSILON)
    upper, inverses, rights, maps = {}, [], [], []
    value = map_of(REST)
    for row in range(REST):
        ratios = [upper[at, row] * inverses[at] for at in range(row)]
        pivot = sum_of(PAIRS.index((row, row))) + (ridge + ridge)
        for at in range(row):
            pivot = pivot - ratios[at] * upper[at, row]
        inverse = reciprocal(pivot)
        yield None
        right = ridge - sum_of(PAIRS.index((row, REST)))
        own = map_of(row)
        for at in range(row):
            right = right - ratios[at] * rights[at]
            own = own - ratios[at] * maps[at]
        yield None
        for col in range(row + 1, REST):
            entry = sum_of(PAIRS.index((row, col))) + ridge
            for at in range(row):
                entry = entry - ratios[at] * upper[at, col]
            upper[row, col] = entry
            yield None
        value = value + (right * inverse) * own
        inverses.append(inverse)
        rights.append(right)
        maps.append(own)
    yield value


def in_step(generators):
    for found in zip(*generators):
        pass
    return found


def ilc_kernel(modes_ref, odd_ref, basis_hbm, ilc_ref, spectra_ref, basis_ref, lhs_ref, maps_ref, sums_ref, low_ref, found_ref, sems):
    groups, shares, rows, width = modes_ref.shape
    columns = basis_ref.shape[2]
    depth = lhs_ref.shape[1]
    pieces, share_rows = found_ref.shape[0], found_ref.shape[2]
    chunks = basis_ref.shape[0] // pieces
    cycles = rows // C
    second = round_up(rows, 16)
    ahead = 2 * pieces
    start_parts(basis_hbm, basis_ref, sems, ahead)
    for group in range(groups):
        span = slice(group * width, (group + 1) * width)
        odd = odd_ref[:, span]
        values = modes_ref[group, 0].astype(jnp.float32)
        for share in range(1, shares):
            values = values + modes_ref[group, share].astype(jnp.float32)
        lhs_ref[0:rows, span] = (values * (1.0 - odd)).astype(jnp.bfloat16)
        lhs_ref[second : second + rows, span] = (values * odd).astype(jnp.bfloat16)
    low_half = lax.broadcasted_iota(jnp.int32, (cycles, LANES), 1) < HALF
    sums_ref[...] = jnp.zeros_like(sums_ref)
    found_ref[...] = jnp.zeros_like(found_ref)
    low_ref[0] = jnp.zeros_like(low_ref[0])

    def store_maps(at, maps):
        squares = maps[0] * maps[0]
        for chan in range(1, C):
            squares = squares + maps[chan] * maps[chan]
            maps_ref[at, chan - 1] = maps[chan] - maps[0]
        maps_ref[at, REST] = maps[0]
        maps_ref[at, C] = squares

    def maps_of_chunk(chunk, carry):
        for piece in range(pieces):
            next_part(basis_hbm, basis_ref, sems, chunk * pieces + piece, ahead)
        basis = basis_ref[pl.ds(chunk * pieces, pieces)].reshape(depth, columns)
        result = jnp.dot(lhs_ref[...], basis, preferred_element_type=jnp.float32)
        for part in range(CHUNK // 2):
            at = CHUNK * chunk + 2 * part
            lanes = slice(part * LANES, (part + 1) * LANES)
            left, right = [], []
            for chan in range(C):
                even_part = result[chan * cycles : (chan + 1) * cycles, lanes]
                odd_part = result[second + chan * cycles : second + (chan + 1) * cycles, lanes]
                near = even_part + odd_part
                far = even_part - odd_part
                left.append(jnp.where(low_half, near, pltpu.roll(far, HALF, 1)))
                right.append(jnp.where(low_half, pltpu.roll(near, HALF, 1), far))
            store_maps(at, left)
            store_maps(at + 1, right)
        vectors = [CHUNK * chunk + part for part in range(CHUNK)]
        for a_at in range(C):
            own = [maps_ref[at, a_at] for at in vectors]
            for b_at in range(a_at, C):
                if (a_at, b_at) == (REST, REST):
                    continue
                pair = PAIRS.index((a_at, b_at))
                total = sums_ref[pair]
                for at, value in zip(vectors, own):
                    total = total + value * (value if a_at == b_at else maps_ref[at, b_at])
                sums_ref[pair] = total
        total = sums_ref[SUMS - 1]
        for at in vectors:
            total = total + maps_ref[at, C]
        sums_ref[SUMS - 1] = total
        return carry

    lax.fori_loop(0, chunks, maps_of_chunk, 0)
    for pair in range(SUMS):
        total = sums_ref[pair]
        sums_ref[pair] = pltpu.roll(total, 1, 1) + pltpu.roll(total, 2, 1)

    def solve_steps(at):
        maps = [maps_ref[at, chan] for chan in range(C + 1)]

        def sum_of(pair):
            own = maps[C] if pair == SUMS - 1 else maps[PAIRS[pair][0]] * maps[PAIRS[pair][1]]
            total = sums_ref[pair] + own
            sums_ref[pair] = total - pltpu.roll(own, 2, 1)
            return total

        return combine_steps(sum_of, lambda chan: pltpu.roll(maps[chan], 1, 1))

    def add_spectra(chunk, part, low):
        lhs = jnp.concatenate([low_ref[low, at] for at in range(pieces)], axis=1)
        found_ref[part] += lax.dot_general(
            lhs, basis_ref[chunk * pieces + part], (((1,), (1,)), ((), ())), preferred_element_type=jnp.float32
        )

    def two_vectors(pair_at, carry):
        at = 2 * pair_at
        chunk, part = pair_at // pieces, pair_at % pieces
        add_spectra(jnp.maximum(chunk - 1, 0), part, chunk)
        found = in_step([solve_steps(at), solve_steps(at + 1)])
        found = [pltpu.roll(value, LANES - 1, 1) for value in found]
        ilc_ref[at] = found[0]
        ilc_ref[at + 1] = found[1]
        near = jnp.where(low_half, found[0], pltpu.roll(found[1], HALF, 1))
        far = jnp.where(low_half, pltpu.roll(found[0], HALF, 1), found[1])
        low_ref[chunk + 1, part] = jnp.concatenate([near, far], axis=0).astype(jnp.bfloat16)
        return carry

    lax.fori_loop(0, HALO // 2, two_vectors, 0)
    for part in range(pieces):
        add_spectra(chunks - 1, part, chunks)
    for group in range(groups):
        span = slice(group * width, (group + 1) * width)
        sign = 1.0 - 2.0 * odd_ref[:, span]
        part, first = group * width // share_rows, group * width % share_rows
        result = found_ref[part, :, first : first + width]
        value = (result[0:cycles] + sign * result[cycles:]).astype(jnp.bfloat16)
        for share in range(shares):
            spectra_ref[group, share] = value


def run_ilc(modes, odd, basis):
    groups, shares, rows, width = modes.shape
    chunks, depth, columns = basis.shape
    pieces = CHUNK // 2
    basis = basis.reshape(chunks * pieces, depth // pieces, columns)
    cycles = rows // C
    vmem = pl.BlockSpec(memory_space=pltpu.VMEM)
    return pl.pallas_call(
        ilc_kernel,
        in_specs=[vmem, vmem, pl.BlockSpec(memory_space=pl.ANY)],
        out_specs=[vmem, vmem],
        out_shape=[
            jax.ShapeDtypeStruct((HALO, cycles, LANES), jnp.float32),
            jax.ShapeDtypeStruct((groups, shares, cycles, width), jnp.bfloat16),
        ],
        scratch_shapes=[
            pltpu.VMEM(basis.shape, jnp.bfloat16),
            pltpu.VMEM((2 * round_up(rows, 16), depth), jnp.bfloat16),
            pltpu.VMEM((HALO, C + 1, cycles, LANES), jnp.float32),
            pltpu.VMEM((SUMS, cycles, LANES), jnp.float32),
            pltpu.VMEM((chunks + 1, pieces, 2 * cycles, LANES), jnp.bfloat16),
            pltpu.VMEM((pieces, 2 * cycles, depth // pieces), jnp.float32),
            pltpu.SemaphoreType.DMA((chunks * pieces,)),
        ],
        cost_estimate=pl.CostEstimate(
            flops=2 * chunks * depth * columns * (2 * rows + 2 * cycles),
            bytes_accessed=chunks * depth * columns * 2,
            transcendentals=0,
        ),
        compiler_params=pltpu.CompilerParams(vmem_limit_bytes=VMEM_LIMIT),
    )(modes, odd, basis)


def modes_kernel(
    alm_hbm, table_hbm, out_hbm, alm_ref, table_ref, lhs_ref, held_ref, turned_ref, out_ref, alm_sems, sems, out_sems
):
    parts = sems.shape[0]
    total_slots, _, total = table_ref.shape
    slots = total_slots // parts
    targets, rows = out_ref.shape[:2]
    cycles = rows // C
    height = held_ref.shape[1] // total_slots
    start_parts(alm_hbm, alm_ref, alm_sems, parts)
    start_parts(table_hbm, table_ref, sems, IN_FLIGHT)
    lhs_ref[...] = jnp.zeros_like(lhs_ref)

    def stack_rows(part, pair):
        for slot in range(2):
            for chan in range(C):
                span = slice(slot * height + 2 * chan, slot * height + 2 * chan + 2)
                own = alm_ref[part * slots + 2 * pair + slot, chan]
                lhs_ref[part % 2, pair, span, :] = own.astype(jnp.float32)

    def two_slots(part, pair):
        at = part * slots + 2 * pair
        both = jnp.concatenate([table_ref[at], table_ref[at + 1]], axis=1)
        lhs = lhs_ref[part % 2, pair].astype(jnp.bfloat16)
        result = jnp.dot(lhs, both, preferred_element_type=jnp.float32)
        for slot in range(2):
            rows = pl.ds(pl.multiple_of((at + slot) * height, 8), height)
            own = result[slot * height : (slot + 1) * height, slot * total : (slot + 1) * total]
            for lanes in range(held_ref.shape[0]):
                held_ref[lanes, rows, :] = own[:, lanes * LANES : (lanes + 1) * LANES]

    def some_slots(part, carry):
        next_part(table_hbm, table_ref, sems, part, IN_FLIGHT)
        for pair in range(slots // 2):
            two_slots(part, pair)
            stack_rows(jnp.minimum(part + 1, parts - 1), pair)
        return carry

    def turn(half):
        count = total_slots // HALVES
        first = half * count * height

        def turn_channel(chan, carry):
            for lanes in range(held_ref.shape[0]):
                at = first + 2 * chan
                both = [held_ref[lanes, pl.ds(at + part, count, stride=height), :] for part in range(2)]
                span = slice(half * 2 * count, (half + 1) * 2 * count)
                turned_ref[chan, lanes * LANES : (lanes + 1) * LANES, span] = jnp.concatenate(both, axis=0).T
            return carry

        lax.fori_loop(0, C, turn_channel, 0)

    for part in range(parts):
        part_copy(alm_hbm, alm_ref, alm_sems, part).wait()
    for pair in range(slots // 2):
        stack_rows(0, pair)
    for half in range(HALVES):
        lax.fori_loop(half * parts // HALVES, (half + 1) * parts // HALVES, some_slots, 0)
        turn(half)
    each = targets // out_sems.shape[0]
    for target in range(targets):
        span = slice(target * cycles, (target + 1) * cycles)
        block = jnp.concatenate([turned_ref[chan, span, :] for chan in range(C)], axis=0)
        out_ref[target] = block.astype(jnp.bfloat16)
        if (target + 1) % each == 0:
            part_copy(out_ref, out_hbm, out_sems, target // each).start()
    for part in range(out_sems.shape[0]):
        part_copy(out_ref, out_hbm, out_sems, part).wait()


def make_modes(alm, legendre, targets):
    slot_count, degrees, total = legendre.shape
    slots = 4
    parts = slot_count // slots
    width = 2 * slot_count
    height = round_up(2 * C, 8)
    out = jax.ShapeDtypeStruct((targets, C * (total // targets), width), jnp.bfloat16)
    return pl.pallas_call(
        modes_kernel,
        in_specs=[pl.BlockSpec(memory_space=pl.ANY)] * 2,
        out_specs=pl.BlockSpec(memory_space=pl.ANY),
        out_shape=out,
        scratch_shapes=[
            pltpu.VMEM(alm.shape, jnp.bfloat16),
            pltpu.VMEM(legendre.shape, jnp.bfloat16),
            pltpu.VMEM((2, slots // 2, 2 * height, degrees), jnp.float32),
            pltpu.VMEM((total // LANES, slot_count * height, LANES), jnp.float32),
            pltpu.VMEM((C, total, width), jnp.float32),
            pltpu.VMEM(out.shape, out.dtype),
            pltpu.SemaphoreType.DMA((parts,)),
            pltpu.SemaphoreType.DMA((parts,)),
            pltpu.SemaphoreType.DMA((4,)),
        ],
        cost_estimate=pl.CostEstimate(
            flops=2 * slot_count * degrees * total * 2 * C,
            bytes_accessed=slot_count * degrees * (total + 2 * C) * 2,
            transcendentals=0,
        ),
        compiler_params=pltpu.CompilerParams(vmem_limit_bytes=62 * 1024 * 1024),
    )(alm, legendre)


def analysis_kernel(table_hbm, spectra_ref, out_ref, table_ref, turned_ref, sems):
    total_slots, degrees, total = table_ref.shape
    slots = 8
    pieces = sems.shape[0] * slots // total_slots
    start_parts(table_hbm, table_ref, sems, IN_FLIGHT)
    turned_ref[...] = spectra_ref[...].astype(jnp.float32).T
    count = total_slots // HALVES
    for first in range(0, total_slots, slots):
        row = first // count * 2 * count + first % count
        rows = [turned_ref[row + share * count : row + share * count + slots, :] for share in range(2)]
        lhs = jnp.concatenate(rows, axis=0).astype(jnp.bfloat16)
        for piece in range(pieces):
            next_part(table_hbm, table_ref, sems, first // slots * pieces + piece, IN_FLIGHT)
        table = table_ref[first : first + slots].reshape(slots * degrees, total)
        result = lax.dot_general(lhs, table, (((1,), (1,)), ((), ())), preferred_element_type=jnp.float32)
        for slot in range(slots):
            span = slice(slot * degrees, (slot + 1) * degrees)
            out_ref[first + slot, 0:1, :] = result[slot : slot + 1, span]
            out_ref[first + slot, 1:2, :] = result[slots + slot : slots + slot + 1, span]


def analyse(legendre, spectra):
    slot_count, degrees, total = legendre.shape
    slots = 8
    width = 2 * slot_count
    vmem = pl.BlockSpec(memory_space=pltpu.VMEM)
    return pl.pallas_call(
        analysis_kernel,
        in_specs=[pl.BlockSpec(memory_space=pl.ANY), vmem],
        out_specs=vmem,
        out_shape=jax.ShapeDtypeStruct((slot_count, 2, degrees), jnp.float32),
        scratch_shapes=[
            pltpu.VMEM(legendre.shape, jnp.bfloat16),
            pltpu.VMEM((width, total), jnp.float32),
            pltpu.SemaphoreType.DMA((slot_count // 4,)),
        ],
        cost_estimate=pl.CostEstimate(
            flops=2 * slot_count * degrees * total * 2 * slots,
            bytes_accessed=slot_count * degrees * total * 2,
            transcendentals=0,
        ),
        compiler_params=pltpu.CompilerParams(vmem_limit_bytes=50 * 1024 * 1024),
    )(legendre, spectra)


def from_other_tiles(sends):
    count = len(sends)
    got = [sends[0]]
    for hop in range(1, count):
        got.append(lax.ppermute(sends[hop], "tile", [(at, (at + hop) % count) for at in range(count)]))
    return got


def in_tile_order(got):
    count = len(got)
    tile_at = lax.axis_index("tile")
    stacked = jnp.stack(got)
    return jnp.stack(
        [lax.dynamic_index_in_dim(stacked, (tile_at - at) % count, 0, keepdims=False) for at in range(count)]
    )


def body(alm, legendre, order_of_slot):
    tile_count = lax.axis_size("tile")
    band_count = lax.axis_size("band")
    tile_at = lax.axis_index("tile")
    slot_count = alm.shape[0]
    targets = band_count * tile_count
    cycles = legendre.shape[2] // targets
    padded = round_up(cycles, 8)
    depth = 2 * L
    width = 2 * slot_count
    group_width = math.lcm(width, LANES)
    groups = depth // group_width
    plain = group_width == width and padded == cycles
    axes = ("band", "tile")

    partial = make_modes(alm, legendre, targets)
    partial = lax.all_to_all(partial, axes, split_axis=0, concat_axis=0, tiled=True)
    modes = partial.reshape(band_count, tile_count, C * cycles, width)
    if not plain:
        modes = jnp.sum(modes.astype(jnp.float32), axis=1).astype(jnp.bfloat16)
        modes = modes.reshape(groups, group_width // width, C, cycles, width)
        modes = modes.transpose(0, 2, 3, 1, 4).reshape(groups, C, cycles, group_width)
        modes = jnp.pad(modes, ((0, 0), (0, 0), (0, padded - cycles), (0, 0)))
        modes = modes.reshape(groups, 1, C * padded, group_width)

    order_rows = order_of_slot.reshape(band_count * HALVES, 1, slot_count // HALVES)
    order_rows = jnp.broadcast_to(order_rows, (band_count * HALVES, 2, slot_count // HALVES)).reshape(depth)
    basis = make_basis(order_rows.astype(jnp.float32)[:, None], slot_count)
    odd = (order_rows % 2).astype(jnp.float32)[None, :]
    vectors, spectra = run_ilc(modes, odd, basis)

    if not plain:
        spectra = spectra[:, 0, :cycles].reshape(groups, cycles, group_width // width, width)
        spectra = spectra.transpose(0, 2, 1, 3).reshape(band_count, 1, cycles, width)
        spectra = jnp.broadcast_to(spectra, (band_count, tile_count, cycles, width))
    spectra = spectra.reshape(targets, cycles, width)
    routed = lax.all_to_all(spectra, axes, split_axis=0, concat_axis=0, tiled=True)
    found = in_tile_order(from_other_tiles([vectors[:, :cycles]] * tile_count))
    lanes = LANES // tile_count
    found = lax.dynamic_slice_in_dim(found, tile_at * lanes, lanes, axis=3)
    ilc_map = found.transpose(0, 2, 3, 1).reshape(tile_count * cycles, NLON // tile_count)
    routed, ilc_map = lax.optimization_barrier((routed, ilc_map))
    ilc_alm = analyse(legendre, routed.reshape(targets * cycles, width))
    return (ilc_map, ilc_alm)


def solution(mesh):
    placed = (P("band", None, None, "tile"), P("band", "tile", None), P())
    return jax.shard_map(
        body,
        mesh=mesh,
        in_specs=placed,
        out_specs=(P("band", "tile"), P("band", None, "tile")),
        check_vma=False,
    )
```

```python
import functools
import math

import jax
import jax.numpy as jnp
from jax import lax
from jax.experimental import pallas as pl
from jax.experimental.pallas import tpu as pltpu
from jax.sharding import PartitionSpec as P

C = 9
L = 1024
NLON = 4096
HALO = 32

RIDGE = 0.1
EPSILON = 1e-06

WINDOW = 2 * HALO + 1
LANES = NLON // HALO
HALF = LANES // 2
REST = C - 1
PAIRS = [(a_at, b_at) for a_at in range(REST) for b_at in range(a_at, REST)] + [(a_at, REST) for a_at in range(REST)]
SUMS = len(PAIRS) + 1
VMEM_LIMIT = 48 * 1024 * 1024
IN_FLIGHT = 6
HALVES = 2
CHUNK = 8


def round_up(value, multiple):
    return (value + multiple - 1) // multiple * multiple


def cos_turns(turns):
    nearest = (turns + 12582912.0) - 12582912.0
    quarter = 1.0 - 4.0 * jnp.abs(turns - nearest)
    square = quarter * quarter
    tail = square * (1.6044118478736e-04 - square * 3.598843235e-06)
    tail = square * (-4.68175413531868e-03 + tail)
    tail = square * (7.96926262461670e-02 + tail)
    tail = square * (-6.45964097506246e-01 + tail)
    return quarter * (1.57079632679490 + tail)


def basis_kernel(slots, order_ref, basis_ref):
    rows = 64
    begin = pl.program_id(0) * order_ref.shape[0]
    row = lax.broadcasted_iota(jnp.int32, (rows, LANES), 0)
    lane = lax.broadcasted_iota(jnp.int32, (rows, LANES), 1)
    cell = (HALO * (lane % HALF) + lane // HALF).astype(jnp.float32) / NLON
    scaling = 1.0 / math.sqrt(L)
    for first in range(0, order_ref.shape[0], rows):
        span = slice(first, first + rows)
        part = (row + (begin + first)) // (slots // HALVES) % 2
        order = jnp.broadcast_to(order_ref[span, :], (rows, LANES))
        turns = order * cell + part.astype(jnp.float32) * 0.25
        step = order * (2.0 / NLON)
        before = cos_turns(turns) * scaling
        now = cos_turns(turns + step) * scaling
        twice = 2.0 * cos_turns(step)
        for column in range(HALO // 2):
            at = column % (CHUNK // 2) * LANES
            basis_ref[column // (CHUNK // 2), span, at : at + LANES] = before.astype(jnp.bfloat16)
            if column < HALO // 2 - 1:
                before, now = now, twice * now - before


def make_basis(order_rows, slots):
    rows = order_rows.shape[0]
    block = 256
    chunks = HALO // CHUNK
    columns = CHUNK // 2 * LANES
    return pl.pallas_call(
        functools.partial(basis_kernel, slots),
        grid=(rows // block,),
        in_specs=[pl.BlockSpec((block, 1), lambda at: (at, 0))],
        out_specs=pl.BlockSpec((chunks, block, columns), lambda at: (0, at, 0)),
        out_shape=jax.ShapeDtypeStruct((chunks, rows, columns), jnp.bfloat16),
        cost_estimate=pl.CostEstimate(
            flops=rows * chunks * columns * 8, bytes_accessed=rows * chunks * columns * 2, transcendentals=0
        ),
        compiler_params=pltpu.CompilerParams(vmem_limit_bytes=VMEM_LIMIT),
    )(order_rows)


def part_copy(source, target, sems, part):
    count = source.shape[0] // sems.shape[0]
    span = pl.ds(part * count, count)
    return pltpu.make_async_copy(source.at[span], target.at[span], sems.at[part])


def start_parts(source, target, sems, count):
    for part in range(min(count, sems.shape[0])):
        part_copy(source, target, sems, part).start()


def next_part(source, target, sems, part, ahead):
    part_copy(source, target, sems, part).wait()
    more = part + ahead < sems.shape[0]
    if isinstance(part, int):
        if more:
            part_copy(source, target, sems, part + ahead).start()
    else:

        @pl.when(more)
        def _():
            part_copy(source, target, sems, part + ahead).start()


def reciprocal(value):
    guess = pl.reciprocal(value, approx=True)
    return guess * (2.0 - value * guess)


def combine_steps(sum_of, map_of):
    ridge = RIDGE * (sum_of(SUMS - 1) * (1.0 / C) + WINDOW * EPSILON)
    upper, inverses, rights, maps = {}, [], [], []
    value = map_of(REST)
    for row in range(REST):
        ratios = [upper[at, row] * inverses[at] for at in range(row)]
        pivot = sum_of(PAIRS.index((row, row))) + (ridge + ridge)
        for at in range(row):
            pivot = pivot - ratios[at] * upper[at, row]
        inverse = reciprocal(pivot)
        yield None
        right = ridge - sum_of(PAIRS.index((row, REST)))
        own = map_of(row)
        for at in range(row):
            right = right - ratios[at] * rights[at]
            own = own - ratios[at] * maps[at]
        yield None
        for col in range(row + 1, REST):
            entry = sum_of(PAIRS.index((row, col))) + ridge
            for at in range(row):
                entry = entry - ratios[at] * upper[at, col]
            upper[row, col] = entry
            yield None
        value = value + (right * inverse) * own
        inverses.append(inverse)
        rights.append(right)
        maps.append(own)
    yield value


def in_step(generators):
    for found in zip(*generators):
        pass
    return found


def ilc_kernel(modes_ref, odd_ref, basis_hbm, ilc_ref, spectra_ref, basis_ref, lhs_ref, maps_ref, sums_ref, low_ref, found_ref, sems):
    groups, shares, rows, width = modes_ref.shape
    columns = basis_ref.shape[2]
    depth = lhs_ref.shape[1]
    pieces, share_rows = found_ref.shape[0], found_ref.shape[2]
    chunks = basis_ref.shape[0] // pieces
    cycles = rows // C
    second = round_up(rows, 16)
    ahead = 2 * pieces
    start_parts(basis_hbm, basis_ref, sems, ahead)
    for group in range(groups):
        span = slice(group * width, (group + 1) * width)
        odd = odd_ref[:, span]
        values = modes_ref[group, 0].astype(jnp.float32)
        for share in range(1, shares):
            values = values + modes_ref[group, share].astype(jnp.float32)
        lhs_ref[0:rows, span] = (values * (1.0 - odd)).astype(jnp.bfloat16)
        lhs_ref[second : second + rows, span] = (values * odd).astype(jnp.bfloat16)
    low_half = lax.broadcasted_iota(jnp.int32, (cycles, LANES), 1) < HALF
    sums_ref[...] = jnp.zeros_like(sums_ref)

    def store_maps(at, maps):
        squares = maps[0] * maps[0]
        for chan in range(1, C):
            squares = squares + maps[chan] * maps[chan]
            maps_ref[at, chan - 1] = maps[chan] - maps[0]
        maps_ref[at, REST] = maps[0]
        maps_ref[at, C] = squares

    def maps_of_chunk(chunk):
        for piece in range(pieces):
            next_part(basis_hbm, basis_ref, sems, chunk * pieces + piece, ahead)
        basis = basis_ref[chunk * pieces : (chunk + 1) * pieces].reshape(depth, columns)
        result = jnp.dot(lhs_ref[...], basis, preferred_element_type=jnp.float32)
        for part in range(CHUNK // 2):
            at = CHUNK * chunk + 2 * part
            lanes = slice(part * LANES, (part + 1) * LANES)
            left, right = [], []
            for chan in range(C):
                even_part = result[chan * cycles : (chan + 1) * cycles, lanes]
                odd_part = result[second + chan * cycles : second + (chan + 1) * cycles, lanes]
                near = even_part + odd_part
                far = even_part - odd_part
                left.append(jnp.where(low_half, near, pltpu.roll(far, HALF, 1)))
                right.append(jnp.where(low_half, pltpu.roll(near, HALF, 1), far))
            store_maps(at, left)
            store_maps(at + 1, right)

    def add_totals(chunk):
        vectors = [CHUNK * chunk + part for part in range(CHUNK)]
        for a_at in range(C):
            own = [maps_ref[at, a_at] for at in vectors]
            for b_at in range(a_at, C):
                if (a_at, b_at) == (REST, REST):
                    continue
                pair = PAIRS.index((a_at, b_at))
                total = sums_ref[pair]
                for at, value in zip(vectors, own):
                    total = total + value * (value if a_at == b_at else maps_ref[at, b_at])
                sums_ref[pair] = total
        total = sums_ref[SUMS - 1]
        for at in vectors:
            total = total + maps_ref[at, C]
        sums_ref[SUMS - 1] = total

    maps_of_chunk(0)
    for chunk in range(1, chunks):
        maps_of_chunk(chunk)
        add_totals(chunk - 1)
    add_totals(chunks - 1)
    for pair in range(SUMS):
        total = sums_ref[pair]
        sums_ref[pair] = pltpu.roll(total, 1, 1) + pltpu.roll(total, 2, 1)

    def solve_steps(at):
        maps = [maps_ref[at, chan] for chan in range(C + 1)]

        def sum_of(pair):
            own = maps[C] if pair == SUMS - 1 else maps[PAIRS[pair][0]] * maps[PAIRS[pair][1]]
            total = sums_ref[pair] + own
            sums_ref[pair] = total - pltpu.roll(own, 2, 1)
            return total

        return combine_steps(sum_of, lambda chan: pltpu.roll(maps[chan], 1, 1))

    def add_spectra(chunk):
        lhs = jnp.concatenate([low_ref[chunk, part] for part in range(pieces)], axis=1)
        for part in range(pieces):
            term = lax.dot_general(
                lhs, basis_ref[chunk * pieces + part], (((1,), (1,)), ((), ())), preferred_element_type=jnp.float32
            )
            found_ref[part] = term if chunk == 0 else found_ref[part] + term

    for pair_at in range(HALO // 2):
        at = 2 * pair_at
        chunk, part = pair_at // pieces, pair_at % pieces
        found = in_step([solve_steps(at), solve_steps(at + 1)])
        found = [pltpu.roll(value, LANES - 1, 1) for value in found]
        ilc_ref[at] = found[0]
        ilc_ref[at + 1] = found[1]
        near = jnp.where(low_half, found[0], pltpu.roll(found[1], HALF, 1))
        far = jnp.where(low_half, pltpu.roll(found[0], HALF, 1), found[1])
        low_ref[chunk, part] = jnp.concatenate([near, far], axis=0).astype(jnp.bfloat16)
        if part == pieces - 1:
            add_spectra(chunk)
    for group in range(groups):
        span = slice(group * width, (group + 1) * width)
        sign = 1.0 - 2.0 * odd_ref[:, span]
        part, first = group * width // share_rows, group * width % share_rows
        result = found_ref[part, :, first : first + width]
        value = (result[0:cycles] + sign * result[cycles:]).astype(jnp.bfloat16)
        for share in range(shares):
            spectra_ref[group, share] = value


def run_ilc(modes, odd, basis):
    groups, shares, rows, width = modes.shape
    chunks, depth, columns = basis.shape
    pieces = CHUNK // 2
    basis = basis.reshape(chunks * pieces, depth // pieces, columns)
    cycles = rows // C
    vmem = pl.BlockSpec(memory_space=pltpu.VMEM)
    return pl.pallas_call(
        ilc_kernel,
        in_specs=[vmem, vmem, pl.BlockSpec(memory_space=pl.ANY)],
        out_specs=[vmem, vmem],
        out_shape=[
            jax.ShapeDtypeStruct((HALO, cycles, LANES), jnp.float32),
            jax.ShapeDtypeStruct((groups, shares, cycles, width), jnp.bfloat16),
        ],
        scratch_shapes=[
            pltpu.VMEM(basis.shape, jnp.bfloat16),
            pltpu.VMEM((2 * round_up(rows, 16), depth), jnp.bfloat16),
            pltpu.VMEM((HALO, C + 1, cycles, LANES), jnp.float32),
            pltpu.VMEM((SUMS, cycles, LANES), jnp.float32),
            pltpu.VMEM((chunks, pieces, 2 * cycles, LANES), jnp.bfloat16),
            pltpu.VMEM((pieces, 2 * cycles, depth // pieces), jnp.float32),
            pltpu.SemaphoreType.DMA((chunks * pieces,)),
        ],
        cost_estimate=pl.CostEstimate(
            flops=2 * chunks * depth * columns * (2 * rows + 2 * cycles),
            bytes_accessed=chunks * depth * columns * 2,
            transcendentals=0,
        ),
        compiler_params=pltpu.CompilerParams(vmem_limit_bytes=VMEM_LIMIT),
    )(modes, odd, basis)


def modes_kernel(alm_hbm, table_hbm, out_hbm, alm_ref, table_ref, held_ref, turned_ref, out_ref, alm_sems, sems, out_sems):
    parts = sems.shape[0]
    total_slots, degrees, total = table_ref.shape
    slots = total_slots // parts
    targets, rows = out_ref.shape[:2]
    cycles = rows // C
    height = 2 * C
    start_parts(alm_hbm, alm_ref, alm_sems, parts)
    start_parts(table_hbm, table_ref, sems, IN_FLIGHT)

    def some_slots(part):
        part_copy(alm_hbm, alm_ref, alm_sems, part).wait()
        next_part(table_hbm, table_ref, sems, part, IN_FLIGHT)
        first = part * slots
        lhs = alm_ref[first : first + slots].reshape(slots * height, degrees)
        rhs = jnp.concatenate([table_ref[first + slot] for slot in range(slots)], axis=1)
        result = jnp.dot(lhs, rhs, preferred_element_type=jnp.float32)
        for slot in range(slots):
            own = result[slot * height : (slot + 1) * height, slot * total : (slot + 1) * total]
            for lanes in range(held_ref.shape[0]):
                span = slice((first + slot) * height, (first + slot + 1) * height)
                held_ref[lanes, span, :] = own[:, lanes * LANES : (lanes + 1) * LANES]

    def turn(half):
        count = total_slots // HALVES
        first = half * count * height
        for chan in range(C):
            for lanes in range(held_ref.shape[0]):
                both = [held_ref[lanes, pl.ds(first + 2 * chan + part, count, stride=height), :] for part in range(2)]
                span = slice(half * 2 * count, (half + 1) * 2 * count)
                turned_ref[chan, lanes * LANES : (lanes + 1) * LANES, span] = jnp.concatenate(both, axis=0).T

    for part in range(parts):
        some_slots(part)
        if (part + 1) * HALVES % parts == 0:
            turn((part + 1) * HALVES // parts - 1)
    each = targets // out_sems.shape[0]
    for target in range(targets):
        span = slice(target * cycles, (target + 1) * cycles)
        block = jnp.concatenate([turned_ref[chan, span, :] for chan in range(C)], axis=0)
        out_ref[target] = block.astype(jnp.bfloat16)
        if (target + 1) % each == 0:
            part_copy(out_ref, out_hbm, out_sems, target // each).start()
    for part in range(out_sems.shape[0]):
        part_copy(out_ref, out_hbm, out_sems, part).wait()


def make_modes(alm, legendre, targets):
    slot_count, degrees, total = legendre.shape
    slots = 4
    parts = slot_count // slots
    width = 2 * slot_count
    height = 2 * C
    out = jax.ShapeDtypeStruct((targets, C * (total // targets), width), jnp.bfloat16)
    return pl.pallas_call(
        modes_kernel,
        in_specs=[pl.BlockSpec(memory_space=pl.ANY)] * 2,
        out_specs=pl.BlockSpec(memory_space=pl.ANY),
        out_shape=out,
        scratch_shapes=[
            pltpu.VMEM(alm.shape, jnp.bfloat16),
            pltpu.VMEM(legendre.shape, jnp.bfloat16),
            pltpu.VMEM((total // LANES, slot_count * height, LANES), jnp.float32),
            pltpu.VMEM((C, total, width), jnp.float32),
            pltpu.VMEM(out.shape, out.dtype),
            pltpu.SemaphoreType.DMA((parts,)),
            pltpu.SemaphoreType.DMA((parts,)),
            pltpu.SemaphoreType.DMA((4,)),
        ],
        cost_estimate=pl.CostEstimate(
            flops=2 * slot_count * degrees * total * 2 * C,
            bytes_accessed=slot_count * degrees * (total + 2 * C) * 2,
            transcendentals=0,
        ),
        compiler_params=pltpu.CompilerParams(vmem_limit_bytes=62 * 1024 * 1024),
    )(alm, legendre)


def analysis_kernel(table_hbm, spectra_ref, out_ref, table_ref, turned_ref, sems):
    total_slots, degrees, total = table_ref.shape
    slots = 8
    pieces = sems.shape[0] * slots // total_slots
    start_parts(table_hbm, table_ref, sems, IN_FLIGHT)
    turned_ref[...] = spectra_ref[...].astype(jnp.float32).T
    count = total_slots // HALVES
    for first in range(0, total_slots, slots):
        row = first // count * 2 * count + first % count
        rows = [turned_ref[row + share * count : row + share * count + slots, :] for share in range(2)]
        lhs = jnp.concatenate(rows, axis=0).astype(jnp.bfloat16)
        for piece in range(pieces):
            next_part(table_hbm, table_ref, sems, first // slots * pieces + piece, IN_FLIGHT)
        table = table_ref[first : first + slots].reshape(slots * degrees, total)
        result = lax.dot_general(lhs, table, (((1,), (1,)), ((), ())), preferred_element_type=jnp.float32)
        for slot in range(slots):
            span = slice(slot * degrees, (slot + 1) * degrees)
            out_ref[first + slot, 0:1, :] = result[slot : slot + 1, span]
            out_ref[first + slot, 1:2, :] = result[slots + slot : slots + slot + 1, span]


def analyse(legendre, spectra):
    slot_count, degrees, total = legendre.shape
    slots = 8
    width = 2 * slot_count
    vmem = pl.BlockSpec(memory_space=pltpu.VMEM)
    return pl.pallas_call(
        analysis_kernel,
        in_specs=[pl.BlockSpec(memory_space=pl.ANY), vmem],
        out_specs=vmem,
        out_shape=jax.ShapeDtypeStruct((slot_count, 2, degrees), jnp.float32),
        scratch_shapes=[
            pltpu.VMEM(legendre.shape, jnp.bfloat16),
            pltpu.VMEM((width, total), jnp.float32),
            pltpu.SemaphoreType.DMA((slot_count // 4,)),
        ],
        cost_estimate=pl.CostEstimate(
            flops=2 * slot_count * degrees * total * 2 * slots,
            bytes_accessed=slot_count * degrees * total * 2,
            transcendentals=0,
        ),
        compiler_params=pltpu.CompilerParams(vmem_limit_bytes=50 * 1024 * 1024),
    )(legendre, spectra)


def from_other_tiles(sends):
    count = len(sends)
    got = [sends[0]]
    for hop in range(1, count):
        got.append(lax.ppermute(sends[hop], "tile", [(at, (at + hop) % count) for at in range(count)]))
    return got


def in_tile_order(got):
    count = len(got)
    tile_at = lax.axis_index("tile")
    stacked = jnp.stack(got)
    return jnp.stack(
        [lax.dynamic_index_in_dim(stacked, (tile_at - at) % count, 0, keepdims=False) for at in range(count)]
    )


def body(alm, legendre, order_of_slot):
    tile_count = lax.axis_size("tile")
    band_count = lax.axis_size("band")
    tile_at = lax.axis_index("tile")
    slot_count = alm.shape[0]
    targets = band_count * tile_count
    cycles = legendre.shape[2] // targets
    padded = round_up(cycles, 8)
    depth = 2 * L
    width = 2 * slot_count
    group_width = math.lcm(width, LANES)
    groups = depth // group_width
    plain = group_width == width and padded == cycles
    axes = ("band", "tile")

    partial = make_modes(alm, legendre, targets)
    partial = lax.all_to_all(partial, axes, split_axis=0, concat_axis=0, tiled=True)
    modes = partial.reshape(band_count, tile_count, C * cycles, width)
    if not plain:
        modes = jnp.sum(modes.astype(jnp.float32), axis=1).astype(jnp.bfloat16)
        modes = modes.reshape(groups, group_width // width, C, cycles, width)
        modes = modes.transpose(0, 2, 3, 1, 4).reshape(groups, C, cycles, group_width)
        modes = jnp.pad(modes, ((0, 0), (0, 0), (0, padded - cycles), (0, 0)))
        modes = modes.reshape(groups, 1, C * padded, group_width)

    order_rows = order_of_slot.reshape(band_count * HALVES, 1, slot_count // HALVES)
    order_rows = jnp.broadcast_to(order_rows, (band_count * HALVES, 2, slot_count // HALVES)).reshape(depth)
    basis = make_basis(order_rows.astype(jnp.float32)[:, None], slot_count)
    odd = (order_rows % 2).astype(jnp.float32)[None, :]
    vectors, spectra = run_ilc(modes, odd, basis)

    if not plain:
        spectra = spectra[:, 0, :cycles].reshape(groups, cycles, group_width // width, width)
        spectra = spectra.transpose(0, 2, 1, 3).reshape(band_count, 1, cycles, width)
        spectra = jnp.broadcast_to(spectra, (band_count, tile_count, cycles, width))
    spectra = spectra.reshape(targets, cycles, width)
    routed = lax.all_to_all(spectra, axes, split_axis=0, concat_axis=0, tiled=True)
    found = in_tile_order(from_other_tiles([vectors[:, :cycles]] * tile_count))
    lanes = LANES // tile_count
    found = lax.dynamic_slice_in_dim(found, tile_at * lanes, lanes, axis=3)
    ilc_map = found.transpose(0, 2, 3, 1).reshape(tile_count * cycles, NLON // tile_count)
    routed, ilc_map = lax.optimization_barrier((routed, ilc_map))
    ilc_alm = analyse(legendre, routed.reshape(targets * cycles, width))
    return (ilc_map, ilc_alm)


def solution(mesh):
    placed = (P("band", None, None, "tile"), P("band", "tile", None), P())
    return jax.shard_map(
        body,
        mesh=mesh,
        in_specs=placed,
        out_specs=(P("band", "tile"), P("band", None, "tile")),
        check_vma=False,
    )
```

```python
import functools
import math

import jax
import jax.numpy as jnp
from jax import lax
from jax.experimental import pallas as pl
from jax.experimental.pallas import tpu as pltpu
from jax.sharding import PartitionSpec as P

C = 9
L = 1024
NLON = 4096
HALO = 32

RIDGE = 0.1
EPSILON = 1e-06

WINDOW = 2 * HALO + 1
LANES = NLON // HALO
HALF = LANES // 2
REST = C - 1
PAIRS = [(a_at, b_at) for a_at in range(REST) for b_at in range(a_at, REST)] + [(a_at, REST) for a_at in range(REST)]
SUMS = len(PAIRS) + 1
VMEM_LIMIT = 48 * 1024 * 1024
IN_FLIGHT = 6
HALVES = 2
CHUNK = 8


def round_up(value, multiple):
    return (value + multiple - 1) // multiple * multiple


def cos_turns(turns):
    nearest = (turns + 12582912.0) - 12582912.0
    quarter = 1.0 - 4.0 * jnp.abs(turns - nearest)
    square = quarter * quarter
    tail = square * (1.6044118478736e-04 - square * 3.598843235e-06)
    tail = square * (-4.68175413531868e-03 + tail)
    tail = square * (7.96926262461670e-02 + tail)
    tail = square * (-6.45964097506246e-01 + tail)
    return quarter * (1.57079632679490 + tail)


def basis_kernel(slots, order_ref, basis_ref):
    rows = 64
    begin = pl.program_id(0) * order_ref.shape[0]
    row = lax.broadcasted_iota(jnp.int32, (rows, LANES), 0)
    lane = lax.broadcasted_iota(jnp.int32, (rows, LANES), 1)
    cell = (HALO * (lane % HALF) + lane // HALF).astype(jnp.float32) / NLON
    scaling = 1.0 / math.sqrt(L)
    for first in range(0, order_ref.shape[0], rows):
        span = slice(first, first + rows)
        part = (row + (begin + first)) // (slots // HALVES) % 2
        order = jnp.broadcast_to(order_ref[span, :], (rows, LANES))
        turns = order * cell + part.astype(jnp.float32) * 0.25
        step = order * (2.0 / NLON)
        before = cos_turns(turns) * scaling
        now = cos_turns(turns + step) * scaling
        twice = 2.0 * cos_turns(step)
        for column in range(HALO // 2):
            at = column % (CHUNK // 2) * LANES
            basis_ref[column // (CHUNK // 2), span, at : at + LANES] = before.astype(jnp.bfloat16)
            if column < HALO // 2 - 1:
                before, now = now, twice * now - before


def make_basis(order_rows, slots):
    rows = order_rows.shape[0]
    block = 256
    chunks = HALO // CHUNK
    columns = CHUNK // 2 * LANES
    return pl.pallas_call(
        functools.partial(basis_kernel, slots),
        grid=(rows // block,),
        in_specs=[pl.BlockSpec((block, 1), lambda at: (at, 0))],
        out_specs=pl.BlockSpec((chunks, block, columns), lambda at: (0, at, 0)),
        out_shape=jax.ShapeDtypeStruct((chunks, rows, columns), jnp.bfloat16),
        cost_estimate=pl.CostEstimate(
            flops=rows * chunks * columns * 8, bytes_accessed=rows * chunks * columns * 2, transcendentals=0
        ),
        compiler_params=pltpu.CompilerParams(vmem_limit_bytes=VMEM_LIMIT),
    )(order_rows)


def part_copy(source, target, sems, part):
    count = source.shape[0] // sems.shape[0]
    span = pl.ds(part * count, count)
    return pltpu.make_async_copy(source.at[span], target.at[span], sems.at[part])


def start_parts(source, target, sems, count):
    for part in range(min(count, sems.shape[0])):
        part_copy(source, target, sems, part).start()


def next_part(source, target, sems, part, ahead):
    part_copy(source, target, sems, part).wait()
    more = part + ahead < sems.shape[0]
    if isinstance(part, int):
        if more:
            part_copy(source, target, sems, part + ahead).start()
    else:

        @pl.when(more)
        def _():
            part_copy(source, target, sems, part + ahead).start()


def reciprocal(value):
    guess = pl.reciprocal(value, approx=True)
    return guess * (2.0 - value * guess)


def combine_steps(sum_of, map_of):
    ridge = RIDGE * (sum_of(SUMS - 1) * (1.0 / C) + WINDOW * EPSILON)
    upper, inverses, rights, maps = {}, [], [], []
    value = map_of(REST)
    for row in range(REST):
        ratios = [upper[at, row] * inverses[at] for at in range(row)]
        pivot = sum_of(PAIRS.index((row, row))) + (ridge + ridge)
        for at in range(row):
            pivot = pivot - ratios[at] * upper[at, row]
        inverse = reciprocal(pivot)
        yield None
        right = ridge - sum_of(PAIRS.index((row, REST)))
        own = map_of(row)
        for at in range(row):
            right = right - ratios[at] * rights[at]
            own = own - ratios[at] * maps[at]
        yield None
        for col in range(row + 1, REST):
            entry = sum_of(PAIRS.index((row, col))) + ridge
            for at in range(row):
                entry = entry - ratios[at] * upper[at, col]
            upper[row, col] = entry
            yield None
        value = value + (right * inverse) * own
        inverses.append(inverse)
        rights.append(right)
        maps.append(own)
    yield value


def in_step(generators):
    for found in zip(*generators):
        pass
    return found


def ilc_kernel(places, modes_ref, odd_ref, basis_hbm, ilc_ref, spectra_ref, basis_ref, lhs_ref, maps_ref, sums_ref, low_ref, found_ref, sems):
    _, rows, width = modes_ref.shape
    groups, shares = len(places), len(places[0])
    columns = basis_ref.shape[2]
    depth = lhs_ref.shape[1]
    pieces, share_rows = found_ref.shape[0], found_ref.shape[2]
    chunks = basis_ref.shape[0] // pieces
    cycles = rows // C
    second = round_up(rows, 16)
    ahead = 2 * pieces
    start_parts(basis_hbm, basis_ref, sems, ahead)
    for group in range(groups):
        span = slice(group * width, (group + 1) * width)
        odd = odd_ref[:, span]
        values = modes_ref[places[group][0]].astype(jnp.float32)
        for place in places[group][1:]:
            values = values + modes_ref[place].astype(jnp.float32)
        lhs_ref[0:rows, span] = (values * (1.0 - odd)).astype(jnp.bfloat16)
        lhs_ref[second : second + rows, span] = (values * odd).astype(jnp.bfloat16)
    low_half = lax.broadcasted_iota(jnp.int32, (cycles, LANES), 1) < HALF
    sums_ref[...] = jnp.zeros_like(sums_ref)

    def store_maps(at, maps):
        squares = maps[0] * maps[0]
        for chan in range(1, C):
            squares = squares + maps[chan] * maps[chan]
            maps_ref[at, chan - 1] = maps[chan] - maps[0]
        maps_ref[at, REST] = maps[0]
        maps_ref[at, C] = squares

    def maps_of_chunk(chunk):
        for piece in range(pieces):
            next_part(basis_hbm, basis_ref, sems, chunk * pieces + piece, ahead)
        basis = basis_ref[chunk * pieces : (chunk + 1) * pieces].reshape(depth, columns)
        result = jnp.dot(lhs_ref[...], basis, preferred_element_type=jnp.float32)
        for part in range(CHUNK // 2):
            at = CHUNK * chunk + 2 * part
            lanes = slice(part * LANES, (part + 1) * LANES)
            left, right = [], []
            for chan in range(C):
                even_part = result[chan * cycles : (chan + 1) * cycles, lanes]
                odd_part = result[second + chan * cycles : second + (chan + 1) * cycles, lanes]
                near = even_part + odd_part
                far = even_part - odd_part
                left.append(jnp.where(low_half, near, pltpu.roll(far, HALF, 1)))
                right.append(jnp.where(low_half, pltpu.roll(near, HALF, 1), far))
            store_maps(at, left)
            store_maps(at + 1, right)

    def add_totals(chunk):
        vectors = [CHUNK * chunk + part for part in range(CHUNK)]
        for a_at in range(C):
            own = [maps_ref[at, a_at] for at in vectors]
            for b_at in range(a_at, C):
                if (a_at, b_at) == (REST, REST):
                    continue
                pair = PAIRS.index((a_at, b_at))
                total = sums_ref[pair]
                for at, value in zip(vectors, own):
                    total = total + value * (value if a_at == b_at else maps_ref[at, b_at])
                sums_ref[pair] = total
        total = sums_ref[SUMS - 1]
        for at in vectors:
            total = total + maps_ref[at, C]
        sums_ref[SUMS - 1] = total

    maps_of_chunk(0)
    for chunk in range(1, chunks):
        maps_of_chunk(chunk)
        add_totals(chunk - 1)
    add_totals(chunks - 1)
    for pair in range(SUMS):
        total = sums_ref[pair]
        sums_ref[pair] = pltpu.roll(total, 1, 1) + pltpu.roll(total, 2, 1)

    def solve_steps(at):
        maps = [maps_ref[at, chan] for chan in range(C + 1)]

        def sum_of(pair):
            own = maps[C] if pair == SUMS - 1 else maps[PAIRS[pair][0]] * maps[PAIRS[pair][1]]
            total = sums_ref[pair] + own
            sums_ref[pair] = total - pltpu.roll(own, 2, 1)
            return total

        return combine_steps(sum_of, lambda chan: pltpu.roll(maps[chan], 1, 1))

    def add_spectra(chunk):
        lhs = jnp.concatenate([low_ref[chunk, part] for part in range(pieces)], axis=1)
        for part in range(pieces):
            term = lax.dot_general(
                lhs, basis_ref[chunk * pieces + part], (((1,), (1,)), ((), ())), preferred_element_type=jnp.float32
            )
            found_ref[part] = term if chunk == 0 else found_ref[part] + term

    for pair_at in range(HALO // 2):
        at = 2 * pair_at
        chunk, part = pair_at // pieces, pair_at % pieces
        found = in_step([solve_steps(at), solve_steps(at + 1)])
        found = [pltpu.roll(value, LANES - 1, 1) for value in found]
        ilc_ref[at] = found[0]
        ilc_ref[at + 1] = found[1]
        near = jnp.where(low_half, found[0], pltpu.roll(found[1], HALF, 1))
        far = jnp.where(low_half, pltpu.roll(found[0], HALF, 1), found[1])
        low_ref[chunk, part] = jnp.concatenate([near, far], axis=0).astype(jnp.bfloat16)
        if part == pieces - 1:
            add_spectra(chunk)
    for group in range(groups):
        span = slice(group * width, (group + 1) * width)
        sign = 1.0 - 2.0 * odd_ref[:, span]
        part, first = group * width // share_rows, group * width % share_rows
        result = found_ref[part, :, first : first + width]
        value = (result[0:cycles] + sign * result[cycles:]).astype(jnp.bfloat16)
        for share in range(shares):
            spectra_ref[group, share] = value


def run_ilc(modes, odd, basis, places):
    _, rows, width = modes.shape
    groups, shares = len(places), len(places[0])
    chunks, depth, columns = basis.shape
    pieces = CHUNK // 2
    basis = basis.reshape(chunks * pieces, depth // pieces, columns)
    cycles = rows // C
    vmem = pl.BlockSpec(memory_space=pltpu.VMEM)
    return pl.pallas_call(
        functools.partial(ilc_kernel, places),
        in_specs=[vmem, vmem, pl.BlockSpec(memory_space=pl.ANY)],
        out_specs=[vmem, vmem],
        out_shape=[
            jax.ShapeDtypeStruct((HALO, cycles, LANES), jnp.float32),
            jax.ShapeDtypeStruct((groups, shares, cycles, width), jnp.bfloat16),
        ],
        scratch_shapes=[
            pltpu.VMEM(basis.shape, jnp.bfloat16),
            pltpu.VMEM((2 * round_up(rows, 16), depth), jnp.bfloat16),
            pltpu.VMEM((HALO, C + 1, cycles, LANES), jnp.float32),
            pltpu.VMEM((SUMS, cycles, LANES), jnp.float32),
            pltpu.VMEM((chunks, pieces, 2 * cycles, LANES), jnp.bfloat16),
            pltpu.VMEM((pieces, 2 * cycles, depth // pieces), jnp.float32),
            pltpu.SemaphoreType.DMA((chunks * pieces,)),
        ],
        cost_estimate=pl.CostEstimate(
            flops=2 * chunks * depth * columns * (2 * rows + 2 * cycles),
            bytes_accessed=chunks * depth * columns * 2,
            transcendentals=0,
        ),
        compiler_params=pltpu.CompilerParams(vmem_limit_bytes=VMEM_LIMIT),
    )(modes, odd, basis)


def modes_kernel(order, alm_hbm, table_hbm, out_hbm, alm_ref, table_ref, held_ref, turned_ref, out_ref, alm_sems, sems, out_sems):
    parts = sems.shape[0]
    total_slots, degrees, total = table_ref.shape
    slots = total_slots // parts
    targets, rows = out_ref.shape[:2]
    cycles = rows // C
    height = 2 * C
    start_parts(alm_hbm, alm_ref, alm_sems, parts)
    start_parts(table_hbm, table_ref, sems, IN_FLIGHT)

    def some_slots(part):
        part_copy(alm_hbm, alm_ref, alm_sems, part).wait()
        next_part(table_hbm, table_ref, sems, part, IN_FLIGHT)
        first = part * slots
        lhs = alm_ref[first : first + slots].reshape(slots * height, degrees)
        rhs = jnp.concatenate([table_ref[first + slot] for slot in range(slots)], axis=1)
        result = jnp.dot(lhs, rhs, preferred_element_type=jnp.float32)
        for slot in range(slots):
            own = result[slot * height : (slot + 1) * height, slot * total : (slot + 1) * total]
            for lanes in range(held_ref.shape[0]):
                span = slice((first + slot) * height, (first + slot + 1) * height)
                held_ref[lanes, span, :] = own[:, lanes * LANES : (lanes + 1) * LANES]

    def turn(half):
        count = total_slots // HALVES
        first = half * count * height
        for chan in range(C):
            for lanes in range(held_ref.shape[0]):
                both = [held_ref[lanes, pl.ds(first + 2 * chan + part, count, stride=height), :] for part in range(2)]
                span = slice(half * 2 * count, (half + 1) * 2 * count)
                turned_ref[chan, lanes * LANES : (lanes + 1) * LANES, span] = jnp.concatenate(both, axis=0).T

    for part in range(parts):
        some_slots(part)
        if (part + 1) * HALVES % parts == 0:
            turn((part + 1) * HALVES // parts - 1)
    each = targets // out_sems.shape[0]
    for at, target in enumerate(order):
        span = slice(target * cycles, (target + 1) * cycles)
        block = jnp.concatenate([turned_ref[chan, span, :] for chan in range(C)], axis=0)
        out_ref[at] = block.astype(jnp.bfloat16)
        if (at + 1) % each == 0:
            part_copy(out_ref, out_hbm, out_sems, at // each).start()
    for part in range(out_sems.shape[0]):
        part_copy(out_ref, out_hbm, out_sems, part).wait()


def make_modes(alm, legendre, order):
    targets = len(order)
    slot_count, degrees, total = legendre.shape
    slots = 4
    parts = slot_count // slots
    width = 2 * slot_count
    height = 2 * C
    out = jax.ShapeDtypeStruct((targets, C * (total // targets), width), jnp.bfloat16)
    return pl.pallas_call(
        functools.partial(modes_kernel, order),
        in_specs=[pl.BlockSpec(memory_space=pl.ANY)] * 2,
        out_specs=pl.BlockSpec(memory_space=pl.ANY),
        out_shape=out,
        scratch_shapes=[
            pltpu.VMEM(alm.shape, jnp.bfloat16),
            pltpu.VMEM(legendre.shape, jnp.bfloat16),
            pltpu.VMEM((total // LANES, slot_count * height, LANES), jnp.float32),
            pltpu.VMEM((C, total, width), jnp.float32),
            pltpu.VMEM(out.shape, out.dtype),
            pltpu.SemaphoreType.DMA((parts,)),
            pltpu.SemaphoreType.DMA((parts,)),
            pltpu.SemaphoreType.DMA((4,)),
        ],
        cost_estimate=pl.CostEstimate(
            flops=2 * slot_count * degrees * total * 2 * C,
            bytes_accessed=slot_count * degrees * (total + 2 * C) * 2,
            transcendentals=0,
        ),
        compiler_params=pltpu.CompilerParams(vmem_limit_bytes=62 * 1024 * 1024),
    )(alm, legendre)


def analysis_kernel(table_hbm, spectra_ref, out_ref, table_ref, turned_ref, sems):
    total_slots, degrees, total = table_ref.shape
    slots = 8
    pieces = sems.shape[0] * slots // total_slots
    start_parts(table_hbm, table_ref, sems, IN_FLIGHT)
    turned_ref[...] = spectra_ref[...].astype(jnp.float32).T
    count = total_slots // HALVES
    for first in range(0, total_slots, slots):
        row = first // count * 2 * count + first % count
        rows = [turned_ref[row + share * count : row + share * count + slots, :] for share in range(2)]
        lhs = jnp.concatenate(rows, axis=0).astype(jnp.bfloat16)
        for piece in range(pieces):
            next_part(table_hbm, table_ref, sems, first // slots * pieces + piece, IN_FLIGHT)
        table = table_ref[first : first + slots].reshape(slots * degrees, total)
        result = lax.dot_general(lhs, table, (((1,), (1,)), ((), ())), preferred_element_type=jnp.float32)
        for slot in range(slots):
            span = slice(slot * degrees, (slot + 1) * degrees)
            out_ref[first + slot, 0:1, :] = result[slot : slot + 1, span]
            out_ref[first + slot, 1:2, :] = result[slots + slot : slots + slot + 1, span]


def analyse(legendre, spectra):
    slot_count, degrees, total = legendre.shape
    slots = 8
    width = 2 * slot_count
    vmem = pl.BlockSpec(memory_space=pltpu.VMEM)
    return pl.pallas_call(
        analysis_kernel,
        in_specs=[pl.BlockSpec(memory_space=pl.ANY), vmem],
        out_specs=vmem,
        out_shape=jax.ShapeDtypeStruct((slot_count, 2, degrees), jnp.float32),
        scratch_shapes=[
            pltpu.VMEM(legendre.shape, jnp.bfloat16),
            pltpu.VMEM((width, total), jnp.float32),
            pltpu.SemaphoreType.DMA((slot_count // 4,)),
        ],
        cost_estimate=pl.CostEstimate(
            flops=2 * slot_count * degrees * total * 2 * slots,
            bytes_accessed=slot_count * degrees * total * 2,
            transcendentals=0,
        ),
        compiler_params=pltpu.CompilerParams(vmem_limit_bytes=50 * 1024 * 1024),
    )(legendre, spectra)


def from_other_tiles(sends):
    count = len(sends)
    got = [sends[0]]
    for hop in range(1, count):
        got.append(lax.ppermute(sends[hop], "tile", [(at, (at + hop) % count) for at in range(count)]))
    return got


def in_tile_order(got):
    count = len(got)
    tile_at = lax.axis_index("tile")
    stacked = jnp.stack(got)
    return jnp.stack(
        [lax.dynamic_index_in_dim(stacked, (tile_at - at) % count, 0, keepdims=False) for at in range(count)]
    )


def body(alm, legendre, order_of_slot):
    tile_count = lax.axis_size("tile")
    chip_count, core_count = lax.axis_size("chip"), lax.axis_size("core")
    band_count = chip_count * core_count
    tile_at = lax.axis_index("tile")
    slot_count = alm.shape[0]
    targets = band_count * tile_count
    cycles = legendre.shape[2] // targets
    padded = round_up(cycles, 8)
    depth = 2 * L
    width = 2 * slot_count
    group_width = math.lcm(width, LANES)
    groups = depth // group_width
    plain = group_width == width and padded == cycles
    order = [
        (chip * core_count + core) * tile_count + tile
        for core in range(core_count)
        for tile in range(tile_count)
        for chip in range(chip_count)
    ]
    partial = make_modes(alm, legendre, order)
    modes = lax.all_to_all(partial, ("core", "tile", "chip"), split_axis=0, concat_axis=0, tiled=True)
    if plain:
        places = [[order.index(band * tile_count + tile) for tile in range(tile_count)] for band in range(band_count)]
    else:
        places = [[group] for group in range(groups)]
        modes = modes.reshape(core_count, tile_count, chip_count, C * cycles, width)
        modes = jnp.sum(modes.astype(jnp.float32), axis=1).astype(jnp.bfloat16).transpose(1, 0, 2, 3)
        modes = modes.reshape(groups, group_width // width, C, cycles, width)
        modes = modes.transpose(0, 2, 3, 1, 4).reshape(groups, C, cycles, group_width)
        modes = jnp.pad(modes, ((0, 0), (0, 0), (0, padded - cycles), (0, 0)))
        modes = modes.reshape(groups, C * padded, group_width)

    order_rows = order_of_slot.reshape(band_count * HALVES, 1, slot_count // HALVES)
    order_rows = jnp.broadcast_to(order_rows, (band_count * HALVES, 2, slot_count // HALVES)).reshape(depth)
    basis = make_basis(order_rows.astype(jnp.float32)[:, None], slot_count)
    odd = (order_rows % 2).astype(jnp.float32)[None, :]
    vectors, spectra = run_ilc(modes, odd, basis, places)

    if not plain:
        spectra = spectra[:, 0, :cycles].reshape(groups, cycles, group_width // width, width)
        spectra = spectra.transpose(0, 2, 1, 3).reshape(band_count, 1, cycles, width)
        spectra = jnp.broadcast_to(spectra, (band_count, tile_count, cycles, width))
    spectra = spectra.reshape(targets, cycles, width)
    routed = lax.all_to_all(spectra, ("chip", "core", "tile"), split_axis=0, concat_axis=0, tiled=True)
    found = in_tile_order(from_other_tiles([vectors[:, :cycles]] * tile_count))
    lanes = LANES // tile_count
    found = lax.dynamic_slice_in_dim(found, tile_at * lanes, lanes, axis=3)
    ilc_map = found.transpose(0, 2, 3, 1).reshape(tile_count * cycles, NLON // tile_count)
    routed, ilc_map = lax.optimization_barrier((routed, ilc_map))
    ilc_alm = analyse(legendre, routed.reshape(targets * cycles, width))
    return (ilc_map, ilc_alm)


def solution(mesh):
    band_count, tile_count = mesh.shape["band"], mesh.shape["tile"]
    core_count = 2 if band_count % 2 == 0 else 1
    fine = jax.sharding.Mesh(
        mesh.devices.reshape(band_count // core_count, core_count, tile_count), ("chip", "core", "tile")
    )
    band = ("chip", "core")
    return jax.shard_map(
        body,
        mesh=fine,
        in_specs=(P(band, None, None, "tile"), P(band, "tile", None), P()),
        out_specs=(P(band, "tile"), P(band, None, "tile")),
        check_vma=False,
    )
```

```python
import functools
import math

import jax
import jax.numpy as jnp
from jax import lax
from jax.experimental import pallas as pl
from jax.experimental.pallas import tpu as pltpu
from jax.sharding import PartitionSpec as P

C = 9
L = 1024
NLON = 4096
HALO = 32

RIDGE = 0.1
EPSILON = 1e-06

WINDOW = 2 * HALO + 1
LANES = NLON // HALO
HALF = LANES // 2
REST = C - 1
PAIRS = [(a_at, b_at) for a_at in range(REST) for b_at in range(a_at, REST)] + [(a_at, REST) for a_at in range(REST)]
SUMS = len(PAIRS) + 1
VMEM_LIMIT = 48 * 1024 * 1024
IN_FLIGHT = 6
FIRST = 3
HALVES = 2
CHUNK = 8


def round_up(value, multiple):
    return (value + multiple - 1) // multiple * multiple


def cos_turns(turns):
    nearest = (turns + 12582912.0) - 12582912.0
    quarter = 1.0 - 4.0 * jnp.abs(turns - nearest)
    square = quarter * quarter
    tail = square * (1.6044118478736e-04 - square * 3.598843235e-06)
    tail = square * (-4.68175413531868e-03 + tail)
    tail = square * (7.96926262461670e-02 + tail)
    tail = square * (-6.45964097506246e-01 + tail)
    return quarter * (1.57079632679490 + tail)


def basis_kernel(slots, order_ref, basis_ref):
    rows = 64
    begin = pl.program_id(0) * order_ref.shape[0]
    row = lax.broadcasted_iota(jnp.int32, (rows, LANES), 0)
    lane = lax.broadcasted_iota(jnp.int32, (rows, LANES), 1)
    cell = (HALO * (lane % HALF) + lane // HALF).astype(jnp.float32) / NLON
    scaling = 1.0 / math.sqrt(L)
    for first in range(0, order_ref.shape[0], rows):
        span = slice(first, first + rows)
        part = (row + (begin + first)) // (slots // HALVES) % 2
        order = jnp.broadcast_to(order_ref[span, :], (rows, LANES))
        turns = order * cell + part.astype(jnp.float32) * 0.25
        step = order * (2.0 / NLON)
        before = cos_turns(turns) * scaling
        now = cos_turns(turns + step) * scaling
        twice = 2.0 * cos_turns(step)
        for column in range(HALO // 2):
            at = column % (CHUNK // 2) * LANES
            basis_ref[column // (CHUNK // 2), span, at : at + LANES] = before.astype(jnp.bfloat16)
            if column < HALO // 2 - 1:
                before, now = now, twice * now - before


def make_basis(order_rows, slots):
    rows = order_rows.shape[0]
    block = 256
    chunks = HALO // CHUNK
    columns = CHUNK // 2 * LANES
    return pl.pallas_call(
        functools.partial(basis_kernel, slots),
        grid=(rows // block,),
        in_specs=[pl.BlockSpec((block, 1), lambda at: (at, 0))],
        out_specs=pl.BlockSpec((chunks, block, columns), lambda at: (0, at, 0)),
        out_shape=jax.ShapeDtypeStruct((chunks, rows, columns), jnp.bfloat16),
        cost_estimate=pl.CostEstimate(
            flops=rows * chunks * columns * 8, bytes_accessed=rows * chunks * columns * 2, transcendentals=0
        ),
        compiler_params=pltpu.CompilerParams(vmem_limit_bytes=VMEM_LIMIT),
    )(order_rows)


def part_copy(source, target, sems, part):
    count = source.shape[0] // sems.shape[0]
    span = pl.ds(part * count, count)
    return pltpu.make_async_copy(source.at[span], target.at[span], sems.at[part])


def started(parts, done, most):
    return min(parts, done + min(most, FIRST + done))


def start_parts(source, target, sems, most):
    for part in range(started(sems.shape[0], 0, most)):
        part_copy(source, target, sems, part).start()


def next_part(source, target, sems, part, most):
    parts = sems.shape[0]
    part_copy(source, target, sems, part).wait()
    for later in range(started(parts, part, most), started(parts, part + 1, most)):
        part_copy(source, target, sems, later).start()


def reciprocal(value):
    guess = pl.reciprocal(value, approx=True)
    return guess * (2.0 - value * guess)


def combine_steps(sum_of, map_of):
    ridge = RIDGE * (sum_of(SUMS - 1) * (1.0 / C) + WINDOW * EPSILON)
    upper, inverses, rights, maps = {}, [], [], []
    value = map_of(REST)
    for row in range(REST):
        ratios = [upper[at, row] * inverses[at] for at in range(row)]
        pivot = sum_of(PAIRS.index((row, row))) + (ridge + ridge)
        for at in range(row):
            pivot = pivot - ratios[at] * upper[at, row]
        inverse = reciprocal(pivot)
        yield None
        right = ridge - sum_of(PAIRS.index((row, REST)))
        own = map_of(row)
        for at in range(row):
            right = right - ratios[at] * rights[at]
            own = own - ratios[at] * maps[at]
        yield None
        for col in range(row + 1, REST):
            entry = sum_of(PAIRS.index((row, col))) + ridge
            for at in range(row):
                entry = entry - ratios[at] * upper[at, col]
            upper[row, col] = entry
            yield None
        value = value + (right * inverse) * own
        inverses.append(inverse)
        rights.append(right)
        maps.append(own)
    yield value


def in_step(generators):
    for found in zip(*generators):
        pass
    return found


def ilc_kernel(modes_ref, odd_ref, basis_hbm, ilc_ref, spectra_ref, basis_ref, lhs_ref, maps_ref, sums_ref, low_ref, found_ref, sems):
    groups, shares, rows, width = modes_ref.shape
    columns = basis_ref.shape[2]
    depth = lhs_ref.shape[1]
    pieces, share_rows = found_ref.shape[0], found_ref.shape[2]
    chunks = basis_ref.shape[0] // pieces
    cycles = rows // C
    second = round_up(rows, 16)
    ahead = 2 * pieces
    start_parts(basis_hbm, basis_ref, sems, ahead)
    for group in range(groups):
        span = slice(group * width, (group + 1) * width)
        odd = odd_ref[:, span]
        values = modes_ref[group, 0].astype(jnp.float32)
        for share in range(1, shares):
            values = values + modes_ref[group, share].astype(jnp.float32)
        lhs_ref[0:rows, span] = (values * (1.0 - odd)).astype(jnp.bfloat16)
        lhs_ref[second : second + rows, span] = (values * odd).astype(jnp.bfloat16)
    low_half = lax.broadcasted_iota(jnp.int32, (cycles, LANES), 1) < HALF
    sums_ref[...] = jnp.zeros_like(sums_ref)

    def store_maps(at, maps):
        squares = maps[0] * maps[0]
        for chan in range(1, C):
            squares = squares + maps[chan] * maps[chan]
            maps_ref[at, chan - 1] = maps[chan] - maps[0]
        maps_ref[at, REST] = maps[0]
        maps_ref[at, C] = squares

    def maps_of_chunk(chunk):
        result = None
        for piece in range(pieces):
            next_part(basis_hbm, basis_ref, sems, chunk * pieces + piece, ahead)
            lhs = lhs_ref[:, piece * share_rows : (piece + 1) * share_rows]
            term = jnp.dot(lhs, basis_ref[chunk * pieces + piece], preferred_element_type=jnp.float32)
            result = term if result is None else result + term
        for part in range(CHUNK // 2):
            at = CHUNK * chunk + 2 * part
            lanes = slice(part * LANES, (part + 1) * LANES)
            left, right = [], []
            for chan in range(C):
                even_part = result[chan * cycles : (chan + 1) * cycles, lanes]
                odd_part = result[second + chan * cycles : second + (chan + 1) * cycles, lanes]
                near = even_part + odd_part
                far = even_part - odd_part
                left.append(jnp.where(low_half, near, pltpu.roll(far, HALF, 1)))
                right.append(jnp.where(low_half, pltpu.roll(near, HALF, 1), far))
            store_maps(at, left)
            store_maps(at + 1, right)

    def add_totals(chunk):
        vectors = [CHUNK * chunk + part for part in range(CHUNK)]
        for a_at in range(C):
            own = [maps_ref[at, a_at] for at in vectors]
            for b_at in range(a_at, C):
                if (a_at, b_at) == (REST, REST):
                    continue
                pair = PAIRS.index((a_at, b_at))
                total = sums_ref[pair]
                for at, value in zip(vectors, own):
                    total = total + value * (value if a_at == b_at else maps_ref[at, b_at])
                sums_ref[pair] = total
        total = sums_ref[SUMS - 1]
        for at in vectors:
            total = total + maps_ref[at, C]
        sums_ref[SUMS - 1] = total

    maps_of_chunk(0)
    for chunk in range(1, chunks):
        maps_of_chunk(chunk)
        add_totals(chunk - 1)
    add_totals(chunks - 1)
    for pair in range(SUMS):
        total = sums_ref[pair]
        sums_ref[pair] = pltpu.roll(total, 1, 1) + pltpu.roll(total, 2, 1)

    def solve_steps(at):
        maps = [maps_ref[at, chan] for chan in range(C + 1)]

        def sum_of(pair):
            own = maps[C] if pair == SUMS - 1 else maps[PAIRS[pair][0]] * maps[PAIRS[pair][1]]
            total = sums_ref[pair] + own
            sums_ref[pair] = total - pltpu.roll(own, 2, 1)
            return total

        return combine_steps(sum_of, lambda chan: pltpu.roll(maps[chan], 1, 1))

    def add_spectra(chunk):
        lhs = jnp.concatenate([low_ref[chunk, part] for part in range(pieces)], axis=1)
        for part in range(pieces):
            term = lax.dot_general(
                lhs, basis_ref[chunk * pieces + part], (((1,), (1,)), ((), ())), preferred_element_type=jnp.float32
            )
            found_ref[part] = term if chunk == 0 else found_ref[part] + term

    for pair_at in range(HALO // 2):
        at = 2 * pair_at
        chunk, part = pair_at // pieces, pair_at % pieces
        found = in_step([solve_steps(at), solve_steps(at + 1)])
        found = [pltpu.roll(value, LANES - 1, 1) for value in found]
        ilc_ref[at] = found[0]
        ilc_ref[at + 1] = found[1]
        near = jnp.where(low_half, found[0], pltpu.roll(found[1], HALF, 1))
        far = jnp.where(low_half, pltpu.roll(found[0], HALF, 1), found[1])
        low_ref[chunk, part] = jnp.concatenate([near, far], axis=0).astype(jnp.bfloat16)
        if part == pieces - 1:
            add_spectra(chunk)
    for group in range(groups):
        span = slice(group * width, (group + 1) * width)
        sign = 1.0 - 2.0 * odd_ref[:, span]
        part, first = group * width // share_rows, group * width % share_rows
        result = found_ref[part, :, first : first + width]
        value = (result[0:cycles] + sign * result[cycles:]).astype(jnp.bfloat16)
        for share in range(shares):
            spectra_ref[group, share] = value


def run_ilc(modes, odd, basis):
    groups, shares, rows, width = modes.shape
    chunks, depth, columns = basis.shape
    pieces = CHUNK // 2
    basis = basis.reshape(chunks * pieces, depth // pieces, columns)
    cycles = rows // C
    vmem = pl.BlockSpec(memory_space=pltpu.VMEM)
    return pl.pallas_call(
        ilc_kernel,
        in_specs=[vmem, vmem, pl.BlockSpec(memory_space=pl.ANY)],
        out_specs=[vmem, vmem],
        out_shape=[
            jax.ShapeDtypeStruct((HALO, cycles, LANES), jnp.float32),
            jax.ShapeDtypeStruct((groups, shares, cycles, width), jnp.bfloat16),
        ],
        scratch_shapes=[
            pltpu.VMEM(basis.shape, jnp.bfloat16),
            pltpu.VMEM((2 * round_up(rows, 16), depth), jnp.bfloat16),
            pltpu.VMEM((HALO, C + 1, cycles, LANES), jnp.float32),
            pltpu.VMEM((SUMS, cycles, LANES), jnp.float32),
            pltpu.VMEM((chunks, pieces, 2 * cycles, LANES), jnp.bfloat16),
            pltpu.VMEM((pieces, 2 * cycles, depth // pieces), jnp.float32),
            pltpu.SemaphoreType.DMA((chunks * pieces,)),
        ],
        cost_estimate=pl.CostEstimate(
            flops=2 * chunks * depth * columns * (2 * rows + 2 * cycles),
            bytes_accessed=chunks * depth * columns * 2,
            transcendentals=0,
        ),
        compiler_params=pltpu.CompilerParams(vmem_limit_bytes=VMEM_LIMIT),
    )(modes, odd, basis)


def modes_kernel(alm_hbm, table_hbm, out_hbm, alm_ref, table_ref, held_ref, turned_ref, out_ref, alm_sems, sems, out_sems):
    parts = sems.shape[0]
    total_slots, degrees, total = table_ref.shape
    slots = total_slots // parts
    targets, rows = out_ref.shape[:2]
    cycles = rows // C
    height = 2 * C
    for part in range(parts):
        part_copy(alm_hbm, alm_ref, alm_sems, part).start()
    start_parts(table_hbm, table_ref, sems, IN_FLIGHT)

    def some_slots(part):
        part_copy(alm_hbm, alm_ref, alm_sems, part).wait()
        next_part(table_hbm, table_ref, sems, part, IN_FLIGHT)
        first = part * slots
        lhs = alm_ref[first : first + slots].reshape(slots * height, degrees)
        rhs = jnp.concatenate([table_ref[first + slot] for slot in range(slots)], axis=1)
        result = jnp.dot(lhs, rhs, preferred_element_type=jnp.float32)
        for slot in range(slots):
            own = result[slot * height : (slot + 1) * height, slot * total : (slot + 1) * total]
            for lanes in range(held_ref.shape[0]):
                span = slice((first + slot) * height, (first + slot + 1) * height)
                held_ref[lanes, span, :] = own[:, lanes * LANES : (lanes + 1) * LANES]

    def turn(half):
        count = total_slots // HALVES
        first = half * count * height
        for chan in range(C):
            for lanes in range(held_ref.shape[0]):
                both = [held_ref[lanes, pl.ds(first + 2 * chan + part, count, stride=height), :] for part in range(2)]
                span = slice(half * 2 * count, (half + 1) * 2 * count)
                turned_ref[chan, lanes * LANES : (lanes + 1) * LANES, span] = jnp.concatenate(both, axis=0).T

    for part in range(parts):
        some_slots(part)
        if (part + 1) * HALVES % parts == 0:
            turn((part + 1) * HALVES // parts - 1)
    each = targets // out_sems.shape[0]
    for target in range(targets):
        span = slice(target * cycles, (target + 1) * cycles)
        block = jnp.concatenate([turned_ref[chan, span, :] for chan in range(C)], axis=0)
        out_ref[target] = block.astype(jnp.bfloat16)
        if (target + 1) % each == 0:
            part_copy(out_ref, out_hbm, out_sems, target // each).start()
    for part in range(out_sems.shape[0]):
        part_copy(out_ref, out_hbm, out_sems, part).wait()


def make_modes(alm, legendre, targets):
    slot_count, degrees, total = legendre.shape
    slots = 4
    parts = slot_count // slots
    width = 2 * slot_count
    height = 2 * C
    out = jax.ShapeDtypeStruct((targets, C * (total // targets), width), jnp.bfloat16)
    return pl.pallas_call(
        modes_kernel,
        in_specs=[pl.BlockSpec(memory_space=pl.ANY)] * 2,
        out_specs=pl.BlockSpec(memory_space=pl.ANY),
        out_shape=out,
        scratch_shapes=[
            pltpu.VMEM(alm.shape, jnp.bfloat16),
            pltpu.VMEM(legendre.shape, jnp.bfloat16),
            pltpu.VMEM((total // LANES, slot_count * height, LANES), jnp.float32),
            pltpu.VMEM((C, total, width), jnp.float32),
            pltpu.VMEM(out.shape, out.dtype),
            pltpu.SemaphoreType.DMA((parts,)),
            pltpu.SemaphoreType.DMA((parts,)),
            pltpu.SemaphoreType.DMA((4,)),
        ],
        cost_estimate=pl.CostEstimate(
            flops=2 * slot_count * degrees * total * 2 * C,
            bytes_accessed=slot_count * degrees * (total + 2 * C) * 2,
            transcendentals=0,
        ),
        compiler_params=pltpu.CompilerParams(vmem_limit_bytes=62 * 1024 * 1024),
    )(alm, legendre)


def analysis_kernel(table_hbm, spectra_ref, out_hbm, table_ref, turned_ref, out_ref, sems, out_sems):
    total_slots, degrees, total = table_ref.shape
    slots = 8
    pieces = sems.shape[0] * slots // total_slots
    start_parts(table_hbm, table_ref, sems, IN_FLIGHT)
    turned_ref[...] = spectra_ref[...].astype(jnp.float32).T
    count = total_slots // HALVES
    for first in range(0, total_slots, slots):
        row = first // count * 2 * count + first % count
        rows = [turned_ref[row + share * count : row + share * count + slots, :] for share in range(2)]
        lhs = jnp.concatenate(rows, axis=0).astype(jnp.bfloat16)
        for piece in range(pieces):
            next_part(table_hbm, table_ref, sems, first // slots * pieces + piece, IN_FLIGHT)
        table = table_ref[first : first + slots].reshape(slots * degrees, total)
        result = lax.dot_general(lhs, table, (((1,), (1,)), ((), ())), preferred_element_type=jnp.float32)
        for slot in range(slots):
            span = slice(slot * degrees, (slot + 1) * degrees)
            out_ref[first + slot, 0:1, :] = result[slot : slot + 1, span]
            out_ref[first + slot, 1:2, :] = result[slots + slot : slots + slot + 1, span]
        part_copy(out_ref, out_hbm, out_sems, first // slots).start()
    for part in range(out_sems.shape[0]):
        part_copy(out_ref, out_hbm, out_sems, part).wait()


def analyse(legendre, spectra):
    slot_count, degrees, total = legendre.shape
    slots = 8
    width = 2 * slot_count
    vmem = pl.BlockSpec(memory_space=pltpu.VMEM)
    return pl.pallas_call(
        analysis_kernel,
        in_specs=[pl.BlockSpec(memory_space=pl.ANY), vmem],
        out_specs=pl.BlockSpec(memory_space=pl.ANY),
        out_shape=jax.ShapeDtypeStruct((slot_count, 2, degrees), jnp.float32),
        scratch_shapes=[
            pltpu.VMEM(legendre.shape, jnp.bfloat16),
            pltpu.VMEM((width, total), jnp.float32),
            pltpu.VMEM((slot_count, 2, degrees), jnp.float32),
            pltpu.SemaphoreType.DMA((slot_count // 4,)),
            pltpu.SemaphoreType.DMA((slot_count // slots,)),
        ],
        cost_estimate=pl.CostEstimate(
            flops=2 * slot_count * degrees * total * 2 * slots,
            bytes_accessed=slot_count * degrees * total * 2,
            transcendentals=0,
        ),
        compiler_params=pltpu.CompilerParams(vmem_limit_bytes=50 * 1024 * 1024),
    )(legendre, spectra)


def from_other_tiles(sends):
    count = len(sends)
    got = [sends[0]]
    for hop in range(1, count):
        got.append(lax.ppermute(sends[hop], "tile", [(at, (at + hop) % count) for at in range(count)]))
    return got


def in_tile_order(got):
    count = len(got)
    tile_at = lax.axis_index("tile")
    stacked = jnp.stack(got)
    return jnp.stack(
        [lax.dynamic_index_in_dim(stacked, (tile_at - at) % count, 0, keepdims=False) for at in range(count)]
    )


def body(alm, legendre, order_of_slot):
    tile_count = lax.axis_size("tile")
    band_count = lax.axis_size("band")
    tile_at = lax.axis_index("tile")
    slot_count = alm.shape[0]
    targets = band_count * tile_count
    cycles = legendre.shape[2] // targets
    padded = round_up(cycles, 8)
    depth = 2 * L
    width = 2 * slot_count
    group_width = math.lcm(width, LANES)
    groups = depth // group_width
    plain = group_width == width and padded == cycles
    axes = ("band", "tile")

    partial = make_modes(alm, legendre, targets)
    partial = lax.all_to_all(partial, axes, split_axis=0, concat_axis=0, tiled=True)
    modes = partial.reshape(band_count, tile_count, C * cycles, width)
    if not plain:
        modes = jnp.sum(modes.astype(jnp.float32), axis=1).astype(jnp.bfloat16)
        modes = modes.reshape(groups, group_width // width, C, cycles, width)
        modes = modes.transpose(0, 2, 3, 1, 4).reshape(groups, C, cycles, group_width)
        modes = jnp.pad(modes, ((0, 0), (0, 0), (0, padded - cycles), (0, 0)))
        modes = modes.reshape(groups, 1, C * padded, group_width)

    order_rows = order_of_slot.reshape(band_count * HALVES, 1, slot_count // HALVES)
    order_rows = jnp.broadcast_to(order_rows, (band_count * HALVES, 2, slot_count // HALVES)).reshape(depth)
    basis = make_basis(order_rows.astype(jnp.float32)[:, None], slot_count)
    odd = (order_rows % 2).astype(jnp.float32)[None, :]
    vectors, spectra = run_ilc(modes, odd, basis)

    if not plain:
        spectra = spectra[:, 0, :cycles].reshape(groups, cycles, group_width // width, width)
        spectra = spectra.transpose(0, 2, 1, 3).reshape(band_count, 1, cycles, width)
        spectra = jnp.broadcast_to(spectra, (band_count, tile_count, cycles, width))
    spectra = spectra.reshape(targets, cycles, width)
    routed = lax.all_to_all(spectra, axes, split_axis=0, concat_axis=0, tiled=True)
    found = in_tile_order(from_other_tiles([vectors[:, :cycles]] * tile_count))
    lanes = LANES // tile_count
    found = lax.dynamic_slice_in_dim(found, tile_at * lanes, lanes, axis=3)
    ilc_map = found.transpose(0, 2, 3, 1).reshape(tile_count * cycles, NLON // tile_count)
    routed, ilc_map = lax.optimization_barrier((routed, ilc_map))
    ilc_alm = analyse(legendre, routed.reshape(targets * cycles, width))
    return (ilc_map, ilc_alm)


def solution(mesh):
    placed = (P("band", None, None, "tile"), P("band", "tile", None), P())
    return jax.shard_map(
        body,
        mesh=mesh,
        in_specs=placed,
        out_specs=(P("band", "tile"), P("band", None, "tile")),
        check_vma=False,
    )
```

```python
import functools
import math

import jax
import jax.numpy as jnp
from jax import lax
from jax.experimental import pallas as pl
from jax.experimental.pallas import tpu as pltpu
from jax.sharding import PartitionSpec as P

C = 9
L = 1024
NLON = 4096
HALO = 32

RIDGE = 0.1
EPSILON = 1e-06

WINDOW = 2 * HALO + 1
LANES = NLON // HALO
HALF = LANES // 2
REST = C - 1
PAIRS = [(a_at, b_at) for a_at in range(REST) for b_at in range(a_at, REST)] + [(a_at, REST) for a_at in range(REST)]
SUMS = len(PAIRS) + 1
VMEM_LIMIT = 48 * 1024 * 1024
IN_FLIGHT = 4
HALVES = 2
CHUNK = 8


def round_up(value, multiple):
    return (value + multiple - 1) // multiple * multiple


def cos_turns(turns):
    nearest = (turns + 12582912.0) - 12582912.0
    quarter = 1.0 - 4.0 * jnp.abs(turns - nearest)
    square = quarter * quarter
    tail = square * (1.6044118478736e-04 - square * 3.598843235e-06)
    tail = square * (-4.68175413531868e-03 + tail)
    tail = square * (7.96926262461670e-02 + tail)
    tail = square * (-6.45964097506246e-01 + tail)
    return quarter * (1.57079632679490 + tail)


def basis_kernel(slots, order_ref, basis_ref):
    rows = 64
    begin = pl.program_id(0) * order_ref.shape[0]
    row = lax.broadcasted_iota(jnp.int32, (rows, LANES), 0)
    lane = lax.broadcasted_iota(jnp.int32, (rows, LANES), 1)
    cell = (HALO * (lane % HALF) + lane // HALF).astype(jnp.float32) / NLON
    scaling = 1.0 / math.sqrt(L)
    for first in range(0, order_ref.shape[0], rows):
        span = slice(first, first + rows)
        part = (row + (begin + first)) // (slots // HALVES) % 2
        order = jnp.broadcast_to(order_ref[span, :], (rows, LANES))
        turns = order * cell + part.astype(jnp.float32) * 0.25
        step = order * (2.0 / NLON)
        before = cos_turns(turns) * scaling
        now = cos_turns(turns + step) * scaling
        twice = 2.0 * cos_turns(step)
        for column in range(HALO // 2):
            at = column % (CHUNK // 2) * LANES
            basis_ref[column // (CHUNK // 2), span, at : at + LANES] = before.astype(jnp.bfloat16)
            if column < HALO // 2 - 1:
                before, now = now, twice * now - before


def make_basis(order_rows, slots):
    rows = order_rows.shape[0]
    block = 256
    chunks = HALO // CHUNK
    columns = CHUNK // 2 * LANES
    return pl.pallas_call(
        functools.partial(basis_kernel, slots),
        grid=(rows // block,),
        in_specs=[pl.BlockSpec((block, 1), lambda at: (at, 0))],
        out_specs=pl.BlockSpec((chunks, block, columns), lambda at: (0, at, 0)),
        out_shape=jax.ShapeDtypeStruct((chunks, rows, columns), jnp.bfloat16),
        cost_estimate=pl.CostEstimate(
            flops=rows * chunks * columns * 8, bytes_accessed=rows * chunks * columns * 2, transcendentals=0
        ),
        compiler_params=pltpu.CompilerParams(vmem_limit_bytes=VMEM_LIMIT),
    )(order_rows)


def part_copy(source, target, sems, part):
    count = source.shape[0] // sems.shape[0]
    span = pl.ds(part * count, count)
    return pltpu.make_async_copy(source.at[span], target.at[span], sems.at[part])


def start_parts(source, target, sems, count):
    for part in range(min(count, sems.shape[0])):
        part_copy(source, target, sems, part).start()


def next_part(source, target, sems, part, ahead):
    part_copy(source, target, sems, part).wait()
    more = part + ahead < sems.shape[0]
    if isinstance(part, int):
        if more:
            part_copy(source, target, sems, part + ahead).start()
    else:

        @pl.when(more)
        def _():
            part_copy(source, target, sems, part + ahead).start()


def reciprocal(value):
    guess = pl.reciprocal(value, approx=True)
    return guess * (2.0 - value * guess)


def combine_steps(sum_of, map_of):
    ridge = RIDGE * (sum_of(SUMS - 1) * (1.0 / C) + WINDOW * EPSILON)
    upper, inverses, rights, maps = {}, [], [], []
    value = map_of(REST)
    for row in range(REST):
        ratios = [upper[at, row] * inverses[at] for at in range(row)]
        pivot = sum_of(PAIRS.index((row, row))) + (ridge + ridge)
        for at in range(row):
            pivot = pivot - ratios[at] * upper[at, row]
        inverse = reciprocal(pivot)
        yield None
        right = ridge - sum_of(PAIRS.index((row, REST)))
        own = map_of(row)
        for at in range(row):
            right = right - ratios[at] * rights[at]
            own = own - ratios[at] * maps[at]
        yield None
        for col in range(row + 1, REST):
            entry = sum_of(PAIRS.index((row, col))) + ridge
            for at in range(row):
                entry = entry - ratios[at] * upper[at, col]
            upper[row, col] = entry
            yield None
        value = value + (right * inverse) * own
        inverses.append(inverse)
        rights.append(right)
        maps.append(own)
    yield value


def in_step(generators):
    for found in zip(*generators):
        pass
    return found


def ilc_kernel(modes_ref, odd_ref, basis_hbm, ilc_ref, spectra_ref, basis_ref, lhs_ref, maps_ref, sums_ref, low_ref, found_ref, sems):
    groups, shares, rows, width = modes_ref.shape
    columns = basis_ref.shape[2]
    depth = lhs_ref.shape[1]
    pieces, share_rows = found_ref.shape[0], found_ref.shape[2]
    chunks = basis_ref.shape[0] // pieces
    cycles = rows // C
    second = round_up(rows, 16)
    ahead = 3
    start_parts(basis_hbm, basis_ref, sems, ahead)
    for group in range(groups):
        span = slice(group * width, (group + 1) * width)
        odd = odd_ref[:, span]
        values = modes_ref[group, 0].astype(jnp.float32)
        for share in range(1, shares):
            values = values + modes_ref[group, share].astype(jnp.float32)
        lhs_ref[0:rows, span] = (values * (1.0 - odd)).astype(jnp.bfloat16)
        lhs_ref[second : second + rows, span] = (values * odd).astype(jnp.bfloat16)
    low_half = lax.broadcasted_iota(jnp.int32, (cycles, LANES), 1) < HALF
    sums_ref[...] = jnp.zeros_like(sums_ref)

    def store_maps(at, maps):
        squares = maps[0] * maps[0]
        for chan in range(1, C):
            squares = squares + maps[chan] * maps[chan]
            maps_ref[at, chan - 1] = maps[chan] - maps[0]
        maps_ref[at, REST] = maps[0]
        maps_ref[at, C] = squares

    def maps_of_chunk(chunk):
        next_part(basis_hbm, basis_ref, sems, chunk, ahead)
        basis = basis_ref[chunk * pieces : (chunk + 1) * pieces].reshape(depth, columns)
        result = jnp.dot(lhs_ref[...], basis, preferred_element_type=jnp.float32)
        for part in range(CHUNK // 2):
            at = CHUNK * chunk + 2 * part
            lanes = slice(part * LANES, (part + 1) * LANES)
            left, right = [], []
            for chan in range(C):
                even_part = result[chan * cycles : (chan + 1) * cycles, lanes]
                odd_part = result[second + chan * cycles : second + (chan + 1) * cycles, lanes]
                near = even_part + odd_part
                far = even_part - odd_part
                left.append(jnp.where(low_half, near, pltpu.roll(far, HALF, 1)))
                right.append(jnp.where(low_half, pltpu.roll(near, HALF, 1), far))
            store_maps(at, left)
            store_maps(at + 1, right)

    def add_totals(chunk):
        vectors = [CHUNK * chunk + part for part in range(CHUNK)]
        for a_at in range(C):
            own = [maps_ref[at, a_at] for at in vectors]
            for b_at in range(a_at, C):
                if (a_at, b_at) == (REST, REST):
                    continue
                pair = PAIRS.index((a_at, b_at))
                total = sums_ref[pair]
                for at, value in zip(vectors, own):
                    total = total + value * (value if a_at == b_at else maps_ref[at, b_at])
                sums_ref[pair] = total
        total = sums_ref[SUMS - 1]
        for at in vectors:
            total = total + maps_ref[at, C]
        sums_ref[SUMS - 1] = total

    maps_of_chunk(0)
    for chunk in range(1, chunks):
        maps_of_chunk(chunk)
        add_totals(chunk - 1)
    add_totals(chunks - 1)
    for pair in range(SUMS):
        total = sums_ref[pair]
        sums_ref[pair] = pltpu.roll(total, 1, 1) + pltpu.roll(total, 2, 1)

    def solve_steps(at):
        maps = [maps_ref[at, chan] for chan in range(C + 1)]

        def sum_of(pair):
            own = maps[C] if pair == SUMS - 1 else maps[PAIRS[pair][0]] * maps[PAIRS[pair][1]]
            total = sums_ref[pair] + own
            sums_ref[pair] = total - pltpu.roll(own, 2, 1)
            return total

        return combine_steps(sum_of, lambda chan: pltpu.roll(maps[chan], 1, 1))

    def add_spectra(chunk):
        lhs = jnp.concatenate([low_ref[chunk, part] for part in range(pieces)], axis=1)
        for part in range(pieces):
            term = lax.dot_general(
                lhs, basis_ref[chunk * pieces + part], (((1,), (1,)), ((), ())), preferred_element_type=jnp.float32
            )
            found_ref[part] = term if chunk == 0 else found_ref[part] + term

    for pair_at in range(HALO // 2):
        at = 2 * pair_at
        chunk, part = pair_at // pieces, pair_at % pieces
        found = in_step([solve_steps(at), solve_steps(at + 1)])
        found = [pltpu.roll(value, LANES - 1, 1) for value in found]
        ilc_ref[at] = found[0]
        ilc_ref[at + 1] = found[1]
        near = jnp.where(low_half, found[0], pltpu.roll(found[1], HALF, 1))
        far = jnp.where(low_half, pltpu.roll(found[0], HALF, 1), found[1])
        low_ref[chunk, part] = jnp.concatenate([near, far], axis=0).astype(jnp.bfloat16)
        if part == pieces - 1:
            add_spectra(chunk)
    for group in range(groups):
        span = slice(group * width, (group + 1) * width)
        sign = 1.0 - 2.0 * odd_ref[:, span]
        part, first = group * width // share_rows, group * width % share_rows
        result = found_ref[part, :, first : first + width]
        value = (result[0:cycles] + sign * result[cycles:]).astype(jnp.bfloat16)
        for share in range(shares):
            spectra_ref[group, share] = value


def run_ilc(modes, odd, basis):
    groups, shares, rows, width = modes.shape
    chunks, depth, columns = basis.shape
    pieces = CHUNK // 2
    basis = basis.reshape(chunks * pieces, depth // pieces, columns)
    cycles = rows // C
    vmem = pl.BlockSpec(memory_space=pltpu.VMEM)
    return pl.pallas_call(
        ilc_kernel,
        in_specs=[vmem, vmem, pl.BlockSpec(memory_space=pl.ANY)],
        out_specs=[vmem, vmem],
        out_shape=[
            jax.ShapeDtypeStruct((HALO, cycles, LANES), jnp.float32),
            jax.ShapeDtypeStruct((groups, shares, cycles, width), jnp.bfloat16),
        ],
        scratch_shapes=[
            pltpu.VMEM(basis.shape, jnp.bfloat16),
            pltpu.VMEM((2 * round_up(rows, 16), depth), jnp.bfloat16),
            pltpu.VMEM((HALO, C + 1, cycles, LANES), jnp.float32),
            pltpu.VMEM((SUMS, cycles, LANES), jnp.float32),
            pltpu.VMEM((chunks, pieces, 2 * cycles, LANES), jnp.bfloat16),
            pltpu.VMEM((pieces, 2 * cycles, depth // pieces), jnp.float32),
            pltpu.SemaphoreType.DMA((chunks,)),
        ],
        cost_estimate=pl.CostEstimate(
            flops=2 * chunks * depth * columns * (2 * rows + 2 * cycles),
            bytes_accessed=chunks * depth * columns * 2,
            transcendentals=0,
        ),
        compiler_params=pltpu.CompilerParams(vmem_limit_bytes=VMEM_LIMIT),
    )(modes, odd, basis)


def modes_kernel(alm_hbm, table_hbm, out_hbm, alm_ref, table_ref, held_ref, turned_ref, out_ref, alm_sem, sems, out_sems):
    parts = sems.shape[0]
    total_slots, degrees, total = table_ref.shape
    each, slots = total_slots // parts, 4
    targets, rows = out_ref.shape[:2]
    cycles = rows // C
    height = 2 * C
    alm_copy = pltpu.make_async_copy(alm_hbm, alm_ref, alm_sem)
    alm_copy.start()
    start_parts(table_hbm, table_ref, sems, IN_FLIGHT)

    def some_slots(first):
        lhs = alm_ref[first : first + slots].reshape(slots * height, degrees)
        rhs = jnp.concatenate([table_ref[first + slot] for slot in range(slots)], axis=1)
        result = jnp.dot(lhs, rhs, preferred_element_type=jnp.float32)
        for slot in range(slots):
            own = result[slot * height : (slot + 1) * height, slot * total : (slot + 1) * total]
            for lanes in range(held_ref.shape[0]):
                span = slice((first + slot) * height, (first + slot + 1) * height)
                held_ref[lanes, span, :] = own[:, lanes * LANES : (lanes + 1) * LANES]

    def turn(half):
        count = total_slots // HALVES
        first = half * count * height
        for chan in range(C):
            for lanes in range(held_ref.shape[0]):
                both = [held_ref[lanes, pl.ds(first + 2 * chan + part, count, stride=height), :] for part in range(2)]
                span = slice(half * 2 * count, (half + 1) * 2 * count)
                turned_ref[chan, lanes * LANES : (lanes + 1) * LANES, span] = jnp.concatenate(both, axis=0).T

    alm_copy.wait()
    for part in range(parts):
        next_part(table_hbm, table_ref, sems, part, IN_FLIGHT)
        for first in range(part * each, (part + 1) * each, slots):
            some_slots(first)
        if (part + 1) * HALVES % parts == 0:
            turn((part + 1) * HALVES // parts - 1)
    each = targets // out_sems.shape[0]
    for target in range(targets):
        span = slice(target * cycles, (target + 1) * cycles)
        block = jnp.concatenate([turned_ref[chan, span, :] for chan in range(C)], axis=0)
        out_ref[target] = block.astype(jnp.bfloat16)
        if (target + 1) % each == 0:
            part_copy(out_ref, out_hbm, out_sems, target // each).start()
    for part in range(out_sems.shape[0]):
        part_copy(out_ref, out_hbm, out_sems, part).wait()


def make_modes(alm, legendre, targets):
    slot_count, degrees, total = legendre.shape
    parts = slot_count // 8
    width = 2 * slot_count
    height = 2 * C
    out = jax.ShapeDtypeStruct((targets, C * (total // targets), width), jnp.bfloat16)
    return pl.pallas_call(
        modes_kernel,
        in_specs=[pl.BlockSpec(memory_space=pl.ANY)] * 2,
        out_specs=pl.BlockSpec(memory_space=pl.ANY),
        out_shape=out,
        scratch_shapes=[
            pltpu.VMEM(alm.shape, jnp.bfloat16),
            pltpu.VMEM(legendre.shape, jnp.bfloat16),
            pltpu.VMEM((total // LANES, slot_count * height, LANES), jnp.float32),
            pltpu.VMEM((C, total, width), jnp.float32),
            pltpu.VMEM(out.shape, out.dtype),
            pltpu.SemaphoreType.DMA,
            pltpu.SemaphoreType.DMA((parts,)),
            pltpu.SemaphoreType.DMA((4,)),
        ],
        cost_estimate=pl.CostEstimate(
            flops=2 * slot_count * degrees * total * 2 * C,
            bytes_accessed=slot_count * degrees * (total + 2 * C) * 2,
            transcendentals=0,
        ),
        compiler_params=pltpu.CompilerParams(vmem_limit_bytes=62 * 1024 * 1024),
    )(alm, legendre)


def analysis_kernel(table_hbm, spectra_ref, out_ref, table_ref, turned_ref, sems):
    total_slots, degrees, total = table_ref.shape
    slots = 8
    start_parts(table_hbm, table_ref, sems, IN_FLIGHT)
    turned_ref[...] = spectra_ref[...].astype(jnp.float32).T
    count = total_slots // HALVES
    for first in range(0, total_slots, slots):
        row = first // count * 2 * count + first % count
        rows = [turned_ref[row + share * count : row + share * count + slots, :] for share in range(2)]
        lhs = jnp.concatenate(rows, axis=0).astype(jnp.bfloat16)
        next_part(table_hbm, table_ref, sems, first // slots, IN_FLIGHT)
        table = table_ref[first : first + slots].reshape(slots * degrees, total)
        result = lax.dot_general(lhs, table, (((1,), (1,)), ((), ())), preferred_element_type=jnp.float32)
        for slot in range(slots):
            span = slice(slot * degrees, (slot + 1) * degrees)
            out_ref[first + slot, 0:1, :] = result[slot : slot + 1, span]
            out_ref[first + slot, 1:2, :] = result[slots + slot : slots + slot + 1, span]


def analyse(legendre, spectra):
    slot_count, degrees, total = legendre.shape
    slots = 8
    width = 2 * slot_count
    vmem = pl.BlockSpec(memory_space=pltpu.VMEM)
    return pl.pallas_call(
        analysis_kernel,
        in_specs=[pl.BlockSpec(memory_space=pl.ANY), vmem],
        out_specs=vmem,
        out_shape=jax.ShapeDtypeStruct((slot_count, 2, degrees), jnp.float32),
        scratch_shapes=[
            pltpu.VMEM(legendre.shape, jnp.bfloat16),
            pltpu.VMEM((width, total), jnp.float32),
            pltpu.SemaphoreType.DMA((slot_count // slots,)),
        ],
        cost_estimate=pl.CostEstimate(
            flops=2 * slot_count * degrees * total * 2 * slots,
            bytes_accessed=slot_count * degrees * total * 2,
            transcendentals=0,
        ),
        compiler_params=pltpu.CompilerParams(vmem_limit_bytes=50 * 1024 * 1024),
    )(legendre, spectra)


def from_other_tiles(sends):
    count = len(sends)
    got = [sends[0]]
    for hop in range(1, count):
        got.append(lax.ppermute(sends[hop], "tile", [(at, (at + hop) % count) for at in range(count)]))
    return got


def in_tile_order(got):
    count = len(got)
    tile_at = lax.axis_index("tile")
    stacked = jnp.stack(got)
    return jnp.stack(
        [lax.dynamic_index_in_dim(stacked, (tile_at - at) % count, 0, keepdims=False) for at in range(count)]
    )


def body(alm, legendre, order_of_slot):
    tile_count = lax.axis_size("tile")
    band_count = lax.axis_size("band")
    tile_at = lax.axis_index("tile")
    slot_count = alm.shape[0]
    targets = band_count * tile_count
    cycles = legendre.shape[2] // targets
    padded = round_up(cycles, 8)
    depth = 2 * L
    width = 2 * slot_count
    group_width = math.lcm(width, LANES)
    groups = depth // group_width
    plain = group_width == width and padded == cycles
    axes = ("band", "tile")

    partial = make_modes(alm, legendre, targets)
    partial = lax.all_to_all(partial, axes, split_axis=0, concat_axis=0, tiled=True)
    modes = partial.reshape(band_count, tile_count, C * cycles, width)
    if not plain:
        modes = jnp.sum(modes.astype(jnp.float32), axis=1).astype(jnp.bfloat16)
        modes = modes.reshape(groups, group_width // width, C, cycles, width)
        modes = modes.transpose(0, 2, 3, 1, 4).reshape(groups, C, cycles, group_width)
        modes = jnp.pad(modes, ((0, 0), (0, 0), (0, padded - cycles), (0, 0)))
        modes = modes.reshape(groups, 1, C * padded, group_width)

    order_rows = order_of_slot.reshape(band_count * HALVES, 1, slot_count // HALVES)
    order_rows = jnp.broadcast_to(order_rows, (band_count * HALVES, 2, slot_count // HALVES)).reshape(depth)
    basis = make_basis(order_rows.astype(jnp.float32)[:, None], slot_count)
    odd = (order_rows % 2).astype(jnp.float32)[None, :]
    vectors, spectra = run_ilc(modes, odd, basis)

    if not plain:
        spectra = spectra[:, 0, :cycles].reshape(groups, cycles, group_width // width, width)
        spectra = spectra.transpose(0, 2, 1, 3).reshape(band_count, 1, cycles, width)
        spectra = jnp.broadcast_to(spectra, (band_count, tile_count, cycles, width))
    spectra = spectra.reshape(targets, cycles, width)
    routed = lax.all_to_all(spectra, axes, split_axis=0, concat_axis=0, tiled=True)
    found = in_tile_order(from_other_tiles([vectors[:, :cycles]] * tile_count))
    lanes = LANES // tile_count
    found = lax.dynamic_slice_in_dim(found, tile_at * lanes, lanes, axis=3)
    ilc_map = found.transpose(0, 2, 3, 1).reshape(tile_count * cycles, NLON // tile_count)
    routed, ilc_map = lax.optimization_barrier((routed, ilc_map))
    ilc_alm = analyse(legendre, routed.reshape(targets * cycles, width))
    return (ilc_map, ilc_alm)


def solution(mesh):
    placed = (P("band", None, None, "tile"), P("band", "tile", None), P())
    return jax.shard_map(
        body,
        mesh=mesh,
        in_specs=placed,
        out_specs=(P("band", "tile"), P("band", None, "tile")),
        check_vma=False,
    )
```

```python
import functools
import math

import jax
import jax.numpy as jnp
from jax import lax
from jax.experimental import pallas as pl
from jax.experimental.pallas import tpu as pltpu
from jax.sharding import PartitionSpec as P

C = 9
L = 1024
NLON = 4096
HALO = 32

RIDGE = 0.1
EPSILON = 1e-06

WINDOW = 2 * HALO + 1
LANES = NLON // HALO
HALF = LANES // 2
REST = C - 1
PAIRS = [(a_at, b_at) for a_at in range(REST) for b_at in range(a_at, REST)] + [(a_at, REST) for a_at in range(REST)]
SUMS = len(PAIRS) + 1
VMEM_LIMIT = 48 * 1024 * 1024
IN_FLIGHT = 4
BUNDLES = 2
HALVES = 2
CHUNK = 8


def round_up(value, multiple):
    return (value + multiple - 1) // multiple * multiple


def cos_turns(turns):
    nearest = (turns + 12582912.0) - 12582912.0
    quarter = 1.0 - 4.0 * jnp.abs(turns - nearest)
    square = quarter * quarter
    tail = square * (1.6044118478736e-04 - square * 3.598843235e-06)
    tail = square * (-4.68175413531868e-03 + tail)
    tail = square * (7.96926262461670e-02 + tail)
    tail = square * (-6.45964097506246e-01 + tail)
    return quarter * (1.57079632679490 + tail)


def basis_kernel(slots, order_ref, basis_ref):
    rows = 64
    begin = pl.program_id(0) * order_ref.shape[0]
    row = lax.broadcasted_iota(jnp.int32, (rows, LANES), 0)
    lane = lax.broadcasted_iota(jnp.int32, (rows, LANES), 1)
    cell = (HALO * (lane % HALF) + lane // HALF).astype(jnp.float32) / NLON
    scaling = 1.0 / math.sqrt(L)
    for first in range(0, order_ref.shape[0], rows):
        span = slice(first, first + rows)
        part = (row + (begin + first)) // (slots // HALVES) % 2
        order = jnp.broadcast_to(order_ref[span, :], (rows, LANES))
        turns = order * cell + part.astype(jnp.float32) * 0.25
        step = order * (2.0 / NLON)
        before = cos_turns(turns) * scaling
        now = cos_turns(turns + step) * scaling
        twice = 2.0 * cos_turns(step)
        for column in range(HALO // 2):
            at = column % (CHUNK // 2) * LANES
            basis_ref[column // (CHUNK // 2), span, at : at + LANES] = before.astype(jnp.bfloat16)
            if column < HALO // 2 - 1:
                before, now = now, twice * now - before


def make_basis(order_rows, slots):
    rows = order_rows.shape[0]
    block = 256
    chunks = HALO // CHUNK
    columns = CHUNK // 2 * LANES
    return pl.pallas_call(
        functools.partial(basis_kernel, slots),
        grid=(rows // block,),
        in_specs=[pl.BlockSpec((block, 1), lambda at: (at, 0))],
        out_specs=pl.BlockSpec((chunks, block, columns), lambda at: (0, at, 0)),
        out_shape=jax.ShapeDtypeStruct((chunks, rows, columns), jnp.bfloat16),
        cost_estimate=pl.CostEstimate(
            flops=rows * chunks * columns * 8, bytes_accessed=rows * chunks * columns * 2, transcendentals=0
        ),
        compiler_params=pltpu.CompilerParams(vmem_limit_bytes=VMEM_LIMIT),
    )(order_rows)


def part_copy(source, target, sems, part):
    count = source.shape[0] // sems.shape[0]
    span = pl.ds(part * count, count)
    return pltpu.make_async_copy(source.at[span], target.at[span], sems.at[part])


def start_parts(source, target, sems, count):
    for part in range(min(count, sems.shape[0])):
        part_copy(source, target, sems, part).start()


def next_part(source, target, sems, part, ahead):
    part_copy(source, target, sems, part).wait()
    more = part + ahead < sems.shape[0]
    if isinstance(part, int):
        if more:
            part_copy(source, target, sems, part + ahead).start()
    else:

        @pl.when(more)
        def _():
            part_copy(source, target, sems, part + ahead).start()


def reciprocal(value):
    guess = pl.reciprocal(value, approx=True)
    return guess * (2.0 - value * guess)


def combine_steps(sum_of, map_of):
    ridge = RIDGE * (sum_of(SUMS - 1) * (1.0 / C) + WINDOW * EPSILON)
    upper, inverses, rights, maps = {}, [], [], []
    value = map_of(REST)
    for row in range(REST):
        ratios = [upper[at, row] * inverses[at] for at in range(row)]
        pivot = sum_of(PAIRS.index((row, row))) + (ridge + ridge)
        for at in range(row):
            pivot = pivot - ratios[at] * upper[at, row]
        inverse = reciprocal(pivot)
        yield None
        right = ridge - sum_of(PAIRS.index((row, REST)))
        own = map_of(row)
        for at in range(row):
            right = right - ratios[at] * rights[at]
            own = own - ratios[at] * maps[at]
        yield None
        for col in range(row + 1, REST):
            entry = sum_of(PAIRS.index((row, col))) + ridge
            for at in range(row):
                entry = entry - ratios[at] * upper[at, col]
            upper[row, col] = entry
            yield None
        value = value + (right * inverse) * own
        inverses.append(inverse)
        rights.append(right)
        maps.append(own)
    yield value


def in_step(generators):
    for found in zip(*generators):
        pass
    return found


def ilc_kernel(bundles, *refs):
    modes_refs, refs = refs[:bundles], refs[bundles:]
    odd_ref, basis_hbm, ilc_ref, spectra_ref, basis_ref, lhs_ref, maps_ref, sums_ref, low_ref, found_ref, sems = refs
    groups, shares, _, width = modes_refs[0].shape
    rows = sum(modes_ref.shape[2] for modes_ref in modes_refs)
    columns = basis_ref.shape[2]
    depth = lhs_ref.shape[1]
    pieces, share_rows = found_ref.shape[0], found_ref.shape[2]
    chunks = basis_ref.shape[0] // pieces
    cycles = rows // C
    second = round_up(rows, 16)
    ahead = 3
    start_parts(basis_hbm, basis_ref, sems, ahead)
    for group in range(groups):
        span = slice(group * width, (group + 1) * width)
        odd = odd_ref[:, span]
        values = []
        for modes_ref in modes_refs:
            value = modes_ref[group, 0].astype(jnp.float32)
            for share in range(1, shares):
                value = value + modes_ref[group, share].astype(jnp.float32)
            values.append(value)
        values = jnp.concatenate(values, axis=0)
        lhs_ref[0:rows, span] = (values * (1.0 - odd)).astype(jnp.bfloat16)
        lhs_ref[second : second + rows, span] = (values * odd).astype(jnp.bfloat16)
    low_half = lax.broadcasted_iota(jnp.int32, (cycles, LANES), 1) < HALF
    sums_ref[...] = jnp.zeros_like(sums_ref)

    def store_maps(at, maps):
        squares = maps[0] * maps[0]
        for chan in range(1, C):
            squares = squares + maps[chan] * maps[chan]
            maps_ref[at, chan - 1] = maps[chan] - maps[0]
        maps_ref[at, REST] = maps[0]
        maps_ref[at, C] = squares

    def maps_of_chunk(chunk):
        next_part(basis_hbm, basis_ref, sems, chunk, ahead)
        basis = basis_ref[chunk * pieces : (chunk + 1) * pieces].reshape(depth, columns)
        result = jnp.dot(lhs_ref[...], basis, preferred_element_type=jnp.float32)
        for part in range(CHUNK // 2):
            at = CHUNK * chunk + 2 * part
            lanes = slice(part * LANES, (part + 1) * LANES)
            left, right = [], []
            for chan in range(C):
                even_part = result[chan * cycles : (chan + 1) * cycles, lanes]
                odd_part = result[second + chan * cycles : second + (chan + 1) * cycles, lanes]
                near = even_part + odd_part
                far = even_part - odd_part
                left.append(jnp.where(low_half, near, pltpu.roll(far, HALF, 1)))
                right.append(jnp.where(low_half, pltpu.roll(near, HALF, 1), far))
            store_maps(at, left)
            store_maps(at + 1, right)

    def add_totals(chunk):
        vectors = [CHUNK * chunk + part for part in range(CHUNK)]
        for a_at in range(C):
            own = [maps_ref[at, a_at] for at in vectors]
            for b_at in range(a_at, C):
                if (a_at, b_at) == (REST, REST):
                    continue
                pair = PAIRS.index((a_at, b_at))
                total = sums_ref[pair]
                for at, value in zip(vectors, own):
                    total = total + value * (value if a_at == b_at else maps_ref[at, b_at])
                sums_ref[pair] = total
        total = sums_ref[SUMS - 1]
        for at in vectors:
            total = total + maps_ref[at, C]
        sums_ref[SUMS - 1] = total

    maps_of_chunk(0)
    for chunk in range(1, chunks):
        maps_of_chunk(chunk)
        add_totals(chunk - 1)
    add_totals(chunks - 1)
    for pair in range(SUMS):
        total = sums_ref[pair]
        sums_ref[pair] = pltpu.roll(total, 1, 1) + pltpu.roll(total, 2, 1)

    def solve_steps(at):
        maps = [maps_ref[at, chan] for chan in range(C + 1)]

        def sum_of(pair):
            own = maps[C] if pair == SUMS - 1 else maps[PAIRS[pair][0]] * maps[PAIRS[pair][1]]
            total = sums_ref[pair] + own
            sums_ref[pair] = total - pltpu.roll(own, 2, 1)
            return total

        return combine_steps(sum_of, lambda chan: pltpu.roll(maps[chan], 1, 1))

    def add_spectra(chunk):
        lhs = jnp.concatenate([low_ref[chunk, part] for part in range(pieces)], axis=1)
        for part in range(pieces):
            term = lax.dot_general(
                lhs, basis_ref[chunk * pieces + part], (((1,), (1,)), ((), ())), preferred_element_type=jnp.float32
            )
            found_ref[part] = term if chunk == 0 else found_ref[part] + term

    for pair_at in range(HALO // 2):
        at = 2 * pair_at
        chunk, part = pair_at // pieces, pair_at % pieces
        found = in_step([solve_steps(at), solve_steps(at + 1)])
        found = [pltpu.roll(value, LANES - 1, 1) for value in found]
        ilc_ref[at] = found[0]
        ilc_ref[at + 1] = found[1]
        near = jnp.where(low_half, found[0], pltpu.roll(found[1], HALF, 1))
        far = jnp.where(low_half, pltpu.roll(found[0], HALF, 1), found[1])
        low_ref[chunk, part] = jnp.concatenate([near, far], axis=0).astype(jnp.bfloat16)
        if part == pieces - 1:
            add_spectra(chunk)
    for group in range(groups):
        span = slice(group * width, (group + 1) * width)
        sign = 1.0 - 2.0 * odd_ref[:, span]
        part, first = group * width // share_rows, group * width % share_rows
        result = found_ref[part, :, first : first + width]
        value = (result[0:cycles] + sign * result[cycles:]).astype(jnp.bfloat16)
        for share in range(shares):
            spectra_ref[group, share] = value


def run_ilc(modes, odd, basis):
    groups, shares, _, width = modes[0].shape
    rows = sum(each.shape[2] for each in modes)
    chunks, depth, columns = basis.shape
    pieces = CHUNK // 2
    basis = basis.reshape(chunks * pieces, depth // pieces, columns)
    cycles = rows // C
    vmem = pl.BlockSpec(memory_space=pltpu.VMEM)
    return pl.pallas_call(
        functools.partial(ilc_kernel, len(modes)),
        in_specs=[vmem] * (len(modes) + 1) + [pl.BlockSpec(memory_space=pl.ANY)],
        out_specs=[vmem, vmem],
        out_shape=[
            jax.ShapeDtypeStruct((HALO, cycles, LANES), jnp.float32),
            jax.ShapeDtypeStruct((groups, shares, cycles, width), jnp.bfloat16),
        ],
        scratch_shapes=[
            pltpu.VMEM(basis.shape, jnp.bfloat16),
            pltpu.VMEM((2 * round_up(rows, 16), depth), jnp.bfloat16),
            pltpu.VMEM((HALO, C + 1, cycles, LANES), jnp.float32),
            pltpu.VMEM((SUMS, cycles, LANES), jnp.float32),
            pltpu.VMEM((chunks, pieces, 2 * cycles, LANES), jnp.bfloat16),
            pltpu.VMEM((pieces, 2 * cycles, depth // pieces), jnp.float32),
            pltpu.SemaphoreType.DMA((chunks,)),
        ],
        cost_estimate=pl.CostEstimate(
            flops=2 * chunks * depth * columns * (2 * rows + 2 * cycles),
            bytes_accessed=chunks * depth * columns * 2,
            transcendentals=0,
        ),
        compiler_params=pltpu.CompilerParams(vmem_limit_bytes=VMEM_LIMIT),
    )(*modes, odd, basis)


def modes_kernel(alm_hbm, table_hbm, *refs):
    out_hbms, (alm_ref, table_ref, held_ref, turned_ref) = refs[:BUNDLES], refs[BUNDLES : BUNDLES + 4]
    out_refs, (alm_sem, sems, out_sems) = refs[BUNDLES + 4 : -3], refs[-3:]
    parts = sems.shape[0]
    total_slots, degrees, total = table_ref.shape
    each, slots = total_slots // parts, 4
    targets = out_refs[0].shape[0]
    cycles = total // targets
    height = 2 * C
    alm_copy = pltpu.make_async_copy(alm_hbm, alm_ref, alm_sem)
    alm_copy.start()
    start_parts(table_hbm, table_ref, sems, IN_FLIGHT)

    def some_slots(first):
        lhs = alm_ref[first : first + slots].reshape(slots * height, degrees)
        rhs = jnp.concatenate([table_ref[first + slot] for slot in range(slots)], axis=1)
        result = jnp.dot(lhs, rhs, preferred_element_type=jnp.float32)
        for slot in range(slots):
            own = result[slot * height : (slot + 1) * height, slot * total : (slot + 1) * total]
            for lanes in range(held_ref.shape[0]):
                span = slice((first + slot) * height, (first + slot + 1) * height)
                held_ref[lanes, span, :] = own[:, lanes * LANES : (lanes + 1) * LANES]

    def turn(half):
        count = total_slots // HALVES
        first = half * count * height
        for chan in range(C):
            for lanes in range(held_ref.shape[0]):
                both = [held_ref[lanes, pl.ds(first + 2 * chan + part, count, stride=height), :] for part in range(2)]
                span = slice(half * 2 * count, (half + 1) * 2 * count)
                turned_ref[chan, lanes * LANES : (lanes + 1) * LANES, span] = jnp.concatenate(both, axis=0).T

    alm_copy.wait()
    for part in range(parts):
        next_part(table_hbm, table_ref, sems, part, IN_FLIGHT)
        for first in range(part * each, (part + 1) * each, slots):
            some_slots(first)
        if (part + 1) * HALVES % parts == 0:
            turn((part + 1) * HALVES // parts - 1)
    for at, (out_ref, out_hbm) in enumerate(zip(out_refs, out_hbms)):
        for target in range(targets):
            span = slice(target * cycles, (target + 1) * cycles)
            block = jnp.concatenate([turned_ref[chan, span, :] for chan in bundle(at)], axis=0)
            out_ref[target] = block.astype(jnp.bfloat16)
        pltpu.make_async_copy(out_ref, out_hbm, out_sems.at[at]).start()
    for at, (out_ref, out_hbm) in enumerate(zip(out_refs, out_hbms)):
        pltpu.make_async_copy(out_ref, out_hbm, out_sems.at[at]).wait()


def bundle(at):
    return range(at * C // BUNDLES, (at + 1) * C // BUNDLES)


def make_modes(alm, legendre, targets):
    slot_count, degrees, total = legendre.shape
    parts = slot_count // 8
    width = 2 * slot_count
    height = 2 * C
    outs = [
        jax.ShapeDtypeStruct((targets, len(bundle(at)) * (total // targets), width), jnp.bfloat16)
        for at in range(BUNDLES)
    ]
    return pl.pallas_call(
        modes_kernel,
        in_specs=[pl.BlockSpec(memory_space=pl.ANY)] * 2,
        out_specs=[pl.BlockSpec(memory_space=pl.ANY)] * BUNDLES,
        out_shape=outs,
        scratch_shapes=[
            pltpu.VMEM(alm.shape, jnp.bfloat16),
            pltpu.VMEM(legendre.shape, jnp.bfloat16),
            pltpu.VMEM((total // LANES, slot_count * height, LANES), jnp.float32),
            pltpu.VMEM((C, total, width), jnp.float32),
            *[pltpu.VMEM(out.shape, out.dtype) for out in outs],
            pltpu.SemaphoreType.DMA,
            pltpu.SemaphoreType.DMA((parts,)),
            pltpu.SemaphoreType.DMA((BUNDLES,)),
        ],
        cost_estimate=pl.CostEstimate(
            flops=2 * slot_count * degrees * total * 2 * C,
            bytes_accessed=slot_count * degrees * (total + 2 * C) * 2,
            transcendentals=0,
        ),
        compiler_params=pltpu.CompilerParams(vmem_limit_bytes=62 * 1024 * 1024),
    )(alm, legendre)


def analysis_kernel(table_hbm, spectra_ref, out_ref, table_ref, turned_ref, sems):
    total_slots, degrees, total = table_ref.shape
    slots = 8
    start_parts(table_hbm, table_ref, sems, IN_FLIGHT)
    turned_ref[...] = spectra_ref[...].astype(jnp.float32).T
    count = total_slots // HALVES
    for first in range(0, total_slots, slots):
        row = first // count * 2 * count + first % count
        rows = [turned_ref[row + share * count : row + share * count + slots, :] for share in range(2)]
        lhs = jnp.concatenate(rows, axis=0).astype(jnp.bfloat16)
        next_part(table_hbm, table_ref, sems, first // slots, IN_FLIGHT)
        table = table_ref[first : first + slots].reshape(slots * degrees, total)
        result = lax.dot_general(lhs, table, (((1,), (1,)), ((), ())), preferred_element_type=jnp.float32)
        for slot in range(slots):
            span = slice(slot * degrees, (slot + 1) * degrees)
            out_ref[first + slot, 0:1, :] = result[slot : slot + 1, span]
            out_ref[first + slot, 1:2, :] = result[slots + slot : slots + slot + 1, span]


def analyse(legendre, spectra):
    slot_count, degrees, total = legendre.shape
    slots = 8
    width = 2 * slot_count
    vmem = pl.BlockSpec(memory_space=pltpu.VMEM)
    return pl.pallas_call(
        analysis_kernel,
        in_specs=[pl.BlockSpec(memory_space=pl.ANY), vmem],
        out_specs=vmem,
        out_shape=jax.ShapeDtypeStruct((slot_count, 2, degrees), jnp.float32),
        scratch_shapes=[
            pltpu.VMEM(legendre.shape, jnp.bfloat16),
            pltpu.VMEM((width, total), jnp.float32),
            pltpu.SemaphoreType.DMA((slot_count // slots,)),
        ],
        cost_estimate=pl.CostEstimate(
            flops=2 * slot_count * degrees * total * 2 * slots,
            bytes_accessed=slot_count * degrees * total * 2,
            transcendentals=0,
        ),
        compiler_params=pltpu.CompilerParams(vmem_limit_bytes=50 * 1024 * 1024),
    )(legendre, spectra)


def from_other_tiles(sends):
    count = len(sends)
    got = [sends[0]]
    for hop in range(1, count):
        got.append(lax.ppermute(sends[hop], "tile", [(at, (at + hop) % count) for at in range(count)]))
    return got


def in_tile_order(got):
    count = len(got)
    tile_at = lax.axis_index("tile")
    stacked = jnp.stack(got)
    return jnp.stack(
        [lax.dynamic_index_in_dim(stacked, (tile_at - at) % count, 0, keepdims=False) for at in range(count)]
    )


def body(alm, legendre, order_of_slot):
    tile_count = lax.axis_size("tile")
    band_count = lax.axis_size("band")
    tile_at = lax.axis_index("tile")
    slot_count = alm.shape[0]
    targets = band_count * tile_count
    cycles = legendre.shape[2] // targets
    padded = round_up(cycles, 8)
    depth = 2 * L
    width = 2 * slot_count
    group_width = math.lcm(width, LANES)
    groups = depth // group_width
    plain = group_width == width and padded == cycles
    axes = ("band", "tile")

    modes = [
        lax.all_to_all(each, axes, split_axis=0, concat_axis=0, tiled=True).reshape(band_count, tile_count, -1, width)
        for each in make_modes(alm, legendre, targets)
    ]
    if not plain:
        modes = jnp.sum(jnp.concatenate(modes, axis=2).astype(jnp.float32), axis=1).astype(jnp.bfloat16)
        modes = modes.reshape(groups, group_width // width, C, cycles, width)
        modes = modes.transpose(0, 2, 3, 1, 4).reshape(groups, C, cycles, group_width)
        modes = jnp.pad(modes, ((0, 0), (0, 0), (0, padded - cycles), (0, 0)))
        modes = [modes.reshape(groups, 1, C * padded, group_width)]

    order_rows = order_of_slot.reshape(band_count * HALVES, 1, slot_count // HALVES)
    order_rows = jnp.broadcast_to(order_rows, (band_count * HALVES, 2, slot_count // HALVES)).reshape(depth)
    basis = make_basis(order_rows.astype(jnp.float32)[:, None], slot_count)
    odd = (order_rows % 2).astype(jnp.float32)[None, :]
    vectors, spectra = run_ilc(modes, odd, basis)

    if not plain:
        spectra = spectra[:, 0, :cycles].reshape(groups, cycles, group_width // width, width)
        spectra = spectra.transpose(0, 2, 1, 3).reshape(band_count, 1, cycles, width)
        spectra = jnp.broadcast_to(spectra, (band_count, tile_count, cycles, width))
    spectra = spectra.reshape(targets, cycles, width)
    routed = lax.all_to_all(spectra, axes, split_axis=0, concat_axis=0, tiled=True)
    found = in_tile_order(from_other_tiles([vectors[:, :cycles]] * tile_count))
    lanes = LANES // tile_count
    found = lax.dynamic_slice_in_dim(found, tile_at * lanes, lanes, axis=3)
    ilc_map = found.transpose(0, 2, 3, 1).reshape(tile_count * cycles, NLON // tile_count)
    routed, ilc_map = lax.optimization_barrier((routed, ilc_map))
    ilc_alm = analyse(legendre, routed.reshape(targets * cycles, width))
    return (ilc_map, ilc_alm)


def solution(mesh):
    placed = (P("band", None, None, "tile"), P("band", "tile", None), P())
    return jax.shard_map(
        body,
        mesh=mesh,
        in_specs=placed,
        out_specs=(P("band", "tile"), P("band", None, "tile")),
        check_vma=False,
    )
```

```python
import functools
import math

import jax
import jax.numpy as jnp
from jax import lax
from jax.experimental import pallas as pl
from jax.experimental.pallas import tpu as pltpu
from jax.sharding import PartitionSpec as P

C = 9
L = 1024
NLON = 4096
HALO = 32

RIDGE = 0.1
EPSILON = 1e-06

WINDOW = 2 * HALO + 1
LANES = NLON // HALO
HALF = LANES // 2
REST = C - 1
PAIRS = [(a_at, b_at) for a_at in range(REST) for b_at in range(a_at, REST)] + [(a_at, REST) for a_at in range(REST)]
SUMS = len(PAIRS) + 1
VMEM_LIMIT = 48 * 1024 * 1024
IN_FLIGHT = 4
HALVES = 1
CHUNK = 8


def round_up(value, multiple):
    return (value + multiple - 1) // multiple * multiple


def cos_turns(turns):
    nearest = (turns + 12582912.0) - 12582912.0
    quarter = 1.0 - 4.0 * jnp.abs(turns - nearest)
    square = quarter * quarter
    tail = square * (1.6044118478736e-04 - square * 3.598843235e-06)
    tail = square * (-4.68175413531868e-03 + tail)
    tail = square * (7.96926262461670e-02 + tail)
    tail = square * (-6.45964097506246e-01 + tail)
    return quarter * (1.57079632679490 + tail)


def basis_kernel(slots, order_ref, basis_ref):
    rows = 64
    begin = pl.program_id(0) * order_ref.shape[0]
    row = lax.broadcasted_iota(jnp.int32, (rows, LANES), 0)
    lane = lax.broadcasted_iota(jnp.int32, (rows, LANES), 1)
    cell = (HALO * (lane % HALF) + lane // HALF).astype(jnp.float32) / NLON
    scaling = 1.0 / math.sqrt(L)
    for first in range(0, order_ref.shape[0], rows):
        span = slice(first, first + rows)
        part = (row + (begin + first)) // (slots // HALVES) % 2
        order = jnp.broadcast_to(order_ref[span, :], (rows, LANES))
        turns = order * cell + part.astype(jnp.float32) * 0.25
        step = order * (2.0 / NLON)
        before = cos_turns(turns) * scaling
        now = cos_turns(turns + step) * scaling
        twice = 2.0 * cos_turns(step)
        for column in range(HALO // 2):
            at = column % (CHUNK // 2) * LANES
            basis_ref[column // (CHUNK // 2), span, at : at + LANES] = before.astype(jnp.bfloat16)
            if column < HALO // 2 - 1:
                before, now = now, twice * now - before


def make_basis(order_rows, slots):
    rows = order_rows.shape[0]
    block = 256
    chunks = HALO // CHUNK
    columns = CHUNK // 2 * LANES
    return pl.pallas_call(
        functools.partial(basis_kernel, slots),
        grid=(rows // block,),
        in_specs=[pl.BlockSpec((block, 1), lambda at: (at, 0))],
        out_specs=pl.BlockSpec((chunks, block, columns), lambda at: (0, at, 0)),
        out_shape=jax.ShapeDtypeStruct((chunks, rows, columns), jnp.bfloat16),
        cost_estimate=pl.CostEstimate(
            flops=rows * chunks * columns * 8, bytes_accessed=rows * chunks * columns * 2, transcendentals=0
        ),
        compiler_params=pltpu.CompilerParams(vmem_limit_bytes=VMEM_LIMIT),
    )(order_rows)


def part_copy(source, target, sems, part):
    count = source.shape[0] // sems.shape[0]
    span = pl.ds(part * count, count)
    return pltpu.make_async_copy(source.at[span], target.at[span], sems.at[part])


def start_parts(source, target, sems, count):
    for part in range(min(count, sems.shape[0])):
        part_copy(source, target, sems, part).start()


def next_part(source, target, sems, part, ahead):
    part_copy(source, target, sems, part).wait()
    more = part + ahead < sems.shape[0]
    if isinstance(part, int):
        if more:
            part_copy(source, target, sems, part + ahead).start()
    else:

        @pl.when(more)
        def _():
            part_copy(source, target, sems, part + ahead).start()


def reciprocal(value):
    guess = pl.reciprocal(value, approx=True)
    return guess * (2.0 - value * guess)


def combine_steps(sum_of, map_of):
    ridge = RIDGE * (sum_of(SUMS - 1) * (1.0 / C) + WINDOW * EPSILON)
    upper, inverses, rights, maps = {}, [], [], []
    value = map_of(REST)
    for row in range(REST):
        ratios = [upper[at, row] * inverses[at] for at in range(row)]
        pivot = sum_of(PAIRS.index((row, row))) + (ridge + ridge)
        for at in range(row):
            pivot = pivot - ratios[at] * upper[at, row]
        inverse = reciprocal(pivot)
        yield None
        right = ridge - sum_of(PAIRS.index((row, REST)))
        own = map_of(row)
        for at in range(row):
            right = right - ratios[at] * rights[at]
            own = own - ratios[at] * maps[at]
        yield None
        for col in range(row + 1, REST):
            entry = sum_of(PAIRS.index((row, col))) + ridge
            for at in range(row):
                entry = entry - ratios[at] * upper[at, col]
            upper[row, col] = entry
            yield None
        value = value + (right * inverse) * own
        inverses.append(inverse)
        rights.append(right)
        maps.append(own)
    yield value


def in_step(generators):
    for found in zip(*generators):
        pass
    return found


def ilc_kernel(modes_ref, odd_ref, basis_hbm, ilc_ref, spectra_ref, basis_ref, lhs_ref, maps_ref, sums_ref, low_ref, found_ref, sems):
    groups, shares, rows, width = modes_ref.shape
    columns = basis_ref.shape[2]
    depth = lhs_ref.shape[1]
    pieces = depth // basis_ref.shape[1]
    chunks = basis_ref.shape[0] // pieces
    cycles = rows // C
    second = round_up(rows, 16)
    ahead = 3
    start_parts(basis_hbm, basis_ref, sems, ahead)
    for group in range(groups):
        span = slice(group * width, (group + 1) * width)
        odd = odd_ref[:, span]
        values = modes_ref[group, 0].astype(jnp.float32)
        for share in range(1, shares):
            values = values + modes_ref[group, share].astype(jnp.float32)
        lhs_ref[0:rows, span] = (values * (1.0 - odd)).astype(jnp.bfloat16)
        lhs_ref[second : second + rows, span] = (values * odd).astype(jnp.bfloat16)
    low_half = lax.broadcasted_iota(jnp.int32, (cycles, LANES), 1) < HALF
    sums_ref[...] = jnp.zeros_like(sums_ref)

    def store_maps(at, maps):
        squares = maps[0] * maps[0]
        for chan in range(1, C):
            squares = squares + maps[chan] * maps[chan]
            maps_ref[at, chan - 1] = maps[chan] - maps[0]
        maps_ref[at, REST] = maps[0]
        maps_ref[at, C] = squares

    def maps_of_chunk(chunk):
        next_part(basis_hbm, basis_ref, sems, chunk, ahead)
        basis = basis_ref[chunk * pieces : (chunk + 1) * pieces].reshape(depth, columns)
        result = jnp.dot(lhs_ref[...], basis, preferred_element_type=jnp.float32)
        for part in range(CHUNK // 2):
            at = CHUNK * chunk + 2 * part
            lanes = slice(part * LANES, (part + 1) * LANES)
            left, right = [], []
            for chan in range(C):
                even_part = result[chan * cycles : (chan + 1) * cycles, lanes]
                odd_part = result[second + chan * cycles : second + (chan + 1) * cycles, lanes]
                near = even_part + odd_part
                far = even_part - odd_part
                left.append(jnp.where(low_half, near, pltpu.roll(far, HALF, 1)))
                right.append(jnp.where(low_half, pltpu.roll(near, HALF, 1), far))
            store_maps(at, left)
            store_maps(at + 1, right)

    def add_totals(chunk):
        vectors = [CHUNK * chunk + part for part in range(CHUNK)]
        for a_at in range(C):
            own = [maps_ref[at, a_at] for at in vectors]
            for b_at in range(a_at, C):
                if (a_at, b_at) == (REST, REST):
                    continue
                pair = PAIRS.index((a_at, b_at))
                total = sums_ref[pair]
                for at, value in zip(vectors, own):
                    total = total + value * (value if a_at == b_at else maps_ref[at, b_at])
                sums_ref[pair] = total
        total = sums_ref[SUMS - 1]
        for at in vectors:
            total = total + maps_ref[at, C]
        sums_ref[SUMS - 1] = total

    maps_of_chunk(0)
    for chunk in range(1, chunks):
        maps_of_chunk(chunk)
        add_totals(chunk - 1)
    add_totals(chunks - 1)
    for pair in range(SUMS):
        total = sums_ref[pair]
        sums_ref[pair] = pltpu.roll(total, 1, 1) + pltpu.roll(total, 2, 1)

    def solve_steps(at):
        maps = [maps_ref[at, chan] for chan in range(C + 1)]

        def sum_of(pair):
            own = maps[C] if pair == SUMS - 1 else maps[PAIRS[pair][0]] * maps[PAIRS[pair][1]]
            total = sums_ref[pair] + own
            sums_ref[pair] = total - pltpu.roll(own, 2, 1)
            return total

        return combine_steps(sum_of, lambda chan: pltpu.roll(maps[chan], 1, 1))

    def add_spectra(chunk):
        lhs = jnp.concatenate([low_ref[chunk, part] for part in range(pieces)], axis=1)
        basis = basis_ref[chunk * pieces : (chunk + 1) * pieces].reshape(depth, columns)
        term = lax.dot_general(lhs, basis, (((1,), (1,)), ((), ())), preferred_element_type=jnp.float32)
        found_ref[...] = term if chunk == 0 else found_ref[...] + term

    for pair_at in range(HALO // 2):
        at = 2 * pair_at
        chunk, part = pair_at // pieces, pair_at % pieces
        found = in_step([solve_steps(at), solve_steps(at + 1)])
        found = [pltpu.roll(value, LANES - 1, 1) for value in found]
        ilc_ref[at] = found[0]
        ilc_ref[at + 1] = found[1]
        near = jnp.where(low_half, found[0], pltpu.roll(found[1], HALF, 1))
        far = jnp.where(low_half, pltpu.roll(found[0], HALF, 1), found[1])
        low_ref[chunk, part] = jnp.concatenate([near, far], axis=0).astype(jnp.bfloat16)
        if part == pieces - 1:
            add_spectra(chunk)
    for group in range(groups):
        span = slice(group * width, (group + 1) * width)
        sign = 1.0 - 2.0 * odd_ref[:, span]
        result = found_ref[:, span]
        value = (result[0:cycles] + sign * result[cycles:]).astype(jnp.bfloat16)
        for share in range(shares):
            spectra_ref[group, share] = value


def run_ilc(modes, odd, basis):
    groups, shares, rows, width = modes.shape
    chunks, depth, columns = basis.shape
    pieces = CHUNK // 2
    basis = basis.reshape(chunks * pieces, depth // pieces, columns)
    cycles = rows // C
    vmem = pl.BlockSpec(memory_space=pltpu.VMEM)
    return pl.pallas_call(
        ilc_kernel,
        in_specs=[vmem, vmem, pl.BlockSpec(memory_space=pl.ANY)],
        out_specs=[vmem, vmem],
        out_shape=[
            jax.ShapeDtypeStruct((HALO, cycles, LANES), jnp.float32),
            jax.ShapeDtypeStruct((groups, shares, cycles, width), jnp.bfloat16),
        ],
        scratch_shapes=[
            pltpu.VMEM(basis.shape, jnp.bfloat16),
            pltpu.VMEM((2 * round_up(rows, 16), depth), jnp.bfloat16),
            pltpu.VMEM((HALO, C + 1, cycles, LANES), jnp.float32),
            pltpu.VMEM((SUMS, cycles, LANES), jnp.float32),
            pltpu.VMEM((chunks, pieces, 2 * cycles, LANES), jnp.bfloat16),
            pltpu.VMEM((2 * cycles, depth), jnp.float32),
            pltpu.SemaphoreType.DMA((chunks,)),
        ],
        cost_estimate=pl.CostEstimate(
            flops=2 * chunks * depth * columns * (2 * rows + 2 * cycles),
            bytes_accessed=chunks * depth * columns * 2,
            transcendentals=0,
        ),
        compiler_params=pltpu.CompilerParams(vmem_limit_bytes=VMEM_LIMIT),
    )(modes, odd, basis)


def modes_kernel(alm_hbm, table_hbm, out_hbm, alm_ref, table_ref, held_ref, turned_ref, out_ref, alm_sem, sems, out_sems):
    parts = sems.shape[0]
    total_slots, degrees, total = table_ref.shape
    each, slots = total_slots // parts, 4
    targets, rows = out_ref.shape[:2]
    cycles = rows // C
    height = 2 * C
    alm_copy = pltpu.make_async_copy(alm_hbm, alm_ref, alm_sem)
    alm_copy.start()
    start_parts(table_hbm, table_ref, sems, IN_FLIGHT)

    def some_slots(first):
        lhs = alm_ref[first : first + slots].reshape(slots * height, degrees)
        rhs = jnp.concatenate([table_ref[first + slot] for slot in range(slots)], axis=1)
        result = jnp.dot(lhs, rhs, preferred_element_type=jnp.float32)
        for slot in range(slots):
            own = result[slot * height : (slot + 1) * height, slot * total : (slot + 1) * total]
            for lanes in range(held_ref.shape[0]):
                span = slice((first + slot) * height, (first + slot + 1) * height)
                held_ref[lanes, span, :] = own[:, lanes * LANES : (lanes + 1) * LANES]

    def rows_of(chan):
        both = [
            jnp.concatenate(
                [
                    held_ref[lanes, pl.ds(2 * chan + part, total_slots, stride=height), :].astype(jnp.bfloat16)
                    for lanes in range(held_ref.shape[0])
                ],
                axis=1,
            )
            for part in range(2)
        ]
        return jnp.concatenate(both, axis=0)

    alm_copy.wait()
    for part in range(parts):
        next_part(table_hbm, table_ref, sems, part, IN_FLIGHT)
        for first in range(part * each, (part + 1) * each, slots):
            some_slots(first)
    one = lax.broadcasted_iota(jnp.int32, (total, total), 0) == lax.broadcasted_iota(jnp.int32, (total, total), 1)
    one = one.astype(jnp.float32).astype(jnp.bfloat16)
    width = 2 * total_slots
    together = C if width % LANES == 0 else 1
    for chan in range(0, C, together):
        rows = jnp.concatenate([rows_of(chan + at) for at in range(together)], axis=0)
        turned = lax.dot_general(one, rows, (((1,), (1,)), ((), ())), preferred_element_type=jnp.float32)
        for at in range(together):
            turned_ref[chan + at] = turned[:, at * width : (at + 1) * width]
    each = targets // out_sems.shape[0]
    for target in range(targets):
        span = slice(target * cycles, (target + 1) * cycles)
        block = jnp.concatenate([turned_ref[chan, span, :] for chan in range(C)], axis=0)
        out_ref[target] = block.astype(jnp.bfloat16)
        if (target + 1) % each == 0:
            part_copy(out_ref, out_hbm, out_sems, target // each).start()
    for part in range(out_sems.shape[0]):
        part_copy(out_ref, out_hbm, out_sems, part).wait()


def make_modes(alm, legendre, targets):
    slot_count, degrees, total = legendre.shape
    parts = slot_count // 8
    width = 2 * slot_count
    height = 2 * C
    out = jax.ShapeDtypeStruct((targets, C * (total // targets), width), jnp.bfloat16)
    return pl.pallas_call(
        modes_kernel,
        in_specs=[pl.BlockSpec(memory_space=pl.ANY)] * 2,
        out_specs=pl.BlockSpec(memory_space=pl.ANY),
        out_shape=out,
        scratch_shapes=[
            pltpu.VMEM(alm.shape, jnp.bfloat16),
            pltpu.VMEM(legendre.shape, jnp.bfloat16),
            pltpu.VMEM((total // LANES, slot_count * height, LANES), jnp.float32),
            pltpu.VMEM((C, total, width), jnp.float32),
            pltpu.VMEM(out.shape, out.dtype),
            pltpu.SemaphoreType.DMA,
            pltpu.SemaphoreType.DMA((parts,)),
            pltpu.SemaphoreType.DMA((4,)),
        ],
        cost_estimate=pl.CostEstimate(
            flops=2 * slot_count * degrees * total * 2 * C,
            bytes_accessed=slot_count * degrees * (total + 2 * C) * 2,
            transcendentals=0,
        ),
        compiler_params=pltpu.CompilerParams(vmem_limit_bytes=62 * 1024 * 1024),
    )(alm, legendre)


def analysis_kernel(table_hbm, spectra_ref, out_ref, table_ref, turned_ref, sems):
    total_slots, degrees, total = table_ref.shape
    slots = 8
    start_parts(table_hbm, table_ref, sems, IN_FLIGHT)
    turned_ref[...] = spectra_ref[...].astype(jnp.float32).T
    count = total_slots // HALVES
    for first in range(0, total_slots, slots):
        row = first // count * 2 * count + first % count
        rows = [turned_ref[row + share * count : row + share * count + slots, :] for share in range(2)]
        lhs = jnp.concatenate(rows, axis=0).astype(jnp.bfloat16)
        next_part(table_hbm, table_ref, sems, first // slots, IN_FLIGHT)
        table = table_ref[first : first + slots].reshape(slots * degrees, total)
        result = lax.dot_general(lhs, table, (((1,), (1,)), ((), ())), preferred_element_type=jnp.float32)
        for slot in range(slots):
            span = slice(slot * degrees, (slot + 1) * degrees)
            out_ref[first + slot, 0:1, :] = result[slot : slot + 1, span]
            out_ref[first + slot, 1:2, :] = result[slots + slot : slots + slot + 1, span]


def analyse(legendre, spectra):
    slot_count, degrees, total = legendre.shape
    slots = 8
    width = 2 * slot_count
    vmem = pl.BlockSpec(memory_space=pltpu.VMEM)
    return pl.pallas_call(
        analysis_kernel,
        in_specs=[pl.BlockSpec(memory_space=pl.ANY), vmem],
        out_specs=vmem,
        out_shape=jax.ShapeDtypeStruct((slot_count, 2, degrees), jnp.float32),
        scratch_shapes=[
            pltpu.VMEM(legendre.shape, jnp.bfloat16),
            pltpu.VMEM((width, total), jnp.float32),
            pltpu.SemaphoreType.DMA((slot_count // slots,)),
        ],
        cost_estimate=pl.CostEstimate(
            flops=2 * slot_count * degrees * total * 2 * slots,
            bytes_accessed=slot_count * degrees * total * 2,
            transcendentals=0,
        ),
        compiler_params=pltpu.CompilerParams(vmem_limit_bytes=50 * 1024 * 1024),
    )(legendre, spectra)


def from_other_tiles(sends):
    count = len(sends)
    got = [sends[0]]
    for hop in range(1, count):
        got.append(lax.ppermute(sends[hop], "tile", [(at, (at + hop) % count) for at in range(count)]))
    return got


def in_tile_order(got):
    count = len(got)
    tile_at = lax.axis_index("tile")
    stacked = jnp.stack(got)
    return jnp.stack(
        [lax.dynamic_index_in_dim(stacked, (tile_at - at) % count, 0, keepdims=False) for at in range(count)]
    )


def body(alm, legendre, order_of_slot):
    tile_count = lax.axis_size("tile")
    band_count = lax.axis_size("band")
    tile_at = lax.axis_index("tile")
    slot_count = alm.shape[0]
    targets = band_count * tile_count
    cycles = legendre.shape[2] // targets
    padded = round_up(cycles, 8)
    depth = 2 * L
    width = 2 * slot_count
    group_width = math.lcm(width, LANES)
    groups = depth // group_width
    plain = group_width == width and padded == cycles
    axes = ("band", "tile")

    partial = make_modes(alm, legendre, targets)
    partial = lax.all_to_all(partial, axes, split_axis=0, concat_axis=0, tiled=True)
    modes = partial.reshape(band_count, tile_count, C * cycles, width)
    if not plain:
        modes = jnp.sum(modes.astype(jnp.float32), axis=1).astype(jnp.bfloat16)
        modes = modes.reshape(groups, group_width // width, C, cycles, width)
        modes = modes.transpose(0, 2, 3, 1, 4).reshape(groups, C, cycles, group_width)
        modes = jnp.pad(modes, ((0, 0), (0, 0), (0, padded - cycles), (0, 0)))
        modes = modes.reshape(groups, 1, C * padded, group_width)

    order_rows = order_of_slot.reshape(band_count * HALVES, 1, slot_count // HALVES)
    order_rows = jnp.broadcast_to(order_rows, (band_count * HALVES, 2, slot_count // HALVES)).reshape(depth)
    basis = make_basis(order_rows.astype(jnp.float32)[:, None], slot_count)
    odd = (order_rows % 2).astype(jnp.float32)[None, :]
    vectors, spectra = run_ilc(modes, odd, basis)

    if not plain:
        spectra = spectra[:, 0, :cycles].reshape(groups, cycles, group_width // width, width)
        spectra = spectra.transpose(0, 2, 1, 3).reshape(band_count, 1, cycles, width)
        spectra = jnp.broadcast_to(spectra, (band_count, tile_count, cycles, width))
    spectra = spectra.reshape(targets, cycles, width)
    routed = lax.all_to_all(spectra, axes, split_axis=0, concat_axis=0, tiled=True)
    found = in_tile_order(from_other_tiles([vectors[:, :cycles]] * tile_count))
    lanes = LANES // tile_count
    found = lax.dynamic_slice_in_dim(found, tile_at * lanes, lanes, axis=3)
    ilc_map = found.transpose(0, 2, 3, 1).reshape(tile_count * cycles, NLON // tile_count)
    routed, ilc_map = lax.optimization_barrier((routed, ilc_map))
    ilc_alm = analyse(legendre, routed.reshape(targets * cycles, width))
    return (ilc_map, ilc_alm)


def solution(mesh):
    placed = (P("band", None, None, "tile"), P("band", "tile", None), P())
    return jax.shard_map(
        body,
        mesh=mesh,
        in_specs=placed,
        out_specs=(P("band", "tile"), P("band", None, "tile")),
        check_vma=False,
    )
```

```python
import functools
import math

import jax
import jax.numpy as jnp
from jax import lax
from jax.experimental import pallas as pl
from jax.experimental.pallas import tpu as pltpu
from jax.sharding import PartitionSpec as P

C = 9
L = 1024
NLON = 4096
HALO = 32

RIDGE = 0.1
EPSILON = 1e-06

WINDOW = 2 * HALO + 1
LANES = NLON // HALO
HALF = LANES // 2
REST = C - 1
PAIRS = [(a_at, b_at) for a_at in range(REST) for b_at in range(a_at, REST)] + [(a_at, REST) for a_at in range(REST)]
SUMS = len(PAIRS) + 1
VMEM_LIMIT = 48 * 1024 * 1024
IN_FLIGHT = 2
HALVES = 1
CHUNK = 8


def round_up(value, multiple):
    return (value + multiple - 1) // multiple * multiple


def cos_turns(turns):
    nearest = (turns + 12582912.0) - 12582912.0
    quarter = 1.0 - 4.0 * jnp.abs(turns - nearest)
    square = quarter * quarter
    tail = square * (1.6044118478736e-04 - square * 3.598843235e-06)
    tail = square * (-4.68175413531868e-03 + tail)
    tail = square * (7.96926262461670e-02 + tail)
    tail = square * (-6.45964097506246e-01 + tail)
    return quarter * (1.57079632679490 + tail)


def basis_kernel(slots, order_ref, basis_ref):
    rows = 64
    begin = pl.program_id(0) * order_ref.shape[0]
    row = lax.broadcasted_iota(jnp.int32, (rows, LANES), 0)
    lane = lax.broadcasted_iota(jnp.int32, (rows, LANES), 1)
    cell = (HALO * (lane % HALF) + lane // HALF).astype(jnp.float32) / NLON
    scaling = 1.0 / math.sqrt(L)
    for first in range(0, order_ref.shape[0], rows):
        span = slice(first, first + rows)
        part = (row + (begin + first)) // (slots // HALVES) % 2
        order = jnp.broadcast_to(order_ref[span, :], (rows, LANES))
        turns = order * cell + part.astype(jnp.float32) * 0.25
        step = order * (2.0 / NLON)
        before = cos_turns(turns) * scaling
        now = cos_turns(turns + step) * scaling
        twice = 2.0 * cos_turns(step)
        for column in range(HALO // 2):
            at = column % (CHUNK // 2) * LANES
            basis_ref[column // (CHUNK // 2), span, at : at + LANES] = before.astype(jnp.bfloat16)
            if column < HALO // 2 - 1:
                before, now = now, twice * now - before


def make_basis(order_rows, slots):
    rows = order_rows.shape[0]
    block = 256
    chunks = HALO // CHUNK
    columns = CHUNK // 2 * LANES
    return pl.pallas_call(
        functools.partial(basis_kernel, slots),
        grid=(rows // block,),
        in_specs=[pl.BlockSpec((block, 1), lambda at: (at, 0))],
        out_specs=pl.BlockSpec((chunks, block, columns), lambda at: (0, at, 0)),
        out_shape=jax.ShapeDtypeStruct((chunks, rows, columns), jnp.bfloat16),
        cost_estimate=pl.CostEstimate(
            flops=rows * chunks * columns * 8, bytes_accessed=rows * chunks * columns * 2, transcendentals=0
        ),
        compiler_params=pltpu.CompilerParams(vmem_limit_bytes=VMEM_LIMIT),
    )(order_rows)


def part_copy(source, target, sems, part):
    count = source.shape[0] // sems.shape[0]
    span = pl.ds(part * count, count)
    return pltpu.make_async_copy(source.at[span], target.at[span], sems.at[part])


def start_parts(source, target, sems, count):
    for part in range(min(count, sems.shape[0])):
        part_copy(source, target, sems, part).start()


def next_part(source, target, sems, part, ahead):
    part_copy(source, target, sems, part).wait()
    more = part + ahead < sems.shape[0]
    if isinstance(part, int):
        if more:
            part_copy(source, target, sems, part + ahead).start()
    else:

        @pl.when(more)
        def _():
            part_copy(source, target, sems, part + ahead).start()


def reciprocal(value):
    guess = pl.reciprocal(value, approx=True)
    return guess * (2.0 - value * guess)


def combine_steps(sum_of, map_of):
    ridge = RIDGE * (sum_of(SUMS - 1) * (1.0 / C) + WINDOW * EPSILON)
    upper, inverses, rights, maps = {}, [], [], []
    value = map_of(REST)
    for row in range(REST):
        ratios = [upper[at, row] * inverses[at] for at in range(row)]
        pivot = sum_of(PAIRS.index((row, row))) + (ridge + ridge)
        for at in range(row):
            pivot = pivot - ratios[at] * upper[at, row]
        inverse = reciprocal(pivot)
        yield None
        right = ridge - sum_of(PAIRS.index((row, REST)))
        own = map_of(row)
        for at in range(row):
            right = right - ratios[at] * rights[at]
            own = own - ratios[at] * maps[at]
        yield None
        for col in range(row + 1, REST):
            entry = sum_of(PAIRS.index((row, col))) + ridge
            for at in range(row):
                entry = entry - ratios[at] * upper[at, col]
            upper[row, col] = entry
            yield None
        value = value + (right * inverse) * own
        inverses.append(inverse)
        rights.append(right)
        maps.append(own)
    yield value


def in_step(generators):
    for found in zip(*generators):
        pass
    return found


def ilc_kernel(modes_ref, odd_ref, basis_hbm, ilc_ref, spectra_ref, basis_ref, lhs_ref, maps_ref, sums_ref, low_ref, found_ref, sems):
    groups, shares, rows, width = modes_ref.shape
    columns = basis_ref.shape[2]
    depth = lhs_ref.shape[1]
    pieces, share_rows = found_ref.shape[0], found_ref.shape[2]
    chunks = basis_ref.shape[0] // pieces
    cycles = rows // C
    second = round_up(rows, 16)
    start_parts(basis_hbm, basis_ref, sems, IN_FLIGHT)
    for group in range(groups):
        span = slice(group * width, (group + 1) * width)
        odd = odd_ref[:, span]
        values = modes_ref[group, 0].astype(jnp.float32)
        for share in range(1, shares):
            values = values + modes_ref[group, share].astype(jnp.float32)
        lhs_ref[0:rows, span] = (values * (1.0 - odd)).astype(jnp.bfloat16)
        lhs_ref[second : second + rows, span] = (values * odd).astype(jnp.bfloat16)
    low_half = lax.broadcasted_iota(jnp.int32, (cycles, LANES), 1) < HALF
    sums_ref[...] = jnp.zeros_like(sums_ref)

    def store_maps(at, maps):
        squares = maps[0] * maps[0]
        for chan in range(1, C):
            squares = squares + maps[chan] * maps[chan]
            maps_ref[at, chan - 1] = maps[chan] - maps[0]
        maps_ref[at, REST] = maps[0]
        maps_ref[at, C] = squares

    def maps_of_chunk(chunk):
        next_part(basis_hbm, basis_ref, sems, chunk, IN_FLIGHT)
        basis = basis_ref[chunk * pieces : (chunk + 1) * pieces].reshape(depth, columns)
        result = jnp.dot(lhs_ref[...], basis, preferred_element_type=jnp.float32)
        for part in range(CHUNK // 2):
            at = CHUNK * chunk + 2 * part
            lanes = slice(part * LANES, (part + 1) * LANES)
            left, right = [], []
            for chan in range(C):
                even_part = result[chan * cycles : (chan + 1) * cycles, lanes]
                odd_part = result[second + chan * cycles : second + (chan + 1) * cycles, lanes]
                near = even_part + odd_part
                far = even_part - odd_part
                left.append(jnp.where(low_half, near, pltpu.roll(far, HALF, 1)))
                right.append(jnp.where(low_half, pltpu.roll(near, HALF, 1), far))
            store_maps(at, left)
            store_maps(at + 1, right)

    def add_totals(chunk):
        vectors = [CHUNK * chunk + part for part in range(CHUNK)]
        for a_at in range(C):
            own = [maps_ref[at, a_at] for at in vectors]
            for b_at in range(a_at, C):
                if (a_at, b_at) == (REST, REST):
                    continue
                pair = PAIRS.index((a_at, b_at))
                total = sums_ref[pair]
                for at, value in zip(vectors, own):
                    total = total + value * (value if a_at == b_at else maps_ref[at, b_at])
                sums_ref[pair] = total
        total = sums_ref[SUMS - 1]
        for at in vectors:
            total = total + maps_ref[at, C]
        sums_ref[SUMS - 1] = total

    maps_of_chunk(0)
    for chunk in range(1, chunks):
        maps_of_chunk(chunk)
        add_totals(chunk - 1)
    add_totals(chunks - 1)
    for pair in range(SUMS):
        total = sums_ref[pair]
        sums_ref[pair] = pltpu.roll(total, 1, 1) + pltpu.roll(total, 2, 1)

    def solve_steps(at):
        maps = [maps_ref[at, chan] for chan in range(C + 1)]

        def sum_of(pair):
            own = maps[C] if pair == SUMS - 1 else maps[PAIRS[pair][0]] * maps[PAIRS[pair][1]]
            total = sums_ref[pair] + own
            sums_ref[pair] = total - pltpu.roll(own, 2, 1)
            return total

        return combine_steps(sum_of, lambda chan: pltpu.roll(maps[chan], 1, 1))

    def add_spectra(chunk):
        lhs = jnp.concatenate([low_ref[chunk, part] for part in range(pieces)], axis=1)
        for part in range(pieces):
            term = lax.dot_general(
                lhs, basis_ref[chunk * pieces + part], (((1,), (1,)), ((), ())), preferred_element_type=jnp.float32
            )
            found_ref[part] = term if chunk == 0 else found_ref[part] + term

    for pair_at in range(HALO // 2):
        at = 2 * pair_at
        chunk, part = pair_at // pieces, pair_at % pieces
        found = in_step([solve_steps(at), solve_steps(at + 1)])
        found = [pltpu.roll(value, LANES - 1, 1) for value in found]
        ilc_ref[at] = found[0]
        ilc_ref[at + 1] = found[1]
        near = jnp.where(low_half, found[0], pltpu.roll(found[1], HALF, 1))
        far = jnp.where(low_half, pltpu.roll(found[0], HALF, 1), found[1])
        low_ref[chunk, part] = jnp.concatenate([near, far], axis=0).astype(jnp.bfloat16)
        if part == pieces - 1:
            add_spectra(chunk)
    for group in range(groups):
        span = slice(group * width, (group + 1) * width)
        sign = 1.0 - 2.0 * odd_ref[:, span]
        part, first = group * width // share_rows, group * width % share_rows
        result = found_ref[part, :, first : first + width]
        value = (result[0:cycles] + sign * result[cycles:]).astype(jnp.bfloat16)
        for share in range(shares):
            spectra_ref[group, share] = value


def run_ilc(modes, odd, basis):
    groups, shares, rows, width = modes.shape
    chunks, depth, columns = basis.shape
    pieces = CHUNK // 2
    basis = basis.reshape(chunks * pieces, depth // pieces, columns)
    cycles = rows // C
    vmem = pl.BlockSpec(memory_space=pltpu.VMEM)
    return pl.pallas_call(
        ilc_kernel,
        in_specs=[vmem, vmem, pl.BlockSpec(memory_space=pl.ANY)],
        out_specs=[vmem, vmem],
        out_shape=[
            jax.ShapeDtypeStruct((HALO, cycles, LANES), jnp.float32),
            jax.ShapeDtypeStruct((groups, shares, cycles, width), jnp.bfloat16),
        ],
        scratch_shapes=[
            pltpu.VMEM(basis.shape, jnp.bfloat16),
            pltpu.VMEM((2 * round_up(rows, 16), depth), jnp.bfloat16),
            pltpu.VMEM((HALO, C + 1, cycles, LANES), jnp.float32),
            pltpu.VMEM((SUMS, cycles, LANES), jnp.float32),
            pltpu.VMEM((chunks, pieces, 2 * cycles, LANES), jnp.bfloat16),
            pltpu.VMEM((pieces, 2 * cycles, depth // pieces), jnp.float32),
            pltpu.SemaphoreType.DMA((chunks,)),
        ],
        cost_estimate=pl.CostEstimate(
            flops=2 * chunks * depth * columns * (2 * rows + 2 * cycles),
            bytes_accessed=chunks * depth * columns * 2,
            transcendentals=0,
        ),
        compiler_params=pltpu.CompilerParams(vmem_limit_bytes=VMEM_LIMIT),
    )(modes, odd, basis)


def modes_kernel(alm_hbm, table_hbm, out_hbm, alm_ref, table_ref, held_ref, out_ref, alm_sem, sems, out_sems):
    parts = sems.shape[0]
    total_slots, degrees, total = table_ref.shape
    each, slots = total_slots // parts, 4
    targets, rows = out_ref.shape[:2]
    cycles = rows // C
    height = 2 * C
    alm_copy = pltpu.make_async_copy(alm_hbm, alm_ref, alm_sem)
    alm_copy.start()
    start_parts(table_hbm, table_ref, sems, IN_FLIGHT)

    def some_slots(first):
        lhs = alm_ref[first : first + slots].reshape(slots * height, degrees)
        rhs = jnp.concatenate([table_ref[first + slot] for slot in range(slots)], axis=1)
        result = jnp.dot(lhs, rhs, preferred_element_type=jnp.float32)
        for slot in range(slots):
            own = result[slot * height : (slot + 1) * height, slot * total : (slot + 1) * total]
            for lanes in range(held_ref.shape[0]):
                span = slice((first + slot) * height, (first + slot + 1) * height)
                held_ref[lanes, span, :] = own[:, lanes * LANES : (lanes + 1) * LANES]

    def rows_of(chan):
        both = [
            jnp.concatenate(
                [
                    held_ref[lanes, pl.ds(2 * chan + part, total_slots, stride=height), :].astype(jnp.bfloat16)
                    for lanes in range(held_ref.shape[0])
                ],
                axis=1,
            )
            for part in range(2)
        ]
        return jnp.concatenate(both, axis=0)

    alm_copy.wait()
    for part in range(parts):
        next_part(table_hbm, table_ref, sems, part, IN_FLIGHT)
        for first in range(part * each, (part + 1) * each, slots):
            some_slots(first)
    one = lax.broadcasted_iota(jnp.int32, (total, total), 0) == lax.broadcasted_iota(jnp.int32, (total, total), 1)
    one = one.astype(jnp.float32).astype(jnp.bfloat16)
    width = 2 * total_slots
    together = C if width % LANES == 0 else 1
    turned = []
    for chan in range(0, C, together):
        rows = jnp.concatenate([rows_of(chan + at) for at in range(together)], axis=0)
        both = lax.dot_general(one, rows, (((1,), (1,)), ((), ())), preferred_element_type=jnp.float32)
        turned += [both[:, at * width : (at + 1) * width] for at in range(together)]
    each = targets // out_sems.shape[0]
    for target in range(targets):
        span = slice(target * cycles, (target + 1) * cycles)
        block = jnp.concatenate([turned[chan][span] for chan in range(C)], axis=0)
        out_ref[target] = block.astype(jnp.bfloat16)
        if (target + 1) % each == 0:
            part_copy(out_ref, out_hbm, out_sems, target // each).start()
    for part in range(out_sems.shape[0]):
        part_copy(out_ref, out_hbm, out_sems, part).wait()


def make_modes(alm, legendre, targets):
    slot_count, degrees, total = legendre.shape
    parts = slot_count // 8
    width = 2 * slot_count
    height = 2 * C
    out = jax.ShapeDtypeStruct((targets, C * (total // targets), width), jnp.bfloat16)
    return pl.pallas_call(
        modes_kernel,
        in_specs=[pl.BlockSpec(memory_space=pl.ANY)] * 2,
        out_specs=pl.BlockSpec(memory_space=pl.ANY),
        out_shape=out,
        scratch_shapes=[
            pltpu.VMEM(alm.shape, jnp.bfloat16),
            pltpu.VMEM(legendre.shape, jnp.bfloat16),
            pltpu.VMEM((total // LANES, slot_count * height, LANES), jnp.float32),
            pltpu.VMEM(out.shape, out.dtype),
            pltpu.SemaphoreType.DMA,
            pltpu.SemaphoreType.DMA((parts,)),
            pltpu.SemaphoreType.DMA((4,)),
        ],
        cost_estimate=pl.CostEstimate(
            flops=2 * slot_count * degrees * total * 2 * C,
            bytes_accessed=slot_count * degrees * (total + 2 * C) * 2,
            transcendentals=0,
        ),
        compiler_params=pltpu.CompilerParams(vmem_limit_bytes=62 * 1024 * 1024),
    )(alm, legendre)


def analysis_kernel(table_hbm, spectra_ref, out_ref, table_ref, turned_ref, sems):
    total_slots, degrees, total = table_ref.shape
    slots = 8
    start_parts(table_hbm, table_ref, sems, IN_FLIGHT)
    turned_ref[...] = spectra_ref[...].astype(jnp.float32).T
    count = total_slots // HALVES
    for first in range(0, total_slots, slots):
        row = first // count * 2 * count + first % count
        rows = [turned_ref[row + share * count : row + share * count + slots, :] for share in range(2)]
        lhs = jnp.concatenate(rows, axis=0).astype(jnp.bfloat16)
        next_part(table_hbm, table_ref, sems, first // slots, IN_FLIGHT)
        table = table_ref[first : first + slots].reshape(slots * degrees, total)
        result = lax.dot_general(lhs, table, (((1,), (1,)), ((), ())), preferred_element_type=jnp.float32)
        for slot in range(slots):
            span = slice(slot * degrees, (slot + 1) * degrees)
            out_ref[first + slot, 0:1, :] = result[slot : slot + 1, span]
            out_ref[first + slot, 1:2, :] = result[slots + slot : slots + slot + 1, span]


def analyse(legendre, spectra):
    slot_count, degrees, total = legendre.shape
    slots = 8
    width = 2 * slot_count
    vmem = pl.BlockSpec(memory_space=pltpu.VMEM)
    return pl.pallas_call(
        analysis_kernel,
        in_specs=[pl.BlockSpec(memory_space=pl.ANY), vmem],
        out_specs=vmem,
        out_shape=jax.ShapeDtypeStruct((slot_count, 2, degrees), jnp.float32),
        scratch_shapes=[
            pltpu.VMEM(legendre.shape, jnp.bfloat16),
            pltpu.VMEM((width, total), jnp.float32),
            pltpu.SemaphoreType.DMA((slot_count // slots,)),
        ],
        cost_estimate=pl.CostEstimate(
            flops=2 * slot_count * degrees * total * 2 * slots,
            bytes_accessed=slot_count * degrees * total * 2,
            transcendentals=0,
        ),
        compiler_params=pltpu.CompilerParams(vmem_limit_bytes=50 * 1024 * 1024),
    )(legendre, spectra)


def from_other_tiles(sends):
    count = len(sends)
    got = [sends[0]]
    for hop in range(1, count):
        got.append(lax.ppermute(sends[hop], "tile", [(at, (at + hop) % count) for at in range(count)]))
    return got


def in_tile_order(got):
    count = len(got)
    tile_at = lax.axis_index("tile")
    stacked = jnp.stack(got)
    return jnp.stack(
        [lax.dynamic_index_in_dim(stacked, (tile_at - at) % count, 0, keepdims=False) for at in range(count)]
    )


def body(alm, legendre, order_of_slot):
    tile_count = lax.axis_size("tile")
    band_count = lax.axis_size("band")
    tile_at = lax.axis_index("tile")
    slot_count = alm.shape[0]
    targets = band_count * tile_count
    cycles = legendre.shape[2] // targets
    padded = round_up(cycles, 8)
    depth = 2 * L
    width = 2 * slot_count
    group_width = math.lcm(width, LANES)
    groups = depth // group_width
    plain = group_width == width and padded == cycles
    axes = ("band", "tile")

    partial = make_modes(alm, legendre, targets)
    partial = lax.all_to_all(partial, axes, split_axis=0, concat_axis=0, tiled=True)
    modes = partial.reshape(band_count, tile_count, C * cycles, width)
    if not plain:
        modes = jnp.sum(modes.astype(jnp.float32), axis=1).astype(jnp.bfloat16)
        modes = modes.reshape(groups, group_width // width, C, cycles, width)
        modes = modes.transpose(0, 2, 3, 1, 4).reshape(groups, C, cycles, group_width)
        modes = jnp.pad(modes, ((0, 0), (0, 0), (0, padded - cycles), (0, 0)))
        modes = modes.reshape(groups, 1, C * padded, group_width)

    order_rows = order_of_slot.reshape(band_count * HALVES, 1, slot_count // HALVES)
    order_rows = jnp.broadcast_to(order_rows, (band_count * HALVES, 2, slot_count // HALVES)).reshape(depth)
    basis = make_basis(order_rows.astype(jnp.float32)[:, None], slot_count)
    odd = (order_rows % 2).astype(jnp.float32)[None, :]
    vectors, spectra = run_ilc(modes, odd, basis)

    if not plain:
        spectra = spectra[:, 0, :cycles].reshape(groups, cycles, group_width // width, width)
        spectra = spectra.transpose(0, 2, 1, 3).reshape(band_count, 1, cycles, width)
        spectra = jnp.broadcast_to(spectra, (band_count, tile_count, cycles, width))
    spectra = spectra.reshape(targets, cycles, width)
    routed = lax.all_to_all(spectra, axes, split_axis=0, concat_axis=0, tiled=True)
    found = in_tile_order(from_other_tiles([vectors[:, :cycles]] * tile_count))
    lanes = LANES // tile_count
    found = lax.dynamic_slice_in_dim(found, tile_at * lanes, lanes, axis=3)
    ilc_map = found.transpose(0, 2, 3, 1).reshape(tile_count * cycles, NLON // tile_count)
    routed, ilc_map = lax.optimization_barrier((routed, ilc_map))
    ilc_alm = analyse(legendre, routed.reshape(targets * cycles, width))
    return (ilc_map, ilc_alm)


def solution(mesh):
    placed = (P("band", None, None, "tile"), P("band", "tile", None), P())
    return jax.shard_map(
        body,
        mesh=mesh,
        in_specs=placed,
        out_specs=(P("band", "tile"), P("band", None, "tile")),
        check_vma=False,
    )
```

```python
import functools
import math

import jax
import jax.numpy as jnp
from jax import lax
from jax.experimental import pallas as pl
from jax.experimental.pallas import tpu as pltpu
from jax.sharding import PartitionSpec as P

C = 9
L = 1024
NLON = 4096
HALO = 32

RIDGE = 0.1
EPSILON = 1e-06

WINDOW = 2 * HALO + 1
LANES = NLON // HALO
HALF = LANES // 2
REST = C - 1
PAIRS = [(a_at, b_at) for a_at in range(REST) for b_at in range(a_at, REST)] + [(a_at, REST) for a_at in range(REST)]
SUMS = len(PAIRS) + 1
VMEM_LIMIT = 48 * 1024 * 1024
IN_FLIGHT = 6
HALVES = 1
CHUNK = 8


def round_up(value, multiple):
    return (value + multiple - 1) // multiple * multiple


def cos_turns(turns):
    nearest = (turns + 12582912.0) - 12582912.0
    quarter = 1.0 - 4.0 * jnp.abs(turns - nearest)
    square = quarter * quarter
    tail = square * (1.6044118478736e-04 - square * 3.598843235e-06)
    tail = square * (-4.68175413531868e-03 + tail)
    tail = square * (7.96926262461670e-02 + tail)
    tail = square * (-6.45964097506246e-01 + tail)
    return quarter * (1.57079632679490 + tail)


def basis_kernel(slots, order_ref, basis_ref):
    rows = 64
    begin = pl.program_id(0) * order_ref.shape[0]
    row = lax.broadcasted_iota(jnp.int32, (rows, LANES), 0)
    lane = lax.broadcasted_iota(jnp.int32, (rows, LANES), 1)
    cell = (HALO * (lane % HALF) + lane // HALF).astype(jnp.float32) / NLON
    scaling = 1.0 / math.sqrt(L)
    for first in range(0, order_ref.shape[0], rows):
        span = slice(first, first + rows)
        part = (row + (begin + first)) // (slots // HALVES) % 2
        order = jnp.broadcast_to(order_ref[span, :], (rows, LANES))
        turns = order * cell + part.astype(jnp.float32) * 0.25
        step = order * (2.0 / NLON)
        before = cos_turns(turns) * scaling
        now = cos_turns(turns + step) * scaling
        twice = 2.0 * cos_turns(step)
        for column in range(HALO // 2):
            at = column % (CHUNK // 2) * LANES
            basis_ref[column // (CHUNK // 2), span, at : at + LANES] = before.astype(jnp.bfloat16)
            if column < HALO // 2 - 1:
                before, now = now, twice * now - before


def make_basis(order_rows, slots):
    rows = order_rows.shape[0]
    block = 256
    chunks = HALO // CHUNK
    columns = CHUNK // 2 * LANES
    return pl.pallas_call(
        functools.partial(basis_kernel, slots),
        grid=(rows // block,),
        in_specs=[pl.BlockSpec((block, 1), lambda at: (at, 0))],
        out_specs=pl.BlockSpec((chunks, block, columns), lambda at: (0, at, 0)),
        out_shape=jax.ShapeDtypeStruct((chunks, rows, columns), jnp.bfloat16),
        cost_estimate=pl.CostEstimate(
            flops=rows * chunks * columns * 8, bytes_accessed=rows * chunks * columns * 2, transcendentals=0
        ),
        compiler_params=pltpu.CompilerParams(vmem_limit_bytes=VMEM_LIMIT),
    )(order_rows)


def part_copy(source, target, sems, part):
    count = source.shape[0] // sems.shape[0]
    span = pl.ds(part * count, count)
    return pltpu.make_async_copy(source.at[span], target.at[span], sems.at[part])


def start_parts(source, target, sems, count):
    for part in range(min(count, sems.shape[0])):
        part_copy(source, target, sems, part).start()


def next_part(source, target, sems, part, ahead):
    part_copy(source, target, sems, part).wait()
    more = part + ahead < sems.shape[0]
    if isinstance(part, int):
        if more:
            part_copy(source, target, sems, part + ahead).start()
    else:

        @pl.when(more)
        def _():
            part_copy(source, target, sems, part + ahead).start()


def reciprocal(value):
    guess = pl.reciprocal(value, approx=True)
    return guess * (2.0 - value * guess)


def combine_steps(sum_of, map_of):
    ridge = RIDGE * (sum_of(SUMS - 1) * (1.0 / C) + WINDOW * EPSILON)
    upper, inverses, rights, maps = {}, [], [], []
    value = map_of(REST)
    for row in range(REST):
        ratios = [upper[at, row] * inverses[at] for at in range(row)]
        pivot = sum_of(PAIRS.index((row, row))) + (ridge + ridge)
        for at in range(row):
            pivot = pivot - ratios[at] * upper[at, row]
        inverse = reciprocal(pivot)
        yield None
        right = ridge - sum_of(PAIRS.index((row, REST)))
        own = map_of(row)
        for at in range(row):
            right = right - ratios[at] * rights[at]
            own = own - ratios[at] * maps[at]
        yield None
        for col in range(row + 1, REST):
            entry = sum_of(PAIRS.index((row, col))) + ridge
            for at in range(row):
                entry = entry - ratios[at] * upper[at, col]
            upper[row, col] = entry
            yield None
        value = value + (right * inverse) * own
        inverses.append(inverse)
        rights.append(right)
        maps.append(own)
    yield value


def in_step(generators):
    for found in zip(*generators):
        pass
    return found


def ilc_kernel(modes_ref, odd_ref, basis_hbm, ilc_ref, spectra_ref, basis_ref, lhs_ref, maps_ref, sums_ref, low_ref, found_ref, sems):
    groups, shares, rows, width = modes_ref.shape
    columns = basis_ref.shape[2]
    depth = lhs_ref.shape[1]
    pieces, share_rows = found_ref.shape[0], found_ref.shape[2]
    chunks = basis_ref.shape[0] // pieces
    cycles = rows // C
    second = round_up(rows, 16)
    start_parts(basis_hbm, basis_ref, sems, IN_FLIGHT)
    for group in range(groups):
        span = slice(group * width, (group + 1) * width)
        odd = odd_ref[:, span]
        values = modes_ref[group, 0].astype(jnp.float32)
        for share in range(1, shares):
            values = values + modes_ref[group, share].astype(jnp.float32)
        lhs_ref[0:rows, span] = (values * (1.0 - odd)).astype(jnp.bfloat16)
        lhs_ref[second : second + rows, span] = (values * odd).astype(jnp.bfloat16)
    low_half = lax.broadcasted_iota(jnp.int32, (cycles, LANES), 1) < HALF
    sums_ref[...] = jnp.zeros_like(sums_ref)

    def store_maps(at, maps):
        squares = maps[0] * maps[0]
        for chan in range(1, C):
            squares = squares + maps[chan] * maps[chan]
            maps_ref[at, chan - 1] = maps[chan] - maps[0]
        maps_ref[at, REST] = maps[0]
        maps_ref[at, C] = squares

    def maps_of_chunk(chunk):
        next_part(basis_hbm, basis_ref, sems, chunk, IN_FLIGHT)
        basis = basis_ref[chunk * pieces : (chunk + 1) * pieces].reshape(depth, columns)
        result = jnp.dot(lhs_ref[...], basis, preferred_element_type=jnp.float32)
        for part in range(CHUNK // 2):
            at = CHUNK * chunk + 2 * part
            lanes = slice(part * LANES, (part + 1) * LANES)
            left, right = [], []
            for chan in range(C):
                even_part = result[chan * cycles : (chan + 1) * cycles, lanes]
                odd_part = result[second + chan * cycles : second + (chan + 1) * cycles, lanes]
                near = even_part + odd_part
                far = even_part - odd_part
                left.append(jnp.where(low_half, near, pltpu.roll(far, HALF, 1)))
                right.append(jnp.where(low_half, pltpu.roll(near, HALF, 1), far))
            store_maps(at, left)
            store_maps(at + 1, right)

    def add_totals(chunk):
        vectors = [CHUNK * chunk + part for part in range(CHUNK)]
        for a_at in range(C):
            own = [maps_ref[at, a_at] for at in vectors]
            for b_at in range(a_at, C):
                if (a_at, b_at) == (REST, REST):
                    continue
                pair = PAIRS.index((a_at, b_at))
                total = sums_ref[pair]
                for at, value in zip(vectors, own):
                    total = total + value * (value if a_at == b_at else maps_ref[at, b_at])
                sums_ref[pair] = total
        total = sums_ref[SUMS - 1]
        for at in vectors:
            total = total + maps_ref[at, C]
        sums_ref[SUMS - 1] = total

    maps_of_chunk(0)
    for chunk in range(1, chunks):
        maps_of_chunk(chunk)
        add_totals(chunk - 1)
    add_totals(chunks - 1)
    for pair in range(SUMS):
        total = sums_ref[pair]
        sums_ref[pair] = pltpu.roll(total, 1, 1) + pltpu.roll(total, 2, 1)

    def solve_steps(at):
        maps = [maps_ref[at, chan] for chan in range(C + 1)]

        def sum_of(pair):
            own = maps[C] if pair == SUMS - 1 else maps[PAIRS[pair][0]] * maps[PAIRS[pair][1]]
            total = sums_ref[pair] + own
            sums_ref[pair] = total - pltpu.roll(own, 2, 1)
            return total

        return combine_steps(sum_of, lambda chan: pltpu.roll(maps[chan], 1, 1))

    def add_spectra(chunk):
        lhs = jnp.concatenate([low_ref[chunk, part] for part in range(pieces)], axis=1)
        for part in range(pieces):
            term = lax.dot_general(
                lhs, basis_ref[chunk * pieces + part], (((1,), (1,)), ((), ())), preferred_element_type=jnp.float32
            )
            found_ref[part] = term if chunk == 0 else found_ref[part] + term

    for pair_at in range(HALO // 2):
        at = 2 * pair_at
        chunk, part = pair_at // pieces, pair_at % pieces
        found = in_step([solve_steps(at), solve_steps(at + 1)])
        found = [pltpu.roll(value, LANES - 1, 1) for value in found]
        ilc_ref[at] = found[0]
        ilc_ref[at + 1] = found[1]
        near = jnp.where(low_half, found[0], pltpu.roll(found[1], HALF, 1))
        far = jnp.where(low_half, pltpu.roll(found[0], HALF, 1), found[1])
        low_ref[chunk, part] = jnp.concatenate([near, far], axis=0).astype(jnp.bfloat16)
        if part == pieces - 1:
            add_spectra(chunk)
    for group in range(groups):
        span = slice(group * width, (group + 1) * width)
        sign = 1.0 - 2.0 * odd_ref[:, span]
        part, first = group * width // share_rows, group * width % share_rows
        result = found_ref[part, :, first : first + width]
        value = (result[0:cycles] + sign * result[cycles:]).astype(jnp.bfloat16)
        for share in range(shares):
            spectra_ref[group, share] = value


def run_ilc(modes, odd, basis):
    groups, shares, rows, width = modes.shape
    chunks, depth, columns = basis.shape
    pieces = CHUNK // 2
    basis = basis.reshape(chunks * pieces, depth // pieces, columns)
    cycles = rows // C
    vmem = pl.BlockSpec(memory_space=pltpu.VMEM)
    return pl.pallas_call(
        ilc_kernel,
        in_specs=[vmem, vmem, pl.BlockSpec(memory_space=pl.ANY)],
        out_specs=[vmem, vmem],
        out_shape=[
            jax.ShapeDtypeStruct((HALO, cycles, LANES), jnp.float32),
            jax.ShapeDtypeStruct((groups, shares, cycles, width), jnp.bfloat16),
        ],
        scratch_shapes=[
            pltpu.VMEM(basis.shape, jnp.bfloat16),
            pltpu.VMEM((2 * round_up(rows, 16), depth), jnp.bfloat16),
            pltpu.VMEM((HALO, C + 1, cycles, LANES), jnp.float32),
            pltpu.VMEM((SUMS, cycles, LANES), jnp.float32),
            pltpu.VMEM((chunks, pieces, 2 * cycles, LANES), jnp.bfloat16),
            pltpu.VMEM((pieces, 2 * cycles, depth // pieces), jnp.float32),
            pltpu.SemaphoreType.DMA((chunks,)),
        ],
        cost_estimate=pl.CostEstimate(
            flops=2 * chunks * depth * columns * (2 * rows + 2 * cycles),
            bytes_accessed=chunks * depth * columns * 2,
            transcendentals=0,
        ),
        compiler_params=pltpu.CompilerParams(vmem_limit_bytes=VMEM_LIMIT),
    )(modes, odd, basis)


def modes_kernel(alm_hbm, table_hbm, out_hbm, alm_ref, table_ref, held_ref, turned_ref, out_ref, alm_sem, sems, out_sems):
    parts = sems.shape[0]
    total_slots, degrees, total = table_ref.shape
    each, slots = total_slots // parts, 4
    targets, rows = out_ref.shape[:2]
    cycles = rows // C
    height = 2 * C
    alm_copy = pltpu.make_async_copy(alm_hbm, alm_ref, alm_sem)
    alm_copy.start()
    start_parts(table_hbm, table_ref, sems, IN_FLIGHT)

    def some_slots(first):
        lhs = alm_ref[first : first + slots].reshape(slots * height, degrees)
        rhs = jnp.concatenate([table_ref[first + slot] for slot in range(slots)], axis=1)
        result = jnp.dot(lhs, rhs, preferred_element_type=jnp.float32)
        for slot in range(slots):
            own = result[slot * height : (slot + 1) * height, slot * total : (slot + 1) * total]
            for lanes in range(held_ref.shape[0]):
                span = slice((first + slot) * height, (first + slot + 1) * height)
                held_ref[lanes, span, :] = own[:, lanes * LANES : (lanes + 1) * LANES]

    def rows_of(chan):
        both = [
            jnp.concatenate(
                [
                    held_ref[lanes, pl.ds(2 * chan + part, total_slots, stride=height), :].astype(jnp.bfloat16)
                    for lanes in range(held_ref.shape[0])
                ],
                axis=1,
            )
            for part in range(2)
        ]
        return jnp.concatenate(both, axis=0)

    alm_copy.wait()
    for part in range(parts):
        next_part(table_hbm, table_ref, sems, part, IN_FLIGHT)
        for first in range(part * each, (part + 1) * each, slots):
            some_slots(first)
    one = lax.broadcasted_iota(jnp.int32, (total, total), 0) == lax.broadcasted_iota(jnp.int32, (total, total), 1)
    one = one.astype(jnp.float32).astype(jnp.bfloat16)
    width = 2 * total_slots
    together = C if width % LANES == 0 else 1
    for chan in range(0, C, together):
        rows = jnp.concatenate([rows_of(chan + at) for at in range(together)], axis=0)
        turned = lax.dot_general(one, rows, (((1,), (1,)), ((), ())), preferred_element_type=jnp.float32)
        for at in range(together):
            turned_ref[chan + at] = turned[:, at * width : (at + 1) * width]
    each = targets // out_sems.shape[0]
    for target in range(targets):
        span = slice(target * cycles, (target + 1) * cycles)
        block = jnp.concatenate([turned_ref[chan, span, :] for chan in range(C)], axis=0)
        out_ref[target] = block.astype(jnp.bfloat16)
        if (target + 1) % each == 0:
            part_copy(out_ref, out_hbm, out_sems, target // each).start()
    for part in range(out_sems.shape[0]):
        part_copy(out_ref, out_hbm, out_sems, part).wait()


def make_modes(alm, legendre, targets):
    slot_count, degrees, total = legendre.shape
    parts = slot_count // 8
    width = 2 * slot_count
    height = 2 * C
    out = jax.ShapeDtypeStruct((targets, C * (total // targets), width), jnp.bfloat16)
    return pl.pallas_call(
        modes_kernel,
        in_specs=[pl.BlockSpec(memory_space=pl.ANY)] * 2,
        out_specs=pl.BlockSpec(memory_space=pl.ANY),
        out_shape=out,
        scratch_shapes=[
            pltpu.VMEM(alm.shape, jnp.bfloat16),
            pltpu.VMEM(legendre.shape, jnp.bfloat16),
            pltpu.VMEM((total // LANES, slot_count * height, LANES), jnp.float32),
            pltpu.VMEM((C, total, width), jnp.float32),
            pltpu.VMEM(out.shape, out.dtype),
            pltpu.SemaphoreType.DMA,
            pltpu.SemaphoreType.DMA((parts,)),
            pltpu.SemaphoreType.DMA((4,)),
        ],
        cost_estimate=pl.CostEstimate(
            flops=2 * slot_count * degrees * total * 2 * C,
            bytes_accessed=slot_count * degrees * (total + 2 * C) * 2,
            transcendentals=0,
        ),
        compiler_params=pltpu.CompilerParams(vmem_limit_bytes=62 * 1024 * 1024),
    )(alm, legendre)


def analysis_kernel(table_hbm, spectra_ref, out_ref, table_ref, turned_ref, sems):
    total_slots, degrees, total = table_ref.shape
    slots = 8
    start_parts(table_hbm, table_ref, sems, IN_FLIGHT)
    turned_ref[...] = spectra_ref[...].astype(jnp.float32).T
    count = total_slots // HALVES
    for first in range(0, total_slots, slots):
        row = first // count * 2 * count + first % count
        rows = [turned_ref[row + share * count : row + share * count + slots, :] for share in range(2)]
        lhs = jnp.concatenate(rows, axis=0).astype(jnp.bfloat16)
        next_part(table_hbm, table_ref, sems, first // slots, IN_FLIGHT)
        table = table_ref[first : first + slots].reshape(slots * degrees, total)
        result = lax.dot_general(lhs, table, (((1,), (1,)), ((), ())), preferred_element_type=jnp.float32)
        for slot in range(slots):
            span = slice(slot * degrees, (slot + 1) * degrees)
            out_ref[first + slot, 0:1, :] = result[slot : slot + 1, span]
            out_ref[first + slot, 1:2, :] = result[slots + slot : slots + slot + 1, span]


def analyse(legendre, spectra):
    slot_count, degrees, total = legendre.shape
    slots = 8
    width = 2 * slot_count
    vmem = pl.BlockSpec(memory_space=pltpu.VMEM)
    return pl.pallas_call(
        analysis_kernel,
        in_specs=[pl.BlockSpec(memory_space=pl.ANY), vmem],
        out_specs=vmem,
        out_shape=jax.ShapeDtypeStruct((slot_count, 2, degrees), jnp.float32),
        scratch_shapes=[
            pltpu.VMEM(legendre.shape, jnp.bfloat16),
            pltpu.VMEM((width, total), jnp.float32),
            pltpu.SemaphoreType.DMA((slot_count // slots,)),
        ],
        cost_estimate=pl.CostEstimate(
            flops=2 * slot_count * degrees * total * 2 * slots,
            bytes_accessed=slot_count * degrees * total * 2,
            transcendentals=0,
        ),
        compiler_params=pltpu.CompilerParams(vmem_limit_bytes=50 * 1024 * 1024),
    )(legendre, spectra)


def from_other_tiles(sends):
    count = len(sends)
    got = [sends[0]]
    for hop in range(1, count):
        got.append(lax.ppermute(sends[hop], "tile", [(at, (at + hop) % count) for at in range(count)]))
    return got


def in_tile_order(got):
    count = len(got)
    tile_at = lax.axis_index("tile")
    stacked = jnp.stack(got)
    return jnp.stack(
        [lax.dynamic_index_in_dim(stacked, (tile_at - at) % count, 0, keepdims=False) for at in range(count)]
    )


def body(alm, legendre, order_of_slot):
    tile_count = lax.axis_size("tile")
    band_count = lax.axis_size("band")
    tile_at = lax.axis_index("tile")
    slot_count = alm.shape[0]
    targets = band_count * tile_count
    cycles = legendre.shape[2] // targets
    padded = round_up(cycles, 8)
    depth = 2 * L
    width = 2 * slot_count
    group_width = math.lcm(width, LANES)
    groups = depth // group_width
    plain = group_width == width and padded == cycles
    axes = ("band", "tile")

    partial = make_modes(alm, legendre, targets)
    partial = lax.all_to_all(partial, axes, split_axis=0, concat_axis=0, tiled=True)
    modes = partial.reshape(band_count, tile_count, C * cycles, width)
    if not plain:
        modes = jnp.sum(modes.astype(jnp.float32), axis=1).astype(jnp.bfloat16)
        modes = modes.reshape(groups, group_width // width, C, cycles, width)
        modes = modes.transpose(0, 2, 3, 1, 4).reshape(groups, C, cycles, group_width)
        modes = jnp.pad(modes, ((0, 0), (0, 0), (0, padded - cycles), (0, 0)))
        modes = modes.reshape(groups, 1, C * padded, group_width)

    order_rows = order_of_slot.reshape(band_count * HALVES, 1, slot_count // HALVES)
    order_rows = jnp.broadcast_to(order_rows, (band_count * HALVES, 2, slot_count // HALVES)).reshape(depth)
    basis = make_basis(order_rows.astype(jnp.float32)[:, None], slot_count)
    odd = (order_rows % 2).astype(jnp.float32)[None, :]
    vectors, spectra = run_ilc(modes, odd, basis)

    if not plain:
        spectra = spectra[:, 0, :cycles].reshape(groups, cycles, group_width // width, width)
        spectra = spectra.transpose(0, 2, 1, 3).reshape(band_count, 1, cycles, width)
        spectra = jnp.broadcast_to(spectra, (band_count, tile_count, cycles, width))
    spectra = spectra.reshape(targets, cycles, width)
    routed = lax.all_to_all(spectra, axes, split_axis=0, concat_axis=0, tiled=True)
    found = in_tile_order(from_other_tiles([vectors[:, :cycles]] * tile_count))
    lanes = LANES // tile_count
    found = lax.dynamic_slice_in_dim(found, tile_at * lanes, lanes, axis=3)
    ilc_map = found.transpose(0, 2, 3, 1).reshape(tile_count * cycles, NLON // tile_count)
    routed, ilc_map = lax.optimization_barrier((routed, ilc_map))
    ilc_alm = analyse(legendre, routed.reshape(targets * cycles, width))
    return (ilc_map, ilc_alm)


def solution(mesh):
    placed = (P("band", None, None, "tile"), P("band", "tile", None), P())
    return jax.shard_map(
        body,
        mesh=mesh,
        in_specs=placed,
        out_specs=(P("band", "tile"), P("band", None, "tile")),
        check_vma=False,
    )
```

```python
import functools
import math

import jax
import jax.numpy as jnp
from jax import lax
from jax.experimental import pallas as pl
from jax.experimental.pallas import tpu as pltpu
from jax.sharding import PartitionSpec as P

C = 9
L = 1024
NLON = 4096
HALO = 32

RIDGE = 0.1
EPSILON = 1e-06

WINDOW = 2 * HALO + 1
LANES = NLON // HALO
HALF = LANES // 2
REST = C - 1
PAIRS = [(a_at, b_at) for a_at in range(REST) for b_at in range(a_at, REST)] + [(a_at, REST) for a_at in range(REST)]
SUMS = len(PAIRS) + 1
VMEM_LIMIT = 48 * 1024 * 1024
IN_FLIGHT = 4
HALVES = 1
CHUNK = 8


def round_up(value, multiple):
    return (value + multiple - 1) // multiple * multiple


def cos_turns(turns):
    nearest = (turns + 12582912.0) - 12582912.0
    quarter = 1.0 - 4.0 * jnp.abs(turns - nearest)
    square = quarter * quarter
    tail = square * (1.6044118478736e-04 - square * 3.598843235e-06)
    tail = square * (-4.68175413531868e-03 + tail)
    tail = square * (7.96926262461670e-02 + tail)
    tail = square * (-6.45964097506246e-01 + tail)
    return quarter * (1.57079632679490 + tail)


def basis_kernel(slots, order_ref, basis_ref):
    rows = 64
    begin = pl.program_id(0) * order_ref.shape[0]
    row = lax.broadcasted_iota(jnp.int32, (rows, LANES), 0)
    lane = lax.broadcasted_iota(jnp.int32, (rows, LANES), 1)
    cell = (HALO * (lane % HALF) + lane // HALF).astype(jnp.float32) / NLON
    scaling = 1.0 / math.sqrt(L)
    for first in range(0, order_ref.shape[0], rows):
        span = slice(first, first + rows)
        part = (row + (begin + first)) // (slots // HALVES) % 2
        order = jnp.broadcast_to(order_ref[span, :], (rows, LANES))
        turns = order * cell + part.astype(jnp.float32) * 0.25
        step = order * (2.0 / NLON)
        before = cos_turns(turns) * scaling
        now = cos_turns(turns + step) * scaling
        twice = 2.0 * cos_turns(step)
        for column in range(HALO // 2):
            at = column % (CHUNK // 2) * LANES
            basis_ref[column // (CHUNK // 2), span, at : at + LANES] = before.astype(jnp.bfloat16)
            if column < HALO // 2 - 1:
                before, now = now, twice * now - before


def make_basis(order_rows, slots):
    rows = order_rows.shape[0]
    block = 256
    chunks = HALO // CHUNK
    columns = CHUNK // 2 * LANES
    return pl.pallas_call(
        functools.partial(basis_kernel, slots),
        grid=(rows // block,),
        in_specs=[pl.BlockSpec((block, 1), lambda at: (at, 0))],
        out_specs=pl.BlockSpec((chunks, block, columns), lambda at: (0, at, 0)),
        out_shape=jax.ShapeDtypeStruct((chunks, rows, columns), jnp.bfloat16),
        cost_estimate=pl.CostEstimate(
            flops=rows * chunks * columns * 8, bytes_accessed=rows * chunks * columns * 2, transcendentals=0
        ),
        compiler_params=pltpu.CompilerParams(vmem_limit_bytes=VMEM_LIMIT),
    )(order_rows)


def part_copy(source, target, sems, part):
    count = source.shape[0] // sems.shape[0]
    span = pl.ds(part * count, count)
    return pltpu.make_async_copy(source.at[span], target.at[span], sems.at[part])


def start_parts(source, target, sems, count):
    for part in range(min(count, sems.shape[0])):
        part_copy(source, target, sems, part).start()


def next_part(source, target, sems, part, ahead):
    part_copy(source, target, sems, part).wait()
    more = part + ahead < sems.shape[0]
    if isinstance(part, int):
        if more:
            part_copy(source, target, sems, part + ahead).start()
    else:

        @pl.when(more)
        def _():
            part_copy(source, target, sems, part + ahead).start()


def reciprocal(value):
    guess = pl.reciprocal(value, approx=True)
    return guess * (2.0 - value * guess)


def combine_steps(sum_of, map_of):
    ridge = RIDGE * (sum_of(SUMS - 1) * (1.0 / C) + WINDOW * EPSILON)
    upper, inverses, rights, maps = {}, [], [], []
    value = map_of(REST)
    for row in range(REST):
        ratios = [upper[at, row] * inverses[at] for at in range(row)]
        pivot = sum_of(PAIRS.index((row, row))) + (ridge + ridge)
        for at in range(row):
            pivot = pivot - ratios[at] * upper[at, row]
        inverse = reciprocal(pivot)
        yield None
        right = ridge - sum_of(PAIRS.index((row, REST)))
        own = map_of(row)
        for at in range(row):
            right = right - ratios[at] * rights[at]
            own = own - ratios[at] * maps[at]
        yield None
        for col in range(row + 1, REST):
            entry = sum_of(PAIRS.index((row, col))) + ridge
            for at in range(row):
                entry = entry - ratios[at] * upper[at, col]
            upper[row, col] = entry
            yield None
        value = value + (right * inverse) * own
        inverses.append(inverse)
        rights.append(right)
        maps.append(own)
    yield value


def in_step(generators):
    for found in zip(*generators):
        pass
    return found


def ilc_kernel(modes_ref, odd_ref, basis_hbm, ilc_ref, spectra_ref, basis_ref, lhs_ref, maps_ref, sums_ref, low_ref, found_ref, sems):
    groups, shares, rows, width = modes_ref.shape
    columns = basis_ref.shape[2]
    depth = lhs_ref.shape[1]
    pieces, share_rows = found_ref.shape[0], found_ref.shape[2]
    chunks = basis_ref.shape[0] // pieces
    cycles = rows // C
    second = round_up(rows, 16)
    start_parts(basis_hbm, basis_ref, sems, IN_FLIGHT - 1)
    for group in range(groups):
        span = slice(group * width, (group + 1) * width)
        odd = odd_ref[:, span]
        values = modes_ref[group, 0].astype(jnp.float32)
        for share in range(1, shares):
            values = values + modes_ref[group, share].astype(jnp.float32)
        lhs_ref[0:rows, span] = (values * (1.0 - odd)).astype(jnp.bfloat16)
        lhs_ref[second : second + rows, span] = (values * odd).astype(jnp.bfloat16)
    low_half = lax.broadcasted_iota(jnp.int32, (cycles, LANES), 1) < HALF
    sums_ref[...] = jnp.zeros_like(sums_ref)

    def store_maps(at, maps):
        squares = maps[0] * maps[0]
        for chan in range(1, C):
            squares = squares + maps[chan] * maps[chan]
            maps_ref[at, chan - 1] = maps[chan] - maps[0]
        maps_ref[at, REST] = maps[0]
        maps_ref[at, C] = squares

    def maps_of_chunk(chunk):
        next_part(basis_hbm, basis_ref, sems, chunk, IN_FLIGHT - 1)
        basis = basis_ref[chunk * pieces : (chunk + 1) * pieces].reshape(depth, columns)
        result = jnp.dot(lhs_ref[...], basis, preferred_element_type=jnp.float32)
        for part in range(CHUNK // 2):
            at = CHUNK * chunk + 2 * part
            lanes = slice(part * LANES, (part + 1) * LANES)
            left, right = [], []
            for chan in range(C):
                even_part = result[chan * cycles : (chan + 1) * cycles, lanes]
                odd_part = result[second + chan * cycles : second + (chan + 1) * cycles, lanes]
                near = even_part + odd_part
                far = even_part - odd_part
                left.append(jnp.where(low_half, near, pltpu.roll(far, HALF, 1)))
                right.append(jnp.where(low_half, pltpu.roll(near, HALF, 1), far))
            store_maps(at, left)
            store_maps(at + 1, right)

    def add_totals(chunk):
        vectors = [CHUNK * chunk + part for part in range(CHUNK)]
        for a_at in range(C):
            own = [maps_ref[at, a_at] for at in vectors]
            for b_at in range(a_at, C):
                if (a_at, b_at) == (REST, REST):
                    continue
                pair = PAIRS.index((a_at, b_at))
                total = sums_ref[pair]
                for at, value in zip(vectors, own):
                    total = total + value * (value if a_at == b_at else maps_ref[at, b_at])
                sums_ref[pair] = total
        total = sums_ref[SUMS - 1]
        for at in vectors:
            total = total + maps_ref[at, C]
        sums_ref[SUMS - 1] = total

    maps_of_chunk(0)
    for chunk in range(1, chunks):
        maps_of_chunk(chunk)
        add_totals(chunk - 1)
    add_totals(chunks - 1)
    for pair in range(SUMS):
        total = sums_ref[pair]
        sums_ref[pair] = pltpu.roll(total, 1, 1) + pltpu.roll(total, 2, 1)

    def solve_steps(at):
        maps = [maps_ref[at, chan] for chan in range(C + 1)]

        def sum_of(pair):
            own = maps[C] if pair == SUMS - 1 else maps[PAIRS[pair][0]] * maps[PAIRS[pair][1]]
            total = sums_ref[pair] + own
            sums_ref[pair] = total - pltpu.roll(own, 2, 1)
            return total

        return combine_steps(sum_of, lambda chan: pltpu.roll(maps[chan], 1, 1))

    def add_spectra(chunk):
        lhs = jnp.concatenate([low_ref[chunk, part] for part in range(pieces)], axis=1)
        for part in range(pieces):
            term = lax.dot_general(
                lhs, basis_ref[chunk * pieces + part], (((1,), (1,)), ((), ())), preferred_element_type=jnp.float32
            )
            found_ref[part] = term if chunk == 0 else found_ref[part] + term

    for pair_at in range(HALO // 2):
        at = 2 * pair_at
        chunk, part = pair_at // pieces, pair_at % pieces
        found = in_step([solve_steps(at), solve_steps(at + 1)])
        found = [pltpu.roll(value, LANES - 1, 1) for value in found]
        ilc_ref[at] = found[0]
        ilc_ref[at + 1] = found[1]
        near = jnp.where(low_half, found[0], pltpu.roll(found[1], HALF, 1))
        far = jnp.where(low_half, pltpu.roll(found[0], HALF, 1), found[1])
        low_ref[chunk, part] = jnp.concatenate([near, far], axis=0).astype(jnp.bfloat16)
        if part == pieces - 1:
            add_spectra(chunk)
    for group in range(groups):
        span = slice(group * width, (group + 1) * width)
        sign = 1.0 - 2.0 * odd_ref[:, span]
        part, first = group * width // share_rows, group * width % share_rows
        result = found_ref[part, :, first : first + width]
        value = (result[0:cycles] + sign * result[cycles:]).astype(jnp.bfloat16)
        for share in range(shares):
            spectra_ref[group, share] = value


def run_ilc(modes, odd, basis):
    groups, shares, rows, width = modes.shape
    chunks, depth, columns = basis.shape
    pieces = CHUNK // 2
    basis = basis.reshape(chunks * pieces, depth // pieces, columns)
    cycles = rows // C
    vmem = pl.BlockSpec(memory_space=pltpu.VMEM)
    return pl.pallas_call(
        ilc_kernel,
        in_specs=[vmem, vmem, pl.BlockSpec(memory_space=pl.ANY)],
        out_specs=[vmem, vmem],
        out_shape=[
            jax.ShapeDtypeStruct((HALO, cycles, LANES), jnp.float32),
            jax.ShapeDtypeStruct((groups, shares, cycles, width), jnp.bfloat16),
        ],
        scratch_shapes=[
            pltpu.VMEM(basis.shape, jnp.bfloat16),
            pltpu.VMEM((2 * round_up(rows, 16), depth), jnp.bfloat16),
            pltpu.VMEM((HALO, C + 1, cycles, LANES), jnp.float32),
            pltpu.VMEM((SUMS, cycles, LANES), jnp.float32),
            pltpu.VMEM((chunks, pieces, 2 * cycles, LANES), jnp.bfloat16),
            pltpu.VMEM((pieces, 2 * cycles, depth // pieces), jnp.float32),
            pltpu.SemaphoreType.DMA((chunks,)),
        ],
        cost_estimate=pl.CostEstimate(
            flops=2 * chunks * depth * columns * (2 * rows + 2 * cycles),
            bytes_accessed=chunks * depth * columns * 2,
            transcendentals=0,
        ),
        compiler_params=pltpu.CompilerParams(vmem_limit_bytes=VMEM_LIMIT),
    )(modes, odd, basis)


def modes_kernel(alm_hbm, table_hbm, out_hbm, alm_ref, table_ref, held_ref, out_ref, alm_sem, sems, out_sems):
    parts = sems.shape[0]
    total_slots, degrees, total = table_ref.shape
    each, slots = total_slots // parts, 4
    targets, rows = out_ref.shape[:2]
    cycles = rows // C
    height = 2 * C
    alm_copy = pltpu.make_async_copy(alm_hbm, alm_ref, alm_sem)
    alm_copy.start()
    start_parts(table_hbm, table_ref, sems, IN_FLIGHT)

    def some_slots(first):
        lhs = alm_ref[first : first + slots].reshape(slots * height, degrees)
        rhs = jnp.concatenate([table_ref[first + slot] for slot in range(slots)], axis=1)
        result = jnp.dot(lhs, rhs, preferred_element_type=jnp.float32)
        for slot in range(slots):
            own = result[slot * height : (slot + 1) * height, slot * total : (slot + 1) * total]
            for lanes in range(held_ref.shape[0]):
                span = slice((first + slot) * height, (first + slot + 1) * height)
                held_ref[lanes, span, :] = own[:, lanes * LANES : (lanes + 1) * LANES]

    def rows_of(chan):
        both = [
            jnp.concatenate(
                [
                    held_ref[lanes, pl.ds(2 * chan + part, total_slots, stride=height), :].astype(jnp.bfloat16)
                    for lanes in range(held_ref.shape[0])
                ],
                axis=1,
            )
            for part in range(2)
        ]
        return jnp.concatenate(both, axis=0)

    alm_copy.wait()
    for part in range(parts):
        next_part(table_hbm, table_ref, sems, part, IN_FLIGHT)
        for first in range(part * each, (part + 1) * each, slots):
            some_slots(first)
    one = lax.broadcasted_iota(jnp.int32, (total, total), 0) == lax.broadcasted_iota(jnp.int32, (total, total), 1)
    one = one.astype(jnp.float32).astype(jnp.bfloat16)
    width = 2 * total_slots
    together = C if width % LANES == 0 else 1
    turned = []
    for chan in range(0, C, together):
        rows = jnp.concatenate([rows_of(chan + at) for at in range(together)], axis=0)
        both = lax.dot_general(one, rows, (((1,), (1,)), ((), ())), preferred_element_type=jnp.float32)
        turned += [both[:, at * width : (at + 1) * width] for at in range(together)]
    each = targets // out_sems.shape[0]
    for target in range(targets):
        span = slice(target * cycles, (target + 1) * cycles)
        block = jnp.concatenate([turned[chan][span] for chan in range(C)], axis=0)
        out_ref[target] = block.astype(jnp.bfloat16)
        if (target + 1) % each == 0:
            part_copy(out_ref, out_hbm, out_sems, target // each).start()
    for part in range(out_sems.shape[0]):
        part_copy(out_ref, out_hbm, out_sems, part).wait()


def make_modes(alm, legendre, targets):
    slot_count, degrees, total = legendre.shape
    parts = slot_count // 8
    width = 2 * slot_count
    height = 2 * C
    out = jax.ShapeDtypeStruct((targets, C * (total // targets), width), jnp.bfloat16)
    return pl.pallas_call(
        modes_kernel,
        in_specs=[pl.BlockSpec(memory_space=pl.ANY)] * 2,
        out_specs=pl.BlockSpec(memory_space=pl.ANY),
        out_shape=out,
        scratch_shapes=[
            pltpu.VMEM(alm.shape, jnp.bfloat16),
            pltpu.VMEM(legendre.shape, jnp.bfloat16),
            pltpu.VMEM((total // LANES, slot_count * height, LANES), jnp.float32),
            pltpu.VMEM(out.shape, out.dtype),
            pltpu.SemaphoreType.DMA,
            pltpu.SemaphoreType.DMA((parts,)),
            pltpu.SemaphoreType.DMA((4,)),
        ],
        cost_estimate=pl.CostEstimate(
            flops=2 * slot_count * degrees * total * 2 * C,
            bytes_accessed=slot_count * degrees * (total + 2 * C) * 2,
            transcendentals=0,
        ),
        compiler_params=pltpu.CompilerParams(vmem_limit_bytes=62 * 1024 * 1024),
    )(alm, legendre)


def analysis_kernel(table_hbm, spectra_ref, out_ref, table_ref, turned_ref, sems):
    total_slots, degrees, total = table_ref.shape
    slots = 8
    start_parts(table_hbm, table_ref, sems, IN_FLIGHT)
    turned_ref[...] = spectra_ref[...].astype(jnp.float32).T
    count = total_slots // HALVES
    for first in range(0, total_slots, slots):
        row = first // count * 2 * count + first % count
        rows = [turned_ref[row + share * count : row + share * count + slots, :] for share in range(2)]
        lhs = jnp.concatenate(rows, axis=0).astype(jnp.bfloat16)
        next_part(table_hbm, table_ref, sems, first // slots, IN_FLIGHT)
        table = table_ref[first : first + slots].reshape(slots * degrees, total)
        result = lax.dot_general(lhs, table, (((1,), (1,)), ((), ())), preferred_element_type=jnp.float32)
        for slot in range(slots):
            span = slice(slot * degrees, (slot + 1) * degrees)
            out_ref[first + slot, 0:1, :] = result[slot : slot + 1, span]
            out_ref[first + slot, 1:2, :] = result[slots + slot : slots + slot + 1, span]


def analyse(legendre, spectra):
    slot_count, degrees, total = legendre.shape
    slots = 8
    width = 2 * slot_count
    vmem = pl.BlockSpec(memory_space=pltpu.VMEM)
    return pl.pallas_call(
        analysis_kernel,
        in_specs=[pl.BlockSpec(memory_space=pl.ANY), vmem],
        out_specs=vmem,
        out_shape=jax.ShapeDtypeStruct((slot_count, 2, degrees), jnp.float32),
        scratch_shapes=[
            pltpu.VMEM(legendre.shape, jnp.bfloat16),
            pltpu.VMEM((width, total), jnp.float32),
            pltpu.SemaphoreType.DMA((slot_count // slots,)),
        ],
        cost_estimate=pl.CostEstimate(
            flops=2 * slot_count * degrees * total * 2 * slots,
            bytes_accessed=slot_count * degrees * total * 2,
            transcendentals=0,
        ),
        compiler_params=pltpu.CompilerParams(vmem_limit_bytes=50 * 1024 * 1024),
    )(legendre, spectra)


def from_other_tiles(sends):
    count = len(sends)
    got = [sends[0]]
    for hop in range(1, count):
        got.append(lax.ppermute(sends[hop], "tile", [(at, (at + hop) % count) for at in range(count)]))
    return got


def in_tile_order(got):
    count = len(got)
    tile_at = lax.axis_index("tile")
    stacked = jnp.stack(got)
    return jnp.stack(
        [lax.dynamic_index_in_dim(stacked, (tile_at - at) % count, 0, keepdims=False) for at in range(count)]
    )


def body(alm, legendre, order_of_slot):
    tile_count = lax.axis_size("tile")
    band_count = lax.axis_size("band")
    tile_at = lax.axis_index("tile")
    slot_count = alm.shape[0]
    targets = band_count * tile_count
    cycles = legendre.shape[2] // targets
    padded = round_up(cycles, 8)
    depth = 2 * L
    width = 2 * slot_count
    group_width = math.lcm(width, LANES)
    groups = depth // group_width
    plain = group_width == width and padded == cycles
    axes = ("band", "tile")

    partial = make_modes(alm, legendre, targets)
    partial = lax.all_to_all(partial, axes, split_axis=0, concat_axis=0, tiled=True)
    modes = partial.reshape(band_count, tile_count, C * cycles, width)
    if not plain:
        modes = jnp.sum(modes.astype(jnp.float32), axis=1).astype(jnp.bfloat16)
        modes = modes.reshape(groups, group_width // width, C, cycles, width)
        modes = modes.transpose(0, 2, 3, 1, 4).reshape(groups, C, cycles, group_width)
        modes = jnp.pad(modes, ((0, 0), (0, 0), (0, padded - cycles), (0, 0)))
        modes = modes.reshape(groups, 1, C * padded, group_width)

    order_rows = order_of_slot.reshape(band_count * HALVES, 1, slot_count // HALVES)
    order_rows = jnp.broadcast_to(order_rows, (band_count * HALVES, 2, slot_count // HALVES)).reshape(depth)
    basis = make_basis(order_rows.astype(jnp.float32)[:, None], slot_count)
    odd = (order_rows % 2).astype(jnp.float32)[None, :]
    vectors, spectra = run_ilc(modes, odd, basis)

    if not plain:
        spectra = spectra[:, 0, :cycles].reshape(groups, cycles, group_width // width, width)
        spectra = spectra.transpose(0, 2, 1, 3).reshape(band_count, 1, cycles, width)
        spectra = jnp.broadcast_to(spectra, (band_count, tile_count, cycles, width))
    spectra = spectra.reshape(targets, cycles, width)
    routed = lax.all_to_all(spectra, axes, split_axis=0, concat_axis=0, tiled=True)
    found = in_tile_order(from_other_tiles([vectors[:, :cycles]] * tile_count))
    lanes = LANES // tile_count
    found = lax.dynamic_slice_in_dim(found, tile_at * lanes, lanes, axis=3)
    ilc_map = found.transpose(0, 2, 3, 1).reshape(tile_count * cycles, NLON // tile_count)
    routed, ilc_map = lax.optimization_barrier((routed, ilc_map))
    ilc_alm = analyse(legendre, routed.reshape(targets * cycles, width))
    return (ilc_map, ilc_alm)


def solution(mesh):
    placed = (P("band", None, None, "tile"), P("band", "tile", None), P())
    return jax.shard_map(
        body,
        mesh=mesh,
        in_specs=placed,
        out_specs=(P("band", "tile"), P("band", None, "tile")),
        check_vma=False,
    )
```
